32 devices in a mesh: dp: 8 (over z, x), tp: 4 (over y, core).
Axes of the slice: x: 2, y: 2, z: 4, core: 2. Of those that a mesh axis runs over, the one named last changes fastest.
Arguments:
- embeddings: bfloat16 [128, 56, 1536], P('dp'), may hold values from -6 to 6
- samples: int32 [128, 56, 32], P('dp'), may hold values from 0 to 31
- seq_lengths: int32 [128], P('dp'), may hold values from 10 to 56, as said below
- gru_weight: float32 [3, 2048, 1024], P(None, None, 'tp'), may hold values from -0.375 to 0.375
- post_weight: float32 [2560, 1024], P(None, 'tp'), may hold values from -0.25 to 0.25
- prior_weight: float32 [1024, 1024], P(None, 'tp'), may hold values from -0.75 to 0.75
- gru_moment: float32 [3, 2048, 1024], P(None, None, 'tp'), may hold values from -0.009765625 to 0.009765625
- post_moment: float32 [2560, 1024], P(None, 'tp'), may hold values from -0.009765625 to 0.009765625
- prior_moment: float32 [1024, 1024], P(None, 'tp'), may hold values from -0.009765625 to 0.009765625
Outputs:
- loss_value: float32 [], replicated
- embed_grad: float32 [128, 56, 1536], P('dp', None, 'tp')
- new_gru: float32 [3, 2048, 1024], P(None, 'dp', 'tp')
- new_post: float32 [2560, 1024], P('dp', 'tp')
- new_prior: float32 [1024, 1024], P('dp', 'tp')
- new_gru_moment: float32 [3, 2048, 1024], P(None, 'dp', 'tp')
- new_post_moment: float32 [2560, 1024], P('dp', 'tp')
- new_prior_moment: float32 [1024, 1024], P('dp', 'tp')
The draws below stay inside these ranges and needn't reach their ends.
Inputs may be any that keep to these rules, and one draw needn't show every extreme that they name: `seq_lengths`: the frames of a sequence at positions below its count are true frames, the rest are padding; the sequences of every index of dp include one with exactly 56, and some sequence has exactly 56 // 6 + 1.
All inputs are finite; a program needn't handle non-finite values.
Results may differ from the reference program's by a relative error of at most 0.025.
Values may be sent and summed in bfloat16 or wider, within the bound.
No kernel may reach another device: no remote copies, remote signals or barrier semaphores. Data moves between devices by JAX's collectives and lax.ppermute only.
A program may use at most 192 MiB of HBM per device.

```python
import math
import jax
import jax.numpy as jnp
from jax import lax

H = 1024
ZG = 32
ZC = 32
E = 1536
SEQ_DEV = 16
FRAMES = 56
Z = 1024
SEQS = 128
N_DP = 8


def draw_seq_lengths(key, part):
    key = jax.random.fold_in(key, 11)
    key_spread, key_full, key_short = jax.random.split(key, 3)
    device_count = SEQS // SEQ_DEV
    device_of = jnp.arange(SEQS, dtype=jnp.int32) // SEQ_DEV
    shortest = FRAMES // 6 + 1
    lowest = shortest + (FRAMES * 3 // 4 - shortest) * device_of // max(device_count - 1, 1)
    spread = jax.random.randint(key_spread, (SEQS,), 0, FRAMES // 4 + 1)
    lengths = jnp.minimum(lowest + spread, FRAMES)
    full_slot = jax.random.randint(key_full, (device_count,), 0, SEQ_DEV)
    full_index = jnp.arange(device_count, dtype=jnp.int32) * SEQ_DEV + full_slot
    lengths = lengths.at[full_index].set(FRAMES)
    short_slot = (full_slot[0] + 1 + jax.random.randint(key_short, (), 0, SEQ_DEV - 1)) % SEQ_DEV
    lengths = lengths.at[short_slot].set(shortest)
    return lengths.astype(jnp.int32)


def with_ends(array, key, low, largest):
    longest = array.shape.index(max(array.shape))
    spots = []
    for shift in (0, 1):
        where = [jax.random.randint(jax.random.fold_in(key, axis), (), 0, length) for axis, length in enumerate(array.shape)]
        where[longest] = (where[longest] + shift) % array.shape[longest]
        spots.append(tuple(where))
    return array.at[spots[0]].set(low).at[spots[1]].set(largest)


def block_levels(stream_key, extent, cuts, least, top_value):
    def one(position, blocks):
        steps = jax.random.uniform(jax.random.fold_in(jax.random.fold_in(stream_key, 6), position), (blocks,), jnp.float32, least / len(cuts), top_value / len(cuts))
        return jnp.repeat(jnp.exp(steps), extent[position] // blocks).reshape((-1,) + (1,) * (len(extent) - position - 1))

    loudness = one(*cuts[0])
    for cut in cuts[1:]:
        loudness = loudness * one(*cut)
    return loudness


def scatter_about(key, shape, width, bound, cuts=(), kind=jnp.bfloat16):
    drawn = jax.random.normal(key, shape, jnp.float32) * width
    if len(cuts) > 0:
        drawn = block_levels(key, shape, cuts, -0.22, 0.18) * drawn
    return jnp.clip(drawn, min=-bound, max=bound).astype(kind)


def setup_inputs(seed: int = 0) -> dict:
    key_list = jax.random.split(jax.random.key(seed), 10)
    embeddings = scatter_about(key_list[0], (SEQS, FRAMES, E), 1.0, 6.0, ((0, 8),))
    samples = with_ends(jax.random.randint(key_list[1], (SEQS, FRAMES, ZG), 0, ZC), jax.random.fold_in(key_list[1], 1), 0, ZC - 1).astype(jnp.int32)
    seq_lengths = draw_seq_lengths(jax.random.fold_in(key_list[9], 71), 0)
    gru_weight = scatter_about(key_list[3], (3, Z + H, H), (H // 4) ** -0.5, 0.375, ((2, 4),), jnp.float32)
    post_weight = scatter_about(key_list[4], (H + E, Z), ((H + E) // 4) ** -0.5, 0.25, ((1, 4),), jnp.float32)
    prior_weight = scatter_about(key_list[5], (H, Z), (H // 16) ** -0.5, 0.75, ((1, 4),), jnp.float32)
    gru_moment = scatter_about(key_list[6], (3, Z + H, H), (0.15 / (SEQ_DEV * N_DP * FRAMES) ** 0.5), 0.009765625, ((2, 4),), jnp.float32)
    post_moment = scatter_about(key_list[7], (H + E, Z), (0.15 / (SEQ_DEV * N_DP * FRAMES) ** 0.5), 0.009765625, ((1, 4),), jnp.float32)
    prior_moment = scatter_about(key_list[8], (H, Z), (0.15 / (SEQ_DEV * N_DP * FRAMES) ** 0.5), 0.009765625, ((1, 4),), jnp.float32)
    return dict(embeddings=embeddings, samples=samples, seq_lengths=seq_lengths, gru_weight=gru_weight, post_weight=post_weight, prior_weight=prior_weight, gru_moment=gru_moment, post_moment=post_moment, prior_moment=prior_moment)


@jax.custom_vjp
def low(v):
    return lax.optimization_barrier(v.astype(jnp.bfloat16)).astype(jnp.float32)

@jax.custom_vjp
def low_back(v):
    return v

def low_keep(v):
    return (low(v), None)

def low_pass(kept, grad):
    return (grad,)

def back_keep(v):
    return (v, None)

def back_low(kept, grad):
    return (low(grad),)
low.defvjp(low_keep, low_pass)
low_back.defvjp(back_keep, back_low)
coeff_linear = 3.4445
coeff_cubic = -4.775
coeff_quintic = 2.0315
momentum_keep = 0.95
learn_rate = 0.2
weight_decay = 0.01
update_scale = 0.2
tiny_value = 1e-07

def dot_high(left_side, right_side):
    return jnp.dot(left_side, right_side, precision=lax.Precision.HIGHEST)

def cross_entropy(logits, target):
    grouped = logits.reshape(logits.shape[0], ZG, ZC)
    return lax.optimization_barrier(jnp.sum(jax.nn.logsumexp(grouped, axis=-1) - lax.optimization_barrier(jnp.sum(grouped * target, axis=-1)), axis=-1))

def orthogonal(matrix):
    row_count, col_count = matrix.shape
    values = matrix.astype(jnp.float32)
    if row_count > col_count:
        values = values.T
    current = (values / (jnp.sqrt(jnp.sum(values * values)) + tiny_value)).astype(jnp.bfloat16)
    for sweep_index in range(5):
        square = lax.dot_general(current, current, (((1,), (1,)), ((), ())), preferred_element_type=jnp.float32).astype(jnp.bfloat16)
        mixture = (coeff_cubic * square.astype(jnp.float32) + coeff_quintic * jnp.dot(square, square, preferred_element_type=jnp.float32)).astype(jnp.bfloat16)
        current = (coeff_linear * current.astype(jnp.float32) + jnp.dot(mixture, current, preferred_element_type=jnp.float32)).astype(jnp.bfloat16)
    result = current.astype(jnp.float32)
    if row_count > col_count:
        result = result.T
    return result

def muon_step(weight, gradient, moment_new):
    preview = (gradient + momentum_keep * moment_new).astype(jnp.bfloat16)
    row_count, col_count = weight.shape
    return weight * (1.0 - learn_rate * weight_decay) - learn_rate * update_scale * math.sqrt(max(row_count, col_count)) * orthogonal(preview)

def reference(embeddings, samples, seq_lengths, gru_weight, post_weight, prior_weight, gru_moment, post_moment, prior_moment):
    positions = jnp.arange(FRAMES, dtype=jnp.int32)
    frame_mask = (positions[None, :] < seq_lengths[:, None]).astype(jnp.float32)
    frame_count = jnp.sum(frame_mask)
    targets = jax.nn.one_hot(samples, ZC, dtype=jnp.float32)
    flattened = targets.reshape(SEQS, FRAMES, Z)
    inputs = jnp.concatenate([jnp.zeros((SEQS, 1, Z), jnp.float32), flattened[:, :-1]], axis=1)
    input_time = jnp.swapaxes(inputs, 0, 1)
    target_time = jnp.swapaxes(targets, 0, 1)
    mask_time = jnp.swapaxes(frame_mask, 0, 1)

    def forward(gru_full, post_full, prior_full, embed_full):
        gru_low = low(gru_full)
        post_low = low(post_full)
        prior_low = low(prior_full)
        embed_time = jnp.swapaxes(embed_full, 0, 1)

        @jax.checkpoint
        def advance(carry, frame_slab):
            hidden_state, state_low, loss_sum = carry
            step_input, step_embed, step_target, step_mask = frame_slab
            preact = jnp.stack([dot_high(step_input, gru_low[gate_index, :Z]) + dot_high(state_low, gru_low[gate_index, Z:]) for gate_index in range(3)])
            preact = low_back(preact)
            reset_gate = jax.nn.sigmoid(preact[0])
            candidate = jnp.tanh(reset_gate * preact[1])
            update = jax.nn.sigmoid(preact[2] - 1.0)
            hidden_state = update * candidate + (1.0 - update) * hidden_state
            state_low = low(hidden_state)
            prior_logits = low_back(dot_high(state_low, prior_low))
            post_logits = low_back(dot_high(state_low, post_low[:H]) + dot_high(step_embed, post_low[H:]))
            frame_loss = cross_entropy(prior_logits, step_target) + cross_entropy(post_logits, step_target)
            loss_sum = loss_sum + jnp.sum(step_mask * frame_loss)
            return ((hidden_state, state_low, loss_sum), None)
        start_carry = (jnp.zeros((SEQS, H), jnp.float32), jnp.zeros((SEQS, H), jnp.float32), jnp.zeros((), jnp.float32))
        final_carry, unused = lax.scan(advance, start_carry, (input_time, embed_time, target_time, mask_time))
        return final_carry[2] / frame_count
    loss_value, pullback = jax.vjp(forward, gru_weight, post_weight, prior_weight, embeddings.astype(jnp.float32))
    gru_grad, post_grad, prior_grad, embed_grad = pullback(jnp.ones((), jnp.float32))
    new_gru_moment = momentum_keep * gru_moment + gru_grad
    new_post_moment = momentum_keep * post_moment + post_grad
    new_prior_moment = momentum_keep * prior_moment + prior_grad
    new_gru = jnp.stack([muon_step(gru_weight[gate_index], gru_grad[gate_index], new_gru_moment[gate_index]) for gate_index in range(3)])
    new_post = muon_step(post_weight, post_grad, new_post_moment)
    new_prior = muon_step(prior_weight, prior_grad, new_prior_moment)
    return (loss_value, embed_grad, new_gru, new_post, new_prior, new_gru_moment, new_post_moment, new_prior_moment)
```

```python
import functools
import math

import jax
import jax.numpy as jnp
from jax import lax
from jax.experimental import pallas as pl
from jax.experimental.pallas import tpu as pltpu
from jax.sharding import PartitionSpec as P

H = 1024
ZC = 32
E = 1536
FRAMES = 56
MATS = 5
Z = 1024
ROWS = (Z + H, Z + H, Z + H, H + E, H)


coeff_linear = 3.4445
coeff_cubic = -4.775
coeff_quintic = 2.0315
momentum_keep = 0.95
learn_rate = 0.2
weight_decay = 0.01
update_scale = 0.2
tiny_value = 1e-07
mib = 1 << 20


def scan_forward(x_ref, w_ref, h_ref, k_ref, u_ref, state):
    parts, frames, seqs = x_ref.shape[:3]
    units = w_ref.shape[3]
    state[...] = jnp.zeros_like(state)

    def step(t, carry):
        low = state[...].astype(jnp.bfloat16)
        for p in range(parts):
            cols = slice(p * units, (p + 1) * units)
            pre = [
                x_ref[p, t, :, k * units : (k + 1) * units]
                + jnp.dot(low, w_ref[p, k], preferred_element_type=jnp.float32)
                for k in range(3)
            ]
            last = h_ref[jnp.maximum(t - 1, 0), :, cols] * jnp.where(t > 0, 1.0, 0.0)
            r = jax.nn.sigmoid(pre[0])
            c = jnp.tanh(r * pre[1])
            u = jax.nn.sigmoid(pre[2] - 1.0)
            rest = 1.0 - u
            new = u * c + rest * last
            inner = u * (1.0 - c * c)
            h_ref[t, :, cols] = new
            state[:, cols] = new
            k_ref[0, t, :, cols] = inner * pre[1] * r * (1.0 - r)
            k_ref[1, t, :, cols] = inner * r
            k_ref[2, t, :, cols] = (c - last) * u * rest
            u_ref[t, :, cols] = rest
        return carry

    lax.fori_loop(0, frames, step, 0)


def scan_backward(d_ref, k_ref, u_ref, w_ref, b_ref, low, kept):
    parts, frames, seqs = b_ref.shape[:3]
    units = b_ref.shape[3] // 3
    low[...] = jnp.zeros_like(low)
    kept[...] = jnp.zeros_like(kept)

    def step(i, carry):
        t = frames - 1 - i
        dh = d_ref[t] + kept[...] + jnp.dot(low[...], w_ref[...], preferred_element_type=jnp.float32)
        kept[...] = dh * u_ref[t]
        for p in range(parts):
            for k in range(3):
                cols = slice(p * units, (p + 1) * units)
                back = (dh[:, cols] * k_ref[k, t, :, cols]).astype(jnp.bfloat16)
                spot = slice((3 * p + k) * units, (3 * p + k + 1) * units)
                low[:, spot] = back
                b_ref[p, t, :, k * units : (k + 1) * units] = back.astype(jnp.float32)
        return carry

    lax.fori_loop(0, frames, step, 0)


def whole(count):
    return [pl.BlockSpec(memory_space=pltpu.VMEM)] * count


def run_forward(inputs, weights):
    parts, frames, seqs = inputs.shape[:3]
    out = jax.ShapeDtypeStruct((frames, seqs, H), jnp.float32)
    return pl.pallas_call(
        scan_forward,
        out_shape=[out, jax.ShapeDtypeStruct((3, frames, seqs, H), jnp.float32), out],
        in_specs=whole(2),
        out_specs=whole(3),
        scratch_shapes=[pltpu.VMEM((seqs, H), jnp.float32)],
        compiler_params=pltpu.CompilerParams(vmem_limit_bytes=40 * mib),
        cost_estimate=pl.CostEstimate(
            flops=2 * frames * 256 * H * 3 * H, bytes_accessed=20 * mib, transcendentals=0
        ),
        name="scan_forward",
    )(inputs, weights)


def run_backward(direct, factors, rest, weights, parts):
    frames, seqs = direct.shape[:2]
    return pl.pallas_call(
        scan_backward,
        out_shape=jax.ShapeDtypeStruct((parts, frames, seqs, 3 * H // parts), jnp.float32),
        in_specs=whole(4),
        out_specs=whole(1)[0],
        scratch_shapes=[
            pltpu.VMEM((seqs, 3 * H), jnp.bfloat16),
            pltpu.VMEM((seqs, H), jnp.float32),
        ],
        compiler_params=pltpu.CompilerParams(vmem_limit_bytes=40 * mib),
        cost_estimate=pl.CostEstimate(
            flops=2 * frames * 256 * H * 3 * H, bytes_accessed=20 * mib, transcendentals=0
        ),
        name="scan_backward",
    )(direct, factors, rest, weights)


def orthogonal_wide(matrix, own, share):
    values = matrix.astype(jnp.float32)
    current = (values / (jnp.sqrt(jnp.sum(values * values)) + tiny_value)).astype(jnp.bfloat16)
    for sweep_index in range(5):
        square = lax.dot_general(
            current, current, (((1,), (1,)), ((), ())), preferred_element_type=jnp.float32
        ).astype(jnp.bfloat16)
        mixture = (
            coeff_cubic * square.astype(jnp.float32)
            + coeff_quintic * jnp.dot(square, square, preferred_element_type=jnp.float32)
        ).astype(jnp.bfloat16)
        kept = current
        if sweep_index == 4:
            mixture = lax.dynamic_slice_in_dim(mixture, own * share, share, 0)
            kept = lax.dynamic_slice_in_dim(current, own * share, share, 0)
        current = (
            coeff_linear * kept.astype(jnp.float32)
            + jnp.dot(mixture, current, preferred_element_type=jnp.float32)
        ).astype(jnp.bfloat16)
    return current


def on_device(
    embeddings,
    samples,
    seq_lengths,
    gru_weight,
    post_weight,
    prior_weight,
    gru_moment,
    post_moment,
    prior_moment,
):
    dp_count = lax.axis_size("dp")
    tp_count = lax.axis_size("tp")
    dp_index = lax.axis_index("dp")
    tp_index = lax.axis_index("tp")
    seq_count = embeddings.shape[0]
    seqs = seq_count // tp_count
    units = gru_weight.shape[2]
    groups = Z // ZC
    f32 = jnp.float32
    bf16 = jnp.bfloat16

    def gather(block):
        return lax.all_gather(block, "tp", axis=0, tiled=False)

    def exchange(block, axis):
        return lax.all_to_all(block, axis, 0, 0, tiled=True)

    gru_low = gru_weight.astype(bf16)
    weights = gather(gru_low[:, Z:])
    turned = gather(jnp.swapaxes(gru_low[:, Z:], 1, 2).reshape(3 * units, H))
    turned = turned.reshape(tp_count * 3 * units, H)
    post_full = jnp.concatenate(list(gather(post_weight.astype(bf16))), axis=1)
    prior_full = jnp.concatenate(list(gather(prior_weight.astype(bf16))), axis=1)

    positions = jnp.arange(FRAMES, dtype=jnp.int32)
    frame_count = lax.psum(
        jnp.sum((positions[:, None] < seq_lengths[None, :]).astype(f32)), "dp"
    )
    own_lengths = lax.dynamic_slice_in_dim(seq_lengths, tp_index * seqs, seqs, 0)
    frame_mask = (positions[:, None] < own_lengths[None, :]).astype(f32)
    classes = jnp.arange(ZC, dtype=jnp.int32)
    by_part = jnp.swapaxes(samples.reshape(tp_count, seqs, FRAMES, groups), 1, 2)
    onehot = (by_part[..., None] == classes).astype(bf16).reshape(tp_count, FRAMES, seqs, Z)
    input_part = jnp.einsum(
        "pfsz,kzj->pfskj", onehot[:, :-1], gru_low[:, :Z], preferred_element_type=f32
    ).reshape(tp_count, FRAMES - 1, seqs, 3 * units)
    input_part = jnp.pad(exchange(input_part, "tp"), ((0, 0), (1, 0), (0, 0), (0, 0)))

    hidden, factors, rest = run_forward(input_part, weights)
    hidden_low = hidden.astype(bf16)

    own_embed = lax.dynamic_slice_in_dim(embeddings, tp_index * seqs, seqs, 0)
    own_samples = lax.dynamic_index_in_dim(by_part, tp_index, 0, keepdims=False)
    target = (own_samples[..., None] == classes).astype(f32)
    prior_logits = jnp.einsum("fsh,hk->fsk", hidden_low, prior_full, preferred_element_type=f32)
    post_logits = jnp.einsum("fsh,hk->fsk", hidden_low, post_full[:H], preferred_element_type=f32)
    post_logits = post_logits + jnp.einsum(
        "sfe,ek->fsk", own_embed, post_full[H:], preferred_element_type=f32
    )

    def head_terms(logits):
        grouped = logits.reshape(FRAMES, seqs, groups, ZC)
        normalizer = jax.nn.logsumexp(grouped, axis=-1)
        losses = jnp.sum(normalizer - jnp.sum(grouped * target, axis=-1), axis=-1)
        probs = jnp.exp(grouped - normalizer[..., None])
        return (jnp.sum(frame_mask * losses), probs - target)

    prior_loss, prior_delta = head_terms(prior_logits)
    post_loss, post_delta = head_terms(post_logits)
    weighting = frame_mask[:, :, None, None] / frame_count
    prior_back = (prior_delta * weighting).astype(bf16).reshape(FRAMES, seqs, Z)
    post_back = (post_delta * weighting).astype(bf16).reshape(FRAMES, seqs, Z)
    direct = jnp.einsum("fsk,hk->fsh", prior_back, prior_full, preferred_element_type=f32)
    direct = direct + jnp.einsum(
        "fsk,hk->fsh", post_back, post_full[:H], preferred_element_type=f32
    )
    loss_value = lax.psum(prior_loss + post_loss, ("dp", "tp")) / frame_count

    all_hidden = gather(hidden_low)
    all_prior = gather(prior_back)
    all_post = gather(post_back)

    back = run_backward(direct, factors, rest, turned, tp_count).astype(bf16)

    own_rows_e = lax.dynamic_slice_in_dim(post_full, H + tp_index * (E // tp_count), E // tp_count, 0)
    embed_grad = jnp.einsum(
        "psfk,ek->psfe", jnp.swapaxes(all_post, 1, 2), own_rows_e, preferred_element_type=f32
    ).reshape(seq_count, FRAMES, E // tp_count)

    own_prior = lax.dynamic_slice_in_dim(all_prior, tp_index * units, units, 3)
    own_post = lax.dynamic_slice_in_dim(all_post, tp_index * units, units, 3)
    prior_grad = jnp.einsum("pfsh,pfsk->hk", all_hidden, own_prior, preferred_element_type=f32)
    post_grad = jnp.concatenate(
        [
            jnp.einsum("pfsh,pfsk->hk", all_hidden, own_post, preferred_element_type=f32),
            jnp.einsum(
                "psfe,pfsk->ek",
                embeddings.reshape(tp_count, seqs, FRAMES, E),
                own_post,
                preferred_element_type=f32,
            ),
        ],
        axis=0,
    )

    def share_rows(grad, axis):
        return lax.psum_scatter(
            grad.astype(bf16), "dp", scatter_dimension=axis, tiled=True
        ).astype(f32)

    prior_grad = share_rows(prior_grad, 0)
    post_grad = share_rows(post_grad, 0)

    own_back = exchange(back, "tp")[:, 1:].reshape(tp_count, FRAMES - 1, seqs, 3, units)
    gru_grad = jnp.concatenate(
        [
            jnp.einsum("pfsz,pfskj->kzj", onehot[:, :-1], own_back, preferred_element_type=f32),
            jnp.einsum("pfsh,pfskj->khj", all_hidden[:, :-1], own_back, preferred_element_type=f32),
        ],
        axis=1,
    )
    gru_grad = share_rows(gru_grad, 1)

    def own_rows(matrix, axis_dim):
        share = matrix.shape[axis_dim] // dp_count
        return lax.dynamic_slice_in_dim(matrix, dp_index * share, share, axis_dim)

    new_gru_moment = momentum_keep * own_rows(gru_moment, 1) + gru_grad
    new_post_moment = momentum_keep * own_rows(post_moment, 0) + post_grad
    new_prior_moment = momentum_keep * own_rows(prior_moment, 0) + prior_grad
    ahead_gru = (gru_grad + momentum_keep * new_gru_moment).astype(bf16)
    ahead_post = (post_grad + momentum_keep * new_post_moment).astype(bf16)
    ahead_prior = (prior_grad + momentum_keep * new_prior_moment).astype(bf16)

    stride = dp_count // MATS
    widest = (H + E) // dp_count

    def to_slots(blocks):
        empty = jnp.zeros((widest, units), bf16)
        slots = [empty] * dp_count
        for m, block in enumerate(blocks):
            slots[m * stride] = jnp.pad(block, ((0, widest - block.shape[0]), (0, 0)))
        return jnp.stack(slots)

    arrived = exchange(
        to_slots([ahead_gru[0], ahead_gru[1], ahead_gru[2], ahead_post, ahead_prior]), "dp"
    )
    wide = gather(arrived.reshape(dp_count * widest, units).T).reshape(H, dp_count * widest)
    result = orthogonal_wide(wide, tp_index, units).T.reshape(dp_count, widest, units)
    results = exchange(result, "dp")

    def renew(weight_rows, index, largest):
        factor = learn_rate * update_scale * math.sqrt(largest)
        shard = results[index * stride, : weight_rows.shape[0]].astype(f32)
        return weight_rows * (1.0 - learn_rate * weight_decay) - factor * shard

    gru_rows = own_rows(gru_weight, 1)
    new_gru = jnp.stack([renew(gru_rows[k], k, gru_weight.shape[1]) for k in range(3)])
    new_post = renew(own_rows(post_weight, 0), 3, max(post_weight.shape[0], Z))
    new_prior = renew(own_rows(prior_weight, 0), 4, max(H, Z))
    return (
        loss_value,
        embed_grad,
        new_gru,
        new_post,
        new_prior,
        new_gru_moment,
        new_post_moment,
        new_prior_moment,
    )


def solution(mesh):
    in_specs = (
        P("dp", None, None),
        P("dp", None, None),
        P("dp"),
        P(None, None, "tp"),
        P(None, "tp"),
        P(None, "tp"),
        P(None, None, "tp"),
        P(None, "tp"),
        P(None, "tp"),
    )
    out_specs = (
        P(),
        P("dp", None, "tp"),
        P(None, "dp", "tp"),
        P("dp", "tp"),
        P("dp", "tp"),
        P(None, "dp", "tp"),
        P("dp", "tp"),
        P("dp", "tp"),
    )
    return jax.shard_map(
        on_device, mesh=mesh, in_specs=in_specs, out_specs=out_specs, check_vma=False
    )
```

```python
import functools
import math

import jax
import jax.numpy as jnp
from jax import lax
from jax.experimental import pallas as pl
from jax.experimental.pallas import tpu as pltpu
from jax.sharding import PartitionSpec as P

H = 1024
ZC = 32
E = 1536
FRAMES = 56
MATS = 5
Z = 1024
ROWS = (Z + H, Z + H, Z + H, H + E, H)
PACK = 8


coeff_linear = 3.4445
coeff_cubic = -4.775
coeff_quintic = 2.0315
momentum_keep = 0.95
learn_rate = 0.2
weight_decay = 0.01
update_scale = 0.2
tiny_value = 1e-07
mib = 1 << 20
f32 = jnp.float32
bf16 = jnp.bfloat16
NT = (((1,), (1,)), ((), ()))


def dot(left, right):
    return jnp.dot(left, right, preferred_element_type=f32)


def dot_nt(left, right):
    return lax.dot_general(left, right, NT, preferred_element_type=f32)


def scan_forward(seqs, x_ref, w_ref, h_ref, k_ref, u_ref, state):
    parts, packs = x_ref.shape[:2]
    units = w_ref.shape[3]
    per_pack = PACK // seqs
    state[...] = jnp.zeros_like(state)

    def pack(i, carry):
        for frame in range(per_pack):
            rows = slice(frame * seqs, (frame + 1) * seqs)
            if frame == 0:
                source, live = jnp.maximum(i - 1, 0), jnp.where(i > 0, 1.0, 0.0)
                spot = slice((per_pack - 1) * seqs, per_pack * seqs)
            else:
                source, live = i, None
                spot = slice((frame - 1) * seqs, frame * seqs)
            before = state[...]
            low = before.astype(bf16)
            for p in range(parts):
                cols = slice(p * units, (p + 1) * units)
                given = x_ref[p, source].astype(f32)[spot]
                if live is not None:
                    given = given * live
                pre = [
                    given[:, k * units : (k + 1) * units] + dot(low, w_ref[p, k]) for k in range(3)
                ]
                last = before[:, cols]
                r = jax.nn.sigmoid(pre[0])
                c = jnp.tanh(r * pre[1])
                u = jax.nn.sigmoid(pre[2] - 1.0)
                rest = 1.0 - u
                new = u * c + rest * last
                inner = u * (1.0 - c * c)
                state[:, cols] = new
                h_ref[i, rows, cols] = new
                k_ref[0, i, rows, cols] = inner * pre[1] * r * (1.0 - r)
                k_ref[1, i, rows, cols] = inner * r
                k_ref[2, i, rows, cols] = (c - last) * u * rest
                u_ref[i, rows, cols] = rest
        return carry

    lax.fori_loop(0, packs, pack, 0)


def scan_backward(seqs, d_ref, k_ref, u_ref, w_ref, b_ref, now, kept):
    parts, packs = b_ref.shape[:2]
    units = w_ref.shape[3]
    per_pack = PACK // seqs
    now[...] = jnp.zeros_like(now)
    kept[...] = jnp.zeros_like(kept)

    def pack(n, carry):
        i = packs - 1 - n
        later = [None] * per_pack
        for frame in reversed(range(per_pack)):
            rows = slice(frame * seqs, (frame + 1) * seqs)
            values = now[...]
            later[frame] = values
            low = values.astype(bf16)
            dh = d_ref[i, rows] + kept[...]
            for p in range(parts):
                for k in range(3):
                    spot = slice((3 * p + k) * units, (3 * p + k + 1) * units)
                    dh = dh + dot_nt(low[:, spot], w_ref[p, k])
            kept[...] = dh * u_ref[i, rows]
            for p in range(parts):
                cols = slice(p * units, (p + 1) * units)
                for k in range(3):
                    spot = slice((3 * p + k) * units, (3 * p + k + 1) * units)
                    now[:, spot] = dh[:, cols] * k_ref[k, i, rows, cols]
        stacked = jnp.concatenate(later, axis=0).astype(bf16)
        for p in range(parts):
            b_ref[p, i] = stacked[:, p * 3 * units : (p + 1) * 3 * units]
        return carry

    lax.fori_loop(0, packs, pack, 0)


def butterfly(values, combine, lane):
    step = 1
    while step < ZC:
        up = pltpu.roll(values, step, 1)
        down = pltpu.roll(values, values.shape[1] - step, 1)
        values = combine(values, jnp.where((lane & step) != 0, up, down))
        step *= 2
    return values


def head_block(h_ref, e_ref, t_ref, m_ref, w_ref, back_ref, d_ref, loss_ref):
    parts = w_ref.shape[0]
    units = w_ref.shape[2]
    rows = h_ref.shape[0]
    low = h_ref[...].astype(bf16)
    mask = m_ref[...]
    lane = lax.broadcasted_iota(jnp.int32, (rows, 128), 1)
    loss = jnp.zeros((rows, 128), f32)
    for p in range(parts):
        post = dot(low, w_ref[p, :H]) + dot(e_ref[...], w_ref[p, H : H + E])
        prior = dot(low, w_ref[p, H + E :])
        for head, logits in enumerate((prior, post)):
            for piece in range(units // 128):
                l = logits[:, piece * 128 : (piece + 1) * 128]
                cols = slice(p * units + piece * 128, p * units + (piece + 1) * 128)
                target = t_ref[:, cols].astype(f32)
                top = butterfly(l, jnp.maximum, lane)
                e = jnp.exp(l - top)
                total = butterfly(e, jnp.add, lane)
                loss = loss + mask * ((top + jnp.log(total)) * (1.0 / ZC) - target * l)
                back_ref[head, :, cols] = (mask * (e / total - target)).astype(bf16)
    loss_ref[...] = jnp.sum(loss, axis=0, keepdims=True)
    direct = jnp.zeros((rows, H), f32)
    for p in range(parts):
        cols = slice(p * units, (p + 1) * units)
        direct = direct + dot_nt(back_ref[0, :, cols], w_ref[p, H + E :])
        direct = direct + dot_nt(back_ref[1, :, cols], w_ref[p, :H])
    d_ref[...] = direct


def orthogonal_block(width, tile, own_ref, g_ref, o_ref, x, a, b):
    side = g_ref.shape[0]
    share = o_ref.shape[0]
    own = pl.ds(pl.multiple_of(own_ref[0] * share, share), share)

    def squares(i, total):
        rows = pl.ds(pl.multiple_of(i * 128, 128), 128)
        v = g_ref[rows, :width].astype(f32)
        return total + jnp.sum(v * v)

    total = lax.fori_loop(0, side // 128, squares, jnp.zeros((), f32))
    scale = 1.0 / (jnp.sqrt(jnp.full((1, 128), total, f32)) + tiny_value)
    scale = jnp.broadcast_to(scale[:, :1], (1, width))

    def shrink(i, carry):
        rows = pl.ds(pl.multiple_of(i * 128, 128), 128)
        x[rows, :] = (g_ref[rows, :width].astype(f32) * scale).astype(bf16)
        return carry

    lax.fori_loop(0, side // 128, shrink, 0)

    def square(j, carry):
        cols = pl.ds(pl.multiple_of(j * tile, tile), tile)
        a[:, cols] = dot_nt(x[...], x[cols, :]).astype(bf16)
        return carry

    def mix(j, carry):
        cols = pl.ds(pl.multiple_of(j * tile, tile), tile)
        b[:, cols] = (
            coeff_cubic * a[:, cols].astype(f32) + coeff_quintic * dot(a[...], a[:, cols])
        ).astype(bf16)
        return carry

    def renew(j, carry):
        cols = pl.ds(pl.multiple_of(j * tile, tile), tile)
        x[:, cols] = (
            coeff_linear * x[:, cols].astype(f32) + dot(b[...], x[:, cols])
        ).astype(bf16)
        return carry

    def sweep(s, carry):
        lax.fori_loop(0, side // tile, square, 0)
        lax.fori_loop(0, side // tile, mix, 0)
        lax.fori_loop(0, width // tile, renew, 0)
        return carry

    lax.fori_loop(0, 4, sweep, 0)
    lax.fori_loop(0, side // tile, square, 0)
    part = (coeff_cubic * a[own, :].astype(f32) + coeff_quintic * dot(a[own, :], a[...])).astype(bf16)

    def last(j, carry):
        cols = pl.ds(pl.multiple_of(j * tile, tile), tile)
        o_ref[:, cols] = (
            coeff_linear * x[own, cols].astype(f32) + dot(part, x[:, cols])
        ).astype(bf16)
        return carry

    lax.fori_loop(0, width // tile, last, 0)
    if width < o_ref.shape[1]:
        o_ref[:, width:] = jnp.zeros((share, o_ref.shape[1] - width), bf16)


def in_vmem(count):
    return [pl.BlockSpec(memory_space=pltpu.VMEM)] * count


def cost(flops, touched):
    return pl.CostEstimate(flops=int(flops), bytes_accessed=int(touched), transcendentals=0)


def run_forward(inputs, weights, seqs):
    parts, packs = inputs.shape[:2]
    out = jax.ShapeDtypeStruct((packs, PACK, H), f32)
    return pl.pallas_call(
        functools.partial(scan_forward, seqs),
        out_shape=[out, jax.ShapeDtypeStruct((3, packs, PACK, H), f32), out],
        in_specs=in_vmem(2),
        out_specs=in_vmem(3),
        scratch_shapes=[pltpu.VMEM((seqs, H), f32)],
        compiler_params=pltpu.CompilerParams(vmem_limit_bytes=40 * mib),
        cost_estimate=cost(6e10, 20 * mib),
        name="scan_forward",
    )(inputs, weights)


def run_backward(direct, factors, rest, weights, seqs):
    packs = direct.shape[0]
    parts, units = weights.shape[0], weights.shape[3]
    return pl.pallas_call(
        functools.partial(scan_backward, seqs),
        out_shape=jax.ShapeDtypeStruct((parts, packs, PACK, 3 * units), bf16),
        in_specs=in_vmem(4),
        out_specs=in_vmem(1)[0],
        scratch_shapes=[pltpu.VMEM((seqs, 3 * H), f32), pltpu.VMEM((seqs, H), f32)],
        compiler_params=pltpu.CompilerParams(vmem_limit_bytes=40 * mib),
        cost_estimate=cost(6e10, 20 * mib),
        name="scan_backward",
    )(direct, factors, rest, weights)


def run_heads(hidden, embed, target, mask, weights):
    rows = hidden.shape[0]
    return pl.pallas_call(
        head_block,
        out_shape=[
            jax.ShapeDtypeStruct((2, rows, Z), bf16),
            jax.ShapeDtypeStruct((rows, H), f32),
            jax.ShapeDtypeStruct((1, 128), f32),
        ],
        in_specs=in_vmem(5),
        out_specs=in_vmem(3),
        compiler_params=pltpu.CompilerParams(vmem_limit_bytes=40 * mib),
        cost_estimate=cost(1e10, 12 * mib),
        name="heads",
    )(hidden, embed, target, mask, weights)


def run_orthogonal(width, share, own, matrix):
    side = matrix.shape[0]
    return pl.pallas_call(
        functools.partial(orthogonal_block, width, 512),
        out_shape=jax.ShapeDtypeStruct((share, matrix.shape[1]), bf16),
        in_specs=[pl.BlockSpec(memory_space=pltpu.SMEM)] + in_vmem(1),
        out_specs=in_vmem(1)[0],
        scratch_shapes=[
            pltpu.VMEM((side, width), bf16),
            pltpu.VMEM((side, side), bf16),
            pltpu.VMEM((side, side), bf16),
        ],
        compiler_params=pltpu.CompilerParams(vmem_limit_bytes=48 * mib),
        cost_estimate=cost(5e10, 6 * mib),
        name=f"orthogonal_{width}",
    )(own, matrix)


def on_device(
    embeddings,
    samples,
    seq_lengths,
    gru_weight,
    post_weight,
    prior_weight,
    gru_moment,
    post_moment,
    prior_moment,
):
    dp_count = lax.axis_size("dp")
    tp_count = lax.axis_size("tp")
    dp_index = lax.axis_index("dp")
    tp_index = lax.axis_index("tp")
    seq_count = embeddings.shape[0]
    seqs = seq_count // tp_count
    units = gru_weight.shape[2]
    groups = Z // ZC
    rows = seqs * FRAMES
    packs = rows // PACK

    def gather(block):
        return lax.all_gather(block, "tp", axis=0, tiled=False)

    def exchange(block, axis):
        return lax.all_to_all(block, axis, 0, 0, tiled=True)

    weights = gather(gru_weight[:, Z:].astype(bf16))
    head_low = jnp.concatenate([post_weight.astype(bf16), prior_weight.astype(bf16)], axis=0)

    by_part = jnp.swapaxes(samples.reshape(tp_count, seqs, FRAMES, groups), 1, 2)
    classes = jnp.arange(Z, dtype=jnp.int32)
    expand = (classes[None, :] // ZC == jnp.arange(groups)[:, None]).astype(bf16)
    chosen = dot(by_part.reshape(tp_count * rows, groups).astype(bf16), expand)
    onehot = (chosen == (classes % ZC).astype(f32)).astype(bf16)
    input_part = jnp.concatenate(
        [dot(onehot, gru_weight[k, :Z].astype(bf16)).astype(bf16) for k in range(3)], axis=1
    ).reshape(tp_count, packs, PACK, 3 * units)
    input_part = exchange(input_part, "tp")
    embed_rows = jnp.swapaxes(embeddings.reshape(tp_count, seqs, FRAMES, E), 1, 2)
    embed_rows = embed_rows.reshape(tp_count, rows, E)
    own_embed = lax.dynamic_index_in_dim(embed_rows, tp_index, 0, keepdims=False)
    onehot = onehot.reshape(tp_count, rows, Z)
    own_target = lax.dynamic_index_in_dim(onehot, tp_index, 0, keepdims=False)
    positions = jnp.arange(FRAMES, dtype=jnp.int32)
    own_lengths = lax.dynamic_slice_in_dim(seq_lengths, tp_index * seqs, seqs, 0)
    frame_mask = (positions[:, None] < own_lengths[None, :]).astype(f32)
    mask_lanes = jnp.broadcast_to(frame_mask.reshape(rows, 1), (rows, 128))

    weights, head_low, own_embed, own_target, mask_lanes, embed_rows, onehot = (
        lax.optimization_barrier(
            (weights, head_low, own_embed, own_target, mask_lanes, embed_rows, onehot)
        )
    )
    head_full = gather(head_low)
    hidden, factors, rest = run_forward(input_part, weights, seqs)
    back_heads, direct, loss_lanes = run_heads(
        hidden.reshape(rows, H), own_embed, own_target, mask_lanes, head_full
    )
    everyone = gather(jnp.stack([hidden.reshape(rows, H).astype(bf16), back_heads[0], back_heads[1]]))
    back = run_backward(direct.reshape(packs, PACK, H), factors, rest, weights, seqs)
    own_back = exchange(back, "tp").reshape(tp_count, rows, 3 * units)

    all_hidden = everyone[:, 0]
    all_post = everyone[:, 2]
    own_heads = lax.dynamic_slice_in_dim(everyone[:, 1:], tp_index * units, units, 3)

    def outer(left, right):
        return jnp.einsum("prm,prn->mn", left, right, preferred_element_type=f32).astype(bf16)

    prior_grad = outer(all_hidden, own_heads[:, 0])
    post_grad = [outer(all_hidden, own_heads[:, 1]), outer(embed_rows, own_heads[:, 1])]
    gru_grads = [
        [outer(left, own_back[:, :, k * units : (k + 1) * units]) for left in (onehot, all_hidden)]
        for k in range(3)
    ]
    shares = [size // dp_count for size in ROWS]
    local = jnp.concatenate(
        [
            jnp.concatenate(mats, axis=0).reshape(dp_count, -1, units)
            for mats in (*gru_grads, post_grad, [prior_grad])
        ],
        axis=1,
    )
    loss_parts = jnp.stack([jnp.sum(loss_lanes), jnp.sum(frame_mask)])
    local, loss_parts = lax.optimization_barrier((local, loss_parts))
    summed = lax.psum_scatter(local, "dp", scatter_dimension=0, tiled=True)[0]
    loss_sum, frame_count = lax.psum(loss_parts, ("dp", "tp"))
    loss_value = loss_sum / frame_count

    embed_part = E // tp_count
    own_rows_e = lax.dynamic_slice_in_dim(head_full, H + tp_index * embed_part, embed_part, 1)
    post_by_seq = jnp.swapaxes(all_post.reshape(tp_count, FRAMES, seqs, Z), 1, 2)
    embed_grad = jnp.einsum(
        "psfk,ek->psfe",
        post_by_seq,
        jnp.concatenate(list(own_rows_e), axis=1),
        preferred_element_type=f32,
    ).reshape(seq_count, FRAMES, embed_part)
    embed_grad = embed_grad / frame_count

    summed = summed.astype(f32) / frame_count
    starts = [sum(shares[:m]) for m in range(MATS)]
    grads = [summed[starts[m] : starts[m] + shares[m]] for m in range(MATS)]

    def own_rows(matrix, axis_dim):
        share = matrix.shape[axis_dim] // dp_count
        return lax.dynamic_slice_in_dim(matrix, dp_index * share, share, axis_dim)

    gru_moments = own_rows(gru_moment, 1)
    moments = [momentum_keep * gru_moments[k] + grads[k] for k in range(3)]
    moments.append(momentum_keep * own_rows(post_moment, 0) + grads[3])
    moments.append(momentum_keep * own_rows(prior_moment, 0) + grads[4])
    ahead = [(grads[m] + momentum_keep * moments[m]).astype(bf16) for m in range(MATS)]

    stride = dp_count // MATS
    widest = max(shares)
    tallest = max(ROWS)
    kind = jnp.clip(dp_index // stride - 2, 0, 2)
    sizes = (ROWS[0], ROWS[3], ROWS[4])

    slots = [jnp.zeros((widest, units), bf16)] * dp_count
    for m in range(MATS):
        slots[m * stride] = jnp.pad(ahead[m], ((0, widest - shares[m]), (0, 0)))
    arrived = exchange(jnp.stack(slots), "dp")

    def compact(size):
        kept = arrived[:, : size // dp_count].reshape(size, units)
        return jnp.pad(kept, ((0, tallest - size), (0, 0)))

    def spread_out(block, size):
        share = size // dp_count
        return jnp.pad(
            block[:size].reshape(dp_count, share, units), ((0, 0), (0, widest - share), (0, 0))
        )

    def select(choices):
        return jnp.where(kind == 0, choices[0], jnp.where(kind == 1, choices[1], choices[2]))

    packed = select([compact(size) for size in sizes])
    wide = gather(packed.T).reshape(H, tallest)
    own = tp_index.astype(jnp.int32).reshape(1)
    result = lax.switch(
        kind,
        [functools.partial(run_orthogonal, size, units) for size in sizes],
        own,
        wide,
    )
    result = result.T
    results = exchange(select([spread_out(result, size) for size in sizes]), "dp")

    def renew(weight_rows, index, largest):
        factor = learn_rate * update_scale * math.sqrt(largest)
        shard = results[index * stride, : weight_rows.shape[0]].astype(f32)
        return weight_rows * (1.0 - learn_rate * weight_decay) - factor * shard

    gru_rows = own_rows(gru_weight, 1)
    new_gru = jnp.stack([renew(gru_rows[k], k, gru_weight.shape[1]) for k in range(3)])
    new_post = renew(own_rows(post_weight, 0), 3, max(post_weight.shape[0], Z))
    new_prior = renew(own_rows(prior_weight, 0), 4, max(H, Z))
    return (
        loss_value,
        embed_grad,
        new_gru,
        new_post,
        new_prior,
        jnp.stack(moments[:3]),
        moments[3],
        moments[4],
    )

def solution(mesh):
    in_specs = (
        P("dp", None, None),
        P("dp", None, None),
        P("dp"),
        P(None, None, "tp"),
        P(None, "tp"),
        P(None, "tp"),
        P(None, None, "tp"),
        P(None, "tp"),
        P(None, "tp"),
    )
    out_specs = (
        P(),
        P("dp", None, "tp"),
        P(None, "dp", "tp"),
        P("dp", "tp"),
        P("dp", "tp"),
        P(None, "dp", "tp"),
        P("dp", "tp"),
        P("dp", "tp"),
    )
    return jax.shard_map(
        on_device, mesh=mesh, in_specs=in_specs, out_specs=out_specs, check_vma=False
    )
```

```python
import functools
import math

import jax
import jax.numpy as jnp
from jax import lax
from jax.experimental import pallas as pl
from jax.experimental.pallas import tpu as pltpu
from jax.sharding import PartitionSpec as P

H = 1024
ZC = 32
E = 1536
FRAMES = 56
MATS = 5
Z = 1024
ROWS = (Z + H, Z + H, Z + H, H + E, H)
PACK = 8


coeff_linear = 3.4445
coeff_cubic = -4.775
coeff_quintic = 2.0315
momentum_keep = 0.95
learn_rate = 0.2
weight_decay = 0.01
update_scale = 0.2
tiny_value = 1e-07
mib = 1 << 20
f32 = jnp.float32
bf16 = jnp.bfloat16
NT = (((1,), (1,)), ((), ()))


def dot(left, right):
    return jnp.dot(left, right, preferred_element_type=f32)


def dot_nt(left, right):
    return lax.dot_general(left, right, NT, preferred_element_type=f32)


def scan_forward(seqs, x_ref, w_ref, h_ref, k_ref, u_ref, state):
    parts, packs = x_ref.shape[:2]
    units = w_ref.shape[3]
    per_pack = PACK // seqs
    state[...] = jnp.zeros_like(state)

    def pack(i, carry):
        for frame in range(per_pack):
            rows = slice(frame * seqs, (frame + 1) * seqs)
            if frame == 0:
                source, live = jnp.maximum(i - 1, 0), jnp.where(i > 0, 1.0, 0.0)
                spot = slice((per_pack - 1) * seqs, per_pack * seqs)
            else:
                source, live = i, None
                spot = slice((frame - 1) * seqs, frame * seqs)
            before = state[...]
            low = before.astype(bf16)
            for p in range(parts):
                cols = slice(p * units, (p + 1) * units)
                given = x_ref[p, source].astype(f32)[spot]
                if live is not None:
                    given = given * live
                pre = [
                    given[:, k * units : (k + 1) * units] + dot(low, w_ref[p, k]) for k in range(3)
                ]
                last = before[:, cols]
                r = jax.nn.sigmoid(pre[0])
                c = jnp.tanh(r * pre[1])
                u = jax.nn.sigmoid(pre[2] - 1.0)
                rest = 1.0 - u
                new = u * c + rest * last
                inner = u * (1.0 - c * c)
                state[:, cols] = new
                h_ref[i, rows, cols] = new
                k_ref[0, i, rows, cols] = inner * pre[1] * r * (1.0 - r)
                k_ref[1, i, rows, cols] = inner * r
                k_ref[2, i, rows, cols] = (c - last) * u * rest
                u_ref[i, rows, cols] = rest
        return carry

    lax.fori_loop(0, packs, pack, 0)


def scan_backward(seqs, d_ref, k_ref, u_ref, w_ref, b_ref, now, kept, turned):
    parts, packs = b_ref.shape[:2]
    units = w_ref.shape[3]
    per_pack = PACK // seqs
    now[...] = jnp.zeros_like(now)
    kept[...] = jnp.zeros_like(kept)

    def turn(n, carry):
        spot = pl.ds(pl.multiple_of(n * units, units), units)
        turned[spot, :] = w_ref[n // 3, n % 3].T
        return carry

    lax.fori_loop(0, 3 * parts, turn, 0)

    def pack(n, carry):
        i = packs - 1 - n
        later = [None] * per_pack
        for frame in reversed(range(per_pack)):
            rows = slice(frame * seqs, (frame + 1) * seqs)
            values = now[...]
            later[frame] = values
            dh = d_ref[i, rows] + kept[...] + dot(values.astype(bf16), turned[...])
            kept[...] = dh * u_ref[i, rows]
            for p in range(parts):
                cols = slice(p * units, (p + 1) * units)
                for k in range(3):
                    spot = slice((3 * p + k) * units, (3 * p + k + 1) * units)
                    now[:, spot] = dh[:, cols] * k_ref[k, i, rows, cols]
        stacked = jnp.concatenate(later, axis=0).astype(bf16)
        for p in range(parts):
            b_ref[p, i] = stacked[:, p * 3 * units : (p + 1) * 3 * units]
        return carry

    lax.fori_loop(0, packs, pack, 0)


def butterfly(values, combine, lane):
    step = 1
    while step < ZC:
        up = pltpu.roll(values, step, 1)
        down = pltpu.roll(values, values.shape[1] - step, 1)
        values = combine(values, jnp.where((lane & step) != 0, up, down))
        step *= 2
    return values


def head_block(h_ref, e_ref, t_ref, m_ref, w_ref, back_ref, d_ref, loss_ref):
    parts = w_ref.shape[0]
    units = w_ref.shape[2]
    rows = h_ref.shape[0]
    low = h_ref[...].astype(bf16)
    mask = m_ref[...]
    lane = lax.broadcasted_iota(jnp.int32, (rows, 128), 1)
    loss = jnp.zeros((rows, 128), f32)
    for p in range(parts):
        post = dot(low, w_ref[p, :H]) + dot(e_ref[...], w_ref[p, H : H + E])
        prior = dot(low, w_ref[p, H + E :])
        for head, logits in enumerate((prior, post)):
            for piece in range(units // 128):
                l = logits[:, piece * 128 : (piece + 1) * 128]
                cols = slice(p * units + piece * 128, p * units + (piece + 1) * 128)
                target = t_ref[:, cols].astype(f32)
                top = butterfly(l, jnp.maximum, lane)
                e = jnp.exp(l - top)
                total = butterfly(e, jnp.add, lane)
                loss = loss + mask * ((top + jnp.log(total)) * (1.0 / ZC) - target * l)
                back_ref[head, :, cols] = (mask * (e / total - target)).astype(bf16)
    loss_ref[...] = jnp.sum(loss, axis=0, keepdims=True)
    direct = jnp.zeros((rows, H), f32)
    for p in range(parts):
        cols = slice(p * units, (p + 1) * units)
        direct = direct + dot_nt(back_ref[0, :, cols], w_ref[p, H + E :])
        direct = direct + dot_nt(back_ref[1, :, cols], w_ref[p, :H])
    d_ref[...] = direct


def orthogonal_block(base, tile, own_ref, g_ref, o_ref, x, a, b):
    side, width = g_ref.shape
    share = o_ref.shape[0]
    own = pl.ds(pl.multiple_of(own_ref[0] * share, share), share)
    wide = own_ref[1] > 0

    def either(run):
        pl.when(wide)(functools.partial(run, width))
        pl.when(jnp.logical_not(wide))(functools.partial(run, base))

    def squares(i, total):
        rows = pl.ds(pl.multiple_of(i * 128, 128), 128)
        v = g_ref[rows, :].astype(f32)
        return total + jnp.sum(v * v)

    total = lax.fori_loop(0, side // 128, squares, jnp.zeros((), f32))
    scale = 1.0 / (jnp.sqrt(jnp.full((1, 128), total, f32)) + tiny_value)
    scale = jnp.broadcast_to(scale[:, :1], (1, width))

    def shrink(i, carry):
        rows = pl.ds(pl.multiple_of(i * 128, 128), 128)
        x[rows, :] = (g_ref[rows, :].astype(f32) * scale).astype(bf16)
        return carry

    lax.fori_loop(0, side // 128, shrink, 0)

    def square(depth):
        def block(j, carry):
            cols = pl.ds(pl.multiple_of(j * tile, tile), tile)
            a[:, cols] = dot_nt(x[:, :depth], x[cols, :depth]).astype(bf16)
            return carry

        lax.fori_loop(0, side // tile, block, 0)

    def mix(j, carry):
        cols = pl.ds(pl.multiple_of(j * tile, tile), tile)
        b[:, cols] = (
            coeff_cubic * a[:, cols].astype(f32) + coeff_quintic * dot(a[...], a[:, cols])
        ).astype(bf16)
        return carry

    def renew(j, carry):
        cols = pl.ds(pl.multiple_of(j * tile, tile), tile)
        x[:, cols] = (
            coeff_linear * x[:, cols].astype(f32) + dot(b[...], x[:, cols])
        ).astype(bf16)
        return carry

    used = jnp.where(wide, width // tile, base // tile)

    def sweep(s, carry):
        either(square)
        lax.fori_loop(0, side // tile, mix, 0)
        lax.fori_loop(0, used, renew, 0)
        return carry

    lax.fori_loop(0, 4, sweep, 0)
    either(square)
    part = (coeff_cubic * a[own, :].astype(f32) + coeff_quintic * dot(a[own, :], a[...])).astype(bf16)

    def last(j, carry):
        cols = pl.ds(pl.multiple_of(j * tile, tile), tile)
        o_ref[:, cols] = (
            coeff_linear * x[own, cols].astype(f32) + dot(part, x[:, cols])
        ).astype(bf16)
        return carry

    lax.fori_loop(0, width // tile, last, 0)


def turn_block(tile, g_ref, o_ref):
    def block(i, carry):
        spot = pl.ds(pl.multiple_of(i * tile, tile), tile)
        o_ref[:, spot] = g_ref[spot, :].T
        return carry

    lax.fori_loop(0, g_ref.shape[0] // tile, block, 0)


def in_vmem(count):
    return [pl.BlockSpec(memory_space=pltpu.VMEM)] * count


def cost(flops, touched):
    return pl.CostEstimate(flops=int(flops), bytes_accessed=int(touched), transcendentals=0)


def run_forward(inputs, weights, seqs):
    parts, packs = inputs.shape[:2]
    out = jax.ShapeDtypeStruct((packs, PACK, H), f32)
    return pl.pallas_call(
        functools.partial(scan_forward, seqs),
        out_shape=[out, jax.ShapeDtypeStruct((3, packs, PACK, H), f32), out],
        in_specs=in_vmem(2),
        out_specs=in_vmem(3),
        scratch_shapes=[pltpu.VMEM((seqs, H), f32)],
        compiler_params=pltpu.CompilerParams(vmem_limit_bytes=40 * mib),
        cost_estimate=cost(6e10, 20 * mib),
        name="scan_forward",
    )(inputs, weights)


def run_backward(direct, factors, rest, weights, seqs):
    packs = direct.shape[0]
    parts, units = weights.shape[0], weights.shape[3]
    return pl.pallas_call(
        functools.partial(scan_backward, seqs),
        out_shape=jax.ShapeDtypeStruct((parts, packs, PACK, 3 * units), bf16),
        in_specs=in_vmem(4),
        out_specs=in_vmem(1)[0],
        scratch_shapes=[
            pltpu.VMEM((seqs, 3 * H), f32),
            pltpu.VMEM((seqs, H), f32),
            pltpu.VMEM((3 * H, H), bf16),
        ],
        compiler_params=pltpu.CompilerParams(vmem_limit_bytes=44 * mib),
        cost_estimate=cost(6e10, 20 * mib),
        name="scan_backward",
    )(direct, factors, rest, weights)


def run_heads(hidden, embed, target, mask, weights):
    rows = hidden.shape[0]
    return pl.pallas_call(
        head_block,
        out_shape=[
            jax.ShapeDtypeStruct((2, rows, Z), bf16),
            jax.ShapeDtypeStruct((rows, H), f32),
            jax.ShapeDtypeStruct((1, 128), f32),
        ],
        in_specs=in_vmem(5),
        out_specs=in_vmem(3),
        compiler_params=pltpu.CompilerParams(vmem_limit_bytes=40 * mib),
        cost_estimate=cost(1e10, 12 * mib),
        name="heads",
    )(hidden, embed, target, mask, weights)


def run_orthogonal(base, share, own, matrix):
    side, width = matrix.shape
    return pl.pallas_call(
        functools.partial(orthogonal_block, base, 512),
        out_shape=jax.ShapeDtypeStruct((share, width), bf16),
        in_specs=[pl.BlockSpec(memory_space=pltpu.SMEM)] + in_vmem(1),
        out_specs=in_vmem(1)[0],
        scratch_shapes=[
            pltpu.VMEM((side, width), bf16),
            pltpu.VMEM((side, side), bf16),
            pltpu.VMEM((side, side), bf16),
        ],
        compiler_params=pltpu.CompilerParams(vmem_limit_bytes=48 * mib),
        cost_estimate=cost(5e10, 6 * mib),
        name="orthogonal",
    )(own, matrix)


def run_turn(matrix):
    return pl.pallas_call(
        functools.partial(turn_block, 256),
        out_shape=jax.ShapeDtypeStruct(matrix.shape[::-1], bf16),
        in_specs=in_vmem(1),
        out_specs=in_vmem(1)[0],
        compiler_params=pltpu.CompilerParams(vmem_limit_bytes=16 * mib),
        cost_estimate=cost(1e6, 3 * mib),
        name="turn",
    )(matrix)


def on_device(
    embeddings,
    samples,
    seq_lengths,
    gru_weight,
    post_weight,
    prior_weight,
    gru_moment,
    post_moment,
    prior_moment,
):
    dp_count = lax.axis_size("dp")
    tp_count = lax.axis_size("tp")
    dp_index = lax.axis_index("dp")
    tp_index = lax.axis_index("tp")
    seq_count = embeddings.shape[0]
    seqs = seq_count // tp_count
    units = gru_weight.shape[2]
    groups = Z // ZC
    rows = seqs * FRAMES
    packs = rows // PACK

    def gather(block):
        return lax.all_gather(block, "tp", axis=0, tiled=False)

    def exchange(block, axis):
        return lax.all_to_all(block, axis, 0, 0, tiled=True)

    weights = gather(gru_weight[:, Z:].astype(bf16))
    head_low = jnp.concatenate([post_weight.astype(bf16), prior_weight.astype(bf16)], axis=0)

    by_part = jnp.swapaxes(samples.reshape(tp_count, seqs, FRAMES, groups), 1, 2)
    classes = jnp.arange(Z, dtype=jnp.int32)
    expand = (classes[None, :] // ZC == jnp.arange(groups)[:, None]).astype(bf16)
    chosen = dot(by_part.reshape(tp_count * rows, groups).astype(bf16), expand)
    onehot = (chosen == (classes % ZC).astype(f32)).astype(bf16)
    input_part = jnp.concatenate(
        [dot(onehot, gru_weight[k, :Z].astype(bf16)).astype(bf16) for k in range(3)], axis=1
    ).reshape(tp_count, packs, PACK, 3 * units)
    input_part = exchange(input_part, "tp")
    embed_rows = jnp.swapaxes(embeddings.reshape(tp_count, seqs, FRAMES, E), 1, 2)
    embed_rows = embed_rows.reshape(tp_count, rows, E)
    own_embed = lax.dynamic_index_in_dim(embed_rows, tp_index, 0, keepdims=False)
    onehot = onehot.reshape(tp_count, rows, Z)
    own_target = lax.dynamic_index_in_dim(onehot, tp_index, 0, keepdims=False)
    positions = jnp.arange(FRAMES, dtype=jnp.int32)
    own_lengths = lax.dynamic_slice_in_dim(seq_lengths, tp_index * seqs, seqs, 0)
    frame_mask = (positions[:, None] < own_lengths[None, :]).astype(f32)
    mask_lanes = jnp.broadcast_to(frame_mask.reshape(rows, 1), (rows, 128))

    weights, input_part, head_low, own_embed, own_target, mask_lanes, embed_rows, onehot = (
        lax.optimization_barrier(
            (weights, input_part, head_low, own_embed, own_target, mask_lanes, embed_rows, onehot)
        )
    )
    head_full = gather(head_low)
    hidden, factors, rest = run_forward(input_part, weights, seqs)
    back_heads, direct, loss_lanes = run_heads(
        hidden.reshape(rows, H), own_embed, own_target, mask_lanes, head_full
    )
    everyone = gather(jnp.stack([hidden.reshape(rows, H).astype(bf16), back_heads[0], back_heads[1]]))
    back = run_backward(direct.reshape(packs, PACK, H), factors, rest, weights, seqs)
    own_back = exchange(back, "tp").reshape(tp_count, rows, 3 * units)

    all_hidden = everyone[:, 0]
    all_post = everyone[:, 2]
    own_heads = lax.dynamic_slice_in_dim(everyone[:, 1:], tp_index * units, units, 3)

    def outer(left, right):
        return jnp.einsum("prm,prn->mn", left, right, preferred_element_type=f32).astype(bf16)

    prior_grad = outer(all_hidden, own_heads[:, 0])
    post_grad = [outer(all_hidden, own_heads[:, 1]), outer(embed_rows, own_heads[:, 1])]
    gru_grads = [
        [outer(left, own_back[:, :, k * units : (k + 1) * units]) for left in (onehot, all_hidden)]
        for k in range(3)
    ]
    shares = [size // dp_count for size in ROWS]
    local = jnp.concatenate(
        [
            jnp.concatenate(mats, axis=0).reshape(dp_count, -1, units)
            for mats in (*gru_grads, post_grad, [prior_grad])
        ],
        axis=1,
    )
    summed = lax.psum_scatter(local, "dp", scatter_dimension=0, tiled=True)[0]
    totals = jnp.stack([jnp.sum(loss_lanes), jnp.sum(frame_mask)])
    totals = jnp.broadcast_to(totals[:, None], (2, 128))
    for axis, count in (("tp", tp_count), ("dp", dp_count)):
        for bit in range(count.bit_length() - 1):
            pairs = [(i, i ^ (1 << bit)) for i in range(count)]
            totals = totals + lax.ppermute(totals, axis, pairs)
    loss_sum, frame_count = totals[0, 0], totals[1, 0]
    loss_value = loss_sum / frame_count

    embed_part = E // tp_count
    own_rows_e = lax.dynamic_slice_in_dim(head_full, H + tp_index * embed_part, embed_part, 1)
    post_by_seq = jnp.swapaxes(all_post.reshape(tp_count, FRAMES, seqs, Z), 1, 2)
    embed_grad = jnp.einsum(
        "psfk,ek->psfe",
        post_by_seq,
        jnp.concatenate(list(own_rows_e), axis=1),
        preferred_element_type=f32,
    ).reshape(seq_count, FRAMES, embed_part)
    embed_grad = embed_grad / frame_count

    summed = summed.astype(f32) / frame_count
    starts = [sum(shares[:m]) for m in range(MATS)]
    grads = [summed[starts[m] : starts[m] + shares[m]] for m in range(MATS)]

    def own_rows(matrix, axis_dim):
        share = matrix.shape[axis_dim] // dp_count
        return lax.dynamic_slice_in_dim(matrix, dp_index * share, share, axis_dim)

    gru_moments = own_rows(gru_moment, 1)
    moments = [momentum_keep * gru_moments[k] + grads[k] for k in range(3)]
    moments.append(momentum_keep * own_rows(post_moment, 0) + grads[3])
    moments.append(momentum_keep * own_rows(prior_moment, 0) + grads[4])
    ahead = [(grads[m] + momentum_keep * moments[m]).astype(bf16) for m in range(MATS)]

    stride = dp_count // MATS
    widest = max(shares)
    base = shares[0]
    slots = [jnp.zeros((widest, units), bf16)] * dp_count
    for m in range(MATS):
        slots[m * stride] = jnp.pad(ahead[m], ((0, widest - shares[m]), (0, 0)))
    arrived = exchange(jnp.stack(slots), "dp")
    packed = jnp.concatenate(
        [arrived[:, :base].reshape(-1, units), arrived[:, base:].reshape(-1, units)], axis=0
    )
    wide = gather(run_turn(packed)).reshape(H, dp_count * widest)
    own = jnp.stack([tp_index, (dp_index == 3 * stride).astype(jnp.int32)]).astype(jnp.int32)
    result = run_orthogonal(dp_count * base, units, own, wide).T
    results = exchange(
        jnp.concatenate(
            [
                result[: dp_count * base].reshape(dp_count, base, units),
                result[dp_count * base :].reshape(dp_count, widest - base, units),
            ],
            axis=1,
        ),
        "dp",
    )

    def renew(weight_rows, index, largest):
        factor = learn_rate * update_scale * math.sqrt(largest)
        shard = results[index * stride, : weight_rows.shape[0]].astype(f32)
        return weight_rows * (1.0 - learn_rate * weight_decay) - factor * shard

    gru_rows = own_rows(gru_weight, 1)
    new_gru = jnp.stack([renew(gru_rows[k], k, gru_weight.shape[1]) for k in range(3)])
    new_post = renew(own_rows(post_weight, 0), 3, max(post_weight.shape[0], Z))
    new_prior = renew(own_rows(prior_weight, 0), 4, max(H, Z))
    return (
        loss_value,
        embed_grad,
        new_gru,
        new_post,
        new_prior,
        jnp.stack(moments[:3]),
        moments[3],
        moments[4],
    )

def solution(mesh):
    in_specs = (
        P("dp", None, None),
        P("dp", None, None),
        P("dp"),
        P(None, None, "tp"),
        P(None, "tp"),
        P(None, "tp"),
        P(None, None, "tp"),
        P(None, "tp"),
        P(None, "tp"),
    )
    out_specs = (
        P(),
        P("dp", None, "tp"),
        P(None, "dp", "tp"),
        P("dp", "tp"),
        P("dp", "tp"),
        P(None, "dp", "tp"),
        P("dp", "tp"),
        P("dp", "tp"),
    )
    return jax.shard_map(
        on_device, mesh=mesh, in_specs=in_specs, out_specs=out_specs, check_vma=False
    )
```

```python
import functools
import math

import jax
import jax.numpy as jnp
from jax import lax
from jax.experimental import pallas as pl
from jax.experimental.pallas import tpu as pltpu
from jax.sharding import PartitionSpec as P

H = 1024
ZC = 32
E = 1536
FRAMES = 56
MATS = 5
Z = 1024
ROWS = (Z + H, Z + H, Z + H, H + E, H)
PACK = 8
EARLY = 10


coeff_linear = 3.4445
coeff_cubic = -4.775
coeff_quintic = 2.0315
momentum_keep = 0.95
learn_rate = 0.2
weight_decay = 0.01
update_scale = 0.2
tiny_value = 1e-07
mib = 1 << 20
f32 = jnp.float32
bf16 = jnp.bfloat16
NT = (((1,), (1,)), ((), ()))


def dot(left, right):
    return jnp.dot(left, right, preferred_element_type=f32)


def dot_nt(left, right):
    return lax.dot_general(left, right, NT, preferred_element_type=f32)


def scan_forward(seqs, x_ref, w_ref, h_ref, k_ref, u_ref, state):
    parts, packs = x_ref.shape[:2]
    units = w_ref.shape[3]
    per_pack = PACK // seqs
    state[...] = jnp.zeros_like(state)

    def pack(i, carry):
        for frame in range(per_pack):
            rows = slice(frame * seqs, (frame + 1) * seqs)
            if frame == 0:
                source, live = jnp.maximum(i - 1, 0), jnp.where(i > 0, 1.0, 0.0)
                spot = slice((per_pack - 1) * seqs, per_pack * seqs)
            else:
                source, live = i, None
                spot = slice((frame - 1) * seqs, frame * seqs)
            before = state[...]
            low = before.astype(bf16)
            for p in range(parts):
                cols = slice(p * units, (p + 1) * units)
                given = x_ref[p, source].astype(f32)[spot]
                if live is not None:
                    given = given * live
                pre = [
                    given[:, k * units : (k + 1) * units] + dot(low, w_ref[p, k]) for k in range(3)
                ]
                last = before[:, cols]
                r = jax.nn.sigmoid(pre[0])
                c = jnp.tanh(r * pre[1])
                u = jax.nn.sigmoid(pre[2] - 1.0)
                rest = 1.0 - u
                new = u * c + rest * last
                inner = u * (1.0 - c * c)
                state[:, cols] = new
                h_ref[i, rows, cols] = new
                k_ref[0, i, rows, cols] = inner * pre[1] * r * (1.0 - r)
                k_ref[1, i, rows, cols] = inner * r
                k_ref[2, i, rows, cols] = (c - last) * u * rest
                u_ref[i, rows, cols] = rest
        return carry

    lax.fori_loop(0, packs, pack, 0)


def scan_backward(
    seqs, first, d_ref, k_ref, u_ref, w_ref, now_in, kept_in, b_ref, now_out, kept_out, now, kept, turned
):
    copies, parts, count = b_ref.shape[:3]
    units = w_ref.shape[3]
    per_pack = PACK // seqs
    now[...] = now_in[...]
    kept[...] = kept_in[...]

    def turn(n, carry):
        spot = pl.ds(pl.multiple_of(n * units, units), units)
        turned[spot, :] = w_ref[n // 3, n % 3].T
        return carry

    lax.fori_loop(0, 3 * parts, turn, 0)

    def pack(n, carry):
        i = first + count - 1 - n
        later = [None] * per_pack
        for frame in reversed(range(per_pack)):
            rows = slice(frame * seqs, (frame + 1) * seqs)
            values = now[...]
            later[frame] = values
            dh = d_ref[i, rows] + kept[...] + dot(values.astype(bf16), turned[...])
            kept[...] = dh * u_ref[i, rows]
            for p in range(parts):
                cols = slice(p * units, (p + 1) * units)
                for k in range(3):
                    spot = slice((3 * p + k) * units, (3 * p + k + 1) * units)
                    now[:, spot] = dh[:, cols] * k_ref[k, i, rows, cols]
        stacked = jnp.concatenate(later, axis=0).astype(bf16)
        for p in range(parts):
            for copy in range(copies):
                b_ref[copy, p, count - 1 - n] = stacked[:, p * 3 * units : (p + 1) * 3 * units]
        return carry

    lax.fori_loop(0, count, pack, 0)
    now_out[...] = now[...]
    kept_out[...] = kept[...]


def butterfly(values, combine, lane):
    step = 1
    while step < ZC:
        up = pltpu.roll(values, step, 1)
        down = pltpu.roll(values, values.shape[1] - step, 1)
        values = combine(values, jnp.where((lane & step) != 0, up, down))
        step *= 2
    return values


def head_block(h_ref, e_ref, t_ref, m_ref, w_ref, back_ref, d_ref, loss_ref):
    parts = w_ref.shape[0]
    units = w_ref.shape[2]
    rows = h_ref.shape[0]
    low = h_ref[...].astype(bf16)
    mask = m_ref[...]
    lane = lax.broadcasted_iota(jnp.int32, (rows, 128), 1)
    loss = jnp.zeros((rows, 128), f32)
    for p in range(parts):
        post = dot(low, w_ref[p, :H]) + dot(e_ref[...], w_ref[p, H : H + E])
        prior = dot(low, w_ref[p, H + E :])
        for head, logits in enumerate((prior, post)):
            for piece in range(units // 128):
                l = logits[:, piece * 128 : (piece + 1) * 128]
                cols = slice(p * units + piece * 128, p * units + (piece + 1) * 128)
                target = t_ref[:, cols].astype(f32)
                top = butterfly(l, jnp.maximum, lane)
                e = jnp.exp(l - top)
                total = butterfly(e, jnp.add, lane)
                loss = loss + mask * ((top + jnp.log(total)) * (1.0 / ZC) - target * l)
                back_ref[head, :, cols] = (mask * (e / total - target)).astype(bf16)
    loss_ref[...] = jnp.sum(loss, axis=0, keepdims=True)
    direct = jnp.zeros((rows, H), f32)
    for p in range(parts):
        cols = slice(p * units, (p + 1) * units)
        direct = direct + dot_nt(back_ref[0, :, cols], w_ref[p, H + E :])
        direct = direct + dot_nt(back_ref[1, :, cols], w_ref[p, :H])
    d_ref[...] = direct


def orthogonal_block(base, tile, own_ref, g_ref, o_ref, x, a, b):
    side, width = g_ref.shape
    share = o_ref.shape[0]
    own = pl.ds(pl.multiple_of(own_ref[0] * share, share), share)
    wide = own_ref[1] > 0

    def either(run):
        pl.when(wide)(functools.partial(run, width))
        pl.when(jnp.logical_not(wide))(functools.partial(run, base))

    def squares(i, total):
        rows = pl.ds(pl.multiple_of(i * 128, 128), 128)
        v = g_ref[rows, :].astype(f32)
        return total + jnp.sum(v * v)

    total = lax.fori_loop(0, side // 128, squares, jnp.zeros((), f32))
    scale = 1.0 / (jnp.sqrt(jnp.full((1, 128), total, f32)) + tiny_value)
    scale = jnp.broadcast_to(scale[:, :1], (1, width))

    def shrink(i, carry):
        rows = pl.ds(pl.multiple_of(i * 128, 128), 128)
        x[rows, :] = (g_ref[rows, :].astype(f32) * scale).astype(bf16)
        return carry

    lax.fori_loop(0, side // 128, shrink, 0)

    def square(depth):
        def block(j, carry):
            cols = pl.ds(pl.multiple_of(j * tile, tile), tile)
            a[:, cols] = dot_nt(x[:, :depth], x[cols, :depth]).astype(bf16)
            return carry

        lax.fori_loop(0, side // tile, block, 0)

    def mix(j, carry):
        cols = pl.ds(pl.multiple_of(j * tile, tile), tile)
        b[:, cols] = (
            coeff_cubic * a[:, cols].astype(f32) + coeff_quintic * dot(a[...], a[:, cols])
        ).astype(bf16)
        return carry

    def renew(j, carry):
        cols = pl.ds(pl.multiple_of(j * tile, tile), tile)
        x[:, cols] = (
            coeff_linear * x[:, cols].astype(f32) + dot(b[...], x[:, cols])
        ).astype(bf16)
        return carry

    used = jnp.where(wide, width // tile, base // tile)

    def sweep(s, carry):
        either(square)
        lax.fori_loop(0, side // tile, mix, 0)
        lax.fori_loop(0, used, renew, 0)
        return carry

    lax.fori_loop(0, 4, sweep, 0)
    either(square)
    part = (coeff_cubic * a[own, :].astype(f32) + coeff_quintic * dot(a[own, :], a[...])).astype(bf16)

    def last(j, carry):
        cols = pl.ds(pl.multiple_of(j * tile, tile), tile)
        o_ref[:, cols] = (
            coeff_linear * x[own, cols].astype(f32) + dot(part, x[:, cols])
        ).astype(bf16)
        return carry

    lax.fori_loop(0, width // tile, last, 0)


def turn_block(tile, g_ref, o_ref):
    def block(i, carry):
        spot = pl.ds(pl.multiple_of(i * tile, tile), tile)
        o_ref[:, spot] = g_ref[spot, :].T
        return carry

    lax.fori_loop(0, g_ref.shape[0] // tile, block, 0)


def in_vmem(count):
    return [pl.BlockSpec(memory_space=pltpu.VMEM)] * count


def cost(flops, touched):
    return pl.CostEstimate(flops=int(flops), bytes_accessed=int(touched), transcendentals=0)


def run_forward(inputs, weights, seqs):
    parts, packs = inputs.shape[:2]
    out = jax.ShapeDtypeStruct((packs, PACK, H), f32)
    return pl.pallas_call(
        functools.partial(scan_forward, seqs),
        out_shape=[out, jax.ShapeDtypeStruct((3, packs, PACK, H), f32), out],
        in_specs=in_vmem(2),
        out_specs=in_vmem(3),
        scratch_shapes=[pltpu.VMEM((seqs, H), f32)],
        compiler_params=pltpu.CompilerParams(vmem_limit_bytes=40 * mib),
        cost_estimate=cost(6e10, 20 * mib),
        name="scan_forward",
    )(inputs, weights)


def run_backward(direct, factors, rest, weights, carried, seqs, first, count, copies):
    parts, units = weights.shape[0], weights.shape[3]
    wide = jax.ShapeDtypeStruct((seqs, 3 * H), f32)
    narrow = jax.ShapeDtypeStruct((seqs, H), f32)
    return pl.pallas_call(
        functools.partial(scan_backward, seqs, first),
        out_shape=[
            jax.ShapeDtypeStruct((copies, parts, count, PACK, 3 * units), bf16),
            wide,
            narrow,
        ],
        in_specs=in_vmem(6),
        out_specs=in_vmem(3),
        scratch_shapes=[
            pltpu.VMEM((seqs, 3 * H), f32),
            pltpu.VMEM((seqs, H), f32),
            pltpu.VMEM((3 * H, H), bf16),
        ],
        compiler_params=pltpu.CompilerParams(vmem_limit_bytes=44 * mib),
        cost_estimate=cost(6e10 * count / direct.shape[0], 20 * mib),
        name="scan_backward",
    )(direct, factors, rest, weights, *carried)


def run_heads(hidden, embed, target, mask, weights):
    rows = hidden.shape[0]
    return pl.pallas_call(
        head_block,
        out_shape=[
            jax.ShapeDtypeStruct((2, rows, Z), bf16),
            jax.ShapeDtypeStruct((rows, H), f32),
            jax.ShapeDtypeStruct((1, 128), f32),
        ],
        in_specs=in_vmem(5),
        out_specs=in_vmem(3),
        compiler_params=pltpu.CompilerParams(vmem_limit_bytes=40 * mib),
        cost_estimate=cost(1e10, 12 * mib),
        name="heads",
    )(hidden, embed, target, mask, weights)


def run_orthogonal(base, share, own, matrix):
    side, width = matrix.shape
    return pl.pallas_call(
        functools.partial(orthogonal_block, base, 512),
        out_shape=jax.ShapeDtypeStruct((share, width), bf16),
        in_specs=[pl.BlockSpec(memory_space=pltpu.SMEM)] + in_vmem(1),
        out_specs=in_vmem(1)[0],
        scratch_shapes=[
            pltpu.VMEM((side, width), bf16),
            pltpu.VMEM((side, side), bf16),
            pltpu.VMEM((side, side), bf16),
        ],
        compiler_params=pltpu.CompilerParams(vmem_limit_bytes=48 * mib),
        cost_estimate=cost(5e10, 6 * mib),
        name="orthogonal",
    )(own, matrix)


def run_turn(matrix):
    return pl.pallas_call(
        functools.partial(turn_block, 256),
        out_shape=jax.ShapeDtypeStruct(matrix.shape[::-1], bf16),
        in_specs=in_vmem(1),
        out_specs=in_vmem(1)[0],
        compiler_params=pltpu.CompilerParams(vmem_limit_bytes=16 * mib),
        cost_estimate=cost(1e6, 3 * mib),
        name="turn",
    )(matrix)


def on_device(
    embeddings,
    samples,
    seq_lengths,
    gru_weight,
    post_weight,
    prior_weight,
    gru_moment,
    post_moment,
    prior_moment,
):
    dz_count = lax.axis_size("dz")
    dx_count = lax.axis_size("dx")
    tp_count = lax.axis_size("tp")
    dp_count = dz_count * dx_count
    dx_index = lax.axis_index("dx")
    tp_index = lax.axis_index("tp")
    dp_index = lax.axis_index("dz") * dx_count + dx_index
    seq_count = embeddings.shape[0]
    seqs = seq_count // tp_count
    units = gru_weight.shape[2]
    groups = Z // ZC
    rows = seqs * FRAMES
    packs = rows // PACK

    def gather(block):
        return lax.all_gather(block, "tp", axis=0, tiled=False)

    def exchange(block, axis):
        return lax.all_to_all(block, axis, 0, 0, tiled=True)

    def mine(block, axis):
        return lax.dynamic_index_in_dim(block, dx_index, axis, keepdims=False)

    weights = gather(gru_weight[:, Z:].astype(bf16))
    head_low = jnp.concatenate([post_weight.astype(bf16), prior_weight.astype(bf16)], axis=0)

    by_part = jnp.swapaxes(samples.reshape(tp_count, seqs, FRAMES, groups), 1, 2)
    by_part = by_part.reshape(tp_count * rows, groups).astype(bf16)

    def one_hot(chosen):
        count = chosen.shape[-1]
        classes = jnp.arange(count * ZC, dtype=jnp.int32)
        expand = (classes[None, :] // ZC == jnp.arange(count)[:, None]).astype(bf16)
        return (dot(chosen, expand) == (classes % ZC).astype(f32)).astype(bf16)

    onehot = one_hot(by_part)
    input_part = jnp.concatenate(
        [dot(onehot, gru_weight[k, :Z].astype(bf16)).astype(bf16) for k in range(3)], axis=1
    ).reshape(tp_count, packs, PACK, 3 * units)
    input_part = exchange(input_part, "tp")
    embed_rows = jnp.swapaxes(embeddings.reshape(tp_count, seqs, FRAMES, E), 1, 2)
    embed_rows = embed_rows.reshape(tp_count, rows, E)
    pair_samples = lax.all_gather(by_part, "dx", axis=0, tiled=False)
    half = Z // dx_count
    pair_half = mine(
        pair_samples.reshape(dx_count * tp_count * rows, dz_count // 2, dx_count, -1), 2
    )
    pair_onehot = one_hot(pair_half.reshape(dx_count * tp_count * rows, groups // dx_count))
    pair_onehot = pair_onehot.reshape(dx_count, tp_count * rows, half)
    own_embed = lax.dynamic_index_in_dim(embed_rows, tp_index, 0, keepdims=False)
    onehot = onehot.reshape(tp_count, rows, Z)
    own_target = lax.dynamic_index_in_dim(onehot, tp_index, 0, keepdims=False)
    positions = jnp.arange(FRAMES, dtype=jnp.int32)
    own_lengths = lax.dynamic_slice_in_dim(seq_lengths, tp_index * seqs, seqs, 0)
    frame_mask = (positions[:, None] < own_lengths[None, :]).astype(f32)
    mask_lanes = jnp.broadcast_to(frame_mask.reshape(rows, 1), (rows, 128))

    weights, input_part, head_low, own_embed, own_target, mask_lanes, embed_rows, pair_onehot = (
        lax.optimization_barrier(
            (weights, input_part, head_low, own_embed, own_target, mask_lanes, embed_rows, pair_onehot)
        )
    )
    head_full = gather(head_low)
    hidden, factors, rest = run_forward(input_part, weights, seqs)
    back_heads, direct, loss_lanes = run_heads(
        hidden.reshape(rows, H), own_embed, own_target, mask_lanes, head_full
    )
    everyone = gather(jnp.stack([hidden.reshape(rows, H).astype(bf16), back_heads[0], back_heads[1]]))
    direct = direct.reshape(packs, PACK, H)
    carried = [jnp.zeros((seqs, 3 * H), f32), jnp.zeros((seqs, H), f32)]
    own_back = []
    for first, last in ((EARLY, packs), (0, EARLY)):
        back, *carried = run_backward(
            direct, factors, rest, weights, carried, seqs, first, last - first, dx_count
        )
        back = back.reshape(dx_count * tp_count, (last - first) * PACK, 3 * units)
        own_back.insert(0, exchange(back, ("dx", "tp")))
    own_back = jnp.concatenate(own_back, axis=1).reshape(dx_count, tp_count * rows, 3 * units)

    shares = [size // dp_count for size in ROWS]
    all_hidden = everyone[:, 0]
    all_post = everyone[:, 2]
    own_heads = lax.dynamic_slice_in_dim(everyone[:, 1:], tp_index * units, units, 3)
    swap = [(i, i ^ 1) for i in range(dx_count)]

    halves = all_hidden.reshape(tp_count * rows, dz_count // 2, dx_count, shares[0])
    here = mine(halves, 2).reshape(tp_count * rows, half)
    there = lax.dynamic_index_in_dim(halves, 1 - dx_index, 2, keepdims=False)
    there = lax.ppermute(there.reshape(tp_count * rows, half), "dx", swap)
    pair_hidden = jnp.where(
        dx_index == 0, jnp.stack([here, there]), jnp.stack([there, here])
    )
    pair_left = jnp.concatenate([pair_onehot, pair_hidden], axis=2)

    def outer(left, right):
        return jnp.einsum("prm,prn->mn", left, right, preferred_element_type=f32).astype(bf16)

    prior_grad = outer(all_hidden, own_heads[:, 0])
    post_grad = jnp.concatenate(
        [outer(all_hidden, own_heads[:, 1]), outer(embed_rows, own_heads[:, 1])], axis=0
    )
    head_grad = jnp.concatenate(
        [
            post_grad.reshape(dz_count, dx_count, shares[3], units),
            prior_grad.reshape(dz_count, dx_count, shares[4], units),
        ],
        axis=2,
    )
    received = lax.ppermute(
        lax.dynamic_index_in_dim(head_grad, 1 - dx_index, 1, keepdims=False), "dx", swap
    )
    head_grad = (mine(head_grad, 1).astype(f32) + received.astype(f32)).astype(bf16)
    local = jnp.concatenate(
        [
            outer(pair_left, own_back[:, :, k * units : (k + 1) * units]).reshape(
                dz_count, shares[0], units
            )
            for k in range(3)
        ]
        + [head_grad],
        axis=1,
    )
    summed = lax.psum_scatter(local, "dz", scatter_dimension=0, tiled=True)[0]
    totals = jnp.stack([jnp.sum(loss_lanes), jnp.sum(frame_mask)])
    totals = jnp.broadcast_to(totals[:, None], (2, 128))
    for axis, count in (("tp", tp_count), ("dx", dx_count), ("dz", dz_count)):
        for bit in range(count.bit_length() - 1):
            pairs = [(i, i ^ (1 << bit)) for i in range(count)]
            totals = totals + lax.ppermute(totals, axis, pairs)
    loss_sum, frame_count = totals[0, 0], totals[1, 0]
    loss_value = loss_sum / frame_count

    embed_part = E // tp_count
    own_rows_e = lax.dynamic_slice_in_dim(head_full, H + tp_index * embed_part, embed_part, 1)
    post_by_seq = jnp.swapaxes(all_post.reshape(tp_count, FRAMES, seqs, Z), 1, 2)
    embed_grad = jnp.einsum(
        "psfk,ek->psfe",
        post_by_seq,
        jnp.concatenate(list(own_rows_e), axis=1),
        preferred_element_type=f32,
    ).reshape(seq_count, FRAMES, embed_part)
    embed_grad = embed_grad / frame_count

    summed = summed.astype(f32) / frame_count
    starts = [sum(shares[:m]) for m in range(MATS)]
    grads = [summed[starts[m] : starts[m] + shares[m]] for m in range(MATS)]

    def own_rows(matrix, axis_dim):
        share = matrix.shape[axis_dim] // dp_count
        return lax.dynamic_slice_in_dim(matrix, dp_index * share, share, axis_dim)

    gru_moments = own_rows(gru_moment, 1)
    moments = [momentum_keep * gru_moments[k] + grads[k] for k in range(3)]
    moments.append(momentum_keep * own_rows(post_moment, 0) + grads[3])
    moments.append(momentum_keep * own_rows(prior_moment, 0) + grads[4])
    ahead = [(grads[m] + momentum_keep * moments[m]).astype(bf16) for m in range(MATS)]

    stride = dp_count // MATS
    widest = max(shares)
    base = shares[0]
    slots = [jnp.zeros((widest, units), bf16)] * dp_count
    for m in range(MATS):
        slots[m * stride] = jnp.pad(ahead[m], ((0, widest - shares[m]), (0, 0)))
    arrived = exchange(jnp.stack(slots), ("dz", "dx"))
    packed = jnp.concatenate(
        [arrived[:, :base].reshape(-1, units), arrived[:, base:].reshape(-1, units)], axis=0
    )
    wide = gather(run_turn(packed)).reshape(H, dp_count * widest)
    own = jnp.stack([tp_index, (dp_index == 3 * stride).astype(jnp.int32)]).astype(jnp.int32)
    result = run_orthogonal(dp_count * base, units, own, wide).T
    results = exchange(
        jnp.concatenate(
            [
                result[: dp_count * base].reshape(dp_count, base, units),
                result[dp_count * base :].reshape(dp_count, widest - base, units),
            ],
            axis=1,
        ),
        ("dz", "dx"),
    )

    def renew(weight_rows, index, largest):
        factor = learn_rate * update_scale * math.sqrt(largest)
        shard = results[index * stride, : weight_rows.shape[0]].astype(f32)
        return weight_rows * (1.0 - learn_rate * weight_decay) - factor * shard

    gru_rows = own_rows(gru_weight, 1)
    new_gru = jnp.stack([renew(gru_rows[k], k, gru_weight.shape[1]) for k in range(3)])
    new_post = renew(own_rows(post_weight, 0), 3, max(post_weight.shape[0], Z))
    new_prior = renew(own_rows(prior_weight, 0), 4, max(H, Z))
    return (
        loss_value,
        embed_grad,
        new_gru,
        new_post,
        new_prior,
        jnp.stack(moments[:3]),
        moments[3],
        moments[4],
    )

def solution(mesh):
    dp_count, tp_count = mesh.devices.shape
    mesh = jax.sharding.Mesh(
        mesh.devices.reshape(dp_count // 2, 2, tp_count), ("dz", "dx", "tp")
    )
    dp = ("dz", "dx")
    in_specs = (
        P(dp, None, None),
        P(dp, None, None),
        P(dp),
        P(None, None, "tp"),
        P(None, "tp"),
        P(None, "tp"),
        P(None, None, "tp"),
        P(None, "tp"),
        P(None, "tp"),
    )
    out_specs = (
        P(),
        P(dp, None, "tp"),
        P(None, dp, "tp"),
        P(dp, "tp"),
        P(dp, "tp"),
        P(None, dp, "tp"),
        P(dp, "tp"),
        P(dp, "tp"),
    )
    return jax.shard_map(
        on_device, mesh=mesh, in_specs=in_specs, out_specs=out_specs, check_vma=False
    )
```

```python
import functools
import math

import jax
import jax.numpy as jnp
from jax import lax
from jax.experimental import pallas as pl
from jax.experimental.pallas import tpu as pltpu
from jax.sharding import PartitionSpec as P

H = 1024
ZC = 32
E = 1536
FRAMES = 56
MATS = 5
Z = 1024
ROWS = (Z + H, Z + H, Z + H, H + E, H)
PACK = 8


coeff_linear = 3.4445
coeff_cubic = -4.775
coeff_quintic = 2.0315
momentum_keep = 0.95
learn_rate = 0.2
weight_decay = 0.01
update_scale = 0.2
tiny_value = 1e-07
mib = 1 << 20
f32 = jnp.float32
bf16 = jnp.bfloat16
NT = (((1,), (1,)), ((), ()))
TN = (((0,), (0,)), ((), ()))


def dot(left, right):
    return jnp.dot(left, right, preferred_element_type=f32)


def dot_tn(left, right):
    return lax.dot_general(left, right, TN, preferred_element_type=f32)


def dot_nt(left, right):
    return lax.dot_general(left, right, NT, preferred_element_type=f32)


def scan_forward(seqs, x_ref, w_ref, h_ref, k_ref, u_ref, state):
    parts, packs = x_ref.shape[:2]
    units = w_ref.shape[3]
    per_pack = PACK // seqs
    state[...] = jnp.zeros_like(state)

    def pack(i, carry):
        for frame in range(per_pack):
            rows = slice(frame * seqs, (frame + 1) * seqs)
            if frame == 0:
                source, live = jnp.maximum(i - 1, 0), jnp.where(i > 0, 1.0, 0.0)
                spot = slice((per_pack - 1) * seqs, per_pack * seqs)
            else:
                source, live = i, None
                spot = slice((frame - 1) * seqs, frame * seqs)
            before = state[...]
            low = before.astype(bf16)
            for p in range(parts):
                cols = slice(p * units, (p + 1) * units)
                given = x_ref[p, source].astype(f32)[spot]
                if live is not None:
                    given = given * live
                pre = [
                    given[:, k * units : (k + 1) * units] + dot(low, w_ref[p, k]) for k in range(3)
                ]
                last = before[:, cols]
                r = jax.nn.sigmoid(pre[0])
                c = jnp.tanh(r * pre[1])
                u = jax.nn.sigmoid(pre[2] - 1.0)
                rest = 1.0 - u
                new = u * c + rest * last
                inner = u * (1.0 - c * c)
                state[:, cols] = new
                h_ref[i, rows, cols] = new
                k_ref[0, i, rows, cols] = inner * pre[1] * r * (1.0 - r)
                k_ref[1, i, rows, cols] = inner * r
                k_ref[2, i, rows, cols] = (c - last) * u * rest
                u_ref[i, rows, cols] = rest
        return carry

    lax.fori_loop(0, packs, pack, 0)


def scan_backward(seqs, d_ref, k_ref, u_ref, w_ref, b_ref, now, kept, turned):
    copies, parts, packs = b_ref.shape[:3]
    units = w_ref.shape[3]
    per_pack = PACK // seqs
    now[...] = jnp.zeros_like(now)
    kept[...] = jnp.zeros_like(kept)

    def turn(n, carry):
        spot = pl.ds(pl.multiple_of(n * units, units), units)
        turned[spot, :] = w_ref[n // 3, n % 3].T
        return carry

    lax.fori_loop(0, 3 * parts, turn, 0)

    def pack(n, carry):
        i = packs - 1 - n
        later = [None] * per_pack
        for frame in reversed(range(per_pack)):
            rows = slice(frame * seqs, (frame + 1) * seqs)
            values = now[...]
            later[frame] = values
            dh = d_ref[i, rows] + kept[...] + dot(values.astype(bf16), turned[...])
            kept[...] = dh * u_ref[i, rows]
            for p in range(parts):
                cols = slice(p * units, (p + 1) * units)
                for k in range(3):
                    spot = slice((3 * p + k) * units, (3 * p + k + 1) * units)
                    now[:, spot] = dh[:, cols] * k_ref[k, i, rows, cols]
        stacked = jnp.concatenate(later, axis=0).astype(bf16)
        for p in range(parts):
            for copy in range(copies):
                b_ref[copy, p, i] = stacked[:, p * 3 * units : (p + 1) * 3 * units]
        return carry

    lax.fori_loop(0, packs, pack, 0)


def butterfly(values, combine, lane):
    step = 1
    while step < ZC:
        up = pltpu.roll(values, step, 1)
        down = pltpu.roll(values, values.shape[1] - step, 1)
        values = combine(values, jnp.where((lane & step) != 0, up, down))
        step *= 2
    return values


def head_block(h_ref, e_ref, t_ref, m_ref, w_ref, back_ref, d_ref, loss_ref):
    parts = w_ref.shape[0]
    units = w_ref.shape[2]
    rows = h_ref.shape[0]
    low = h_ref[...].astype(bf16)
    mask = m_ref[...]
    lane = lax.broadcasted_iota(jnp.int32, (rows, 128), 1)
    loss = jnp.zeros((rows, 128), f32)
    for p in range(parts):
        post = dot(low, w_ref[p, :H]) + dot(e_ref[...], w_ref[p, H : H + E])
        prior = dot(low, w_ref[p, H + E :])
        for head, logits in enumerate((prior, post)):
            for piece in range(units // 128):
                l = logits[:, piece * 128 : (piece + 1) * 128]
                cols = slice(p * units + piece * 128, p * units + (piece + 1) * 128)
                target = t_ref[:, cols].astype(f32)
                top = butterfly(l, jnp.maximum, lane)
                e = jnp.exp(l - top)
                total = butterfly(e, jnp.add, lane)
                loss = loss + mask * ((top + jnp.log(total)) * (1.0 / ZC) - target * l)
                back_ref[head, :, cols] = (mask * (e / total - target)).astype(bf16)
    loss_ref[...] = jnp.sum(loss, axis=0, keepdims=True)
    direct = jnp.zeros((rows, H), f32)
    for p in range(parts):
        cols = slice(p * units, (p + 1) * units)
        direct = direct + dot_nt(back_ref[0, :, cols], w_ref[p, H + E :])
        direct = direct + dot_nt(back_ref[1, :, cols], w_ref[p, :H])
    d_ref[...] = direct


def head_grads(spot_ref, all_ref, e_ref, o_ref):
    parts, rows = e_ref.shape[0], e_ref.shape[1]
    units = o_ref.shape[1]
    frames = parts * rows
    own = pl.ds(pl.multiple_of(spot_ref[0] * units, units), units)
    post = all_ref[:, 3, :, own].reshape(frames, units)
    both = jnp.concatenate([post, all_ref[:, 2, :, own].reshape(frames, units)], axis=1)
    for m in range(H // 256):
        spot = slice(m * 256, (m + 1) * 256)
        grad = dot_tn(all_ref[:, 0, :, spot].reshape(frames, 256), both).astype(bf16)
        o_ref[m * 256 : (m + 1) * 256] = grad[:, :units]
        o_ref[H + E + m * 256 : H + E + (m + 1) * 256] = grad[:, units:]
    for m in range(E // 256):
        spot = slice(m * 256, (m + 1) * 256)
        grad = dot_tn(e_ref[:, :, spot].reshape(frames, 256), post).astype(bf16)
        o_ref[H + m * 256 : H + (m + 1) * 256] = grad


def gru_grads(spot_ref, one_ref, all_ref, b_ref, o_ref):
    parts, rows = all_ref.shape[0], all_ref.shape[2]
    units = o_ref.shape[2]
    frames = parts * rows
    share = o_ref.shape[1] // 3
    half = o_ref.shape[0] // 2
    me = spot_ref[1]
    back = [b_ref[x].reshape(frames, 3 * units) for x in (me, 1 - me)]
    for z in range(2 * half):
        if z < half:
            spot = slice(z * share, (z + 1) * share)
            left = [one_ref[x, :, spot] for x in (me, 1 - me)]
        else:
            spot = pl.ds(pl.multiple_of(((z - half) * 2 + me) * share, share), share)
            left = [all_ref[:, n, :, spot].reshape(frames, share) for n in (0, 1)]
        grad = (dot_tn(left[0], back[0]) + dot_tn(left[1], back[1])).astype(bf16)
        for k in range(3):
            o_ref[z, k * share : (k + 1) * share] = grad[:, k * units : (k + 1) * units]


def orthogonal_block(base, tile, own_ref, g_ref, o_ref, x, a, b):
    side, width = g_ref.shape
    share = o_ref.shape[0]
    own = pl.ds(pl.multiple_of(own_ref[0] * share, share), share)
    wide = own_ref[1] > 0

    def either(run):
        pl.when(wide)(functools.partial(run, width))
        pl.when(jnp.logical_not(wide))(functools.partial(run, base))

    def squares(i, total):
        rows = pl.ds(pl.multiple_of(i * 128, 128), 128)
        v = g_ref[rows, :].astype(f32)
        return total + jnp.sum(v * v)

    total = lax.fori_loop(0, side // 128, squares, jnp.zeros((), f32))
    scale = 1.0 / (jnp.sqrt(jnp.full((1, 128), total, f32)) + tiny_value)
    scale = jnp.broadcast_to(scale[:, :1], (1, width))

    def shrink(i, carry):
        rows = pl.ds(pl.multiple_of(i * 128, 128), 128)
        x[rows, :] = (g_ref[rows, :].astype(f32) * scale).astype(bf16)
        return carry

    lax.fori_loop(0, side // 128, shrink, 0)

    def square(depth):
        def block(j, carry):
            cols = pl.ds(pl.multiple_of(j * tile, tile), tile)
            a[:, cols] = dot_nt(x[:, :depth], x[cols, :depth]).astype(bf16)
            return carry

        lax.fori_loop(0, side // tile, block, 0)

    def mix(j, carry):
        cols = pl.ds(pl.multiple_of(j * tile, tile), tile)
        b[:, cols] = (
            coeff_cubic * a[:, cols].astype(f32) + coeff_quintic * dot(a[...], a[:, cols])
        ).astype(bf16)
        return carry

    def renew(j, carry):
        cols = pl.ds(pl.multiple_of(j * tile, tile), tile)
        x[:, cols] = (
            coeff_linear * x[:, cols].astype(f32) + dot(b[...], x[:, cols])
        ).astype(bf16)
        return carry

    used = jnp.where(wide, width // tile, base // tile)

    def sweep(s, carry):
        either(square)
        lax.fori_loop(0, side // tile, mix, 0)
        lax.fori_loop(0, used, renew, 0)
        return carry

    lax.fori_loop(0, 4, sweep, 0)
    either(square)
    part = (coeff_cubic * a[own, :].astype(f32) + coeff_quintic * dot(a[own, :], a[...])).astype(bf16)

    def last(j, carry):
        cols = pl.ds(pl.multiple_of(j * tile, tile), tile)
        o_ref[:, cols] = (
            coeff_linear * x[own, cols].astype(f32) + dot(part, x[:, cols])
        ).astype(bf16)
        return carry

    lax.fori_loop(0, width // tile, last, 0)


def turn_block(tile, g_ref, o_ref):
    def block(i, carry):
        spot = pl.ds(pl.multiple_of(i * tile, tile), tile)
        o_ref[:, spot] = g_ref[spot, :].T
        return carry

    lax.fori_loop(0, g_ref.shape[0] // tile, block, 0)


def in_vmem(count):
    return [pl.BlockSpec(memory_space=pltpu.VMEM)] * count


def cost(flops, touched):
    return pl.CostEstimate(flops=int(flops), bytes_accessed=int(touched), transcendentals=0)


def run_forward(inputs, weights, seqs):
    parts, packs = inputs.shape[:2]
    out = jax.ShapeDtypeStruct((packs, PACK, H), f32)
    return pl.pallas_call(
        functools.partial(scan_forward, seqs),
        out_shape=[out, jax.ShapeDtypeStruct((3, packs, PACK, H), f32), out],
        in_specs=in_vmem(2),
        out_specs=in_vmem(3),
        scratch_shapes=[pltpu.VMEM((seqs, H), f32)],
        compiler_params=pltpu.CompilerParams(vmem_limit_bytes=40 * mib),
        cost_estimate=cost(6e10, 20 * mib),
        name="scan_forward",
    )(inputs, weights)


def run_backward(direct, factors, rest, weights, seqs, copies):
    packs = direct.shape[0]
    parts, units = weights.shape[0], weights.shape[3]
    return pl.pallas_call(
        functools.partial(scan_backward, seqs),
        out_shape=jax.ShapeDtypeStruct((copies, parts, packs, PACK, 3 * units), bf16),
        in_specs=in_vmem(4),
        out_specs=in_vmem(1)[0],
        scratch_shapes=[
            pltpu.VMEM((seqs, 3 * H), f32),
            pltpu.VMEM((seqs, H), f32),
            pltpu.VMEM((3 * H, H), bf16),
        ],
        compiler_params=pltpu.CompilerParams(vmem_limit_bytes=44 * mib),
        cost_estimate=cost(6e10, 20 * mib),
        name="scan_backward",
    )(direct, factors, rest, weights)


def run_heads(hidden, embed, target, mask, weights):
    rows = hidden.shape[0]
    return pl.pallas_call(
        head_block,
        out_shape=[
            jax.ShapeDtypeStruct((2, rows, Z), bf16),
            jax.ShapeDtypeStruct((rows, H), f32),
            jax.ShapeDtypeStruct((1, 128), f32),
        ],
        in_specs=in_vmem(5),
        out_specs=in_vmem(3),
        compiler_params=pltpu.CompilerParams(vmem_limit_bytes=40 * mib),
        cost_estimate=cost(1e10, 12 * mib),
        name="heads",
    )(hidden, embed, target, mask, weights)


def run_head_grads(spot, everyone, embed):
    units = everyone.shape[3] // everyone.shape[0]
    return pl.pallas_call(
        head_grads,
        out_shape=jax.ShapeDtypeStruct((H + E + H, units), bf16),
        in_specs=[pl.BlockSpec(memory_space=pltpu.SMEM)] + in_vmem(2),
        out_specs=in_vmem(1)[0],
        compiler_params=pltpu.CompilerParams(vmem_limit_bytes=40 * mib),
        cost_estimate=cost(4e9, 12 * mib),
        name="head_grads",
    )(spot, everyone, embed)


def run_gru_grads(spot, onehot, everyone, back, dz_count):
    units = back.shape[3] // 3
    share = (Z + H) // (2 * dz_count)
    return pl.pallas_call(
        gru_grads,
        out_shape=jax.ShapeDtypeStruct((dz_count, 3 * share, units), bf16),
        in_specs=[pl.BlockSpec(memory_space=pltpu.SMEM)] + in_vmem(3),
        out_specs=in_vmem(1)[0],
        compiler_params=pltpu.CompilerParams(vmem_limit_bytes=48 * mib),
        cost_estimate=cost(4e9, 12 * mib),
        name="gru_grads",
    )(spot, onehot, everyone, back)


def plain_gru_grads(dx_index, onehot, everyone, back, dz_count):
    units = back.shape[3] // 3
    share = (Z + H) // (2 * dz_count)
    total = 0.0
    for n, x in enumerate((dx_index, 1 - dx_index)):
        hidden = everyone[:, n].reshape(-1, dz_count // 2, 2, share)
        hidden = lax.dynamic_index_in_dim(hidden, dx_index, 2, keepdims=False)
        ones = lax.dynamic_index_in_dim(onehot, x, 0, keepdims=False)
        left = jnp.concatenate([ones, hidden.reshape(ones.shape)], axis=1)
        right = lax.dynamic_index_in_dim(back, x, 0, keepdims=False)
        total = total + dot_tn(left, right.reshape(-1, 3 * units))
    grads = total.astype(bf16).reshape(dz_count, share, 3, units)
    return jnp.swapaxes(grads, 1, 2).reshape(dz_count, 3 * share, units)


def run_orthogonal(base, share, own, matrix):
    side, width = matrix.shape
    return pl.pallas_call(
        functools.partial(orthogonal_block, base, 512),
        out_shape=jax.ShapeDtypeStruct((share, width), bf16),
        in_specs=[pl.BlockSpec(memory_space=pltpu.SMEM)] + in_vmem(1),
        out_specs=in_vmem(1)[0],
        scratch_shapes=[
            pltpu.VMEM((side, width), bf16),
            pltpu.VMEM((side, side), bf16),
            pltpu.VMEM((side, side), bf16),
        ],
        compiler_params=pltpu.CompilerParams(vmem_limit_bytes=48 * mib),
        cost_estimate=cost(5e10, 6 * mib),
        name="orthogonal",
    )(own, matrix)


def run_turn(matrix):
    return pl.pallas_call(
        functools.partial(turn_block, 256),
        out_shape=jax.ShapeDtypeStruct(matrix.shape[::-1], bf16),
        in_specs=in_vmem(1),
        out_specs=in_vmem(1)[0],
        compiler_params=pltpu.CompilerParams(vmem_limit_bytes=16 * mib),
        cost_estimate=cost(1e6, 3 * mib),
        name="turn",
    )(matrix)


def on_device(
    embeddings,
    samples,
    seq_lengths,
    gru_weight,
    post_weight,
    prior_weight,
    gru_moment,
    post_moment,
    prior_moment,
):
    dz_count = lax.axis_size("dz")
    dx_count = lax.axis_size("dx")
    tp_count = lax.axis_size("tp")
    dp_count = dz_count * dx_count
    dx_index = lax.axis_index("dx")
    tp_index = lax.axis_index("tp")
    dp_index = lax.axis_index("dz") * dx_count + dx_index
    seq_count = embeddings.shape[0]
    seqs = seq_count // tp_count
    units = gru_weight.shape[2]
    groups = Z // ZC
    rows = seqs * FRAMES
    packs = rows // PACK

    def gather(block):
        return lax.all_gather(block, "tp", axis=0, tiled=False)

    def exchange(block, axis):
        return lax.all_to_all(block, axis, 0, 0, tiled=True)

    def mine(block, axis):
        return lax.dynamic_index_in_dim(block, dx_index, axis, keepdims=False)

    weights = gather(gru_weight[:, Z:].astype(bf16))
    head_low = jnp.concatenate([post_weight.astype(bf16), prior_weight.astype(bf16)], axis=0)

    by_part = jnp.swapaxes(samples.reshape(tp_count, seqs, FRAMES, groups), 1, 2)
    by_part = by_part.reshape(tp_count * rows, groups).astype(bf16)

    def one_hot(chosen):
        count = chosen.shape[-1]
        classes = jnp.arange(count * ZC, dtype=jnp.int32)
        expand = (classes[None, :] // ZC == jnp.arange(count)[:, None]).astype(bf16)
        return (dot(chosen, expand) == (classes % ZC).astype(f32)).astype(bf16)

    onehot = one_hot(by_part)
    input_part = jnp.concatenate(
        [dot(onehot, gru_weight[k, :Z].astype(bf16)).astype(bf16) for k in range(3)], axis=1
    ).reshape(tp_count, packs, PACK, 3 * units)
    input_part = exchange(input_part, "tp")
    embed_rows = jnp.swapaxes(embeddings.reshape(tp_count, seqs, FRAMES, E), 1, 2)
    embed_rows = embed_rows.reshape(tp_count, rows, E)
    pair_samples = lax.all_gather(by_part, "dx", axis=0, tiled=False)
    half = Z // dx_count
    pair_half = mine(
        pair_samples.reshape(dx_count * tp_count * rows, dz_count // 2, dx_count, -1), 2
    )
    pair_onehot = one_hot(pair_half.reshape(dx_count * tp_count * rows, groups // dx_count))
    pair_onehot = pair_onehot.reshape(dx_count, tp_count * rows, half)
    own_embed = lax.dynamic_index_in_dim(embed_rows, tp_index, 0, keepdims=False)
    onehot = onehot.reshape(tp_count, rows, Z)
    own_target = lax.dynamic_index_in_dim(onehot, tp_index, 0, keepdims=False)
    positions = jnp.arange(FRAMES, dtype=jnp.int32)
    own_lengths = lax.dynamic_slice_in_dim(seq_lengths, tp_index * seqs, seqs, 0)
    frame_mask = (positions[:, None] < own_lengths[None, :]).astype(f32)
    mask_lanes = jnp.broadcast_to(frame_mask.reshape(rows, 1), (rows, 128))

    weights, input_part, head_low, own_embed, own_target, mask_lanes, embed_rows, pair_onehot = (
        lax.optimization_barrier(
            (weights, input_part, head_low, own_embed, own_target, mask_lanes, embed_rows, pair_onehot)
        )
    )
    head_full = gather(head_low)
    hidden, factors, rest = run_forward(input_part, weights, seqs)
    hidden = hidden.reshape(rows, H)
    hidden_low = hidden.astype(bf16)
    swap = [(i, i ^ 1) for i in range(dx_count)]
    neighbour = lax.ppermute(hidden_low, "dx", swap)
    back_heads, direct, loss_lanes = run_heads(
        hidden, own_embed, own_target, mask_lanes, head_full
    )
    everyone = gather(jnp.concatenate([hidden_low[None], neighbour[None], back_heads], axis=0))
    back = run_backward(
        direct.reshape(packs, PACK, H), factors, rest, weights, seqs, dx_count
    )
    own_back = exchange(back.reshape(dx_count * tp_count, rows, 3 * units), ("dx", "tp"))
    own_back = own_back.reshape(dx_count, tp_count, rows, 3 * units)

    shares = [size // dp_count for size in ROWS]
    all_post = everyone[:, 3]
    spot = jnp.stack([tp_index, dx_index]).astype(jnp.int32)

    head_grad = run_head_grads(spot, everyone, embed_rows)

    def half_of(x):
        return jnp.concatenate(
            [
                lax.dynamic_index_in_dim(
                    block.reshape(dz_count, dx_count, -1, units), x, 1, keepdims=False
                )
                for block in (head_grad[: H + E], head_grad[H + E :])
            ],
            axis=1,
        )

    received = lax.ppermute(half_of(1 - dx_index), "dx", swap)
    if shares[0] % 128 == 0:
        gru_grad = run_gru_grads(spot, pair_onehot, everyone, own_back, dz_count)
    else:
        gru_grad = plain_gru_grads(dx_index, pair_onehot, everyone, own_back, dz_count)
    both = (half_of(dx_index).astype(f32) + received.astype(f32)).astype(bf16)
    local = jnp.concatenate([gru_grad, both], axis=1)
    summed = lax.psum_scatter(local, "dz", scatter_dimension=0, tiled=True)[0]
    totals = jnp.stack([jnp.sum(loss_lanes), jnp.sum(frame_mask)])
    totals = jnp.broadcast_to(totals[:, None], (2, 128))
    for axis, count in (("tp", tp_count), ("dx", dx_count), ("dz", dz_count)):
        for bit in range(count.bit_length() - 1):
            pairs = [(i, i ^ (1 << bit)) for i in range(count)]
            totals = totals + lax.ppermute(totals, axis, pairs)
    loss_sum, frame_count = totals[0, 0], totals[1, 0]
    loss_value = loss_sum / frame_count

    embed_part = E // tp_count
    own_rows_e = lax.dynamic_slice_in_dim(head_full, H + tp_index * embed_part, embed_part, 1)
    post_by_seq = jnp.swapaxes(all_post.reshape(tp_count, FRAMES, seqs, Z), 1, 2)
    embed_grad = jnp.einsum(
        "psfk,ek->psfe",
        post_by_seq,
        jnp.concatenate(list(own_rows_e), axis=1),
        preferred_element_type=f32,
    ).reshape(seq_count, FRAMES, embed_part)
    embed_grad = embed_grad / frame_count

    summed = summed.astype(f32) / frame_count
    starts = [sum(shares[:m]) for m in range(MATS)]
    grads = [summed[starts[m] : starts[m] + shares[m]] for m in range(MATS)]

    def own_rows(matrix, axis_dim):
        share = matrix.shape[axis_dim] // dp_count
        return lax.dynamic_slice_in_dim(matrix, dp_index * share, share, axis_dim)

    gru_moments = own_rows(gru_moment, 1)
    moments = [momentum_keep * gru_moments[k] + grads[k] for k in range(3)]
    moments.append(momentum_keep * own_rows(post_moment, 0) + grads[3])
    moments.append(momentum_keep * own_rows(prior_moment, 0) + grads[4])
    ahead = [(grads[m] + momentum_keep * moments[m]).astype(bf16) for m in range(MATS)]

    stride = dp_count // MATS
    widest = max(shares)
    base = shares[0]
    slots = [jnp.zeros((widest, units), bf16)] * dp_count
    for m in range(MATS):
        slots[m * stride] = jnp.pad(ahead[m], ((0, widest - shares[m]), (0, 0)))
    arrived = exchange(jnp.stack(slots), ("dz", "dx"))
    packed = jnp.concatenate(
        [arrived[:, :base].reshape(-1, units), arrived[:, base:].reshape(-1, units)], axis=0
    )
    wide = gather(run_turn(packed)).reshape(H, dp_count * widest)
    own = jnp.stack([tp_index, (dp_index == 3 * stride).astype(jnp.int32)]).astype(jnp.int32)
    result = run_orthogonal(dp_count * base, units, own, wide).T
    results = exchange(
        jnp.concatenate(
            [
                result[: dp_count * base].reshape(dp_count, base, units),
                result[dp_count * base :].reshape(dp_count, widest - base, units),
            ],
            axis=1,
        ),
        ("dz", "dx"),
    )

    def renew(weight_rows, index, largest):
        factor = learn_rate * update_scale * math.sqrt(largest)
        shard = results[index * stride, : weight_rows.shape[0]].astype(f32)
        return weight_rows * (1.0 - learn_rate * weight_decay) - factor * shard

    gru_rows = own_rows(gru_weight, 1)
    new_gru = jnp.stack([renew(gru_rows[k], k, gru_weight.shape[1]) for k in range(3)])
    new_post = renew(own_rows(post_weight, 0), 3, max(post_weight.shape[0], Z))
    new_prior = renew(own_rows(prior_weight, 0), 4, max(H, Z))
    return (
        loss_value,
        embed_grad,
        new_gru,
        new_post,
        new_prior,
        jnp.stack(moments[:3]),
        moments[3],
        moments[4],
    )

def solution(mesh):
    dp_count, tp_count = mesh.devices.shape
    mesh = jax.sharding.Mesh(
        mesh.devices.reshape(dp_count // 2, 2, tp_count), ("dz", "dx", "tp")
    )
    dp = ("dz", "dx")
    in_specs = (
        P(dp, None, None),
        P(dp, None, None),
        P(dp),
        P(None, None, "tp"),
        P(None, "tp"),
        P(None, "tp"),
        P(None, None, "tp"),
        P(None, "tp"),
        P(None, "tp"),
    )
    out_specs = (
        P(),
        P(dp, None, "tp"),
        P(None, dp, "tp"),
        P(dp, "tp"),
        P(dp, "tp"),
        P(None, dp, "tp"),
        P(dp, "tp"),
        P(dp, "tp"),
    )
    return jax.shard_map(
        on_device, mesh=mesh, in_specs=in_specs, out_specs=out_specs, check_vma=False
    )
```

```python
import functools
import math

import jax
import jax.numpy as jnp
from jax import lax
from jax.experimental import pallas as pl
from jax.experimental.pallas import tpu as pltpu
from jax.sharding import PartitionSpec as P

H = 1024
ZC = 32
E = 1536
FRAMES = 56
MATS = 5
Z = 1024
ROWS = (Z + H, Z + H, Z + H, H + E, H)
PACK = 8


coeff_linear = 3.4445
coeff_cubic = -4.775
coeff_quintic = 2.0315
momentum_keep = 0.95
learn_rate = 0.2
weight_decay = 0.01
update_scale = 0.2
tiny_value = 1e-07
mib = 1 << 20
f32 = jnp.float32
bf16 = jnp.bfloat16
NT = (((1,), (1,)), ((), ()))
TN = (((0,), (0,)), ((), ()))


def dot(left, right):
    return jnp.dot(left, right, preferred_element_type=f32)


def dot_tn(left, right):
    return lax.dot_general(left, right, TN, preferred_element_type=f32)


def dot_nt(left, right):
    return lax.dot_general(left, right, NT, preferred_element_type=f32)


def scan_forward(seqs, x_ref, w_ref, h_ref, k_ref, u_ref, state):
    parts, packs = x_ref.shape[:2]
    units = w_ref.shape[3]
    per_pack = PACK // seqs
    state[...] = jnp.zeros_like(state)

    def pack(i, carry):
        for frame in range(per_pack):
            rows = slice(frame * seqs, (frame + 1) * seqs)
            if frame == 0:
                source, live = jnp.maximum(i - 1, 0), jnp.where(i > 0, 1.0, 0.0)
                spot = slice((per_pack - 1) * seqs, per_pack * seqs)
            else:
                source, live = i, None
                spot = slice((frame - 1) * seqs, frame * seqs)
            before = state[...]
            low = before.astype(bf16)
            for p in range(parts):
                cols = slice(p * units, (p + 1) * units)
                given = x_ref[p, source].astype(f32)[spot]
                if live is not None:
                    given = given * live
                pre = [
                    given[:, k * units : (k + 1) * units] + dot(low, w_ref[p, k]) for k in range(3)
                ]
                last = before[:, cols]
                r = jax.nn.sigmoid(pre[0])
                c = jnp.tanh(r * pre[1])
                u = jax.nn.sigmoid(pre[2] - 1.0)
                rest = 1.0 - u
                new = u * c + rest * last
                inner = u * (1.0 - c * c)
                state[:, cols] = new
                h_ref[i, rows, cols] = new
                k_ref[0, i, rows, cols] = inner * pre[1] * r * (1.0 - r)
                k_ref[1, i, rows, cols] = inner * r
                k_ref[2, i, rows, cols] = (c - last) * u * rest
                u_ref[i, rows, cols] = rest
        return carry

    lax.fori_loop(0, packs, pack, 0)


def scan_backward(seqs, d_ref, k_ref, u_ref, w_ref, b_ref, now, kept, turned):
    copies, parts, packs = b_ref.shape[:3]
    units = w_ref.shape[3]
    per_pack = PACK // seqs
    now[...] = jnp.zeros_like(now)
    kept[...] = jnp.zeros_like(kept)

    def turn(n, carry):
        spot = pl.ds(pl.multiple_of(n * units, units), units)
        turned[spot, :] = w_ref[n // 3, n % 3].T
        return carry

    lax.fori_loop(0, 3 * parts, turn, 0)

    def pack(n, carry):
        i = packs - 1 - n
        later = [None] * per_pack
        for frame in reversed(range(per_pack)):
            rows = slice(frame * seqs, (frame + 1) * seqs)
            values = now[...]
            later[frame] = values
            dh = d_ref[i, rows] + kept[...] + dot(values.astype(bf16), turned[...])
            kept[...] = dh * u_ref[i, rows]
            for p in range(parts):
                cols = slice(p * units, (p + 1) * units)
                for k in range(3):
                    spot = slice((3 * p + k) * units, (3 * p + k + 1) * units)
                    now[:, spot] = dh[:, cols] * k_ref[k, i, rows, cols]
        stacked = jnp.concatenate(later, axis=0).astype(bf16)
        for p in range(parts):
            for copy in range(copies):
                b_ref[copy, p, i] = stacked[:, p * 3 * units : (p + 1) * 3 * units]
        return carry

    lax.fori_loop(0, packs, pack, 0)


def butterfly(values, combine, lane):
    step = 1
    while step < ZC:
        up = pltpu.roll(values, step, 1)
        down = pltpu.roll(values, values.shape[1] - step, 1)
        values = combine(values, jnp.where((lane & step) != 0, up, down))
        step *= 2
    return values


def head_block(h_ref, e_ref, t_ref, m_ref, w_ref, back_ref, d_ref, loss_ref):
    parts = w_ref.shape[0]
    units = w_ref.shape[2]
    rows = h_ref.shape[0]
    low = h_ref[...].astype(bf16)
    mask = m_ref[...]
    lane = lax.broadcasted_iota(jnp.int32, (rows, 128), 1)
    loss = jnp.zeros((rows, 128), f32)
    for p in range(parts):
        post = dot(low, w_ref[p, :H]) + dot(e_ref[...], w_ref[p, H : H + E])
        prior = dot(low, w_ref[p, H + E :])
        for head, logits in enumerate((prior, post)):
            for piece in range(units // 128):
                l = logits[:, piece * 128 : (piece + 1) * 128]
                cols = slice(p * units + piece * 128, p * units + (piece + 1) * 128)
                target = t_ref[:, cols].astype(f32)
                top = butterfly(l, jnp.maximum, lane)
                e = jnp.exp(l - top)
                total = butterfly(e, jnp.add, lane)
                loss = loss + mask * ((top + jnp.log(total)) * (1.0 / ZC) - target * l)
                back_ref[head, :, cols] = (mask * (e / total - target)).astype(bf16)
    loss_ref[...] = jnp.sum(loss, axis=0, keepdims=True)
    direct = jnp.zeros((rows, H), f32)
    for p in range(parts):
        cols = slice(p * units, (p + 1) * units)
        direct = direct + dot_nt(back_ref[0, :, cols], w_ref[p, H + E :])
        direct = direct + dot_nt(back_ref[1, :, cols], w_ref[p, :H])
    d_ref[...] = direct


def head_grads(spot_ref, all_ref, e_ref, o_ref):
    parts, rows = e_ref.shape[0], e_ref.shape[1]
    units = o_ref.shape[1]
    frames = parts * rows
    own = pl.ds(pl.multiple_of(spot_ref[0] * units, units), units)
    post = all_ref[:, 3, :, own].reshape(frames, units)
    both = jnp.concatenate([post, all_ref[:, 2, :, own].reshape(frames, units)], axis=1)
    for m in range(H // 256):
        spot = slice(m * 256, (m + 1) * 256)
        grad = dot_tn(all_ref[:, 0, :, spot].reshape(frames, 256), both).astype(bf16)
        o_ref[m * 256 : (m + 1) * 256] = grad[:, :units]
        o_ref[H + E + m * 256 : H + E + (m + 1) * 256] = grad[:, units:]
    for m in range(E // 256):
        spot = slice(m * 256, (m + 1) * 256)
        grad = dot_tn(e_ref[:, :, spot].reshape(frames, 256), post).astype(bf16)
        o_ref[H + m * 256 : H + (m + 1) * 256] = grad


def gru_grads(spot_ref, one_ref, all_ref, b_ref, o_ref):
    parts, rows = all_ref.shape[0], all_ref.shape[2]
    units = o_ref.shape[2]
    frames = parts * rows
    share = o_ref.shape[1] // 3
    half = o_ref.shape[0] // 2
    me = spot_ref[1]
    back = [b_ref[x].reshape(frames, 3 * units) for x in (me, 1 - me)]
    for z in range(2 * half):
        if z < half:
            spot = slice(z * share, (z + 1) * share)
            left = [one_ref[x, :, spot] for x in (me, 1 - me)]
        else:
            spot = pl.ds(pl.multiple_of(((z - half) * 2 + me) * share, share), share)
            left = [all_ref[:, n, :, spot].reshape(frames, share) for n in (0, 1)]
        grad = (dot_tn(left[0], back[0]) + dot_tn(left[1], back[1])).astype(bf16)
        for k in range(3):
            o_ref[z, k * share : (k + 1) * share] = grad[:, k * units : (k + 1) * units]


def orthogonal_block(base, tile, own_ref, g_ref, o_ref, x, a, b):
    side, width = g_ref.shape
    share = o_ref.shape[0]
    own = pl.ds(pl.multiple_of(own_ref[0] * share, share), share)
    wide = own_ref[1] > 0

    def either(run):
        pl.when(wide)(functools.partial(run, width))
        pl.when(jnp.logical_not(wide))(functools.partial(run, base))

    def squares(i, total):
        rows = pl.ds(pl.multiple_of(i * 128, 128), 128)
        v = g_ref[rows, :].astype(f32)
        return total + jnp.sum(v * v)

    total = lax.fori_loop(0, side // 128, squares, jnp.zeros((), f32))
    scale = 1.0 / (jnp.sqrt(jnp.full((1, 128), total, f32)) + tiny_value)
    scale = jnp.broadcast_to(scale[:, :1], (1, width))

    def shrink(i, carry):
        rows = pl.ds(pl.multiple_of(i * 128, 128), 128)
        x[rows, :] = (g_ref[rows, :].astype(f32) * scale).astype(bf16)
        return carry

    lax.fori_loop(0, side // 128, shrink, 0)

    def lower(out, product):
        for start in range(0, side, 256):
            stop = start + 256
            block = product(slice(start, side), slice(start, stop)).astype(bf16)
            out[start:, start:stop] = block
            if stop < side:
                out[start:stop, stop:] = block[256:].T

    def square(depth):
        lower(a, lambda rows, cols: dot_nt(x[rows, :depth], x[cols, :depth]))

    def mix():
        lower(
            b,
            lambda rows, cols: coeff_cubic * a[rows, cols].astype(f32)
            + coeff_quintic * dot(a[rows, :], a[:, cols]),
        )

    def renew(j, carry):
        cols = pl.ds(pl.multiple_of(j * tile, tile), tile)
        x[:, cols] = (
            coeff_linear * x[:, cols].astype(f32) + dot(b[...], x[:, cols])
        ).astype(bf16)
        return carry

    used = jnp.where(wide, width // tile, base // tile)

    def sweep(s, carry):
        either(square)
        mix()
        lax.fori_loop(0, used, renew, 0)
        return carry

    lax.fori_loop(0, 4, sweep, 0)
    either(square)
    part = (coeff_cubic * a[own, :].astype(f32) + coeff_quintic * dot(a[own, :], a[...])).astype(bf16)

    def last(j, carry):
        cols = pl.ds(pl.multiple_of(j * tile, tile), tile)
        o_ref[:, cols] = (
            coeff_linear * x[own, cols].astype(f32) + dot(part, x[:, cols])
        ).astype(bf16)
        return carry

    lax.fori_loop(0, width // tile, last, 0)


def turn_block(tile, g_ref, o_ref):
    def block(i, carry):
        spot = pl.ds(pl.multiple_of(i * tile, tile), tile)
        o_ref[:, spot] = g_ref[spot, :].T
        return carry

    lax.fori_loop(0, g_ref.shape[0] // tile, block, 0)


def in_vmem(count):
    return [pl.BlockSpec(memory_space=pltpu.VMEM)] * count


def cost(flops, touched):
    return pl.CostEstimate(flops=int(flops), bytes_accessed=int(touched), transcendentals=0)


def run_forward(inputs, weights, seqs):
    parts, packs = inputs.shape[:2]
    out = jax.ShapeDtypeStruct((packs, PACK, H), f32)
    return pl.pallas_call(
        functools.partial(scan_forward, seqs),
        out_shape=[out, jax.ShapeDtypeStruct((3, packs, PACK, H), f32), out],
        in_specs=in_vmem(2),
        out_specs=in_vmem(3),
        scratch_shapes=[pltpu.VMEM((seqs, H), f32)],
        compiler_params=pltpu.CompilerParams(vmem_limit_bytes=6 * mib),
        cost_estimate=cost(6e10, 20 * mib),
        name="scan_forward",
    )(inputs, weights)


def run_backward(direct, factors, rest, weights, seqs, copies):
    packs = direct.shape[0]
    parts, units = weights.shape[0], weights.shape[3]
    return pl.pallas_call(
        functools.partial(scan_backward, seqs),
        out_shape=jax.ShapeDtypeStruct((copies, parts, packs, PACK, 3 * units), bf16),
        in_specs=in_vmem(4),
        out_specs=in_vmem(1)[0],
        scratch_shapes=[
            pltpu.VMEM((seqs, 3 * H), f32),
            pltpu.VMEM((seqs, H), f32),
            pltpu.VMEM((3 * H, H), bf16),
        ],
        compiler_params=pltpu.CompilerParams(vmem_limit_bytes=18 * mib),
        cost_estimate=cost(6e10, 20 * mib),
        name="scan_backward",
    )(direct, factors, rest, weights)


def run_heads(hidden, embed, target, mask, weights):
    rows = hidden.shape[0]
    return pl.pallas_call(
        head_block,
        out_shape=[
            jax.ShapeDtypeStruct((2, rows, Z), bf16),
            jax.ShapeDtypeStruct((rows, H), f32),
            jax.ShapeDtypeStruct((1, 128), f32),
        ],
        in_specs=in_vmem(5),
        out_specs=in_vmem(3),
        compiler_params=pltpu.CompilerParams(vmem_limit_bytes=6 * mib),
        cost_estimate=cost(1e10, 12 * mib),
        name="heads",
    )(hidden, embed, target, mask, weights)


def run_head_grads(spot, everyone, embed):
    units = everyone.shape[3] // everyone.shape[0]
    return pl.pallas_call(
        head_grads,
        out_shape=jax.ShapeDtypeStruct((H + E + H, units), bf16),
        in_specs=[pl.BlockSpec(memory_space=pltpu.SMEM)] + in_vmem(2),
        out_specs=in_vmem(1)[0],
        compiler_params=pltpu.CompilerParams(vmem_limit_bytes=6 * mib),
        cost_estimate=cost(4e9, 12 * mib),
        name="head_grads",
    )(spot, everyone, embed)


def run_gru_grads(spot, onehot, everyone, back, dz_count):
    units = back.shape[3] // 3
    share = (Z + H) // (2 * dz_count)
    return pl.pallas_call(
        gru_grads,
        out_shape=jax.ShapeDtypeStruct((dz_count, 3 * share, units), bf16),
        in_specs=[pl.BlockSpec(memory_space=pltpu.SMEM)] + in_vmem(3),
        out_specs=in_vmem(1)[0],
        compiler_params=pltpu.CompilerParams(vmem_limit_bytes=16 * mib),
        cost_estimate=cost(4e9, 12 * mib),
        name="gru_grads",
    )(spot, onehot, everyone, back)


def plain_gru_grads(dx_index, onehot, everyone, back, dz_count):
    units = back.shape[3] // 3
    share = (Z + H) // (2 * dz_count)
    total = 0.0
    for n, x in enumerate((dx_index, 1 - dx_index)):
        hidden = everyone[:, n].reshape(-1, dz_count // 2, 2, share)
        hidden = lax.dynamic_index_in_dim(hidden, dx_index, 2, keepdims=False)
        ones = lax.dynamic_index_in_dim(onehot, x, 0, keepdims=False)
        left = jnp.concatenate([ones, hidden.reshape(ones.shape)], axis=1)
        right = lax.dynamic_index_in_dim(back, x, 0, keepdims=False)
        total = total + dot_tn(left, right.reshape(-1, 3 * units))
    grads = total.astype(bf16).reshape(dz_count, share, 3, units)
    return jnp.swapaxes(grads, 1, 2).reshape(dz_count, 3 * share, units)


def run_orthogonal(base, share, own, matrix):
    side, width = matrix.shape
    return pl.pallas_call(
        functools.partial(orthogonal_block, base, 512),
        out_shape=jax.ShapeDtypeStruct((share, width), bf16),
        in_specs=[pl.BlockSpec(memory_space=pltpu.SMEM)] + in_vmem(1),
        out_specs=in_vmem(1)[0],
        scratch_shapes=[
            pltpu.VMEM((side, width), bf16),
            pltpu.VMEM((side, side), bf16),
            pltpu.VMEM((side, side), bf16),
        ],
        compiler_params=pltpu.CompilerParams(vmem_limit_bytes=28 * mib),
        cost_estimate=cost(5e10, 6 * mib),
        name="orthogonal",
    )(own, matrix)


def run_turn(matrix):
    return pl.pallas_call(
        functools.partial(turn_block, 256),
        out_shape=jax.ShapeDtypeStruct(matrix.shape[::-1], bf16),
        in_specs=in_vmem(1),
        out_specs=in_vmem(1)[0],
        compiler_params=pltpu.CompilerParams(vmem_limit_bytes=6 * mib),
        cost_estimate=cost(1e6, 3 * mib),
        name="turn",
    )(matrix)


def on_device(
    embeddings,
    samples,
    seq_lengths,
    gru_weight,
    post_weight,
    prior_weight,
    gru_moment,
    post_moment,
    prior_moment,
):
    dz_count = lax.axis_size("dz")
    dx_count = lax.axis_size("dx")
    tp_count = lax.axis_size("tp")
    dp_count = dz_count * dx_count
    dx_index = lax.axis_index("dx")
    tp_index = lax.axis_index("tp")
    dp_index = lax.axis_index("dz") * dx_count + dx_index
    seq_count = embeddings.shape[0]
    seqs = seq_count // tp_count
    units = gru_weight.shape[2]
    groups = Z // ZC
    rows = seqs * FRAMES
    packs = rows // PACK

    def gather(block):
        return lax.all_gather(block, "tp", axis=0, tiled=False)

    def exchange(block, axis):
        return lax.all_to_all(block, axis, 0, 0, tiled=True)

    def mine(block, axis):
        return lax.dynamic_index_in_dim(block, dx_index, axis, keepdims=False)

    weights = gather(gru_weight[:, Z:].astype(bf16))
    head_low = jnp.concatenate([post_weight.astype(bf16), prior_weight.astype(bf16)], axis=0)

    by_part = jnp.swapaxes(samples.reshape(tp_count, seqs, FRAMES, groups), 1, 2)
    by_part = by_part.reshape(tp_count * rows, groups).astype(bf16)

    def one_hot(chosen):
        count = chosen.shape[-1]
        classes = jnp.arange(count * ZC, dtype=jnp.int32)
        expand = (classes[None, :] // ZC == jnp.arange(count)[:, None]).astype(bf16)
        return (dot(chosen, expand) == (classes % ZC).astype(f32)).astype(bf16)

    onehot = one_hot(by_part)
    input_part = jnp.concatenate(
        [dot(onehot, gru_weight[k, :Z].astype(bf16)).astype(bf16) for k in range(3)], axis=1
    ).reshape(tp_count, packs, PACK, 3 * units)
    input_part = exchange(input_part, "tp")
    embed_rows = jnp.swapaxes(embeddings.reshape(tp_count, seqs, FRAMES, E), 1, 2)
    embed_rows = embed_rows.reshape(tp_count, rows, E)
    pair_samples = lax.all_gather(by_part, "dx", axis=0, tiled=False)
    half = Z // dx_count
    pair_half = mine(
        pair_samples.reshape(dx_count * tp_count * rows, dz_count // 2, dx_count, -1), 2
    )
    pair_onehot = one_hot(pair_half.reshape(dx_count * tp_count * rows, groups // dx_count))
    pair_onehot = pair_onehot.reshape(dx_count, tp_count * rows, half)
    own_embed = lax.dynamic_index_in_dim(embed_rows, tp_index, 0, keepdims=False)
    onehot = onehot.reshape(tp_count, rows, Z)
    own_target = lax.dynamic_index_in_dim(onehot, tp_index, 0, keepdims=False)
    positions = jnp.arange(FRAMES, dtype=jnp.int32)
    own_lengths = lax.dynamic_slice_in_dim(seq_lengths, tp_index * seqs, seqs, 0)
    frame_mask = (positions[:, None] < own_lengths[None, :]).astype(f32)
    mask_lanes = jnp.broadcast_to(frame_mask.reshape(rows, 1), (rows, 128))

    weights, input_part, head_low, own_embed, own_target, mask_lanes, embed_rows, pair_onehot = (
        lax.optimization_barrier(
            (weights, input_part, head_low, own_embed, own_target, mask_lanes, embed_rows, pair_onehot)
        )
    )
    head_full = gather(head_low)
    hidden, factors, rest = run_forward(input_part, weights, seqs)
    hidden = hidden.reshape(rows, H)
    hidden_low = hidden.astype(bf16)
    swap = [(i, i ^ 1) for i in range(dx_count)]
    neighbour = lax.ppermute(hidden_low, "dx", swap)
    back_heads, direct, loss_lanes = run_heads(
        hidden, own_embed, own_target, mask_lanes, head_full
    )
    everyone = gather(jnp.concatenate([hidden_low[None], neighbour[None], back_heads], axis=0))
    back = run_backward(
        direct.reshape(packs, PACK, H), factors, rest, weights, seqs, dx_count
    )
    own_back = exchange(back.reshape(dx_count * tp_count, rows, 3 * units), ("dx", "tp"))
    own_back = own_back.reshape(dx_count, tp_count, rows, 3 * units)

    shares = [size // dp_count for size in ROWS]
    all_post = everyone[:, 3]
    spot = jnp.stack([tp_index, dx_index]).astype(jnp.int32)

    head_grad = run_head_grads(spot, everyone, embed_rows)

    head_grad = jnp.concatenate(
        [
            block.reshape(dz_count, dx_count, -1, units)
            for block in (head_grad[: H + E], head_grad[H + E :])
        ],
        axis=2,
    )

    def share_rows(block):
        return lax.psum_scatter(block, "dz", scatter_dimension=0, tiled=True)[0]

    head_sum = share_rows(head_grad)
    received = lax.ppermute(
        lax.dynamic_index_in_dim(head_sum, 1 - dx_index, 0, keepdims=False), "dx", swap
    )
    head_sum = mine(head_sum, 0).astype(f32) + received.astype(f32)
    if shares[0] % 128 == 0:
        gru_grad = run_gru_grads(spot, pair_onehot, everyone, own_back, dz_count)
    else:
        gru_grad = plain_gru_grads(dx_index, pair_onehot, everyone, own_back, dz_count)
    gru_sum = share_rows(gru_grad).astype(f32)
    totals = jnp.stack([jnp.sum(loss_lanes), jnp.sum(frame_mask)])
    totals = jnp.broadcast_to(totals[:, None], (2, 128))
    for axis, count in (("tp", tp_count), ("dx", dx_count), ("dz", dz_count)):
        for bit in range(count.bit_length() - 1):
            pairs = [(i, i ^ (1 << bit)) for i in range(count)]
            totals = totals + lax.ppermute(totals, axis, pairs)
    loss_sum, frame_count = totals[0, 0], totals[1, 0]
    loss_value = loss_sum / frame_count

    embed_part = E // tp_count
    own_rows_e = lax.dynamic_slice_in_dim(head_full, H + tp_index * embed_part, embed_part, 1)
    post_by_seq = jnp.swapaxes(all_post.reshape(tp_count, FRAMES, seqs, Z), 1, 2)
    embed_grad = jnp.einsum(
        "psfk,ek->psfe",
        post_by_seq,
        jnp.concatenate(list(own_rows_e), axis=1),
        preferred_element_type=f32,
    ).reshape(seq_count, FRAMES, embed_part)
    embed_grad = embed_grad / frame_count

    gru_sum = gru_sum / frame_count
    head_sum = head_sum / frame_count
    grads = [gru_sum[k * shares[0] : (k + 1) * shares[0]] for k in range(3)]
    grads += [head_sum[: shares[3]], head_sum[shares[3] :]]

    def own_rows(matrix, axis_dim):
        share = matrix.shape[axis_dim] // dp_count
        return lax.dynamic_slice_in_dim(matrix, dp_index * share, share, axis_dim)

    gru_moments = own_rows(gru_moment, 1)
    moments = [momentum_keep * gru_moments[k] + grads[k] for k in range(3)]
    moments.append(momentum_keep * own_rows(post_moment, 0) + grads[3])
    moments.append(momentum_keep * own_rows(prior_moment, 0) + grads[4])
    ahead = [(grads[m] + momentum_keep * moments[m]).astype(bf16) for m in range(MATS)]

    stride = dp_count // MATS
    widest = max(shares)
    base = shares[0]
    slots = [jnp.zeros((widest, units), bf16)] * dp_count
    for m in range(MATS):
        slots[m * stride] = jnp.pad(ahead[m], ((0, widest - shares[m]), (0, 0)))
    arrived = exchange(jnp.stack(slots), ("dz", "dx"))
    packed = jnp.concatenate(
        [arrived[:, :base].reshape(-1, units), arrived[:, base:].reshape(-1, units)], axis=0
    )
    wide = gather(run_turn(packed)).reshape(H, dp_count * widest)
    own = jnp.stack([tp_index, (dp_index == 3 * stride).astype(jnp.int32)]).astype(jnp.int32)
    result = run_orthogonal(dp_count * base, units, own, wide).T
    results = exchange(
        jnp.concatenate(
            [
                result[: dp_count * base].reshape(dp_count, base, units),
                result[dp_count * base :].reshape(dp_count, widest - base, units),
            ],
            axis=1,
        ),
        ("dz", "dx"),
    )

    def renew(weight_rows, index, largest):
        factor = learn_rate * update_scale * math.sqrt(largest)
        shard = results[index * stride, : weight_rows.shape[0]].astype(f32)
        return weight_rows * (1.0 - learn_rate * weight_decay) - factor * shard

    gru_rows = own_rows(gru_weight, 1)
    new_gru = jnp.stack([renew(gru_rows[k], k, gru_weight.shape[1]) for k in range(3)])
    new_post = renew(own_rows(post_weight, 0), 3, max(post_weight.shape[0], Z))
    new_prior = renew(own_rows(prior_weight, 0), 4, max(H, Z))
    return (
        loss_value,
        embed_grad,
        new_gru,
        new_post,
        new_prior,
        jnp.stack(moments[:3]),
        moments[3],
        moments[4],
    )

def solution(mesh):
    dp_count, tp_count = mesh.devices.shape
    mesh = jax.sharding.Mesh(
        mesh.devices.reshape(dp_count // 2, 2, tp_count), ("dz", "dx", "tp")
    )
    dp = ("dz", "dx")
    in_specs = (
        P(dp, None, None),
        P(dp, None, None),
        P(dp),
        P(None, None, "tp"),
        P(None, "tp"),
        P(None, "tp"),
        P(None, None, "tp"),
        P(None, "tp"),
        P(None, "tp"),
    )
    out_specs = (
        P(),
        P(dp, None, "tp"),
        P(None, dp, "tp"),
        P(dp, "tp"),
        P(dp, "tp"),
        P(None, dp, "tp"),
        P(dp, "tp"),
        P(dp, "tp"),
    )
    return jax.shard_map(
        on_device, mesh=mesh, in_specs=in_specs, out_specs=out_specs, check_vma=False
    )
```

```python
import functools
import math

import jax
import jax.numpy as jnp
from jax import lax
from jax.experimental import pallas as pl
from jax.experimental.pallas import tpu as pltpu
from jax.sharding import PartitionSpec as P

H = 1024
ZC = 32
E = 1536
FRAMES = 56
MATS = 5
Z = 1024
ROWS = (Z + H, Z + H, Z + H, H + E, H)
PACK = 8


coeff_linear = 3.4445
coeff_cubic = -4.775
coeff_quintic = 2.0315
momentum_keep = 0.95
learn_rate = 0.2
weight_decay = 0.01
update_scale = 0.2
tiny_value = 1e-07
mib = 1 << 20
f32 = jnp.float32
bf16 = jnp.bfloat16
NT = (((1,), (1,)), ((), ()))
TN = (((0,), (0,)), ((), ()))


def dot(left, right):
    return jnp.dot(left, right, preferred_element_type=f32)


def dot_tn(left, right):
    return lax.dot_general(left, right, TN, preferred_element_type=f32)


def dot_nt(left, right):
    return lax.dot_general(left, right, NT, preferred_element_type=f32)


def scan_forward(seqs, x_ref, w_ref, h_ref, k_ref, u_ref, state):
    parts, packs = x_ref.shape[:2]
    units = w_ref.shape[3]
    per_pack = PACK // seqs
    state[...] = jnp.zeros_like(state)

    def pack(i, carry):
        for frame in range(per_pack):
            rows = slice(frame * seqs, (frame + 1) * seqs)
            if frame == 0:
                source, live = jnp.maximum(i - 1, 0), jnp.where(i > 0, 1.0, 0.0)
                spot = slice((per_pack - 1) * seqs, per_pack * seqs)
            else:
                source, live = i, None
                spot = slice((frame - 1) * seqs, frame * seqs)
            before = state[...]
            low = before.astype(bf16)
            for p in range(parts):
                cols = slice(p * units, (p + 1) * units)
                given = x_ref[p, source].astype(f32)[spot]
                if live is not None:
                    given = given * live
                pre = [
                    given[:, k * units : (k + 1) * units] + dot(low, w_ref[p, k]) for k in range(3)
                ]
                last = before[:, cols]
                r = jax.nn.sigmoid(pre[0])
                c = jnp.tanh(r * pre[1])
                u = jax.nn.sigmoid(pre[2] - 1.0)
                rest = 1.0 - u
                new = u * c + rest * last
                inner = u * (1.0 - c * c)
                state[:, cols] = new
                h_ref[i, rows, cols] = new
                k_ref[0, i, rows, cols] = inner * pre[1] * r * (1.0 - r)
                k_ref[1, i, rows, cols] = inner * r
                k_ref[2, i, rows, cols] = (c - last) * u * rest
                u_ref[i, rows, cols] = rest
        return carry

    lax.fori_loop(0, packs, pack, 0)


def scan_backward(seqs, d_ref, k_ref, u_ref, w_ref, b_ref, now, kept, turned):
    copies, parts, packs = b_ref.shape[:3]
    units = w_ref.shape[3]
    per_pack = PACK // seqs
    now[...] = jnp.zeros_like(now)
    kept[...] = jnp.zeros_like(kept)

    def turn(n, carry):
        spot = pl.ds(pl.multiple_of(n * units, units), units)
        turned[spot, :] = w_ref[n // 3, n % 3].T
        return carry

    lax.fori_loop(0, 3 * parts, turn, 0)

    def pack(n, carry):
        i = packs - 1 - n
        later = [None] * per_pack
        for frame in reversed(range(per_pack)):
            rows = slice(frame * seqs, (frame + 1) * seqs)
            values = now[...]
            later[frame] = values
            dh = d_ref[i, rows] + kept[...] + dot(values.astype(bf16), turned[...])
            kept[...] = dh * u_ref[i, rows]
            for p in range(parts):
                cols = slice(p * units, (p + 1) * units)
                for k in range(3):
                    spot = slice((3 * p + k) * units, (3 * p + k + 1) * units)
                    now[:, spot] = dh[:, cols] * k_ref[k, i, rows, cols]
        stacked = jnp.concatenate(later, axis=0).astype(bf16)
        for p in range(parts):
            for copy in range(copies):
                b_ref[copy, p, i] = stacked[:, p * 3 * units : (p + 1) * 3 * units]
        return carry

    lax.fori_loop(0, packs, pack, 0)


def butterfly(values, combine, lane):
    step = 1
    while step < ZC:
        up = pltpu.roll(values, step, 1)
        down = pltpu.roll(values, values.shape[1] - step, 1)
        values = combine(values, jnp.where((lane & step) != 0, up, down))
        step *= 2
    return values


def head_block(h_ref, e_ref, t_ref, m_ref, w_ref, back_ref, d_ref, loss_ref):
    parts = w_ref.shape[0]
    units = w_ref.shape[2]
    rows = h_ref.shape[0]
    low = h_ref[...].astype(bf16)
    mask = m_ref[...]
    lane = lax.broadcasted_iota(jnp.int32, (rows, 128), 1)
    loss = jnp.zeros((rows, 128), f32)
    for p in range(parts):
        post = dot(low, w_ref[p, :H]) + dot(e_ref[...], w_ref[p, H : H + E])
        prior = dot(low, w_ref[p, H + E :])
        for head, logits in enumerate((prior, post)):
            for piece in range(units // 128):
                l = logits[:, piece * 128 : (piece + 1) * 128]
                cols = slice(p * units + piece * 128, p * units + (piece + 1) * 128)
                target = t_ref[:, cols].astype(f32)
                top = butterfly(l, jnp.maximum, lane)
                e = jnp.exp(l - top)
                total = butterfly(e, jnp.add, lane)
                loss = loss + mask * ((top + jnp.log(total)) * (1.0 / ZC) - target * l)
                back_ref[head, :, cols] = (mask * (e / total - target)).astype(bf16)
    loss_ref[...] = jnp.sum(loss, axis=0, keepdims=True)
    direct = jnp.zeros((rows, H), f32)
    for p in range(parts):
        cols = slice(p * units, (p + 1) * units)
        direct = direct + dot_nt(back_ref[0, :, cols], w_ref[p, H + E :])
        direct = direct + dot_nt(back_ref[1, :, cols], w_ref[p, :H])
    d_ref[...] = direct


def head_grads(spot_ref, all_ref, e_ref, o_ref):
    parts, rows = e_ref.shape[0], e_ref.shape[1]
    units = o_ref.shape[1]
    frames = parts * rows
    own = pl.ds(pl.multiple_of(spot_ref[0] * units, units), units)
    post = all_ref[:, 3, :, own].reshape(frames, units)
    both = jnp.concatenate([post, all_ref[:, 2, :, own].reshape(frames, units)], axis=1)
    for m in range(H // 256):
        spot = slice(m * 256, (m + 1) * 256)
        grad = dot_tn(all_ref[:, 0, :, spot].reshape(frames, 256), both).astype(bf16)
        o_ref[m * 256 : (m + 1) * 256] = grad[:, :units]
        o_ref[H + E + m * 256 : H + E + (m + 1) * 256] = grad[:, units:]
    for m in range(E // 256):
        spot = slice(m * 256, (m + 1) * 256)
        grad = dot_tn(e_ref[:, :, spot].reshape(frames, 256), post).astype(bf16)
        o_ref[H + m * 256 : H + (m + 1) * 256] = grad


def gru_grads(spot_ref, one_ref, all_ref, b_ref, o_ref):
    parts, rows = all_ref.shape[0], all_ref.shape[2]
    units = o_ref.shape[2]
    frames = parts * rows
    share = o_ref.shape[1] // 3
    half = o_ref.shape[0] // 2
    me = spot_ref[1]
    back = [b_ref[x].reshape(frames, 3 * units) for x in (me, 1 - me)]
    for z in range(2 * half):
        if z < half:
            spot = slice(z * share, (z + 1) * share)
            left = [one_ref[x, :, spot] for x in (me, 1 - me)]
        else:
            spot = pl.ds(pl.multiple_of(((z - half) * 2 + me) * share, share), share)
            left = [all_ref[:, n, :, spot].reshape(frames, share) for n in (0, 1)]
        grad = (dot_tn(left[0], back[0]) + dot_tn(left[1], back[1])).astype(bf16)
        for k in range(3):
            o_ref[z, k * share : (k + 1) * share] = grad[:, k * units : (k + 1) * units]


def orthogonal_block(base, tile, own_ref, g_ref, o_ref, x, a, b):
    side, width = g_ref.shape
    share = o_ref.shape[0]
    own = pl.ds(pl.multiple_of(own_ref[0] * share, share), share)
    wide = own_ref[1] > 0

    def either(run):
        pl.when(wide)(functools.partial(run, width))
        pl.when(jnp.logical_not(wide))(functools.partial(run, base))

    def squares(i, total):
        rows = pl.ds(pl.multiple_of(i * 128, 128), 128)
        v = g_ref[rows, :].astype(f32)
        return total + jnp.sum(v * v)

    total = lax.fori_loop(0, side // 128, squares, jnp.zeros((), f32))
    scale = 1.0 / (jnp.sqrt(jnp.full((1, 128), total, f32)) + tiny_value)
    scale = jnp.broadcast_to(scale[:, :1], (1, width))

    def shrink(i, carry):
        rows = pl.ds(pl.multiple_of(i * 128, 128), 128)
        x[rows, :] = (g_ref[rows, :].astype(f32) * scale).astype(bf16)
        return carry

    lax.fori_loop(0, side // 128, shrink, 0)

    def lower(out, product):
        for start in range(0, side, 256):
            stop = start + 256
            block = product(slice(start, side), slice(start, stop)).astype(bf16)
            out[start:, start:stop] = block
            if stop < side:
                out[start:stop, stop:] = block[256:].T

    def square(depth):
        lower(a, lambda rows, cols: dot_nt(x[rows, :depth], x[cols, :depth]))

    def mix():
        lower(
            b,
            lambda rows, cols: coeff_cubic * a[rows, cols].astype(f32)
            + coeff_quintic * dot(a[rows, :], a[:, cols]),
        )

    def renew(j, carry):
        cols = pl.ds(pl.multiple_of(j * tile, tile), tile)
        x[:, cols] = (
            coeff_linear * x[:, cols].astype(f32) + dot(b[...], x[:, cols])
        ).astype(bf16)
        return carry

    used = jnp.where(wide, width // tile, base // tile)

    def sweep(s, carry):
        either(square)
        mix()
        lax.fori_loop(0, used, renew, 0)
        return carry

    lax.fori_loop(0, 4, sweep, 0)
    either(square)
    part = (coeff_cubic * a[own, :].astype(f32) + coeff_quintic * dot(a[own, :], a[...])).astype(bf16)

    def last(j, carry):
        cols = pl.ds(pl.multiple_of(j * tile, tile), tile)
        o_ref[:, cols] = (
            coeff_linear * x[own, cols].astype(f32) + dot(part, x[:, cols])
        ).astype(bf16)
        return carry

    lax.fori_loop(0, width // tile, last, 0)


def turn_block(tile, g_ref, o_ref):
    def block(i, carry):
        spot = pl.ds(pl.multiple_of(i * tile, tile), tile)
        o_ref[:, spot] = g_ref[spot, :].T
        return carry

    lax.fori_loop(0, g_ref.shape[0] // tile, block, 0)


def collect_block(spot_ref, *refs):
    *pieces, o_ref, extra = refs
    steps = len(pieces) // 2
    base, widest = pieces[0].shape[0], pieces[-1].shape[0]
    more = widest - base
    head = spot_ref[1] > 0
    for step in range(steps):
        d = spot_ref[0] ^ step
        block = jnp.where(head, pieces[steps + step][:base], pieces[step][...])
        o_ref[:, pl.ds(pl.multiple_of(d * base, base), base)] = block.T
        rest = pieces[steps + step][base:]
        extra[pl.ds(pl.multiple_of(d * more, more), more), :] = jnp.where(head, rest, jnp.zeros_like(rest))
    o_ref[:, steps * base :] = extra[...].T


def in_vmem(count):
    return [pl.BlockSpec(memory_space=pltpu.VMEM)] * count


def cost(flops, touched):
    return pl.CostEstimate(flops=int(flops), bytes_accessed=int(touched), transcendentals=0)


def run_forward(inputs, weights, seqs):
    parts, packs = inputs.shape[:2]
    out = jax.ShapeDtypeStruct((packs, PACK, H), f32)
    return pl.pallas_call(
        functools.partial(scan_forward, seqs),
        out_shape=[out, jax.ShapeDtypeStruct((3, packs, PACK, H), f32), out],
        in_specs=in_vmem(2),
        out_specs=in_vmem(3),
        scratch_shapes=[pltpu.VMEM((seqs, H), f32)],
        compiler_params=pltpu.CompilerParams(vmem_limit_bytes=6 * mib),
        cost_estimate=cost(6e10, 20 * mib),
        name="scan_forward",
    )(inputs, weights)


def run_backward(direct, factors, rest, weights, seqs, copies):
    packs = direct.shape[0]
    parts, units = weights.shape[0], weights.shape[3]
    return pl.pallas_call(
        functools.partial(scan_backward, seqs),
        out_shape=jax.ShapeDtypeStruct((copies, parts, packs, PACK, 3 * units), bf16),
        in_specs=in_vmem(4),
        out_specs=in_vmem(1)[0],
        scratch_shapes=[
            pltpu.VMEM((seqs, 3 * H), f32),
            pltpu.VMEM((seqs, H), f32),
            pltpu.VMEM((3 * H, H), bf16),
        ],
        compiler_params=pltpu.CompilerParams(vmem_limit_bytes=18 * mib),
        cost_estimate=cost(6e10, 20 * mib),
        name="scan_backward",
    )(direct, factors, rest, weights)


def run_heads(hidden, embed, target, mask, weights):
    rows = hidden.shape[0]
    return pl.pallas_call(
        head_block,
        out_shape=[
            jax.ShapeDtypeStruct((2, rows, Z), bf16),
            jax.ShapeDtypeStruct((rows, H), f32),
            jax.ShapeDtypeStruct((1, 128), f32),
        ],
        in_specs=in_vmem(5),
        out_specs=in_vmem(3),
        compiler_params=pltpu.CompilerParams(vmem_limit_bytes=6 * mib),
        cost_estimate=cost(1e10, 12 * mib),
        name="heads",
    )(hidden, embed, target, mask, weights)


def run_head_grads(spot, everyone, embed):
    units = everyone.shape[3] // everyone.shape[0]
    return pl.pallas_call(
        head_grads,
        out_shape=jax.ShapeDtypeStruct((H + E + H, units), bf16),
        in_specs=[pl.BlockSpec(memory_space=pltpu.SMEM)] + in_vmem(2),
        out_specs=in_vmem(1)[0],
        compiler_params=pltpu.CompilerParams(vmem_limit_bytes=6 * mib),
        cost_estimate=cost(4e9, 12 * mib),
        name="head_grads",
    )(spot, everyone, embed)


def run_gru_grads(spot, onehot, everyone, back, dz_count):
    units = back.shape[3] // 3
    share = (Z + H) // (2 * dz_count)
    return pl.pallas_call(
        gru_grads,
        out_shape=jax.ShapeDtypeStruct((dz_count, 3 * share, units), bf16),
        in_specs=[pl.BlockSpec(memory_space=pltpu.SMEM)] + in_vmem(3),
        out_specs=in_vmem(1)[0],
        compiler_params=pltpu.CompilerParams(vmem_limit_bytes=16 * mib),
        cost_estimate=cost(4e9, 12 * mib),
        name="gru_grads",
    )(spot, onehot, everyone, back)


def plain_gru_grads(dx_index, onehot, everyone, back, dz_count):
    units = back.shape[3] // 3
    share = (Z + H) // (2 * dz_count)
    total = 0.0
    for n, x in enumerate((dx_index, 1 - dx_index)):
        hidden = everyone[:, n].reshape(-1, dz_count // 2, 2, share)
        hidden = lax.dynamic_index_in_dim(hidden, dx_index, 2, keepdims=False)
        ones = lax.dynamic_index_in_dim(onehot, x, 0, keepdims=False)
        left = jnp.concatenate([ones, hidden.reshape(ones.shape)], axis=1)
        right = lax.dynamic_index_in_dim(back, x, 0, keepdims=False)
        total = total + dot_tn(left, right.reshape(-1, 3 * units))
    grads = total.astype(bf16).reshape(dz_count, share, 3, units)
    return jnp.swapaxes(grads, 1, 2).reshape(dz_count, 3 * share, units)


def run_orthogonal(base, share, own, matrix):
    side, width = matrix.shape
    return pl.pallas_call(
        functools.partial(orthogonal_block, base, 512),
        out_shape=jax.ShapeDtypeStruct((share, width), bf16),
        in_specs=[pl.BlockSpec(memory_space=pltpu.SMEM)] + in_vmem(1),
        out_specs=in_vmem(1)[0],
        scratch_shapes=[
            pltpu.VMEM((side, width), bf16),
            pltpu.VMEM((side, side), bf16),
            pltpu.VMEM((side, side), bf16),
        ],
        compiler_params=pltpu.CompilerParams(vmem_limit_bytes=28 * mib),
        cost_estimate=cost(5e10, 6 * mib),
        name="orthogonal",
    )(own, matrix)


def run_turn(matrix):
    return pl.pallas_call(
        functools.partial(turn_block, 256),
        out_shape=jax.ShapeDtypeStruct(matrix.shape[::-1], bf16),
        in_specs=in_vmem(1),
        out_specs=in_vmem(1)[0],
        compiler_params=pltpu.CompilerParams(vmem_limit_bytes=6 * mib),
        cost_estimate=cost(1e6, 3 * mib),
        name="turn",
    )(matrix)


def run_collect(spot, pieces):
    steps = len(pieces) // 2
    base, units = pieces[0].shape
    widest = pieces[-1].shape[0]
    return pl.pallas_call(
        collect_block,
        out_shape=jax.ShapeDtypeStruct((units, steps * widest), bf16),
        in_specs=[pl.BlockSpec(memory_space=pltpu.SMEM)] + in_vmem(len(pieces)),
        out_specs=in_vmem(1)[0],
        scratch_shapes=[pltpu.VMEM((steps * (widest - base), units), bf16)],
        compiler_params=pltpu.CompilerParams(vmem_limit_bytes=8 * mib),
        cost_estimate=cost(1e6, 4 * mib),
        name="collect",
    )(spot, *pieces)


def on_device(
    embeddings,
    samples,
    seq_lengths,
    gru_weight,
    post_weight,
    prior_weight,
    gru_moment,
    post_moment,
    prior_moment,
):
    dz_count = lax.axis_size("dz")
    dx_count = lax.axis_size("dx")
    tp_count = lax.axis_size("tp")
    dp_count = dz_count * dx_count
    dx_index = lax.axis_index("dx")
    tp_index = lax.axis_index("tp")
    dp_index = lax.axis_index("dz") * dx_count + dx_index
    seq_count = embeddings.shape[0]
    seqs = seq_count // tp_count
    units = gru_weight.shape[2]
    groups = Z // ZC
    rows = seqs * FRAMES
    packs = rows // PACK

    def gather(block):
        return lax.all_gather(block, "tp", axis=0, tiled=False)

    def exchange(block, axis):
        return lax.all_to_all(block, axis, 0, 0, tiled=True)

    def mine(block, axis):
        return lax.dynamic_index_in_dim(block, dx_index, axis, keepdims=False)

    weights = gather(gru_weight[:, Z:].astype(bf16))
    head_low = jnp.concatenate([post_weight.astype(bf16), prior_weight.astype(bf16)], axis=0)

    by_part = jnp.swapaxes(samples.reshape(tp_count, seqs, FRAMES, groups), 1, 2)
    by_part = by_part.reshape(tp_count * rows, groups).astype(bf16)

    def one_hot(chosen):
        count = chosen.shape[-1]
        classes = jnp.arange(count * ZC, dtype=jnp.int32)
        expand = (classes[None, :] // ZC == jnp.arange(count)[:, None]).astype(bf16)
        return (dot(chosen, expand) == (classes % ZC).astype(f32)).astype(bf16)

    onehot = one_hot(by_part)
    input_part = jnp.concatenate(
        [dot(onehot, gru_weight[k, :Z].astype(bf16)).astype(bf16) for k in range(3)], axis=1
    ).reshape(tp_count, packs, PACK, 3 * units)
    input_part = exchange(input_part, "tp")
    embed_rows = jnp.swapaxes(embeddings.reshape(tp_count, seqs, FRAMES, E), 1, 2)
    embed_rows = embed_rows.reshape(tp_count, rows, E)
    pair_samples = lax.all_gather(by_part, "dx", axis=0, tiled=False)
    half = Z // dx_count
    pair_half = mine(
        pair_samples.reshape(dx_count * tp_count * rows, dz_count // 2, dx_count, -1), 2
    )
    pair_onehot = one_hot(pair_half.reshape(dx_count * tp_count * rows, groups // dx_count))
    pair_onehot = pair_onehot.reshape(dx_count, tp_count * rows, half)
    own_embed = lax.dynamic_index_in_dim(embed_rows, tp_index, 0, keepdims=False)
    onehot = onehot.reshape(tp_count, rows, Z)
    own_target = lax.dynamic_index_in_dim(onehot, tp_index, 0, keepdims=False)
    positions = jnp.arange(FRAMES, dtype=jnp.int32)
    own_lengths = lax.dynamic_slice_in_dim(seq_lengths, tp_index * seqs, seqs, 0)
    frame_mask = (positions[:, None] < own_lengths[None, :]).astype(f32)
    mask_lanes = jnp.broadcast_to(frame_mask.reshape(rows, 1), (rows, 128))

    weights, input_part, head_low, own_embed, own_target, mask_lanes, embed_rows, pair_onehot = (
        lax.optimization_barrier(
            (weights, input_part, head_low, own_embed, own_target, mask_lanes, embed_rows, pair_onehot)
        )
    )
    head_full = gather(head_low)
    hidden, factors, rest = run_forward(input_part, weights, seqs)
    hidden = hidden.reshape(rows, H)
    hidden_low = hidden.astype(bf16)
    swap = [(i, i ^ 1) for i in range(dx_count)]
    neighbour = lax.ppermute(hidden_low, "dx", swap)
    back_heads, direct, loss_lanes = run_heads(
        hidden, own_embed, own_target, mask_lanes, head_full
    )
    everyone = gather(jnp.concatenate([hidden_low[None], neighbour[None], back_heads], axis=0))
    back = run_backward(
        direct.reshape(packs, PACK, H), factors, rest, weights, seqs, dx_count
    )
    own_back = exchange(back.reshape(dx_count * tp_count, rows, 3 * units), ("dx", "tp"))
    own_back = own_back.reshape(dx_count, tp_count, rows, 3 * units)

    shares = [size // dp_count for size in ROWS]
    all_post = everyone[:, 3]
    spot = jnp.stack([tp_index, dx_index]).astype(jnp.int32)

    head_grad = run_head_grads(spot, everyone, embed_rows)
    own_back, head_grad = lax.optimization_barrier((own_back, head_grad))

    head_grad = jnp.concatenate(
        [
            block.reshape(dz_count, dx_count, -1, units)
            for block in (head_grad[: H + E], head_grad[H + E :])
        ],
        axis=2,
    )

    def share_rows(block):
        return lax.psum_scatter(block, "dz", scatter_dimension=0, tiled=True)[0]

    head_done = share_rows(head_grad)
    if shares[0] % 128 == 0:
        gru_grad = run_gru_grads(spot, pair_onehot, everyone, own_back, dz_count)
    else:
        gru_grad = plain_gru_grads(dx_index, pair_onehot, everyone, own_back, dz_count)
    gru_grad, head_done = lax.optimization_barrier((gru_grad, head_done))
    gru_sum = share_rows(gru_grad).astype(f32)
    received = lax.ppermute(
        lax.dynamic_index_in_dim(head_done, 1 - dx_index, 0, keepdims=False), "dx", swap
    )
    head_sum = mine(head_done, 0).astype(f32) + received.astype(f32)
    totals = jnp.stack([jnp.sum(loss_lanes), jnp.sum(frame_mask)])
    totals = jnp.broadcast_to(totals[:, None], (2, 128))
    for axis, count in (("tp", tp_count), ("dx", dx_count), ("dz", dz_count)):
        for bit in range(count.bit_length() - 1):
            pairs = [(i, i ^ (1 << bit)) for i in range(count)]
            totals = totals + lax.ppermute(totals, axis, pairs)
    loss_sum, frame_count = totals[0, 0], totals[1, 0]
    loss_value = loss_sum / frame_count

    embed_part = E // tp_count
    own_rows_e = lax.dynamic_slice_in_dim(head_full, H + tp_index * embed_part, embed_part, 1)
    post_by_seq = jnp.swapaxes(all_post.reshape(tp_count, FRAMES, seqs, Z), 1, 2)
    embed_grad = jnp.einsum(
        "psfk,ek->psfe",
        post_by_seq,
        jnp.concatenate(list(own_rows_e), axis=1),
        preferred_element_type=f32,
    ).reshape(seq_count, FRAMES, embed_part)
    embed_grad = embed_grad / frame_count

    gru_sum = gru_sum / frame_count
    head_sum = head_sum / frame_count
    grads = [gru_sum[k * shares[0] : (k + 1) * shares[0]] for k in range(3)]
    grads += [head_sum[: shares[3]], head_sum[shares[3] :]]

    def own_rows(matrix, axis_dim):
        share = matrix.shape[axis_dim] // dp_count
        return lax.dynamic_slice_in_dim(matrix, dp_index * share, share, axis_dim)

    gru_moments = own_rows(gru_moment, 1)
    moments = [momentum_keep * gru_moments[k] + grads[k] for k in range(3)]
    moments.append(momentum_keep * own_rows(post_moment, 0) + grads[3])
    moments.append(momentum_keep * own_rows(prior_moment, 0) + grads[4])
    ahead = [(grads[m] + momentum_keep * moments[m]).astype(bf16) for m in range(MATS)]

    owners = [m * dp_count // 8 for m in (0, 3, 4, 7, 5)]
    widest = max(shares)
    base = shares[0]
    holds_post = (dp_index == owners[3]).astype(jnp.int32)
    if dp_count == 8:
        kept = jnp.array([owners.index(d) if d in owners else 0 for d in range(dp_count)])
        heads = jnp.stack(
            [jnp.pad(block, ((0, widest - block.shape[0]), (0, 0))) for block in ahead[3:]]
        )
        groups_of = ((owners[:3], jnp.stack(ahead[:3]), 0), (owners[3:], heads, 3))
        pieces = []
        for targets, blocks, first in groups_of:
            for step in range(dp_count):
                index = jnp.clip(kept[dp_index ^ step] - first, 0, blocks.shape[0] - 1)
                block = lax.dynamic_index_in_dim(blocks, index, 0, keepdims=False)
                if step > 0:
                    pairs = [(d ^ step, d) for d in targets]
                    block = lax.ppermute(block, ("dz", "dx"), pairs)
                pieces.append(block)
        holds_head = (kept[dp_index] >= 3).astype(jnp.int32)
        turned = run_collect(jnp.stack([dp_index, holds_head]).astype(jnp.int32), pieces)
    else:
        slots = [jnp.zeros((widest, units), bf16)] * dp_count
        for m in range(MATS):
            slots[owners[m]] = jnp.pad(ahead[m], ((0, widest - shares[m]), (0, 0)))
        arrived = exchange(jnp.stack(slots), ("dz", "dx"))
        turned = run_turn(
            jnp.concatenate(
                [arrived[:, :base].reshape(-1, units), arrived[:, base:].reshape(-1, units)], axis=0
            )
        )
    wide = gather(turned).reshape(H, dp_count * widest)
    own = jnp.stack([tp_index, holds_post]).astype(jnp.int32)
    result = run_orthogonal(dp_count * base, units, own, wide).T
    results = exchange(
        jnp.concatenate(
            [
                result[: dp_count * base].reshape(dp_count, base, units),
                result[dp_count * base :].reshape(dp_count, widest - base, units),
            ],
            axis=1,
        ),
        ("dz", "dx"),
    )

    def renew(weight_rows, index, largest):
        factor = learn_rate * update_scale * math.sqrt(largest)
        shard = results[owners[index], : weight_rows.shape[0]].astype(f32)
        return weight_rows * (1.0 - learn_rate * weight_decay) - factor * shard

    gru_rows = own_rows(gru_weight, 1)
    new_gru = jnp.stack([renew(gru_rows[k], k, gru_weight.shape[1]) for k in range(3)])
    new_post = renew(own_rows(post_weight, 0), 3, max(post_weight.shape[0], Z))
    new_prior = renew(own_rows(prior_weight, 0), 4, max(H, Z))
    return (
        loss_value,
        embed_grad,
        new_gru,
        new_post,
        new_prior,
        jnp.stack(moments[:3]),
        moments[3],
        moments[4],
    )

def solution(mesh):
    dp_count, tp_count = mesh.devices.shape
    mesh = jax.sharding.Mesh(
        mesh.devices.reshape(dp_count // 2, 2, tp_count), ("dz", "dx", "tp")
    )
    dp = ("dz", "dx")
    in_specs = (
        P(dp, None, None),
        P(dp, None, None),
        P(dp),
        P(None, None, "tp"),
        P(None, "tp"),
        P(None, "tp"),
        P(None, None, "tp"),
        P(None, "tp"),
        P(None, "tp"),
    )
    out_specs = (
        P(),
        P(dp, None, "tp"),
        P(None, dp, "tp"),
        P(dp, "tp"),
        P(dp, "tp"),
        P(None, dp, "tp"),
        P(dp, "tp"),
        P(dp, "tp"),
    )
    return jax.shard_map(
        on_device, mesh=mesh, in_specs=in_specs, out_specs=out_specs, check_vma=False
    )
```

```python
import functools
import math

import jax
import jax.numpy as jnp
from jax import lax
from jax.experimental import pallas as pl
from jax.experimental.pallas import tpu as pltpu
from jax.sharding import PartitionSpec as P

H = 1024
ZC = 32
E = 1536
FRAMES = 56
MATS = 5
Z = 1024
ROWS = (Z + H, Z + H, Z + H, H + E, H)
PACK = 8


coeff_linear = 3.4445
coeff_cubic = -4.775
coeff_quintic = 2.0315
momentum_keep = 0.95
learn_rate = 0.2
weight_decay = 0.01
update_scale = 0.2
tiny_value = 1e-07
mib = 1 << 20
f32 = jnp.float32
bf16 = jnp.bfloat16
NT = (((1,), (1,)), ((), ()))
TN = (((0,), (0,)), ((), ()))


def dot(left, right):
    return jnp.dot(left, right, preferred_element_type=f32)


def dot_tn(left, right):
    return lax.dot_general(left, right, TN, preferred_element_type=f32)


def dot_nt(left, right):
    return lax.dot_general(left, right, NT, preferred_element_type=f32)


def scan_forward(seqs, x_ref, w_ref, h_ref, k_ref, u_ref, state):
    parts, packs = x_ref.shape[:2]
    units = w_ref.shape[3]
    per_pack = PACK // seqs
    state[...] = jnp.zeros_like(state)

    def pack(i, carry):
        for frame in range(per_pack):
            rows = slice(frame * seqs, (frame + 1) * seqs)
            if frame == 0:
                source, live = jnp.maximum(i - 1, 0), jnp.where(i > 0, 1.0, 0.0)
                spot = slice((per_pack - 1) * seqs, per_pack * seqs)
            else:
                source, live = i, None
                spot = slice((frame - 1) * seqs, frame * seqs)
            before = state[...]
            low = before.astype(bf16)
            for p in range(parts):
                cols = slice(p * units, (p + 1) * units)
                given = x_ref[p, source].astype(f32)[spot]
                if live is not None:
                    given = given * live
                pre = [
                    given[:, k * units : (k + 1) * units] + dot(low, w_ref[p, k]) for k in range(3)
                ]
                last = before[:, cols]
                r = jax.nn.sigmoid(pre[0])
                c = jnp.tanh(r * pre[1])
                u = jax.nn.sigmoid(pre[2] - 1.0)
                rest = 1.0 - u
                new = u * c + rest * last
                inner = u * (1.0 - c * c)
                state[:, cols] = new
                h_ref[i, rows, cols] = new
                k_ref[0, i, rows, cols] = inner * pre[1] * r * (1.0 - r)
                k_ref[1, i, rows, cols] = inner * r
                k_ref[2, i, rows, cols] = (c - last) * u * rest
                u_ref[i, rows, cols] = rest
        return carry

    lax.fori_loop(0, packs, pack, 0)


def scan_backward(seqs, d_ref, k_ref, u_ref, w_ref, b_ref, now, kept, turned):
    copies, parts, packs = b_ref.shape[:3]
    units = w_ref.shape[3]
    per_pack = PACK // seqs
    now[...] = jnp.zeros_like(now)
    kept[...] = jnp.zeros_like(kept)

    def turn(n, carry):
        spot = pl.ds(pl.multiple_of(n * units, units), units)
        turned[spot, :] = w_ref[n // 3, n % 3].T
        return carry

    lax.fori_loop(0, 3 * parts, turn, 0)

    def pack(n, carry):
        i = packs - 1 - n
        later = [None] * per_pack
        for frame in reversed(range(per_pack)):
            rows = slice(frame * seqs, (frame + 1) * seqs)
            values = now[...]
            later[frame] = values
            dh = d_ref[i, rows] + kept[...] + dot(values.astype(bf16), turned[...])
            kept[...] = dh * u_ref[i, rows]
            for p in range(parts):
                cols = slice(p * units, (p + 1) * units)
                for k in range(3):
                    spot = slice((3 * p + k) * units, (3 * p + k + 1) * units)
                    now[:, spot] = dh[:, cols] * k_ref[k, i, rows, cols]
        stacked = jnp.concatenate(later, axis=0).astype(bf16)
        for p in range(parts):
            for copy in range(copies):
                b_ref[copy, p, i] = stacked[:, p * 3 * units : (p + 1) * 3 * units]
        return carry

    lax.fori_loop(0, packs, pack, 0)


def butterfly(values, combine, lane):
    step = 1
    while step < ZC:
        up = pltpu.roll(values, step, 1)
        down = pltpu.roll(values, values.shape[1] - step, 1)
        values = combine(values, jnp.where((lane & step) != 0, up, down))
        step *= 2
    return values


def head_block(h_ref, e_ref, t_ref, m_ref, w_ref, back_ref, d_ref, loss_ref):
    parts = w_ref.shape[0]
    units = w_ref.shape[2]
    rows = h_ref.shape[0]
    low = h_ref[...].astype(bf16)
    mask = m_ref[...]
    lane = lax.broadcasted_iota(jnp.int32, (rows, 128), 1)
    loss = jnp.zeros((rows, 128), f32)
    for p in range(parts):
        post = dot(low, w_ref[p, :H]) + dot(e_ref[...], w_ref[p, H : H + E])
        prior = dot(low, w_ref[p, H + E :])
        for head, logits in enumerate((prior, post)):
            for piece in range(units // 128):
                l = logits[:, piece * 128 : (piece + 1) * 128]
                cols = slice(p * units + piece * 128, p * units + (piece + 1) * 128)
                target = t_ref[:, cols].astype(f32)
                top = butterfly(l, jnp.maximum, lane)
                e = jnp.exp(l - top)
                total = butterfly(e, jnp.add, lane)
                loss = loss + mask * ((top + jnp.log(total)) * (1.0 / ZC) - target * l)
                back_ref[head, :, cols] = (mask * (e / total - target)).astype(bf16)
    loss_ref[...] = jnp.sum(loss, axis=0, keepdims=True)
    direct = jnp.zeros((rows, H), f32)
    for p in range(parts):
        cols = slice(p * units, (p + 1) * units)
        direct = direct + dot_nt(back_ref[0, :, cols], w_ref[p, H + E :])
        direct = direct + dot_nt(back_ref[1, :, cols], w_ref[p, :H])
    d_ref[...] = direct


def head_grads(spot_ref, scale_ref, all_ref, e_ref, o_ref):
    scale = scale_ref[0]
    parts, rows = e_ref.shape[0], e_ref.shape[1]
    units = o_ref.shape[1]
    frames = parts * rows
    own = pl.ds(pl.multiple_of(spot_ref[0] * units, units), units)
    post = all_ref[:, 3, :, own].reshape(frames, units)
    both = jnp.concatenate([post, all_ref[:, 2, :, own].reshape(frames, units)], axis=1)
    for m in range(H // 256):
        spot = slice(m * 256, (m + 1) * 256)
        grad = (dot_tn(all_ref[:, 0, :, spot].reshape(frames, 256), both) * scale).astype(bf16)
        o_ref[m * 256 : (m + 1) * 256] = grad[:, :units]
        o_ref[H + E + m * 256 : H + E + (m + 1) * 256] = grad[:, units:]
    for m in range(E // 256):
        spot = slice(m * 256, (m + 1) * 256)
        grad = (dot_tn(e_ref[:, :, spot].reshape(frames, 256), post) * scale).astype(bf16)
        o_ref[H + m * 256 : H + (m + 1) * 256] = grad


def gru_grads(spot_ref, scale_ref, one_ref, all_ref, b_ref, earlier_ref, o_ref):
    scale = scale_ref[0]
    parts, rows = all_ref.shape[0], all_ref.shape[2]
    units = o_ref.shape[2]
    frames = parts * rows
    share = o_ref.shape[1] // 3
    half = o_ref.shape[0] // 2
    me = spot_ref[1]
    back = [b_ref[x].reshape(frames, 3 * units) for x in (me, 1 - me)]
    for z in range(2 * half):
        if z < half:
            spot = slice(z * share, (z + 1) * share)
            left = [one_ref[x, :, spot] for x in (me, 1 - me)]
        else:
            spot = pl.ds(pl.multiple_of(((z - half) * 2 + me) * share, share), share)
            left = [all_ref[:, n, :, spot].reshape(frames, share) for n in (0, 1)]
        grad = (dot_tn(left[0], back[0]) + dot_tn(left[1], back[1])) * scale
        grad = grad.astype(bf16)
        for k in range(3):
            o_ref[z, k * share : (k + 1) * share] = grad[:, k * units : (k + 1) * units]


def orthogonal_block(tile, own_ref, g_ref, e_ref, o_ref, x, a, b):
    side, base = g_ref.shape
    width = base + e_ref.shape[1]
    share = o_ref.shape[0]
    own = pl.ds(pl.multiple_of(own_ref[0] * share, share), share)
    wide = own_ref[1] > 0

    def either(run):
        pl.when(wide)(functools.partial(run, width))
        pl.when(jnp.logical_not(wide))(functools.partial(run, base))

    def squares(i, total):
        rows = pl.ds(pl.multiple_of(i * 128, 128), 128)
        v = g_ref[rows, :].astype(f32)
        w = e_ref[rows, :].astype(f32)
        return total + jnp.sum(v * v) + jnp.sum(w * w)

    total = lax.fori_loop(0, side // 128, squares, jnp.zeros((), f32))
    scale = 1.0 / (jnp.sqrt(jnp.full((1, 128), total, f32)) + tiny_value)
    scale = scale[:, :1]

    def shrink(i, carry):
        rows = pl.ds(pl.multiple_of(i * 128, 128), 128)
        x[rows, :base] = (g_ref[rows, :].astype(f32) * scale).astype(bf16)
        x[rows, base:] = (e_ref[rows, :].astype(f32) * scale).astype(bf16)
        return carry

    lax.fori_loop(0, side // 128, shrink, 0)

    def lower(out, product):
        for start in range(0, side, 256):
            stop = start + 256
            block = product(slice(start, side), slice(start, stop)).astype(bf16)
            out[start:, start:stop] = block
            if stop < side:
                out[start:stop, stop:] = block[256:].T

    def square(depth):
        lower(a, lambda rows, cols: dot_nt(x[rows, :depth], x[cols, :depth]))

    def mix():
        lower(
            b,
            lambda rows, cols: coeff_cubic * a[rows, cols].astype(f32)
            + coeff_quintic * dot(a[rows, :], a[:, cols]),
        )

    def renew(j, carry):
        cols = pl.ds(pl.multiple_of(j * tile, tile), tile)
        x[:, cols] = (
            coeff_linear * x[:, cols].astype(f32) + dot(b[...], x[:, cols])
        ).astype(bf16)
        return carry

    used = jnp.where(wide, width // tile, base // tile)

    def sweep(s, carry):
        either(square)
        mix()
        lax.fori_loop(0, used, renew, 0)
        return carry

    lax.fori_loop(0, 4, sweep, 0)
    either(square)
    part = (coeff_cubic * a[own, :].astype(f32) + coeff_quintic * dot(a[own, :], a[...])).astype(bf16)

    def last(j, carry):
        cols = pl.ds(pl.multiple_of(j * tile, tile), tile)
        o_ref[:, cols] = (
            coeff_linear * x[own, cols].astype(f32) + dot(part, x[:, cols])
        ).astype(bf16)
        return carry

    lax.fori_loop(0, width // tile, last, 0)


def turn_block(tile, g_ref, o_ref):
    def block(i, carry):
        spot = pl.ds(pl.multiple_of(i * tile, tile), tile)
        o_ref[:, spot] = g_ref[spot, :].T
        return carry

    lax.fori_loop(0, g_ref.shape[0] // tile, block, 0)


def collect_main(spot_ref, *refs):
    *pieces, earlier_ref, o_ref = refs
    steps = len(pieces) // 2
    base = pieces[0].shape[0]
    head = spot_ref[1] > 0
    for step in range(steps):
        d = spot_ref[0] ^ step
        block = jnp.where(head, pieces[steps + step][:base], pieces[step][...])
        o_ref[:, pl.ds(pl.multiple_of(d * base, base), base)] = block.T


def collect_rest(spot_ref, *refs):
    *pieces, o_ref, rows = refs
    more = rows.shape[0] // len(pieces)
    head = spot_ref[1] > 0
    for step, piece in enumerate(pieces):
        rest = piece[piece.shape[0] - more :]
        d = spot_ref[0] ^ step
        rows[pl.ds(pl.multiple_of(d * more, more), more), :] = jnp.where(head, rest, jnp.zeros_like(rest))
    o_ref[...] = rows[...].T


def deal_block(base, spot_ref, g_ref, o_ref, rows):
    steps, widest = o_ref.shape[:2]
    more = widest - base
    rows[...] = g_ref[:, steps * base :].T
    for step in range(steps):
        d = spot_ref[0] ^ step
        o_ref[step, :base] = g_ref[:, pl.ds(pl.multiple_of(d * base, base), base)].T
        o_ref[step, base:] = rows[pl.ds(pl.multiple_of(d * more, more), more), :]


def finish_block(owners, spot_ref, *refs):
    pieces, (gru_ref, post_ref, prior_ref), (gru_out, post_out, prior_out), all_ref = (
        refs[:-7],
        refs[-7:-4],
        refs[-4:-1],
        refs[-1],
    )
    for step, piece in enumerate(pieces):
        all_ref[step] = piece[...]

    def renewed(old, m):
        change = all_ref[spot_ref[0] ^ owners[m], : old.shape[0]].astype(f32)
        factor = learn_rate * update_scale * math.sqrt(max(ROWS[m], Z))
        return old * (1.0 - learn_rate * weight_decay) - factor * change

    for k in range(3):
        gru_out[k] = renewed(gru_ref[k], k)
    post_out[...] = renewed(post_ref[...], 3)
    prior_out[...] = renewed(prior_ref[...], 4)


def in_vmem(count):
    return [pl.BlockSpec(memory_space=pltpu.VMEM)] * count


def cost(flops, touched):
    return pl.CostEstimate(flops=int(flops), bytes_accessed=int(touched), transcendentals=0)


def run_forward(inputs, weights, seqs):
    parts, packs = inputs.shape[:2]
    out = jax.ShapeDtypeStruct((packs, PACK, H), f32)
    return pl.pallas_call(
        functools.partial(scan_forward, seqs),
        out_shape=[out, jax.ShapeDtypeStruct((3, packs, PACK, H), f32), out],
        in_specs=in_vmem(2),
        out_specs=in_vmem(3),
        scratch_shapes=[pltpu.VMEM((seqs, H), f32)],
        compiler_params=pltpu.CompilerParams(vmem_limit_bytes=6 * mib),
        cost_estimate=cost(6e10, 20 * mib),
        name="scan_forward",
    )(inputs, weights)


def run_backward(direct, factors, rest, weights, seqs, copies):
    packs = direct.shape[0]
    parts, units = weights.shape[0], weights.shape[3]
    return pl.pallas_call(
        functools.partial(scan_backward, seqs),
        out_shape=jax.ShapeDtypeStruct((copies, parts, packs, PACK, 3 * units), bf16),
        in_specs=in_vmem(4),
        out_specs=in_vmem(1)[0],
        scratch_shapes=[
            pltpu.VMEM((seqs, 3 * H), f32),
            pltpu.VMEM((seqs, H), f32),
            pltpu.VMEM((3 * H, H), bf16),
        ],
        compiler_params=pltpu.CompilerParams(vmem_limit_bytes=18 * mib),
        cost_estimate=cost(6e10, 20 * mib),
        name="scan_backward",
    )(direct, factors, rest, weights)


def run_heads(hidden, embed, target, mask, weights):
    rows = hidden.shape[0]
    return pl.pallas_call(
        head_block,
        out_shape=[
            jax.ShapeDtypeStruct((2, rows, Z), bf16),
            jax.ShapeDtypeStruct((rows, H), f32),
            jax.ShapeDtypeStruct((1, 128), f32),
        ],
        in_specs=in_vmem(5),
        out_specs=in_vmem(3),
        compiler_params=pltpu.CompilerParams(vmem_limit_bytes=6 * mib),
        cost_estimate=cost(1e10, 12 * mib),
        name="heads",
    )(hidden, embed, target, mask, weights)


def in_smem(count):
    return [pl.BlockSpec(memory_space=pltpu.SMEM)] * count


def anywhere(count):
    return [pl.BlockSpec(memory_space=pl.ANY)] * count


def run_head_grads(spot, scale, everyone, embed):
    units = everyone.shape[3] // everyone.shape[0]
    return pl.pallas_call(
        head_grads,
        out_shape=jax.ShapeDtypeStruct((H + E + H, units), bf16),
        in_specs=in_smem(2) + in_vmem(2),
        out_specs=in_vmem(1)[0],
        compiler_params=pltpu.CompilerParams(vmem_limit_bytes=6 * mib),
        cost_estimate=cost(4e9, 12 * mib),
        name="head_grads",
    )(spot, scale, everyone, embed)


def run_gru_grads(spot, scale, onehot, everyone, back, earlier, dz_count):
    units = back.shape[3] // 3
    share = (Z + H) // (2 * dz_count)
    return pl.pallas_call(
        gru_grads,
        out_shape=jax.ShapeDtypeStruct((dz_count, 3 * share, units), bf16),
        in_specs=in_smem(2) + in_vmem(3) + anywhere(1),
        out_specs=in_vmem(1)[0],
        compiler_params=pltpu.CompilerParams(vmem_limit_bytes=16 * mib),
        cost_estimate=cost(4e9, 12 * mib),
        name="gru_grads",
    )(spot, scale, onehot, everyone, back, earlier)


def plain_gru_grads(dx_index, scale, onehot, everyone, back, dz_count):
    units = back.shape[3] // 3
    share = (Z + H) // (2 * dz_count)
    total = 0.0
    for n, x in enumerate((dx_index, 1 - dx_index)):
        hidden = everyone[:, n].reshape(-1, dz_count // 2, 2, share)
        hidden = lax.dynamic_index_in_dim(hidden, dx_index, 2, keepdims=False)
        ones = lax.dynamic_index_in_dim(onehot, x, 0, keepdims=False)
        left = jnp.concatenate([ones, hidden.reshape(ones.shape)], axis=1)
        right = lax.dynamic_index_in_dim(back, x, 0, keepdims=False)
        total = total + dot_tn(left, right.reshape(-1, 3 * units))
    grads = (total * scale).astype(bf16).reshape(dz_count, share, 3, units)
    return jnp.swapaxes(grads, 1, 2).reshape(dz_count, 3 * share, units)


def run_orthogonal(share, own, main, extra):
    side = main.shape[0]
    width = main.shape[1] + extra.shape[1]
    return pl.pallas_call(
        functools.partial(orthogonal_block, 512),
        out_shape=jax.ShapeDtypeStruct((share, width), bf16),
        in_specs=in_smem(1) + in_vmem(2),
        out_specs=in_vmem(1)[0],
        scratch_shapes=[
            pltpu.VMEM((side, width), bf16),
            pltpu.VMEM((side, side), bf16),
            pltpu.VMEM((side, side), bf16),
        ],
        compiler_params=pltpu.CompilerParams(vmem_limit_bytes=28 * mib),
        cost_estimate=cost(5e10, 6 * mib),
        name="orthogonal",
    )(own, main, extra)


def run_turn(matrix):
    return pl.pallas_call(
        functools.partial(turn_block, 256),
        out_shape=jax.ShapeDtypeStruct(matrix.shape[::-1], bf16),
        in_specs=in_vmem(1),
        out_specs=in_vmem(1)[0],
        compiler_params=pltpu.CompilerParams(vmem_limit_bytes=6 * mib),
        cost_estimate=cost(1e6, 3 * mib),
        name="turn",
    )(matrix)


def small_kernel(body, out_shape, scratch, specs, arguments, name):
    return pl.pallas_call(
        body,
        out_shape=out_shape,
        in_specs=specs,
        out_specs=jax.tree.map(lambda _: in_vmem(1)[0], out_shape),
        scratch_shapes=scratch,
        compiler_params=pltpu.CompilerParams(vmem_limit_bytes=8 * mib),
        cost_estimate=cost(1e6, 4 * mib),
        name=name,
    )(*arguments)


def run_collect(spot, pieces, extra):
    steps = len(pieces) // 2
    base, units = pieces[0].shape
    return small_kernel(
        collect_main,
        jax.ShapeDtypeStruct((units, steps * base), bf16),
        [],
        in_smem(1) + in_vmem(len(pieces)) + anywhere(1),
        (spot, *pieces, extra),
        "collect_main",
    )


def run_collect_rest(spot, pieces, more):
    steps = len(pieces)
    units = pieces[0].shape[1]
    return small_kernel(
        collect_rest,
        jax.ShapeDtypeStruct((units, steps * more), bf16),
        [pltpu.VMEM((steps * more, units), bf16)],
        in_smem(1) + in_vmem(steps),
        (spot, *pieces),
        "collect_rest",
    )


def run_deal(spot, result, steps, base):
    units, width = result.shape
    widest = width // steps
    return small_kernel(
        functools.partial(deal_block, base),
        jax.ShapeDtypeStruct((steps, widest, units), bf16),
        [pltpu.VMEM((steps * (widest - base), units), bf16)],
        in_smem(1) + in_vmem(1),
        (spot, result),
        "deal",
    )


def run_finish(owners, spot, pieces, rows):
    return small_kernel(
        functools.partial(finish_block, owners),
        [jax.ShapeDtypeStruct(block.shape, f32) for block in rows],
        [pltpu.VMEM((len(pieces), *pieces[0].shape), bf16)],
        in_smem(1) + in_vmem(len(pieces) + len(rows)),
        (spot, *pieces, *rows),
        "finish",
    )


def on_device(
    embeddings,
    samples,
    seq_lengths,
    gru_weight,
    post_weight,
    prior_weight,
    gru_moment,
    post_moment,
    prior_moment,
):
    dz_count = lax.axis_size("dz")
    dx_count = lax.axis_size("dx")
    tp_count = lax.axis_size("tp")
    dp_count = dz_count * dx_count
    dx_index = lax.axis_index("dx")
    tp_index = lax.axis_index("tp")
    dp_index = lax.axis_index("dz") * dx_count + dx_index
    seq_count = embeddings.shape[0]
    seqs = seq_count // tp_count
    units = gru_weight.shape[2]
    groups = Z // ZC
    rows = seqs * FRAMES
    packs = rows // PACK

    def gather(block):
        return lax.all_gather(block, "tp", axis=0, tiled=False)

    def exchange(block, axis):
        return lax.all_to_all(block, axis, 0, 0, tiled=True)

    def mine(block, axis):
        return lax.dynamic_index_in_dim(block, dx_index, axis, keepdims=False)

    weights = gather(gru_weight[:, Z:].astype(bf16))
    head_low = jnp.concatenate([post_weight.astype(bf16), prior_weight.astype(bf16)], axis=0)

    by_part = jnp.swapaxes(samples.reshape(tp_count, seqs, FRAMES, groups), 1, 2)
    by_part = by_part.reshape(tp_count * rows, groups).astype(bf16)

    def one_hot(chosen):
        count = chosen.shape[-1]
        classes = jnp.arange(count * ZC, dtype=jnp.int32)
        expand = (classes[None, :] // ZC == jnp.arange(count)[:, None]).astype(bf16)
        return (dot(chosen, expand) == (classes % ZC).astype(f32)).astype(bf16)

    onehot = one_hot(by_part)
    input_part = jnp.concatenate(
        [dot(onehot, gru_weight[k, :Z].astype(bf16)).astype(bf16) for k in range(3)], axis=1
    ).reshape(tp_count, packs, PACK, 3 * units)
    input_part = exchange(input_part, "tp")
    embed_rows = jnp.swapaxes(embeddings.reshape(tp_count, seqs, FRAMES, E), 1, 2)
    embed_rows = embed_rows.reshape(tp_count, rows, E)
    pair_samples = lax.all_gather(by_part, "dx", axis=0, tiled=False)
    half = Z // dx_count
    pair_half = mine(
        pair_samples.reshape(dx_count * tp_count * rows, dz_count // 2, dx_count, -1), 2
    )
    pair_onehot = one_hot(pair_half.reshape(dx_count * tp_count * rows, groups // dx_count))
    pair_onehot = pair_onehot.reshape(dx_count, tp_count * rows, half)
    own_embed = lax.dynamic_index_in_dim(embed_rows, tp_index, 0, keepdims=False)
    onehot = onehot.reshape(tp_count, rows, Z)
    own_target = lax.dynamic_index_in_dim(onehot, tp_index, 0, keepdims=False)
    positions = jnp.arange(FRAMES, dtype=jnp.int32)
    own_lengths = lax.dynamic_slice_in_dim(seq_lengths, tp_index * seqs, seqs, 0)
    frame_mask = (positions[:, None] < own_lengths[None, :]).astype(f32)
    mask_lanes = jnp.broadcast_to(frame_mask.reshape(rows, 1), (rows, 128))

    every_mask = (positions[:, None] < seq_lengths[None, :]).astype(f32)
    frame_count = jnp.broadcast_to(jnp.sum(every_mask), (8, 128))
    for axis, bits in (("dx", dx_count), ("dz", dz_count)):
        for bit in range(bits.bit_length() - 1):
            pairs = [(i, i ^ (1 << bit)) for i in range(bits)]
            frame_count = frame_count + lax.ppermute(frame_count, axis, pairs)
    frame_count = frame_count[0, 0]
    scale = (1.0 / frame_count).reshape(1)

    early = (head_low, own_embed, own_target, mask_lanes, embed_rows, pair_onehot, scale)
    weights, input_part, early = lax.optimization_barrier((weights, input_part, early))
    head_low, own_embed, own_target, mask_lanes, embed_rows, pair_onehot, scale = early
    head_full = gather(head_low)
    hidden, factors, rest = run_forward(input_part, weights, seqs)
    hidden = hidden.reshape(rows, H)
    hidden_low = hidden.astype(bf16)
    swap = [(i, i ^ 1) for i in range(dx_count)]
    neighbour = lax.ppermute(hidden_low, "dx", swap)
    back_heads, direct, loss_lanes = run_heads(
        hidden, own_embed, own_target, mask_lanes, head_full
    )
    everyone = gather(jnp.concatenate([hidden_low[None], neighbour[None], back_heads], axis=0))
    back = run_backward(
        direct.reshape(packs, PACK, H), factors, rest, weights, seqs, dx_count
    )
    own_back = exchange(back.reshape(dx_count * tp_count, rows, 3 * units), ("dx", "tp"))
    own_back = own_back.reshape(dx_count, tp_count, rows, 3 * units)

    shares = [size // dp_count for size in ROWS]
    all_post = everyone[:, 3]
    spot = jnp.stack([tp_index, dx_index]).astype(jnp.int32)

    head_grad = run_head_grads(spot, scale, everyone, embed_rows)

    head_grad = jnp.concatenate(
        [
            block.reshape(dz_count, dx_count, -1, units)
            for block in (head_grad[: H + E], head_grad[H + E :])
        ],
        axis=2,
    )

    def share_rows(block):
        return lax.psum_scatter(block, "dz", scatter_dimension=0, tiled=True)[0]

    head_done = share_rows(head_grad)
    if shares[0] % 128 == 0:
        gru_grad = run_gru_grads(spot, scale, pair_onehot, everyone, own_back, head_grad, dz_count)
    else:
        gru_grad = plain_gru_grads(dx_index, scale, pair_onehot, everyone, own_back, dz_count)
    gru_grad, head_done = lax.optimization_barrier((gru_grad, head_done))
    gru_sum = share_rows(gru_grad).astype(f32)
    received = lax.ppermute(
        lax.dynamic_index_in_dim(head_done, 1 - dx_index, 0, keepdims=False), "dx", swap
    )
    head_sum = mine(head_done, 0).astype(f32) + received.astype(f32)
    loss_sum = jnp.broadcast_to(jnp.sum(loss_lanes), (8, 128))
    for axis, bits in (("tp", tp_count), ("dx", dx_count), ("dz", dz_count)):
        for bit in range(bits.bit_length() - 1):
            pairs = [(i, i ^ (1 << bit)) for i in range(bits)]
            loss_sum = loss_sum + lax.ppermute(loss_sum, axis, pairs)
    loss_sum = loss_sum[0, 0]
    loss_value = loss_sum / frame_count

    embed_part = E // tp_count
    own_rows_e = lax.dynamic_slice_in_dim(head_full, H + tp_index * embed_part, embed_part, 1)
    post_by_seq = jnp.swapaxes(all_post.reshape(tp_count, FRAMES, seqs, Z), 1, 2)
    embed_grad = jnp.einsum(
        "psfk,ek->psfe",
        post_by_seq,
        jnp.concatenate(list(own_rows_e), axis=1),
        preferred_element_type=f32,
    ).reshape(seq_count, FRAMES, embed_part)
    embed_grad = embed_grad * scale[0]

    grads = [gru_sum[k * shares[0] : (k + 1) * shares[0]] for k in range(3)]
    grads += [head_sum[: shares[3]], head_sum[shares[3] :]]

    def own_rows(matrix, axis_dim):
        share = matrix.shape[axis_dim] // dp_count
        return lax.dynamic_slice_in_dim(matrix, dp_index * share, share, axis_dim)

    gru_moments = own_rows(gru_moment, 1)
    moments = [momentum_keep * gru_moments[k] + grads[k] for k in range(3)]
    moments.append(momentum_keep * own_rows(post_moment, 0) + grads[3])
    moments.append(momentum_keep * own_rows(prior_moment, 0) + grads[4])
    ahead = [(grads[m] + momentum_keep * moments[m]).astype(bf16) for m in range(MATS)]

    owners = [m * dp_count // 8 for m in (0, 3, 4, 7, 5)]
    widest = max(shares)
    base = shares[0]
    holds_post = (dp_index == owners[3]).astype(jnp.int32)
    if dp_count == 8:
        kept = jnp.array([owners.index(d) if d in owners else 0 for d in range(dp_count)])
        heads = jnp.stack(
            [jnp.pad(block, ((0, widest - block.shape[0]), (0, 0))) for block in ahead[3:]]
        )
        groups_of = ((owners[:3], jnp.stack(ahead[:3]), 0), (owners[3:], heads, 3))
        pieces = []
        for targets, blocks, first in groups_of:
            for step in range(dp_count):
                index = jnp.clip(kept[dp_index ^ step] - first, 0, blocks.shape[0] - 1)
                block = lax.dynamic_index_in_dim(blocks, index, 0, keepdims=False)
                if step > 0:
                    pairs = [(d ^ step, d) for d in targets]
                    block = lax.ppermute(block, ("dz", "dx"), pairs)
                pieces.append(block)
        holds_head = (kept[dp_index] >= 3).astype(jnp.int32)
        where = jnp.stack([dp_index, holds_head]).astype(jnp.int32)
        extra = run_collect_rest(where, pieces[dp_count:], widest - base)
        extra = gather(extra).reshape(H, dp_count * (widest - base))
        main = gather(run_collect(where, pieces, extra)).reshape(H, dp_count * base)
    else:
        slots = [jnp.zeros((widest, units), bf16)] * dp_count
        for m in range(MATS):
            slots[owners[m]] = jnp.pad(ahead[m], ((0, widest - shares[m]), (0, 0)))
        arrived = exchange(jnp.stack(slots), ("dz", "dx"))
        turned = run_turn(
            jnp.concatenate(
                [arrived[:, :base].reshape(-1, units), arrived[:, base:].reshape(-1, units)], axis=0
            )
        )
        wide = gather(turned).reshape(H, dp_count * widest)
        main, extra = wide[:, : dp_count * base], wide[:, dp_count * base :]
    own = jnp.stack([tp_index, holds_post]).astype(jnp.int32)
    result = run_orthogonal(units, own, main, extra)
    old_rows = (own_rows(gru_weight, 1), own_rows(post_weight, 0), own_rows(prior_weight, 0))
    if dp_count == 8:
        dealt = run_deal(where, result, dp_count, base)
        pieces = [dealt[0]]
        for step in range(1, dp_count):
            pairs = [(d, d ^ step) for d in owners]
            pieces.append(lax.ppermute(dealt[step], ("dz", "dx"), pairs))
        new_gru, new_post, new_prior = run_finish(owners, where, pieces, old_rows)
    else:
        result = result.T
        results = exchange(
            jnp.concatenate(
                [
                    result[: dp_count * base].reshape(dp_count, base, units),
                    result[dp_count * base :].reshape(dp_count, widest - base, units),
                ],
                axis=1,
            ),
            ("dz", "dx"),
        )

        def renew(old, m):
            factor = learn_rate * update_scale * math.sqrt(max(ROWS[m], Z))
            change = results[owners[m], : old.shape[0]].astype(f32)
            return old * (1.0 - learn_rate * weight_decay) - factor * change

        new_gru = jnp.stack([renew(old_rows[0][k], k) for k in range(3)])
        new_post = renew(old_rows[1], 3)
        new_prior = renew(old_rows[2], 4)
    return (
        loss_value,
        embed_grad,
        new_gru,
        new_post,
        new_prior,
        jnp.stack(moments[:3]),
        moments[3],
        moments[4],
    )

def solution(mesh):
    dp_count, tp_count = mesh.devices.shape
    mesh = jax.sharding.Mesh(
        mesh.devices.reshape(dp_count // 2, 2, tp_count), ("dz", "dx", "tp")
    )
    dp = ("dz", "dx")
    in_specs = (
        P(dp, None, None),
        P(dp, None, None),
        P(dp),
        P(None, None, "tp"),
        P(None, "tp"),
        P(None, "tp"),
        P(None, None, "tp"),
        P(None, "tp"),
        P(None, "tp"),
    )
    out_specs = (
        P(),
        P(dp, None, "tp"),
        P(None, dp, "tp"),
        P(dp, "tp"),
        P(dp, "tp"),
        P(None, dp, "tp"),
        P(dp, "tp"),
        P(dp, "tp"),
    )
    return jax.shard_map(
        on_device, mesh=mesh, in_specs=in_specs, out_specs=out_specs, check_vma=False
    )
```

```python
import functools
import math

import jax
import jax.numpy as jnp
from jax import lax
from jax.experimental import pallas as pl
from jax.experimental.pallas import tpu as pltpu
from jax.sharding import PartitionSpec as P

H = 1024
ZC = 32
E = 1536
FRAMES = 56
MATS = 5
Z = 1024
ROWS = (Z + H, Z + H, Z + H, H + E, H)
PACK = 8


coeff_linear = 3.4445
coeff_cubic = -4.775
coeff_quintic = 2.0315
momentum_keep = 0.95
learn_rate = 0.2
weight_decay = 0.01
update_scale = 0.2
tiny_value = 1e-07
mib = 1 << 20
f32 = jnp.float32
bf16 = jnp.bfloat16
NT = (((1,), (1,)), ((), ()))
TN = (((0,), (0,)), ((), ()))


def dot(left, right):
    return jnp.dot(left, right, preferred_element_type=f32)


def dot_tn(left, right):
    return lax.dot_general(left, right, TN, preferred_element_type=f32)


def dot_nt(left, right):
    return lax.dot_general(left, right, NT, preferred_element_type=f32)


def scan_forward(seqs, x_ref, w_ref, h_ref, k_ref, u_ref, state):
    parts, packs = x_ref.shape[:2]
    units = w_ref.shape[3]
    per_pack = PACK // seqs
    state[...] = jnp.zeros_like(state)

    def pack(i, carry):
        for frame in range(per_pack):
            rows = slice(frame * seqs, (frame + 1) * seqs)
            if frame == 0:
                source, live = jnp.maximum(i - 1, 0), jnp.where(i > 0, 1.0, 0.0)
                spot = slice((per_pack - 1) * seqs, per_pack * seqs)
            else:
                source, live = i, None
                spot = slice((frame - 1) * seqs, frame * seqs)
            before = state[...]
            low = before.astype(bf16)
            for p in range(parts):
                cols = slice(p * units, (p + 1) * units)
                given = x_ref[p, source].astype(f32)[spot]
                if live is not None:
                    given = given * live
                pre = [
                    given[:, k * units : (k + 1) * units] + dot(low, w_ref[p, k]) for k in range(3)
                ]
                last = before[:, cols]
                r = jax.nn.sigmoid(pre[0])
                c = jnp.tanh(r * pre[1])
                u = jax.nn.sigmoid(pre[2] - 1.0)
                rest = 1.0 - u
                new = u * c + rest * last
                inner = u * (1.0 - c * c)
                state[:, cols] = new
                h_ref[i, rows, cols] = new
                k_ref[0, i, rows, cols] = inner * pre[1] * r * (1.0 - r)
                k_ref[1, i, rows, cols] = inner * r
                k_ref[2, i, rows, cols] = (c - last) * u * rest
                u_ref[i, rows, cols] = rest
        return carry

    lax.fori_loop(0, packs, pack, 0)


def scan_backward(seqs, d_ref, k_ref, u_ref, w_ref, b_ref, now, kept, turned):
    copies, parts, packs = b_ref.shape[:3]
    units = w_ref.shape[3]
    per_pack = PACK // seqs
    now[...] = jnp.zeros_like(now)
    kept[...] = jnp.zeros_like(kept)

    def turn(n, carry):
        spot = pl.ds(pl.multiple_of(n * units, units), units)
        turned[spot, :] = w_ref[n // 3, n % 3].T
        return carry

    lax.fori_loop(0, 3 * parts, turn, 0)

    def pack(n, carry):
        i = packs - 1 - n
        later = [None] * per_pack
        for frame in reversed(range(per_pack)):
            rows = slice(frame * seqs, (frame + 1) * seqs)
            values = now[...]
            later[frame] = values
            dh = d_ref[i, rows] + kept[...] + dot(values.astype(bf16), turned[...])
            kept[...] = dh * u_ref[i, rows]
            for p in range(parts):
                cols = slice(p * units, (p + 1) * units)
                for k in range(3):
                    spot = slice((3 * p + k) * units, (3 * p + k + 1) * units)
                    now[:, spot] = dh[:, cols] * k_ref[k, i, rows, cols]
        stacked = jnp.concatenate(later, axis=0).astype(bf16)
        for p in range(parts):
            for copy in range(copies):
                b_ref[copy, p, i] = stacked[:, p * 3 * units : (p + 1) * 3 * units]
        return carry

    lax.fori_loop(0, packs, pack, 0)


def butterfly(values, combine, lane):
    step = 1
    while step < ZC:
        up = pltpu.roll(values, step, 1)
        down = pltpu.roll(values, values.shape[1] - step, 1)
        values = combine(values, jnp.where((lane & step) != 0, up, down))
        step *= 2
    return values


def head_block(h_ref, e_ref, t_ref, m_ref, w_ref, back_ref, d_ref, loss_ref):
    parts = w_ref.shape[0]
    units = w_ref.shape[2]
    rows = h_ref.shape[0]
    low = h_ref[...].astype(bf16)
    mask = m_ref[...]
    lane = lax.broadcasted_iota(jnp.int32, (rows, 128), 1)
    loss = jnp.zeros((rows, 128), f32)
    for p in range(parts):
        post = dot(low, w_ref[p, :H]) + dot(e_ref[...], w_ref[p, H : H + E])
        prior = dot(low, w_ref[p, H + E :])
        for head, logits in enumerate((prior, post)):
            for piece in range(units // 128):
                l = logits[:, piece * 128 : (piece + 1) * 128]
                cols = slice(p * units + piece * 128, p * units + (piece + 1) * 128)
                target = t_ref[:, cols].astype(f32)
                top = butterfly(l, jnp.maximum, lane)
                e = jnp.exp(l - top)
                total = butterfly(e, jnp.add, lane)
                loss = loss + mask * ((top + jnp.log(total)) * (1.0 / ZC) - target * l)
                back_ref[head, :, cols] = (mask * (e / total - target)).astype(bf16)
    loss_ref[...] = jnp.sum(loss, axis=0, keepdims=True)
    direct = jnp.zeros((rows, H), f32)
    for p in range(parts):
        cols = slice(p * units, (p + 1) * units)
        direct = direct + dot_nt(back_ref[0, :, cols], w_ref[p, H + E :])
        direct = direct + dot_nt(back_ref[1, :, cols], w_ref[p, :H])
    d_ref[...] = direct


def head_grads(spot_ref, scale_ref, all_ref, e_ref, earlier_ref, o_ref):
    scale = scale_ref[0]
    parts, rows = e_ref.shape[0], e_ref.shape[1]
    units = o_ref.shape[1]
    frames = parts * rows
    own = pl.ds(pl.multiple_of(spot_ref[0] * units, units), units)
    post = all_ref[:, 3, :, own].reshape(frames, units)
    both = jnp.concatenate([post, all_ref[:, 2, :, own].reshape(frames, units)], axis=1)
    for m in range(H // 256):
        spot = slice(m * 256, (m + 1) * 256)
        grad = (dot_tn(all_ref[:, 0, :, spot].reshape(frames, 256), both) * scale).astype(bf16)
        o_ref[m * 256 : (m + 1) * 256] = grad[:, :units]
        o_ref[H + E + m * 256 : H + E + (m + 1) * 256] = grad[:, units:]
    for m in range(E // 256):
        spot = slice(m * 256, (m + 1) * 256)
        grad = (dot_tn(e_ref[:, :, spot].reshape(frames, 256), post) * scale).astype(bf16)
        o_ref[H + m * 256 : H + (m + 1) * 256] = grad


def gru_grads(spot_ref, scale_ref, one_ref, all_ref, b_ref, earlier_ref, o_ref):
    scale = scale_ref[0]
    parts, rows = all_ref.shape[0], all_ref.shape[2]
    units = o_ref.shape[2]
    frames = parts * rows
    share = o_ref.shape[1] // 3
    half = o_ref.shape[0] // 2
    me = spot_ref[1]
    back = [b_ref[x].reshape(frames, 3 * units) for x in (me, 1 - me)]
    for z in range(2 * half):
        if z < half:
            spot = slice(z * share, (z + 1) * share)
            left = [one_ref[x, :, spot] for x in (me, 1 - me)]
        else:
            spot = pl.ds(pl.multiple_of(((z - half) * 2 + me) * share, share), share)
            left = [all_ref[:, n, :, spot].reshape(frames, share) for n in (0, 1)]
        grad = (dot_tn(left[0], back[0]) + dot_tn(left[1], back[1])) * scale
        grad = grad.astype(bf16)
        for k in range(3):
            o_ref[z, k * share : (k + 1) * share] = grad[:, k * units : (k + 1) * units]


def orthogonal_block(base, tile, own_ref, g_ref, earlier_ref, last_ref, o_ref, x, a, b):
    side, width = g_ref.shape
    share = o_ref.shape[0]
    own = pl.ds(pl.multiple_of(own_ref[0] * share, share), share)
    wide = own_ref[1] > 0

    def either(run):
        pl.when(wide)(functools.partial(run, width))
        pl.when(jnp.logical_not(wide))(functools.partial(run, base))

    def squares(i, total):
        rows = pl.ds(pl.multiple_of(i * 128, 128), 128)
        v = g_ref[rows, :].astype(f32)
        return total + jnp.sum(v * v)

    total = lax.fori_loop(0, side // 128, squares, jnp.zeros((), f32))
    scale = 1.0 / (jnp.sqrt(jnp.full((1, 128), total, f32)) + tiny_value)
    scale = scale[:, :1]

    def shrink(i, carry):
        rows = pl.ds(pl.multiple_of(i * 128, 128), 128)
        x[rows, :] = (g_ref[rows, :].astype(f32) * scale).astype(bf16)
        return carry

    lax.fori_loop(0, side // 128, shrink, 0)

    def lower(out, product):
        for start in range(0, side, 256):
            stop = start + 256
            block = product(slice(start, side), slice(start, stop)).astype(bf16)
            out[start:, start:stop] = block
            if stop < side:
                out[start:stop, stop:] = block[256:].T

    def square(depth):
        lower(a, lambda rows, cols: dot_nt(x[rows, :depth], x[cols, :depth]))

    def mix():
        lower(
            b,
            lambda rows, cols: coeff_cubic * a[rows, cols].astype(f32)
            + coeff_quintic * dot(a[rows, :], a[:, cols]),
        )

    def renew(j, carry):
        cols = pl.ds(pl.multiple_of(j * tile, tile), tile)
        x[:, cols] = (
            coeff_linear * x[:, cols].astype(f32) + dot(b[...], x[:, cols])
        ).astype(bf16)
        return carry

    used = jnp.where(wide, width // tile, base // tile)

    def sweep(s, carry):
        either(square)
        mix()
        lax.fori_loop(0, used, renew, 0)
        return carry

    lax.fori_loop(0, 4, sweep, 0)
    either(square)
    part = (coeff_cubic * a[own, :].astype(f32) + coeff_quintic * dot(a[own, :], a[...])).astype(bf16)

    def last(j, carry):
        cols = pl.ds(pl.multiple_of(j * tile, tile), tile)
        o_ref[:, cols] = (
            coeff_linear * x[own, cols].astype(f32) + dot(part, x[:, cols])
        ).astype(bf16)
        return carry

    lax.fori_loop(0, width // tile, last, 0)


def turn_block(tile, g_ref, o_ref):
    def block(i, carry):
        spot = pl.ds(pl.multiple_of(i * tile, tile), tile)
        o_ref[:, spot] = g_ref[spot, :].T
        return carry

    lax.fori_loop(0, g_ref.shape[0] // tile, block, 0)


def collect_block(spot_ref, *refs):
    *pieces, o_ref, extra = refs
    steps = len(pieces) // 2
    base, widest = pieces[0].shape[0], pieces[-1].shape[0]
    more = widest - base
    head = spot_ref[1] > 0
    for step in range(steps):
        d = spot_ref[0] ^ step
        block = jnp.where(head, pieces[steps + step][:base], pieces[step][...])
        o_ref[:, pl.ds(pl.multiple_of(d * base, base), base)] = block.T
        rest = pieces[steps + step][base:]
        extra[pl.ds(pl.multiple_of(d * more, more), more), :] = jnp.where(head, rest, jnp.zeros_like(rest))
    o_ref[:, steps * base :] = extra[...].T


def deal_block(base, spot_ref, g_ref, o_ref, rows):
    steps, widest = o_ref.shape[:2]
    more = widest - base
    rows[...] = g_ref[:, steps * base :].T
    for step in range(steps):
        d = spot_ref[0] ^ step
        o_ref[step, :base] = g_ref[:, pl.ds(pl.multiple_of(d * base, base), base)].T
        o_ref[step, base:] = rows[pl.ds(pl.multiple_of(d * more, more), more), :]


def finish_block(owners, spot_ref, *refs):
    pieces, (gru_ref, post_ref, prior_ref), (gru_out, post_out, prior_out), all_ref = (
        refs[:-7],
        refs[-7:-4],
        refs[-4:-1],
        refs[-1],
    )
    for step, piece in enumerate(pieces):
        all_ref[step] = piece[...]

    def renewed(old, m):
        change = all_ref[spot_ref[0] ^ owners[m], : old.shape[0]].astype(f32)
        factor = learn_rate * update_scale * math.sqrt(max(ROWS[m], Z))
        return old * (1.0 - learn_rate * weight_decay) - factor * change

    for k in range(3):
        gru_out[k] = renewed(gru_ref[k], k)
    post_out[...] = renewed(post_ref[...], 3)
    prior_out[...] = renewed(prior_ref[...], 4)


def in_vmem(count):
    return [pl.BlockSpec(memory_space=pltpu.VMEM)] * count


def cost(flops, touched):
    return pl.CostEstimate(flops=int(flops), bytes_accessed=int(touched), transcendentals=0)


def run_forward(inputs, weights, seqs):
    parts, packs = inputs.shape[:2]
    out = jax.ShapeDtypeStruct((packs, PACK, H), f32)
    return pl.pallas_call(
        functools.partial(scan_forward, seqs),
        out_shape=[out, jax.ShapeDtypeStruct((3, packs, PACK, H), f32), out],
        in_specs=in_vmem(2),
        out_specs=in_vmem(3),
        scratch_shapes=[pltpu.VMEM((seqs, H), f32)],
        compiler_params=pltpu.CompilerParams(vmem_limit_bytes=6 * mib),
        cost_estimate=cost(6e10, 20 * mib),
        name="scan_forward",
    )(inputs, weights)


def run_backward(direct, factors, rest, weights, seqs, copies):
    packs = direct.shape[0]
    parts, units = weights.shape[0], weights.shape[3]
    return pl.pallas_call(
        functools.partial(scan_backward, seqs),
        out_shape=jax.ShapeDtypeStruct((copies, parts, packs, PACK, 3 * units), bf16),
        in_specs=in_vmem(4),
        out_specs=in_vmem(1)[0],
        scratch_shapes=[
            pltpu.VMEM((seqs, 3 * H), f32),
            pltpu.VMEM((seqs, H), f32),
            pltpu.VMEM((3 * H, H), bf16),
        ],
        compiler_params=pltpu.CompilerParams(vmem_limit_bytes=18 * mib),
        cost_estimate=cost(6e10, 20 * mib),
        name="scan_backward",
    )(direct, factors, rest, weights)


def run_heads(hidden, embed, target, mask, weights):
    rows = hidden.shape[0]
    return pl.pallas_call(
        head_block,
        out_shape=[
            jax.ShapeDtypeStruct((2, rows, Z), bf16),
            jax.ShapeDtypeStruct((rows, H), f32),
            jax.ShapeDtypeStruct((1, 128), f32),
        ],
        in_specs=in_vmem(5),
        out_specs=in_vmem(3),
        compiler_params=pltpu.CompilerParams(vmem_limit_bytes=6 * mib),
        cost_estimate=cost(1e10, 12 * mib),
        name="heads",
    )(hidden, embed, target, mask, weights)


def in_smem(count):
    return [pl.BlockSpec(memory_space=pltpu.SMEM)] * count


def anywhere(count):
    return [pl.BlockSpec(memory_space=pl.ANY)] * count


def run_head_grads(spot, scale, everyone, embed, earlier):
    units = everyone.shape[3] // everyone.shape[0]
    return pl.pallas_call(
        head_grads,
        out_shape=jax.ShapeDtypeStruct((H + E + H, units), bf16),
        in_specs=in_smem(2) + in_vmem(2) + anywhere(1),
        out_specs=in_vmem(1)[0],
        compiler_params=pltpu.CompilerParams(vmem_limit_bytes=6 * mib),
        cost_estimate=cost(4e9, 12 * mib),
        name="head_grads",
    )(spot, scale, everyone, embed, earlier)


def run_gru_grads(spot, scale, onehot, everyone, back, earlier, dz_count):
    units = back.shape[3] // 3
    share = (Z + H) // (2 * dz_count)
    return pl.pallas_call(
        gru_grads,
        out_shape=jax.ShapeDtypeStruct((dz_count, 3 * share, units), bf16),
        in_specs=in_smem(2) + in_vmem(3) + anywhere(1),
        out_specs=in_vmem(1)[0],
        compiler_params=pltpu.CompilerParams(vmem_limit_bytes=16 * mib),
        cost_estimate=cost(4e9, 12 * mib),
        name="gru_grads",
    )(spot, scale, onehot, everyone, back, earlier)


def plain_gru_grads(dx_index, scale, onehot, everyone, back, dz_count):
    units = back.shape[3] // 3
    share = (Z + H) // (2 * dz_count)
    total = 0.0
    for n, x in enumerate((dx_index, 1 - dx_index)):
        hidden = everyone[:, n].reshape(-1, dz_count // 2, 2, share)
        hidden = lax.dynamic_index_in_dim(hidden, dx_index, 2, keepdims=False)
        ones = lax.dynamic_index_in_dim(onehot, x, 0, keepdims=False)
        left = jnp.concatenate([ones, hidden.reshape(ones.shape)], axis=1)
        right = lax.dynamic_index_in_dim(back, x, 0, keepdims=False)
        total = total + dot_tn(left, right.reshape(-1, 3 * units))
    grads = (total * scale).astype(bf16).reshape(dz_count, share, 3, units)
    return jnp.swapaxes(grads, 1, 2).reshape(dz_count, 3 * share, units)


def run_orthogonal(base, share, own, matrix, earlier):
    side, width = matrix.shape
    return pl.pallas_call(
        functools.partial(orthogonal_block, base, 512),
        out_shape=jax.ShapeDtypeStruct((share, width), bf16),
        in_specs=in_smem(1) + in_vmem(1) + anywhere(2),
        out_specs=in_vmem(1)[0],
        scratch_shapes=[
            pltpu.VMEM((side, width), bf16),
            pltpu.VMEM((side, side), bf16),
            pltpu.VMEM((side, side), bf16),
        ],
        compiler_params=pltpu.CompilerParams(vmem_limit_bytes=28 * mib),
        cost_estimate=cost(5e10, 6 * mib),
        name="orthogonal",
    )(own, matrix, *earlier)


def run_turn(matrix):
    return pl.pallas_call(
        functools.partial(turn_block, 256),
        out_shape=jax.ShapeDtypeStruct(matrix.shape[::-1], bf16),
        in_specs=in_vmem(1),
        out_specs=in_vmem(1)[0],
        compiler_params=pltpu.CompilerParams(vmem_limit_bytes=6 * mib),
        cost_estimate=cost(1e6, 3 * mib),
        name="turn",
    )(matrix)


def small_kernel(body, out_shape, scratch, specs, arguments, name):
    return pl.pallas_call(
        body,
        out_shape=out_shape,
        in_specs=specs,
        out_specs=jax.tree.map(lambda _: in_vmem(1)[0], out_shape),
        scratch_shapes=scratch,
        compiler_params=pltpu.CompilerParams(vmem_limit_bytes=8 * mib),
        cost_estimate=cost(1e6, 4 * mib),
        name=name,
    )(*arguments)


def run_collect(spot, pieces):
    steps = len(pieces) // 2
    base, units = pieces[0].shape
    widest = pieces[-1].shape[0]
    return small_kernel(
        collect_block,
        jax.ShapeDtypeStruct((units, steps * widest), bf16),
        [pltpu.VMEM((steps * (widest - base), units), bf16)],
        in_smem(1) + in_vmem(len(pieces)),
        (spot, *pieces),
        "collect",
    )


def run_deal(spot, result, steps, base):
    units, width = result.shape
    widest = width // steps
    return small_kernel(
        functools.partial(deal_block, base),
        jax.ShapeDtypeStruct((steps, widest, units), bf16),
        [pltpu.VMEM((steps * (widest - base), units), bf16)],
        in_smem(1) + in_vmem(1),
        (spot, result),
        "deal",
    )


def run_finish(owners, spot, pieces, rows):
    return small_kernel(
        functools.partial(finish_block, owners),
        [jax.ShapeDtypeStruct(block.shape, f32) for block in rows],
        [pltpu.VMEM((len(pieces), *pieces[0].shape), bf16)],
        in_smem(1) + in_vmem(len(pieces) + len(rows)),
        (spot, *pieces, *rows),
        "finish",
    )


def on_device(
    embeddings,
    samples,
    seq_lengths,
    gru_weight,
    post_weight,
    prior_weight,
    gru_moment,
    post_moment,
    prior_moment,
):
    dz_count = lax.axis_size("dz")
    dx_count = lax.axis_size("dx")
    tp_count = lax.axis_size("tp")
    dp_count = dz_count * dx_count
    dx_index = lax.axis_index("dx")
    tp_index = lax.axis_index("tp")
    dp_index = lax.axis_index("dz") * dx_count + dx_index
    seq_count = embeddings.shape[0]
    seqs = seq_count // tp_count
    units = gru_weight.shape[2]
    groups = Z // ZC
    rows = seqs * FRAMES
    packs = rows // PACK

    def gather(block):
        return lax.all_gather(block, "tp", axis=0, tiled=False)

    def exchange(block, axis):
        return lax.all_to_all(block, axis, 0, 0, tiled=True)

    def mine(block, axis):
        return lax.dynamic_index_in_dim(block, dx_index, axis, keepdims=False)

    weights = gather(gru_weight[:, Z:].astype(bf16))
    head_low = jnp.concatenate([post_weight.astype(bf16), prior_weight.astype(bf16)], axis=0)

    by_part = jnp.swapaxes(samples.reshape(tp_count, seqs, FRAMES, groups), 1, 2)
    by_part = by_part.reshape(tp_count * rows, groups).astype(bf16)

    def one_hot(chosen):
        count = chosen.shape[-1]
        classes = jnp.arange(count * ZC, dtype=jnp.int32)
        expand = (classes[None, :] // ZC == jnp.arange(count)[:, None]).astype(bf16)
        return (dot(chosen, expand) == (classes % ZC).astype(f32)).astype(bf16)

    onehot = one_hot(by_part)
    input_part = jnp.concatenate(
        [dot(onehot, gru_weight[k, :Z].astype(bf16)).astype(bf16) for k in range(3)], axis=1
    ).reshape(tp_count, packs, PACK, 3 * units)
    input_part = exchange(input_part, "tp")
    embed_rows = jnp.swapaxes(embeddings.reshape(tp_count, seqs, FRAMES, E), 1, 2)
    embed_rows = embed_rows.reshape(tp_count, rows, E)
    pair_samples = lax.all_gather(by_part, "dx", axis=0, tiled=False)
    half = Z // dx_count
    pair_half = mine(
        pair_samples.reshape(dx_count * tp_count * rows, dz_count // 2, dx_count, -1), 2
    )
    pair_onehot = one_hot(pair_half.reshape(dx_count * tp_count * rows, groups // dx_count))
    pair_onehot = pair_onehot.reshape(dx_count, tp_count * rows, half)
    own_embed = lax.dynamic_index_in_dim(embed_rows, tp_index, 0, keepdims=False)
    onehot = onehot.reshape(tp_count, rows, Z)
    own_target = lax.dynamic_index_in_dim(onehot, tp_index, 0, keepdims=False)
    positions = jnp.arange(FRAMES, dtype=jnp.int32)
    own_lengths = lax.dynamic_slice_in_dim(seq_lengths, tp_index * seqs, seqs, 0)
    frame_mask = (positions[:, None] < own_lengths[None, :]).astype(f32)
    mask_lanes = jnp.broadcast_to(frame_mask.reshape(rows, 1), (rows, 128))

    every_mask = (positions[:, None] < seq_lengths[None, :]).astype(f32)
    frame_count = jnp.broadcast_to(jnp.sum(every_mask), (8, 128))
    for axis, bits in (("dx", dx_count), ("dz", dz_count)):
        for bit in range(bits.bit_length() - 1):
            pairs = [(i, i ^ (1 << bit)) for i in range(bits)]
            frame_count = frame_count + lax.ppermute(frame_count, axis, pairs)
    frame_count = frame_count[0, 0]
    scale = (1.0 / frame_count).reshape(1)

    early = (head_low, own_embed, own_target, mask_lanes, embed_rows, pair_onehot, scale)
    weights, input_part, early = lax.optimization_barrier((weights, input_part, early))
    head_low, own_embed, own_target, mask_lanes, embed_rows, pair_onehot, scale = early
    head_full = gather(head_low)
    hidden, factors, rest = run_forward(input_part, weights, seqs)
    hidden = hidden.reshape(rows, H)
    hidden_low = hidden.astype(bf16)
    swap = [(i, i ^ 1) for i in range(dx_count)]
    neighbour = lax.ppermute(hidden_low, "dx", swap)
    back_heads, direct, loss_lanes = run_heads(
        hidden, own_embed, own_target, mask_lanes, head_full
    )
    everyone = gather(jnp.concatenate([hidden_low[None], neighbour[None], back_heads], axis=0))
    back = run_backward(
        direct.reshape(packs, PACK, H), factors, rest, weights, seqs, dx_count
    )
    own_back = exchange(back.reshape(dx_count * tp_count, rows, 3 * units), ("dx", "tp"))
    own_back = own_back.reshape(dx_count, tp_count, rows, 3 * units)

    shares = [size // dp_count for size in ROWS]
    all_post = everyone[:, 3]
    spot = jnp.stack([tp_index, dx_index]).astype(jnp.int32)

    head_grad = run_head_grads(spot, scale, everyone, embed_rows, back)

    head_grad = jnp.concatenate(
        [
            block.reshape(dz_count, dx_count, -1, units)
            for block in (head_grad[: H + E], head_grad[H + E :])
        ],
        axis=2,
    )

    def share_rows(block):
        return lax.psum_scatter(block, "dz", scatter_dimension=0, tiled=True)[0]

    head_done = share_rows(head_grad)
    if shares[0] % 128 == 0:
        gru_grad = run_gru_grads(spot, scale, pair_onehot, everyone, own_back, head_grad, dz_count)
    else:
        gru_grad = plain_gru_grads(dx_index, scale, pair_onehot, everyone, own_back, dz_count)
    gru_grad, head_done = lax.optimization_barrier((gru_grad, head_done))
    gru_sum = share_rows(gru_grad).astype(f32)
    received = lax.ppermute(
        lax.dynamic_index_in_dim(head_done, 1 - dx_index, 0, keepdims=False), "dx", swap
    )
    head_sum = mine(head_done, 0).astype(f32) + received.astype(f32)
    loss_sum = jnp.broadcast_to(jnp.sum(loss_lanes), (8, 128))
    for axis, bits in (("tp", tp_count), ("dx", dx_count), ("dz", dz_count)):
        for bit in range(bits.bit_length() - 1):
            pairs = [(i, i ^ (1 << bit)) for i in range(bits)]
            loss_sum = loss_sum + lax.ppermute(loss_sum, axis, pairs)
    loss_sum = loss_sum[0, 0]
    loss_value = loss_sum / frame_count

    embed_part = E // tp_count
    own_rows_e = lax.dynamic_slice_in_dim(head_full, H + tp_index * embed_part, embed_part, 1)
    post_by_seq = jnp.swapaxes(all_post.reshape(tp_count, FRAMES, seqs, Z), 1, 2)
    embed_grad = jnp.einsum(
        "psfk,ek->psfe",
        post_by_seq,
        jnp.concatenate(list(own_rows_e), axis=1),
        preferred_element_type=f32,
    ).reshape(seq_count, FRAMES, embed_part)
    embed_grad = embed_grad * scale[0]

    grads = [gru_sum[k * shares[0] : (k + 1) * shares[0]] for k in range(3)]
    grads += [head_sum[: shares[3]], head_sum[shares[3] :]]

    def own_rows(matrix, axis_dim):
        share = matrix.shape[axis_dim] // dp_count
        return lax.dynamic_slice_in_dim(matrix, dp_index * share, share, axis_dim)

    gru_moments = own_rows(gru_moment, 1)
    moments = [momentum_keep * gru_moments[k] + grads[k] for k in range(3)]
    moments.append(momentum_keep * own_rows(post_moment, 0) + grads[3])
    moments.append(momentum_keep * own_rows(prior_moment, 0) + grads[4])
    ahead = [(grads[m] + momentum_keep * moments[m]).astype(bf16) for m in range(MATS)]

    owners = [m * dp_count // 8 for m in (0, 3, 4, 7, 5)]
    widest = max(shares)
    base = shares[0]
    holds_post = (dp_index == owners[3]).astype(jnp.int32)
    if dp_count == 8:
        kept = jnp.array([owners.index(d) if d in owners else 0 for d in range(dp_count)])
        heads = jnp.stack(
            [jnp.pad(block, ((0, widest - block.shape[0]), (0, 0))) for block in ahead[3:]]
        )
        groups_of = ((owners[:3], jnp.stack(ahead[:3]), 0), (owners[3:], heads, 3))
        pieces = []
        for targets, blocks, first in groups_of:
            for step in range(dp_count):
                index = jnp.clip(kept[dp_index ^ step] - first, 0, blocks.shape[0] - 1)
                block = lax.dynamic_index_in_dim(blocks, index, 0, keepdims=False)
                if step > 0:
                    pairs = [(d ^ step, d) for d in targets]
                    block = lax.ppermute(block, ("dz", "dx"), pairs)
                pieces.append(block)
        holds_head = (kept[dp_index] >= 3).astype(jnp.int32)
        where = jnp.stack([dp_index, holds_head]).astype(jnp.int32)
        turned = run_collect(where, pieces)
    else:
        slots = [jnp.zeros((widest, units), bf16)] * dp_count
        for m in range(MATS):
            slots[owners[m]] = jnp.pad(ahead[m], ((0, widest - shares[m]), (0, 0)))
        arrived = exchange(jnp.stack(slots), ("dz", "dx"))
        turned = run_turn(
            jnp.concatenate(
                [arrived[:, :base].reshape(-1, units), arrived[:, base:].reshape(-1, units)], axis=0
            )
        )
    wide = gather(turned).reshape(H, dp_count * widest)
    own = jnp.stack([tp_index, holds_post]).astype(jnp.int32)
    result = run_orthogonal(dp_count * base, units, own, wide, (embed_grad, loss_value.reshape(1, 1)))
    old_rows = (own_rows(gru_weight, 1), own_rows(post_weight, 0), own_rows(prior_weight, 0))
    if dp_count == 8:
        dealt = run_deal(where, result, dp_count, base)
        pieces = [dealt[0]]
        for step in range(1, dp_count):
            pairs = [(d, d ^ step) for d in owners]
            pieces.append(lax.ppermute(dealt[step], ("dz", "dx"), pairs))
        new_gru, new_post, new_prior = run_finish(owners, where, pieces, old_rows)
    else:
        result = result.T
        results = exchange(
            jnp.concatenate(
                [
                    result[: dp_count * base].reshape(dp_count, base, units),
                    result[dp_count * base :].reshape(dp_count, widest - base, units),
                ],
                axis=1,
            ),
            ("dz", "dx"),
        )

        def renew(old, m):
            factor = learn_rate * update_scale * math.sqrt(max(ROWS[m], Z))
            change = results[owners[m], : old.shape[0]].astype(f32)
            return old * (1.0 - learn_rate * weight_decay) - factor * change

        new_gru = jnp.stack([renew(old_rows[0][k], k) for k in range(3)])
        new_post = renew(old_rows[1], 3)
        new_prior = renew(old_rows[2], 4)
    return (
        loss_value,
        embed_grad,
        new_gru,
        new_post,
        new_prior,
        jnp.stack(moments[:3]),
        moments[3],
        moments[4],
    )

def solution(mesh):
    dp_count, tp_count = mesh.devices.shape
    mesh = jax.sharding.Mesh(
        mesh.devices.reshape(dp_count // 2, 2, tp_count), ("dz", "dx", "tp")
    )
    dp = ("dz", "dx")
    in_specs = (
        P(dp, None, None),
        P(dp, None, None),
        P(dp),
        P(None, None, "tp"),
        P(None, "tp"),
        P(None, "tp"),
        P(None, None, "tp"),
        P(None, "tp"),
        P(None, "tp"),
    )
    out_specs = (
        P(),
        P(dp, None, "tp"),
        P(None, dp, "tp"),
        P(dp, "tp"),
        P(dp, "tp"),
        P(None, dp, "tp"),
        P(dp, "tp"),
        P(dp, "tp"),
    )
    return jax.shard_map(
        on_device, mesh=mesh, in_specs=in_specs, out_specs=out_specs, check_vma=False
    )
```

```python
import functools
import math

import jax
import jax.numpy as jnp
from jax import lax
from jax.experimental import pallas as pl
from jax.experimental.pallas import tpu as pltpu
from jax.sharding import PartitionSpec as P

H = 1024
ZC = 32
E = 1536
FRAMES = 56
MATS = 5
Z = 1024
ROWS = (Z + H, Z + H, Z + H, H + E, H)
PACK = 8


coeff_linear = 3.4445
coeff_cubic = -4.775
coeff_quintic = 2.0315
momentum_keep = 0.95
learn_rate = 0.2
weight_decay = 0.01
update_scale = 0.2
tiny_value = 1e-07
mib = 1 << 20
f32 = jnp.float32
bf16 = jnp.bfloat16
NT = (((1,), (1,)), ((), ()))
TN = (((0,), (0,)), ((), ()))


def dot(left, right):
    return jnp.dot(left, right, preferred_element_type=f32)


def dot_tn(left, right):
    return lax.dot_general(left, right, TN, preferred_element_type=f32)


def dot_nt(left, right):
    return lax.dot_general(left, right, NT, preferred_element_type=f32)


def scan_forward(seqs, x_ref, w_ref, h_ref, k_ref, u_ref, state):
    parts, packs = x_ref.shape[:2]
    units = w_ref.shape[3]
    per_pack = PACK // seqs
    state[...] = jnp.zeros_like(state)

    def pack(i, carry):
        for frame in range(per_pack):
            rows = slice(frame * seqs, (frame + 1) * seqs)
            if frame == 0:
                source, live = jnp.maximum(i - 1, 0), jnp.where(i > 0, 1.0, 0.0)
                spot = slice((per_pack - 1) * seqs, per_pack * seqs)
            else:
                source, live = i, None
                spot = slice((frame - 1) * seqs, frame * seqs)
            before = state[...]
            low = before.astype(bf16)
            for p in range(parts):
                cols = slice(p * units, (p + 1) * units)
                given = x_ref[p, source].astype(f32)[spot]
                if live is not None:
                    given = given * live
                pre = [
                    given[:, k * units : (k + 1) * units] + dot(low, w_ref[p, k]) for k in range(3)
                ]
                last = before[:, cols]
                r = jax.nn.sigmoid(pre[0])
                c = jnp.tanh(r * pre[1])
                u = jax.nn.sigmoid(pre[2] - 1.0)
                rest = 1.0 - u
                new = u * c + rest * last
                inner = u * (1.0 - c * c)
                state[:, cols] = new
                h_ref[i, rows, cols] = new
                k_ref[0, i, rows, cols] = inner * pre[1] * r * (1.0 - r)
                k_ref[1, i, rows, cols] = inner * r
                k_ref[2, i, rows, cols] = (c - last) * u * rest
                u_ref[i, rows, cols] = rest
        return carry

    lax.fori_loop(0, packs, pack, 0)


def scan_backward(seqs, d_ref, k_ref, u_ref, w_ref, b_ref, now, kept, turned):
    copies, parts, packs = b_ref.shape[:3]
    units = w_ref.shape[3]
    per_pack = PACK // seqs
    now[...] = jnp.zeros_like(now)
    kept[...] = jnp.zeros_like(kept)

    def turn(n, carry):
        spot = pl.ds(pl.multiple_of(n * units, units), units)
        turned[spot, :] = w_ref[n // 3, n % 3].T
        return carry

    lax.fori_loop(0, 3 * parts, turn, 0)

    def pack(n, carry):
        i = packs - 1 - n
        later = [None] * per_pack
        for frame in reversed(range(per_pack)):
            rows = slice(frame * seqs, (frame + 1) * seqs)
            values = now[...]
            later[frame] = values
            dh = d_ref[i, rows] + kept[...] + dot(values.astype(bf16), turned[...])
            kept[...] = dh * u_ref[i, rows]
            for p in range(parts):
                cols = slice(p * units, (p + 1) * units)
                for k in range(3):
                    spot = slice((3 * p + k) * units, (3 * p + k + 1) * units)
                    now[:, spot] = dh[:, cols] * k_ref[k, i, rows, cols]
        stacked = jnp.concatenate(later, axis=0).astype(bf16)
        for p in range(parts):
            for copy in range(copies):
                b_ref[copy, p, i] = stacked[:, p * 3 * units : (p + 1) * 3 * units]
        return carry

    lax.fori_loop(0, packs, pack, 0)


def butterfly(values, combine, lane):
    step = 1
    while step < ZC:
        up = pltpu.roll(values, step, 1)
        down = pltpu.roll(values, values.shape[1] - step, 1)
        values = combine(values, jnp.where((lane & step) != 0, up, down))
        step *= 2
    return values


def head_block(h_ref, e_ref, t_ref, m_ref, w_ref, back_ref, d_ref, loss_ref):
    parts = w_ref.shape[0]
    units = w_ref.shape[2]
    rows = h_ref.shape[0]
    low = h_ref[...].astype(bf16)
    mask = m_ref[...]
    lane = lax.broadcasted_iota(jnp.int32, (rows, 128), 1)
    loss = jnp.zeros((rows, 128), f32)
    for p in range(parts):
        post = dot(low, w_ref[p, :H]) + dot(e_ref[...], w_ref[p, H : H + E])
        prior = dot(low, w_ref[p, H + E :])
        for head, logits in enumerate((prior, post)):
            for piece in range(units // 128):
                l = logits[:, piece * 128 : (piece + 1) * 128]
                cols = slice(p * units + piece * 128, p * units + (piece + 1) * 128)
                target = t_ref[:, cols].astype(f32)
                top = butterfly(l, jnp.maximum, lane)
                e = jnp.exp(l - top)
                total = butterfly(e, jnp.add, lane)
                loss = loss + mask * ((top + jnp.log(total)) * (1.0 / ZC) - target * l)
                back_ref[head, :, cols] = (mask * (e / total - target)).astype(bf16)
    loss_ref[...] = jnp.sum(loss, axis=0, keepdims=True)
    direct = jnp.zeros((rows, H), f32)
    for p in range(parts):
        cols = slice(p * units, (p + 1) * units)
        direct = direct + dot_nt(back_ref[0, :, cols], w_ref[p, H + E :])
        direct = direct + dot_nt(back_ref[1, :, cols], w_ref[p, :H])
    d_ref[...] = direct


def head_grads(spot_ref, scale_ref, all_ref, e_ref, earlier_ref, o_ref):
    scale = scale_ref[0]
    parts, rows = e_ref.shape[0], e_ref.shape[1]
    units = o_ref.shape[1]
    frames = parts * rows
    own = pl.ds(pl.multiple_of(spot_ref[0] * units, units), units)
    post = all_ref[:, 3, :, own].reshape(frames, units)
    both = jnp.concatenate([post, all_ref[:, 2, :, own].reshape(frames, units)], axis=1)
    for m in range(H // 256):
        spot = slice(m * 256, (m + 1) * 256)
        grad = (dot_tn(all_ref[:, 0, :, spot].reshape(frames, 256), both) * scale).astype(bf16)
        o_ref[m * 256 : (m + 1) * 256] = grad[:, :units]
        o_ref[H + E + m * 256 : H + E + (m + 1) * 256] = grad[:, units:]
    for m in range(E // 256):
        spot = slice(m * 256, (m + 1) * 256)
        grad = (dot_tn(e_ref[:, :, spot].reshape(frames, 256), post) * scale).astype(bf16)
        o_ref[H + m * 256 : H + (m + 1) * 256] = grad


def gru_grads(spot_ref, scale_ref, one_ref, all_ref, b_ref, earlier_ref, o_ref):
    scale = scale_ref[0]
    parts, rows = all_ref.shape[0], all_ref.shape[2]
    units = o_ref.shape[2]
    frames = parts * rows
    share = o_ref.shape[1] // 3
    half = o_ref.shape[0] // 2
    me = spot_ref[1]
    back = [b_ref[x].reshape(frames, 3 * units) for x in (me, 1 - me)]
    for z in range(2 * half):
        if z < half:
            spot = slice(z * share, (z + 1) * share)
            left = [one_ref[x, :, spot] for x in (me, 1 - me)]
        else:
            spot = pl.ds(pl.multiple_of(((z - half) * 2 + me) * share, share), share)
            left = [all_ref[:, n, :, spot].reshape(frames, share) for n in (0, 1)]
        grad = (dot_tn(left[0], back[0]) + dot_tn(left[1], back[1])) * scale
        grad = grad.astype(bf16)
        for k in range(3):
            o_ref[z, k * share : (k + 1) * share] = grad[:, k * units : (k + 1) * units]


def orthogonal_block(base, tile, own_ref, g_ref, earlier_ref, last_ref, o_ref, x, a, b):
    side, width = g_ref.shape
    share = o_ref.shape[0]
    own = pl.ds(pl.multiple_of(own_ref[0] * share, share), share)
    wide = own_ref[1] > 0

    def either(run):
        pl.when(wide)(functools.partial(run, width))
        pl.when(jnp.logical_not(wide))(functools.partial(run, base))

    def squares(i, total):
        rows = pl.ds(pl.multiple_of(i * 128, 128), 128)
        v = g_ref[rows, :].astype(f32)
        return total + jnp.sum(v * v)

    total = lax.fori_loop(0, side // 128, squares, jnp.zeros((), f32))
    scale = 1.0 / (jnp.sqrt(jnp.full((1, 128), total, f32)) + tiny_value)
    scale = scale[:, :1]

    def shrink(i, carry):
        rows = pl.ds(pl.multiple_of(i * 128, 128), 128)
        x[rows, :] = (g_ref[rows, :].astype(f32) * scale).astype(bf16)
        return carry

    lax.fori_loop(0, side // 128, shrink, 0)

    def lower(out, product):
        for start in range(0, side, 256):
            stop = start + 256
            block = product(slice(start, side), slice(start, stop)).astype(bf16)
            out[start:, start:stop] = block
            if stop < side:
                out[start:stop, stop:] = block[256:].T

    def square(depth):
        lower(a, lambda rows, cols: dot_nt(x[rows, :depth], x[cols, :depth]))

    def mix():
        lower(
            b,
            lambda rows, cols: coeff_cubic * a[rows, cols].astype(f32)
            + coeff_quintic * dot(a[rows, :], a[:, cols]),
        )

    def renew_all(depth):
        for start in range(0, depth, tile):
            cols = slice(start, start + tile)
            x[:, cols] = (
                coeff_linear * x[:, cols].astype(f32) + dot(b[...], x[:, cols])
            ).astype(bf16)

    def sweep(s, carry):
        either(square)
        mix()
        either(renew_all)
        return carry

    lax.fori_loop(0, 4, sweep, 0)
    either(square)
    part = (coeff_cubic * a[own, :].astype(f32) + coeff_quintic * dot(a[own, :], a[...])).astype(bf16)

    def last(j, carry):
        cols = pl.ds(pl.multiple_of(j * tile, tile), tile)
        o_ref[:, cols] = (
            coeff_linear * x[own, cols].astype(f32) + dot(part, x[:, cols])
        ).astype(bf16)
        return carry

    lax.fori_loop(0, width // tile, last, 0)


def turn_block(tile, g_ref, o_ref):
    def block(i, carry):
        spot = pl.ds(pl.multiple_of(i * tile, tile), tile)
        o_ref[:, spot] = g_ref[spot, :].T
        return carry

    lax.fori_loop(0, g_ref.shape[0] // tile, block, 0)


def collect_block(base, spot_ref, *refs):
    *pieces, o_ref, rows = refs
    steps = len(pieces)
    more = pieces[0].shape[0] - base
    for step, piece in enumerate(pieces):
        d = spot_ref[0] ^ step
        o_ref[:, pl.ds(pl.multiple_of(d * base, base), base)] = piece[:base].T
        rows[pl.ds(pl.multiple_of(d * more, more), more), :] = piece[base:]
    o_ref[:, steps * base :] = rows[...].T


def deal_block(base, spot_ref, g_ref, o_ref, rows):
    steps, widest = o_ref.shape[:2]
    more = widest - base
    rows[...] = g_ref[:, steps * base :].T
    for step in range(steps):
        d = spot_ref[0] ^ step
        o_ref[step, :base] = g_ref[:, pl.ds(pl.multiple_of(d * base, base), base)].T
        o_ref[step, base:] = rows[pl.ds(pl.multiple_of(d * more, more), more), :]


def finish_block(owners, spot_ref, *refs):
    pieces, (gru_ref, post_ref, prior_ref), (gru_out, post_out, prior_out), all_ref = (
        refs[:-7],
        refs[-7:-4],
        refs[-4:-1],
        refs[-1],
    )
    for step, piece in enumerate(pieces):
        all_ref[step] = piece[...]

    def renewed(old, m):
        change = all_ref[spot_ref[0] ^ owners[m], : old.shape[0]].astype(f32)
        factor = learn_rate * update_scale * math.sqrt(max(ROWS[m], Z))
        return old * (1.0 - learn_rate * weight_decay) - factor * change

    for k in range(3):
        gru_out[k] = renewed(gru_ref[k], k)
    post_out[...] = renewed(post_ref[...], 3)
    prior_out[...] = renewed(prior_ref[...], 4)


def in_vmem(count):
    return [pl.BlockSpec(memory_space=pltpu.VMEM)] * count


def cost(flops, touched):
    return pl.CostEstimate(flops=int(flops), bytes_accessed=int(touched), transcendentals=0)


def cast_block(g_ref, o_ref):
    o_ref[...] = g_ref[...].astype(bf16)


def run_cast(weights, tile=256):
    parts, rows, units = weights.shape
    skip = Z // tile
    return pl.pallas_call(
        cast_block,
        out_shape=jax.ShapeDtypeStruct((parts, rows - Z, units), bf16),
        grid=(parts, (rows - Z) // tile),
        in_specs=[pl.BlockSpec((1, tile, units), lambda k, i: (k, i + skip, 0))],
        out_specs=pl.BlockSpec((1, tile, units), lambda k, i: (k, i, 0)),
        compiler_params=pltpu.CompilerParams(vmem_limit_bytes=6 * mib),
        cost_estimate=cost(1e6, 5 * mib),
        name="cast",
    )(weights)


def run_forward(inputs, weights, seqs):
    parts, packs = inputs.shape[:2]
    out = jax.ShapeDtypeStruct((packs, PACK, H), f32)
    return pl.pallas_call(
        functools.partial(scan_forward, seqs),
        out_shape=[out, jax.ShapeDtypeStruct((3, packs, PACK, H), f32), out],
        in_specs=in_vmem(2),
        out_specs=in_vmem(3),
        scratch_shapes=[pltpu.VMEM((seqs, H), f32)],
        compiler_params=pltpu.CompilerParams(vmem_limit_bytes=6 * mib),
        cost_estimate=cost(6e10, 20 * mib),
        name="scan_forward",
    )(inputs, weights)


def run_backward(direct, factors, rest, weights, seqs, copies):
    packs = direct.shape[0]
    parts, units = weights.shape[0], weights.shape[3]
    return pl.pallas_call(
        functools.partial(scan_backward, seqs),
        out_shape=jax.ShapeDtypeStruct((copies, parts, packs, PACK, 3 * units), bf16),
        in_specs=in_vmem(4),
        out_specs=in_vmem(1)[0],
        scratch_shapes=[
            pltpu.VMEM((seqs, 3 * H), f32),
            pltpu.VMEM((seqs, H), f32),
            pltpu.VMEM((3 * H, H), bf16),
        ],
        compiler_params=pltpu.CompilerParams(vmem_limit_bytes=18 * mib),
        cost_estimate=cost(6e10, 20 * mib),
        name="scan_backward",
    )(direct, factors, rest, weights)


def run_heads(hidden, embed, target, mask, weights):
    rows = hidden.shape[0]
    return pl.pallas_call(
        head_block,
        out_shape=[
            jax.ShapeDtypeStruct((2, rows, Z), bf16),
            jax.ShapeDtypeStruct((rows, H), f32),
            jax.ShapeDtypeStruct((1, 128), f32),
        ],
        in_specs=in_vmem(5),
        out_specs=in_vmem(3),
        compiler_params=pltpu.CompilerParams(vmem_limit_bytes=6 * mib),
        cost_estimate=cost(1e10, 12 * mib),
        name="heads",
    )(hidden, embed, target, mask, weights)


def in_smem(count):
    return [pl.BlockSpec(memory_space=pltpu.SMEM)] * count


def anywhere(count):
    return [pl.BlockSpec(memory_space=pl.ANY)] * count


def run_head_grads(spot, scale, everyone, embed, earlier):
    units = everyone.shape[3] // everyone.shape[0]
    return pl.pallas_call(
        head_grads,
        out_shape=jax.ShapeDtypeStruct((H + E + H, units), bf16),
        in_specs=in_smem(2) + in_vmem(2) + anywhere(1),
        out_specs=in_vmem(1)[0],
        compiler_params=pltpu.CompilerParams(vmem_limit_bytes=6 * mib),
        cost_estimate=cost(4e9, 12 * mib),
        name="head_grads",
    )(spot, scale, everyone, embed, earlier)


def run_gru_grads(spot, scale, onehot, everyone, back, earlier, dz_count):
    units = back.shape[3] // 3
    share = (Z + H) // (2 * dz_count)
    return pl.pallas_call(
        gru_grads,
        out_shape=jax.ShapeDtypeStruct((dz_count, 3 * share, units), bf16),
        in_specs=in_smem(2) + in_vmem(3) + anywhere(1),
        out_specs=in_vmem(1)[0],
        compiler_params=pltpu.CompilerParams(vmem_limit_bytes=16 * mib),
        cost_estimate=cost(4e9, 12 * mib),
        name="gru_grads",
    )(spot, scale, onehot, everyone, back, earlier)


def plain_gru_grads(dx_index, scale, onehot, everyone, back, dz_count):
    units = back.shape[3] // 3
    share = (Z + H) // (2 * dz_count)
    total = 0.0
    for n, x in enumerate((dx_index, 1 - dx_index)):
        hidden = everyone[:, n].reshape(-1, dz_count // 2, 2, share)
        hidden = lax.dynamic_index_in_dim(hidden, dx_index, 2, keepdims=False)
        ones = lax.dynamic_index_in_dim(onehot, x, 0, keepdims=False)
        left = jnp.concatenate([ones, hidden.reshape(ones.shape)], axis=1)
        right = lax.dynamic_index_in_dim(back, x, 0, keepdims=False)
        total = total + dot_tn(left, right.reshape(-1, 3 * units))
    grads = (total * scale).astype(bf16).reshape(dz_count, share, 3, units)
    return jnp.swapaxes(grads, 1, 2).reshape(dz_count, 3 * share, units)


def run_orthogonal(base, share, own, matrix, earlier):
    side, width = matrix.shape
    return pl.pallas_call(
        functools.partial(orthogonal_block, base, 512),
        out_shape=jax.ShapeDtypeStruct((share, width), bf16),
        in_specs=in_smem(1) + in_vmem(1) + anywhere(2),
        out_specs=in_vmem(1)[0],
        scratch_shapes=[
            pltpu.VMEM((side, width), bf16),
            pltpu.VMEM((side, side), bf16),
            pltpu.VMEM((side, side), bf16),
        ],
        compiler_params=pltpu.CompilerParams(vmem_limit_bytes=28 * mib),
        cost_estimate=cost(5e10, 6 * mib),
        name="orthogonal",
    )(own, matrix, *earlier)


def run_turn(matrix):
    return pl.pallas_call(
        functools.partial(turn_block, 256),
        out_shape=jax.ShapeDtypeStruct(matrix.shape[::-1], bf16),
        in_specs=in_vmem(1),
        out_specs=in_vmem(1)[0],
        compiler_params=pltpu.CompilerParams(vmem_limit_bytes=6 * mib),
        cost_estimate=cost(1e6, 3 * mib),
        name="turn",
    )(matrix)


def small_kernel(body, out_shape, scratch, specs, arguments, name):
    return pl.pallas_call(
        body,
        out_shape=out_shape,
        in_specs=specs,
        out_specs=jax.tree.map(lambda _: in_vmem(1)[0], out_shape),
        scratch_shapes=scratch,
        compiler_params=pltpu.CompilerParams(vmem_limit_bytes=8 * mib),
        cost_estimate=cost(1e6, 4 * mib),
        name=name,
    )(*arguments)


def run_collect(spot, pieces, base):
    steps = len(pieces)
    widest, units = pieces[0].shape
    return small_kernel(
        functools.partial(collect_block, base),
        jax.ShapeDtypeStruct((units, steps * widest), bf16),
        [pltpu.VMEM((steps * (widest - base), units), bf16)],
        in_smem(1) + in_vmem(steps),
        (spot, *pieces),
        "collect",
    )


def run_deal(spot, result, steps, base):
    units, width = result.shape
    widest = width // steps
    return small_kernel(
        functools.partial(deal_block, base),
        jax.ShapeDtypeStruct((steps, widest, units), bf16),
        [pltpu.VMEM((steps * (widest - base), units), bf16)],
        in_smem(1) + in_vmem(1),
        (spot, result),
        "deal",
    )


def run_finish(owners, spot, pieces, rows):
    return small_kernel(
        functools.partial(finish_block, owners),
        [jax.ShapeDtypeStruct(block.shape, f32) for block in rows],
        [pltpu.VMEM((len(pieces), *pieces[0].shape), bf16)],
        in_smem(1) + in_vmem(len(pieces) + len(rows)),
        (spot, *pieces, *rows),
        "finish",
    )


def on_device(
    embeddings,
    samples,
    seq_lengths,
    gru_weight,
    post_weight,
    prior_weight,
    gru_moment,
    post_moment,
    prior_moment,
):
    dz_count = lax.axis_size("dz")
    dx_count = lax.axis_size("dx")
    tp_count = lax.axis_size("tp")
    dp_count = dz_count * dx_count
    dx_index = lax.axis_index("dx")
    tp_index = lax.axis_index("tp")
    dp_index = lax.axis_index("dz") * dx_count + dx_index
    seq_count = embeddings.shape[0]
    seqs = seq_count // tp_count
    units = gru_weight.shape[2]
    groups = Z // ZC
    rows = seqs * FRAMES
    packs = rows // PACK

    def gather(block):
        return lax.all_gather(block, "tp", axis=0, tiled=False)

    def exchange(block, axis):
        return lax.all_to_all(block, axis, 0, 0, tiled=True)

    def mine(block, axis):
        return lax.dynamic_index_in_dim(block, dx_index, axis, keepdims=False)

    weights = gather(run_cast(gru_weight, tile=512))
    head_low = jnp.concatenate([post_weight.astype(bf16), prior_weight.astype(bf16)], axis=0)

    by_part = jnp.swapaxes(samples.reshape(tp_count, seqs, FRAMES, groups), 1, 2)
    by_part = by_part.reshape(tp_count * rows, groups).astype(bf16)

    def one_hot(chosen):
        count = chosen.shape[-1]
        classes = jnp.arange(count * ZC, dtype=jnp.int32)
        expand = (classes[None, :] // ZC == jnp.arange(count)[:, None]).astype(bf16)
        return (dot(chosen, expand) == (classes % ZC).astype(f32)).astype(bf16)

    onehot = one_hot(by_part)
    input_part = jnp.concatenate(
        [dot(onehot, gru_weight[k, :Z].astype(bf16)).astype(bf16) for k in range(3)], axis=1
    ).reshape(tp_count, packs, PACK, 3 * units)
    input_part = exchange(input_part, "tp")
    embed_rows = jnp.swapaxes(embeddings.reshape(tp_count, seqs, FRAMES, E), 1, 2)
    embed_rows = embed_rows.reshape(tp_count, rows, E)
    pair_samples = lax.all_gather(by_part, "dx", axis=0, tiled=False)
    half = Z // dx_count
    pair_half = mine(
        pair_samples.reshape(dx_count * tp_count * rows, dz_count // 2, dx_count, -1), 2
    )
    pair_onehot = one_hot(pair_half.reshape(dx_count * tp_count * rows, groups // dx_count))
    pair_onehot = pair_onehot.reshape(dx_count, tp_count * rows, half)
    own_embed = lax.dynamic_index_in_dim(embed_rows, tp_index, 0, keepdims=False)
    onehot = onehot.reshape(tp_count, rows, Z)
    own_target = lax.dynamic_index_in_dim(onehot, tp_index, 0, keepdims=False)
    positions = jnp.arange(FRAMES, dtype=jnp.int32)
    own_lengths = lax.dynamic_slice_in_dim(seq_lengths, tp_index * seqs, seqs, 0)
    frame_mask = (positions[:, None] < own_lengths[None, :]).astype(f32)
    mask_lanes = jnp.broadcast_to(frame_mask.reshape(rows, 1), (rows, 128))

    every_mask = (positions[:, None] < seq_lengths[None, :]).astype(f32)
    frame_count = jnp.broadcast_to(jnp.sum(every_mask), (8, 128))
    for axis, bits in (("dx", dx_count), ("dz", dz_count)):
        for bit in range(bits.bit_length() - 1):
            pairs = [(i, i ^ (1 << bit)) for i in range(bits)]
            frame_count = frame_count + lax.ppermute(frame_count, axis, pairs)
    frame_count = frame_count[0, 0]
    scale = (1.0 / frame_count).reshape(1)

    early = (head_low, own_embed, own_target, mask_lanes, embed_rows, pair_onehot, scale)
    weights, input_part, early = lax.optimization_barrier((weights, input_part, early))
    head_low, own_embed, own_target, mask_lanes, embed_rows, pair_onehot, scale = early
    head_full = gather(head_low)
    hidden, factors, rest = run_forward(input_part, weights, seqs)
    hidden = hidden.reshape(rows, H)
    hidden_low = hidden.astype(bf16)
    swap = [(i, i ^ 1) for i in range(dx_count)]
    neighbour = lax.ppermute(hidden_low, "dx", swap)
    back_heads, direct, loss_lanes = run_heads(
        hidden, own_embed, own_target, mask_lanes, head_full
    )
    everyone = gather(jnp.concatenate([hidden_low[None], neighbour[None], back_heads], axis=0))
    back = run_backward(
        direct.reshape(packs, PACK, H), factors, rest, weights, seqs, dx_count
    )
    own_back = exchange(back.reshape(dx_count * tp_count, rows, 3 * units), ("dx", "tp"))
    own_back = own_back.reshape(dx_count, tp_count, rows, 3 * units)

    shares = [size // dp_count for size in ROWS]
    all_post = everyone[:, 3]
    spot = jnp.stack([tp_index, dx_index]).astype(jnp.int32)

    head_grad = run_head_grads(spot, scale, everyone, embed_rows, back)

    head_grad = jnp.concatenate(
        [
            block.reshape(dz_count, dx_count, -1, units)
            for block in (head_grad[: H + E], head_grad[H + E :])
        ],
        axis=2,
    )

    def share_rows(block):
        return lax.psum_scatter(block, "dz", scatter_dimension=0, tiled=True)[0]

    head_done = share_rows(head_grad)
    if shares[0] % 128 == 0:
        gru_grad = run_gru_grads(spot, scale, pair_onehot, everyone, own_back, head_grad, dz_count)
    else:
        gru_grad = plain_gru_grads(dx_index, scale, pair_onehot, everyone, own_back, dz_count)
    gru_grad, head_done = lax.optimization_barrier((gru_grad, head_done))
    gru_sum = share_rows(gru_grad).astype(f32)
    received = lax.ppermute(
        lax.dynamic_index_in_dim(head_done, 1 - dx_index, 0, keepdims=False), "dx", swap
    )
    head_sum = mine(head_done, 0).astype(f32) + received.astype(f32)
    loss_sum = jnp.broadcast_to(jnp.sum(loss_lanes), (8, 128))
    for axis, bits in (("tp", tp_count), ("dx", dx_count), ("dz", dz_count)):
        for bit in range(bits.bit_length() - 1):
            pairs = [(i, i ^ (1 << bit)) for i in range(bits)]
            loss_sum = loss_sum + lax.ppermute(loss_sum, axis, pairs)
    loss_sum = loss_sum[0, 0]
    loss_value = loss_sum / frame_count

    embed_part = E // tp_count
    own_rows_e = lax.dynamic_slice_in_dim(head_full, H + tp_index * embed_part, embed_part, 1)
    post_by_seq = jnp.swapaxes(all_post.reshape(tp_count, FRAMES, seqs, Z), 1, 2)
    embed_grad = jnp.einsum(
        "psfk,ek->psfe",
        post_by_seq,
        jnp.concatenate(list(own_rows_e), axis=1),
        preferred_element_type=f32,
    ).reshape(seq_count, FRAMES, embed_part)
    embed_grad = embed_grad * scale[0]

    grads = [gru_sum[k * shares[0] : (k + 1) * shares[0]] for k in range(3)]
    grads += [head_sum[: shares[3]], head_sum[shares[3] :]]

    def own_rows(matrix, axis_dim):
        share = matrix.shape[axis_dim] // dp_count
        return lax.dynamic_slice_in_dim(matrix, dp_index * share, share, axis_dim)

    gru_moments = own_rows(gru_moment, 1)
    moments = [momentum_keep * gru_moments[k] + grads[k] for k in range(3)]
    moments.append(momentum_keep * own_rows(post_moment, 0) + grads[3])
    moments.append(momentum_keep * own_rows(prior_moment, 0) + grads[4])
    ahead = [(grads[m] + momentum_keep * moments[m]).astype(bf16) for m in range(MATS)]

    owners = [m * dp_count // 8 for m in (0, 3, 4, 7, 5)]
    widest = max(shares)
    base = shares[0]
    holds_post = (dp_index == owners[3]).astype(jnp.int32)
    if dp_count == 8:
        kept = jnp.array([owners.index(d) if d in owners else 0 for d in range(dp_count)])
        blocks = jnp.stack(
            [jnp.pad(block, ((0, widest - block.shape[0]), (0, 0))) for block in ahead]
        )
        where = dp_index.astype(jnp.int32).reshape(1)
        pieces = []
        for step in range(dp_count):
            block = lax.dynamic_index_in_dim(blocks, kept[dp_index ^ step], 0, keepdims=False)
            if step > 0:
                block = lax.ppermute(block, ("dz", "dx"), [(d ^ step, d) for d in owners])
            pieces.append(block)
        turned = run_collect(where, pieces, base)
    else:
        slots = [jnp.zeros((widest, units), bf16)] * dp_count
        for m in range(MATS):
            slots[owners[m]] = jnp.pad(ahead[m], ((0, widest - shares[m]), (0, 0)))
        arrived = exchange(jnp.stack(slots), ("dz", "dx"))
        turned = run_turn(
            jnp.concatenate(
                [arrived[:, :base].reshape(-1, units), arrived[:, base:].reshape(-1, units)], axis=0
            )
        )
    wide = gather(turned).reshape(H, dp_count * widest)
    own = jnp.stack([tp_index, holds_post]).astype(jnp.int32)
    result = run_orthogonal(dp_count * base, units, own, wide, (embed_grad, loss_value.reshape(1, 1)))
    old_rows = (own_rows(gru_weight, 1), own_rows(post_weight, 0), own_rows(prior_weight, 0))
    if dp_count == 8:
        dealt = run_deal(where, result, dp_count, base)
        pieces = [dealt[0]]
        for step in range(1, dp_count):
            pairs = [(d, d ^ step) for d in owners]
            pieces.append(lax.ppermute(dealt[step], ("dz", "dx"), pairs))
        new_gru, new_post, new_prior = run_finish(owners, where, pieces, old_rows)
    else:
        result = result.T
        results = exchange(
            jnp.concatenate(
                [
                    result[: dp_count * base].reshape(dp_count, base, units),
                    result[dp_count * base :].reshape(dp_count, widest - base, units),
                ],
                axis=1,
            ),
            ("dz", "dx"),
        )

        def renew(old, m):
            factor = learn_rate * update_scale * math.sqrt(max(ROWS[m], Z))
            change = results[owners[m], : old.shape[0]].astype(f32)
            return old * (1.0 - learn_rate * weight_decay) - factor * change

        new_gru = jnp.stack([renew(old_rows[0][k], k) for k in range(3)])
        new_post = renew(old_rows[1], 3)
        new_prior = renew(old_rows[2], 4)
    return (
        loss_value,
        embed_grad,
        new_gru,
        new_post,
        new_prior,
        jnp.stack(moments[:3]),
        moments[3],
        moments[4],
    )

def solution(mesh):
    dp_count, tp_count = mesh.devices.shape
    mesh = jax.sharding.Mesh(
        mesh.devices.reshape(dp_count // 2, 2, tp_count), ("dz", "dx", "tp")
    )
    dp = ("dz", "dx")
    in_specs = (
        P(dp, None, None),
        P(dp, None, None),
        P(dp),
        P(None, None, "tp"),
        P(None, "tp"),
        P(None, "tp"),
        P(None, None, "tp"),
        P(None, "tp"),
        P(None, "tp"),
    )
    out_specs = (
        P(),
        P(dp, None, "tp"),
        P(None, dp, "tp"),
        P(dp, "tp"),
        P(dp, "tp"),
        P(None, dp, "tp"),
        P(dp, "tp"),
        P(dp, "tp"),
    )
    return jax.shard_map(
        on_device, mesh=mesh, in_specs=in_specs, out_specs=out_specs, check_vma=False
    )
```

```python
import functools
import math

import jax
import jax.numpy as jnp
from jax import lax
from jax.experimental import pallas as pl
from jax.experimental.pallas import tpu as pltpu
from jax.sharding import PartitionSpec as P

H = 1024
ZC = 32
E = 1536
FRAMES = 56
MATS = 5
Z = 1024
ROWS = (Z + H, Z + H, Z + H, H + E, H)
PACK = 8
CHUNK = 4


coeff_linear = 3.4445
coeff_cubic = -4.775
coeff_quintic = 2.0315
momentum_keep = 0.95
learn_rate = 0.2
weight_decay = 0.01
update_scale = 0.2
tiny_value = 1e-07
mib = 1 << 20
LARGE = 56 * mib
f32 = jnp.float32
bf16 = jnp.bfloat16
NT = (((1,), (1,)), ((), ()))
TN = (((0,), (0,)), ((), ()))


def dot(left, right):
    return jnp.dot(left, right, preferred_element_type=f32)


def dot_tn(left, right):
    return lax.dot_general(left, right, TN, preferred_element_type=f32)


def dot_nt(left, right):
    return lax.dot_general(left, right, NT, preferred_element_type=f32)


def copy(source, target, semaphore):
    return pltpu.make_async_copy(source, target, semaphore)


def scan_forward(
    seqs, chunk, x_ref, w_hbm, h_ref, k_hbm, u_hbm, t_hbm, state, w, k_ref, u_ref, t, w_sem, k_sem, u_sem, t_sem
):
    parts, packs = x_ref.shape[:2]
    units = w.shape[3]
    per_pack = PACK // seqs
    loads = [copy(w_hbm.at[p], w.at[p], w_sem.at[p]) for p in range(parts)]
    for load in loads:
        load.start()
    state[...] = jnp.zeros_like(state)
    for load in loads:
        load.wait()

    def stores(c):
        at = pl.ds(c * chunk, chunk)
        return (
            copy(k_ref.at[:, at], k_hbm.at[:, at], k_sem.at[c]),
            copy(u_ref.at[at], u_hbm.at[at], u_sem.at[c]),
        )

    def pack(i, carry):
        states = []
        for frame in range(per_pack):
            rows = slice(frame * seqs, (frame + 1) * seqs)
            if frame == 0:
                source, live = jnp.maximum(i - 1, 0), jnp.where(i > 0, 1.0, 0.0)
                spot = slice((per_pack - 1) * seqs, per_pack * seqs)
            else:
                source, live = i, None
                spot = slice((frame - 1) * seqs, frame * seqs)
            before = state[...]
            low = before.astype(bf16)
            news = []
            for p in range(parts):
                cols = slice(p * units, (p + 1) * units)
                given = x_ref[p, source].astype(f32)[spot]
                if live is not None:
                    given = given * live
                pre = [
                    given[:, k * units : (k + 1) * units] + dot(low, w[p, k]) for k in range(3)
                ]
                last = before[:, cols]
                r = jax.nn.sigmoid(pre[0])
                c = jnp.tanh(r * pre[1])
                u = jax.nn.sigmoid(pre[2] - 1.0)
                rest = 1.0 - u
                new = u * c + rest * last
                inner = u * (1.0 - c * c)
                state[:, cols] = new
                news.append(new)
                k_ref[0, i, rows, cols] = inner * pre[1] * r * (1.0 - r)
                k_ref[1, i, rows, cols] = inner * r
                k_ref[2, i, rows, cols] = (c - last) * u * rest
                u_ref[i, rows, cols] = rest
            states.append(jnp.concatenate(news, axis=1))
        h_ref[i] = jnp.concatenate(states, axis=0).astype(bf16)

        @pl.when(i % chunk == chunk - 1)
        def _():
            for store in stores(i // chunk):
                store.start()

        return carry

    def pack_and_turn(i, carry):
        t[pl.ds(pl.multiple_of(i * units, units), units), :] = w[i // 3, i % 3].T
        return pack(i, carry)

    lax.fori_loop(0, 3 * parts, pack_and_turn, 0)
    turned = copy(t, t_hbm, t_sem)
    turned.start()
    lax.fori_loop(3 * parts, packs, pack, 0)
    turned.wait()
    for c in range(packs // chunk):
        for store in stores(c):
            store.wait()


def scan_backward(
    seqs, chunk, d_ref, k_hbm, u_hbm, t_hbm, b_hbm, now, kept, w, k_ref, u_ref, b_ref, t_sem, k_sem, u_sem, b_sem
):
    copies, parts, packs = b_hbm.shape[:3]
    units = b_ref.shape[3] // 3
    per_pack = PACK // seqs
    chunks = packs // chunk

    def loads(c):
        at = pl.ds(c * chunk, chunk)
        return (
            copy(k_hbm.at[:, at], k_ref.at[:, at], k_sem.at[c]),
            copy(u_hbm.at[at], u_ref.at[at], u_sem.at[c]),
        )

    def stores(c):
        at = pl.ds(c * chunk, chunk)
        return [
            copy(b_ref.at[:, at], b_hbm.at[n, :, at], b_sem.at[n * chunks + c]) for n in range(copies)
        ]

    turned = copy(t_hbm, w, t_sem)
    turned.start()
    for c in reversed(range(chunks)):
        for load in loads(c):
            load.start()
    now[...] = jnp.zeros_like(now)
    kept[...] = jnp.zeros_like(kept)
    turned.wait()

    def pack(n, carry):
        i = packs - 1 - n

        @pl.when(i % chunk == chunk - 1)
        def _():
            for load in loads(i // chunk):
                load.wait()

        later = [None] * per_pack
        for frame in reversed(range(per_pack)):
            rows = slice(frame * seqs, (frame + 1) * seqs)
            values = now[...]
            later[frame] = values
            dh = d_ref[i, rows] + kept[...] + dot(values.astype(bf16), w[...])
            kept[...] = dh * u_ref[i, rows]
            for p in range(parts):
                cols = slice(p * units, (p + 1) * units)
                for k in range(3):
                    spot = slice((3 * p + k) * units, (3 * p + k + 1) * units)
                    now[:, spot] = dh[:, cols] * k_ref[k, i, rows, cols]
        stacked = jnp.concatenate(later, axis=0).astype(bf16)
        for p in range(parts):
            b_ref[p, i] = stacked[:, p * 3 * units : (p + 1) * 3 * units]

        @pl.when(i % chunk == 0)
        def _():
            for store in stores(i // chunk):
                store.start()

        return carry

    lax.fori_loop(0, packs, pack, 0)
    for c in range(chunks):
        for store in stores(c):
            store.wait()


def butterfly(values, combine, lane):
    step = 1
    while step < ZC:
        up = pltpu.roll(values, step, 1)
        down = pltpu.roll(values, values.shape[1] - step, 1)
        values = combine(values, jnp.where((lane & step) != 0, up, down))
        step *= 2
    return values


def head_block(h_ref, e_ref, t_ref, m_ref, w_hbm, back_ref, d_ref, loss_ref, w_ref, w_sem):
    parts = w_ref.shape[0]
    loads = [copy(w_hbm.at[p], w_ref.at[p], w_sem.at[p]) for p in range(parts)]
    for load in loads:
        load.start()
    units = w_ref.shape[2]
    rows = h_ref.shape[0]
    low = h_ref[...]
    mask = m_ref[...]
    lane = lax.broadcasted_iota(jnp.int32, (rows, 128), 1)
    loss = jnp.zeros((rows, 128), f32)
    for p in range(parts):
        loads[p].wait()
        post = dot(low, w_ref[p, :H]) + dot(e_ref[...], w_ref[p, H : H + E])
        prior = dot(low, w_ref[p, H + E :])
        for head, logits in enumerate((prior, post)):
            for piece in range(units // 128):
                l = logits[:, piece * 128 : (piece + 1) * 128]
                cols = slice(p * units + piece * 128, p * units + (piece + 1) * 128)
                target = t_ref[:, cols].astype(f32)
                top = butterfly(l, jnp.maximum, lane)
                e = jnp.exp(l - top)
                total = butterfly(e, jnp.add, lane)
                loss = loss + mask * ((top + jnp.log(total)) * (1.0 / ZC) - target * l)
                back_ref[head + 1, :, cols] = (mask * (e / total - target)).astype(bf16)
    loss_ref[...] = jnp.sum(loss, axis=0, keepdims=True)
    direct = jnp.zeros((rows, H), f32)
    for p in range(parts):
        cols = slice(p * units, (p + 1) * units)
        direct = direct + dot_nt(back_ref[1, :, cols], w_ref[p, H + E :])
        direct = direct + dot_nt(back_ref[2, :, cols], w_ref[p, :H])
    d_ref[...] = direct


def head_grads(spot_ref, scale_ref, h_hbm, r_hbm, e_hbm, earlier_ref, o_ref, h_ref, r_ref, e_ref, sems):
    parts, rows = e_ref.shape[0], e_ref.shape[1]
    units = o_ref.shape[1]
    frames = parts * rows
    scale = scale_ref[0]
    own = pl.ds(pl.multiple_of(spot_ref[0] * units, units), units)
    loads = [
        copy(r_hbm.at[:, pl.ds(1, 2), :, own], r_ref, sems.at[0]),
        copy(h_hbm, h_ref, sems.at[1]),
        copy(e_hbm, e_ref, sems.at[2]),
    ]
    for load in loads:
        load.start()
    loads[0].wait()
    loads[1].wait()
    post = r_ref[:, 1].reshape(frames, units)
    both = jnp.concatenate([post, r_ref[:, 0].reshape(frames, units)], axis=1)
    for m in range(H // 256):
        spot = slice(m * 256, (m + 1) * 256)
        grad = (dot_tn(h_ref[:, :, spot].reshape(frames, 256), both) * scale).astype(bf16)
        o_ref[m * 256 : (m + 1) * 256] = grad[:, :units]
        o_ref[H + E + m * 256 : H + E + (m + 1) * 256] = grad[:, units:]
    loads[2].wait()
    for m in range(E // 256):
        spot = slice(m * 256, (m + 1) * 256)
        grad = (dot_tn(e_ref[:, :, spot].reshape(frames, 256), post) * scale).astype(bf16)
        o_ref[H + m * 256 : H + (m + 1) * 256] = grad


def gru_grads(
    spot_ref, scale_ref, one_hbm, h_hbm, r_hbm, b_hbm, earlier_ref, o_ref, one_ref, l_ref, b_ref, sems
):
    parts, rows = b_ref.shape[1], b_ref.shape[2]
    units = o_ref.shape[2]
    frames = parts * rows
    share = o_ref.shape[1] // 3
    half = o_ref.shape[0] // 2
    scale = scale_ref[0]
    me = spot_ref[1]
    loads = [copy(b_hbm, b_ref, sems.at[0]), copy(one_hbm, one_ref, sems.at[1])]
    for z in range(half):
        spot = pl.ds(pl.multiple_of((z * 2 + me) * share, share), share)
        loads.append(copy(h_hbm.at[:, :, spot], l_ref.at[0, z], sems.at[2 + 2 * z]))
        loads.append(copy(r_hbm.at[:, 0, :, spot], l_ref.at[1, z], sems.at[3 + 2 * z]))
    for load in loads:
        load.start()
    loads[0].wait()
    loads[1].wait()
    back = [b_ref[x].reshape(frames, 3 * units) for x in (me, 1 - me)]
    for z in range(2 * half):
        if z < half:
            spot = slice(z * share, (z + 1) * share)
            left = [one_ref[x, :, spot] for x in (me, 1 - me)]
        else:
            loads[2 * (z - half) + 2].wait()
            loads[2 * (z - half) + 3].wait()
            left = [l_ref[n, z - half].reshape(frames, share) for n in (0, 1)]
        grad = (dot_tn(left[0], back[0]) + dot_tn(left[1], back[1])) * scale
        grad = grad.astype(bf16)
        for k in range(3):
            o_ref[z, k * share : (k + 1) * share] = grad[:, k * units : (k + 1) * units]


def orthogonal_block(base, tile, own_ref, g_ref, earlier_ref, last_ref, o_ref, x, a, b):
    side, width = g_ref.shape
    share = o_ref.shape[0]
    own = pl.ds(pl.multiple_of(own_ref[0] * share, share), share)
    wide = own_ref[1] > 0

    def either(run):
        pl.when(wide)(functools.partial(run, width))
        pl.when(jnp.logical_not(wide))(functools.partial(run, base))

    def squares(i, total):
        rows = pl.ds(pl.multiple_of(i * 128, 128), 128)
        v = g_ref[rows, :].astype(f32)
        return total + jnp.sum(v * v)

    total = lax.fori_loop(0, side // 128, squares, jnp.zeros((), f32))
    scale = 1.0 / (jnp.sqrt(jnp.full((1, 128), total, f32)) + tiny_value)
    scale = scale[:, :1]

    def shrink(i, carry):
        rows = pl.ds(pl.multiple_of(i * 128, 128), 128)
        x[rows, :] = (g_ref[rows, :].astype(f32) * scale).astype(bf16)
        return carry

    lax.fori_loop(0, side // 128, shrink, 0)

    def lower(out, product):
        for start in range(0, side, 256):
            stop = start + 256
            block = product(slice(start, side), slice(start, stop)).astype(bf16)
            out[start:, start:stop] = block
            if stop < side:
                out[start:stop, stop:] = block[256:].T

    def square(depth):
        lower(a, lambda rows, cols: dot_nt(x[rows, :depth], x[cols, :depth]))

    def mix():
        lower(
            b,
            lambda rows, cols: coeff_cubic * a[rows, cols].astype(f32)
            + coeff_quintic * dot(a[rows, :], a[:, cols]),
        )

    def renew_all(depth):
        for start in range(0, depth, tile):
            cols = slice(start, start + tile)
            x[:, cols] = (
                coeff_linear * x[:, cols].astype(f32) + dot(b[...], x[:, cols])
            ).astype(bf16)

    def sweep(s, carry):
        either(square)
        mix()
        either(renew_all)
        return carry

    lax.fori_loop(0, 4, sweep, 0)
    either(square)
    part = (coeff_cubic * a[own, :].astype(f32) + coeff_quintic * dot(a[own, :], a[...])).astype(bf16)

    def last(j, carry):
        cols = pl.ds(pl.multiple_of(j * tile, tile), tile)
        o_ref[:, cols] = (
            coeff_linear * x[own, cols].astype(f32) + dot(part, x[:, cols])
        ).astype(bf16)
        return carry

    lax.fori_loop(0, width // tile, last, 0)


def turn_block(tile, g_ref, o_ref):
    def block(i, carry):
        spot = pl.ds(pl.multiple_of(i * tile, tile), tile)
        o_ref[:, spot] = g_ref[spot, :].T
        return carry

    lax.fori_loop(0, g_ref.shape[0] // tile, block, 0)


def collect_block(base, spot_ref, *refs):
    *pieces, o_ref, rows = refs
    steps = len(pieces)
    more = pieces[0].shape[0] - base
    for step, piece in enumerate(pieces):
        d = spot_ref[0] ^ step
        o_ref[:, pl.ds(pl.multiple_of(d * base, base), base)] = piece[:base].T
        rows[pl.ds(pl.multiple_of(d * more, more), more), :] = piece[base:]
    o_ref[:, steps * base :] = rows[...].T


def deal_block(base, spot_ref, g_ref, o_ref, rows):
    steps, widest = o_ref.shape[:2]
    more = widest - base
    rows[...] = g_ref[:, steps * base :].T
    for step in range(steps):
        d = spot_ref[0] ^ step
        o_ref[step, :base] = g_ref[:, pl.ds(pl.multiple_of(d * base, base), base)].T
        o_ref[step, base:] = rows[pl.ds(pl.multiple_of(d * more, more), more), :]


def finish_block(owners, spot_ref, *refs):
    pieces, (gru_ref, post_ref, prior_ref), (gru_out, post_out, prior_out), all_ref = (
        refs[:-7],
        refs[-7:-4],
        refs[-4:-1],
        refs[-1],
    )
    for step, piece in enumerate(pieces):
        all_ref[step] = piece[...]

    def renewed(old, m):
        change = all_ref[spot_ref[0] ^ owners[m], : old.shape[0]].astype(f32)
        factor = learn_rate * update_scale * math.sqrt(max(ROWS[m], Z))
        return old * (1.0 - learn_rate * weight_decay) - factor * change

    for k in range(3):
        gru_out[k] = renewed(gru_ref[k], k)
    post_out[...] = renewed(post_ref[...], 3)
    prior_out[...] = renewed(prior_ref[...], 4)


def in_vmem(count):
    return [pl.BlockSpec(memory_space=pltpu.VMEM)] * count


def cost(flops, touched):
    return pl.CostEstimate(flops=int(flops), bytes_accessed=int(touched), transcendentals=0)


def cast_block(g_ref, o_ref):
    o_ref[...] = g_ref[...].astype(bf16)


def run_cast(weights, tile=256):
    parts, rows, units = weights.shape
    skip = Z // tile
    return pl.pallas_call(
        cast_block,
        out_shape=jax.ShapeDtypeStruct((parts, rows - Z, units), bf16),
        grid=(parts, (rows - Z) // tile),
        in_specs=[pl.BlockSpec((1, tile, units), lambda k, i: (k, i + skip, 0))],
        out_specs=pl.BlockSpec((1, tile, units), lambda k, i: (k, i, 0)),
        compiler_params=pltpu.CompilerParams(vmem_limit_bytes=LARGE),
        cost_estimate=cost(1e6, 5 * mib),
        name="cast",
    )(weights)


def run_forward(inputs, weights, seqs):
    parts, packs = inputs.shape[:2]
    units = weights.shape[3]
    chunks = packs // CHUNK
    return pl.pallas_call(
        functools.partial(scan_forward, seqs, CHUNK),
        out_shape=[
            jax.ShapeDtypeStruct((packs, PACK, H), bf16),
            jax.ShapeDtypeStruct((3, packs, PACK, H), f32),
            jax.ShapeDtypeStruct((packs, PACK, H), f32),
            jax.ShapeDtypeStruct((3 * H, H), bf16),
        ],
        in_specs=in_vmem(1) + anywhere(1),
        out_specs=in_vmem(1) + anywhere(3),
        scratch_shapes=[
            pltpu.VMEM((seqs, H), f32),
            pltpu.VMEM((parts, 3, H, units), bf16),
            pltpu.VMEM((3, packs, PACK, H), f32),
            pltpu.VMEM((packs, PACK, H), f32),
            pltpu.VMEM((3 * H, H), bf16),
            pltpu.SemaphoreType.DMA((parts,)),
            pltpu.SemaphoreType.DMA((chunks,)),
            pltpu.SemaphoreType.DMA((chunks,)),
            pltpu.SemaphoreType.DMA,
        ],
        compiler_params=pltpu.CompilerParams(vmem_limit_bytes=LARGE),
        cost_estimate=cost(6e10, 20 * mib),
        name="scan_forward",
    )(inputs, weights)


def run_backward(direct, factors, rest, turned, parts, seqs, copies):
    packs = direct.shape[0]
    units = H // parts
    chunks = packs // CHUNK
    return pl.pallas_call(
        functools.partial(scan_backward, seqs, CHUNK),
        out_shape=jax.ShapeDtypeStruct((copies, parts, packs, PACK, 3 * units), bf16),
        in_specs=in_vmem(1) + anywhere(3),
        out_specs=anywhere(1)[0],
        scratch_shapes=[
            pltpu.VMEM((seqs, 3 * H), f32),
            pltpu.VMEM((seqs, H), f32),
            pltpu.VMEM((3 * H, H), bf16),
            pltpu.VMEM((3, packs, PACK, H), f32),
            pltpu.VMEM((packs, PACK, H), f32),
            pltpu.VMEM((parts, packs, PACK, 3 * units), bf16),
            pltpu.SemaphoreType.DMA,
            pltpu.SemaphoreType.DMA((chunks,)),
            pltpu.SemaphoreType.DMA((chunks,)),
            pltpu.SemaphoreType.DMA((copies * chunks,)),
        ],
        compiler_params=pltpu.CompilerParams(vmem_limit_bytes=LARGE),
        cost_estimate=cost(6e10, 20 * mib),
        name="scan_backward",
    )(direct, factors, rest, turned)


def run_heads(hidden, embed, target, mask, weights):
    rows = hidden.shape[0]
    return pl.pallas_call(
        head_block,
        out_shape=[
            jax.ShapeDtypeStruct((3, rows, Z), bf16),
            jax.ShapeDtypeStruct((rows, H), f32),
            jax.ShapeDtypeStruct((1, 128), f32),
        ],
        in_specs=in_vmem(4) + anywhere(1),
        out_specs=in_vmem(3),
        scratch_shapes=[
            pltpu.VMEM(weights.shape, bf16),
            pltpu.SemaphoreType.DMA((weights.shape[0],)),
        ],
        compiler_params=pltpu.CompilerParams(vmem_limit_bytes=LARGE),
        cost_estimate=cost(1e10, 12 * mib),
        name="heads",
    )(hidden, embed, target, mask, weights)


def in_smem(count):
    return [pl.BlockSpec(memory_space=pltpu.SMEM)] * count


def anywhere(count):
    return [pl.BlockSpec(memory_space=pl.ANY)] * count


def run_head_grads(spot, scale, hidden, others, embed, earlier):
    parts, rows = hidden.shape[:2]
    units = H // parts
    return pl.pallas_call(
        head_grads,
        out_shape=jax.ShapeDtypeStruct((H + E + H, units), bf16),
        in_specs=in_smem(2) + anywhere(4),
        out_specs=in_vmem(1)[0],
        scratch_shapes=[
            pltpu.VMEM(hidden.shape, bf16),
            pltpu.VMEM((parts, 2, rows, units), bf16),
            pltpu.VMEM(embed.shape, bf16),
            pltpu.SemaphoreType.DMA((3,)),
        ],
        compiler_params=pltpu.CompilerParams(vmem_limit_bytes=LARGE),
        cost_estimate=cost(4e9, 12 * mib),
        name="head_grads",
    )(spot, scale, hidden, others, embed, earlier)


def run_gru_grads(spot, scale, onehot, hidden, others, back, earlier, dz_count):
    parts, rows = hidden.shape[:2]
    units = back.shape[3] // 3
    share = (Z + H) // (2 * dz_count)
    return pl.pallas_call(
        gru_grads,
        out_shape=jax.ShapeDtypeStruct((dz_count, 3 * share, units), bf16),
        in_specs=in_smem(2) + anywhere(5),
        out_specs=in_vmem(1)[0],
        scratch_shapes=[
            pltpu.VMEM(onehot.shape, bf16),
            pltpu.VMEM((2, dz_count // 2, parts, rows, share), bf16),
            pltpu.VMEM(back.shape, bf16),
            pltpu.SemaphoreType.DMA((2 + dz_count,)),
        ],
        compiler_params=pltpu.CompilerParams(vmem_limit_bytes=LARGE),
        cost_estimate=cost(4e9, 12 * mib),
        name="gru_grads",
    )(spot, scale, onehot, hidden, others, back, earlier)


def plain_gru_grads(dx_index, scale, onehot, hidden, others, back, dz_count):
    units = back.shape[3] // 3
    share = (Z + H) // (2 * dz_count)
    total = 0.0
    for states, x in ((hidden, dx_index), (others[:, 0], 1 - dx_index)):
        states = states.reshape(-1, dz_count // 2, 2, share)
        states = lax.dynamic_index_in_dim(states, dx_index, 2, keepdims=False)
        ones = lax.dynamic_index_in_dim(onehot, x, 0, keepdims=False)
        left = jnp.concatenate([ones, states.reshape(ones.shape)], axis=1)
        right = lax.dynamic_index_in_dim(back, x, 0, keepdims=False)
        total = total + dot_tn(left, right.reshape(-1, 3 * units))
    grads = (total * scale).astype(bf16).reshape(dz_count, share, 3, units)
    return jnp.swapaxes(grads, 1, 2).reshape(dz_count, 3 * share, units)


def run_orthogonal(base, share, own, matrix, earlier):
    side, width = matrix.shape
    return pl.pallas_call(
        functools.partial(orthogonal_block, base, 512),
        out_shape=jax.ShapeDtypeStruct((share, width), bf16),
        in_specs=in_smem(1) + in_vmem(1) + anywhere(2),
        out_specs=in_vmem(1)[0],
        scratch_shapes=[
            pltpu.VMEM((side, width), bf16),
            pltpu.VMEM((side, side), bf16),
            pltpu.VMEM((side, side), bf16),
        ],
        compiler_params=pltpu.CompilerParams(vmem_limit_bytes=28 * mib),
        cost_estimate=cost(5e10, 6 * mib),
        name="orthogonal",
    )(own, matrix, *earlier)


def run_turn(matrix):
    return pl.pallas_call(
        functools.partial(turn_block, 256),
        out_shape=jax.ShapeDtypeStruct(matrix.shape[::-1], bf16),
        in_specs=in_vmem(1),
        out_specs=in_vmem(1)[0],
        compiler_params=pltpu.CompilerParams(vmem_limit_bytes=6 * mib),
        cost_estimate=cost(1e6, 3 * mib),
        name="turn",
    )(matrix)


def small_kernel(body, out_shape, scratch, specs, arguments, name):
    return pl.pallas_call(
        body,
        out_shape=out_shape,
        in_specs=specs,
        out_specs=jax.tree.map(lambda _: in_vmem(1)[0], out_shape),
        scratch_shapes=scratch,
        compiler_params=pltpu.CompilerParams(vmem_limit_bytes=8 * mib),
        cost_estimate=cost(1e6, 4 * mib),
        name=name,
    )(*arguments)


def run_collect(spot, pieces, base):
    steps = len(pieces)
    widest, units = pieces[0].shape
    return small_kernel(
        functools.partial(collect_block, base),
        jax.ShapeDtypeStruct((units, steps * widest), bf16),
        [pltpu.VMEM((steps * (widest - base), units), bf16)],
        in_smem(1) + in_vmem(steps),
        (spot, *pieces),
        "collect",
    )


def run_deal(spot, result, steps, base):
    units, width = result.shape
    widest = width // steps
    return small_kernel(
        functools.partial(deal_block, base),
        jax.ShapeDtypeStruct((steps, widest, units), bf16),
        [pltpu.VMEM((steps * (widest - base), units), bf16)],
        in_smem(1) + in_vmem(1),
        (spot, result),
        "deal",
    )


def run_finish(owners, spot, pieces, rows):
    return small_kernel(
        functools.partial(finish_block, owners),
        [jax.ShapeDtypeStruct(block.shape, f32) for block in rows],
        [pltpu.VMEM((len(pieces), *pieces[0].shape), bf16)],
        in_smem(1) + in_vmem(len(pieces) + len(rows)),
        (spot, *pieces, *rows),
        "finish",
    )


def on_device(
    embeddings,
    samples,
    seq_lengths,
    gru_weight,
    post_weight,
    prior_weight,
    gru_moment,
    post_moment,
    prior_moment,
):
    dz_count = lax.axis_size("dz")
    dx_count = lax.axis_size("dx")
    tp_count = lax.axis_size("tp")
    dp_count = dz_count * dx_count
    dx_index = lax.axis_index("dx")
    tp_index = lax.axis_index("tp")
    dp_index = lax.axis_index("dz") * dx_count + dx_index
    seq_count = embeddings.shape[0]
    seqs = seq_count // tp_count
    units = gru_weight.shape[2]
    groups = Z // ZC
    rows = seqs * FRAMES
    packs = rows // PACK

    def gather(block):
        return lax.all_gather(block, "tp", axis=0, tiled=False)

    def exchange(block, axis):
        return lax.all_to_all(block, axis, 0, 0, tiled=True)

    def mine(block, axis):
        return lax.dynamic_index_in_dim(block, dx_index, axis, keepdims=False)

    weights = gather(run_cast(gru_weight, tile=512))
    head_low = jnp.concatenate([post_weight.astype(bf16), prior_weight.astype(bf16)], axis=0)

    by_part = jnp.swapaxes(samples.reshape(tp_count, seqs, FRAMES, groups), 1, 2)
    by_part = by_part.reshape(tp_count * rows, groups).astype(bf16)

    def one_hot(chosen):
        count = chosen.shape[-1]
        classes = jnp.arange(count * ZC, dtype=jnp.int32)
        expand = (classes[None, :] // ZC == jnp.arange(count)[:, None]).astype(bf16)
        return (dot(chosen, expand) == (classes % ZC).astype(f32)).astype(bf16)

    onehot = one_hot(by_part)
    input_part = jnp.concatenate(
        [dot(onehot, gru_weight[k, :Z].astype(bf16)).astype(bf16) for k in range(3)], axis=1
    ).reshape(tp_count, packs, PACK, 3 * units)
    input_part = exchange(input_part, "tp")
    embed_rows = jnp.swapaxes(embeddings.reshape(tp_count, seqs, FRAMES, E), 1, 2)
    embed_rows = embed_rows.reshape(tp_count, rows, E)
    pair_samples = lax.all_gather(by_part, "dx", axis=0, tiled=False)
    half = Z // dx_count
    pair_half = mine(
        pair_samples.reshape(dx_count * tp_count * rows, dz_count // 2, dx_count, -1), 2
    )
    pair_onehot = one_hot(pair_half.reshape(dx_count * tp_count * rows, groups // dx_count))
    pair_onehot = pair_onehot.reshape(dx_count, tp_count * rows, half)
    own_embed = lax.dynamic_index_in_dim(embed_rows, tp_index, 0, keepdims=False)
    onehot = onehot.reshape(tp_count, rows, Z)
    own_target = lax.dynamic_index_in_dim(onehot, tp_index, 0, keepdims=False)
    positions = jnp.arange(FRAMES, dtype=jnp.int32)
    own_lengths = lax.dynamic_slice_in_dim(seq_lengths, tp_index * seqs, seqs, 0)
    frame_mask = (positions[:, None] < own_lengths[None, :]).astype(f32)
    mask_lanes = jnp.broadcast_to(frame_mask.reshape(rows, 1), (rows, 128))

    every_mask = (positions[:, None] < seq_lengths[None, :]).astype(f32)
    frame_count = jnp.broadcast_to(jnp.sum(every_mask), (8, 128))
    for axis, bits in (("dx", dx_count), ("dz", dz_count)):
        for bit in range(bits.bit_length() - 1):
            pairs = [(i, i ^ (1 << bit)) for i in range(bits)]
            frame_count = frame_count + lax.ppermute(frame_count, axis, pairs)
    frame_count = frame_count[0, 0]
    scale = (1.0 / frame_count).reshape(1)

    early = (head_low, own_embed, own_target, mask_lanes, embed_rows, pair_onehot, scale)
    weights, input_part, early = lax.optimization_barrier((weights, input_part, early))
    head_low, own_embed, own_target, mask_lanes, embed_rows, pair_onehot, scale = early
    head_full = gather(head_low)
    hidden, factors, rest, turned = run_forward(input_part, weights, seqs)
    hidden = hidden.reshape(rows, H)
    swap = [(i, i ^ 1) for i in range(dx_count)]
    neighbour = lax.ppermute(hidden, "dx", swap)
    all_hidden = gather(hidden)
    backs, direct, loss_lanes = run_heads(hidden, own_embed, own_target, mask_lanes, head_full)
    others = gather(lax.dynamic_update_slice(backs, neighbour[None], (0, 0, 0)))
    back = run_backward(
        direct.reshape(packs, PACK, H), factors, rest, turned, tp_count, seqs, dx_count
    )
    own_back = exchange(back.reshape(dx_count * tp_count, rows, 3 * units), ("dx", "tp"))
    own_back = own_back.reshape(dx_count, tp_count, rows, 3 * units)

    shares = [size // dp_count for size in ROWS]
    all_post = others[:, 2]
    spot = jnp.stack([tp_index, dx_index]).astype(jnp.int32)

    head_grad = run_head_grads(spot, scale, all_hidden, others, embed_rows, back)

    head_grad = jnp.concatenate(
        [
            block.reshape(dz_count, dx_count, -1, units)
            for block in (head_grad[: H + E], head_grad[H + E :])
        ],
        axis=2,
    )

    def share_rows(block):
        return lax.psum_scatter(block, "dz", scatter_dimension=0, tiled=True)[0]

    head_done = share_rows(head_grad)
    if shares[0] % 128 == 0:
        gru_grad = run_gru_grads(
            spot, scale, pair_onehot, all_hidden, others, own_back, head_grad, dz_count
        )
    else:
        gru_grad = plain_gru_grads(
            dx_index, scale, pair_onehot, all_hidden, others, own_back, dz_count
        )
    gru_grad, head_done = lax.optimization_barrier((gru_grad, head_done))
    gru_sum = share_rows(gru_grad).astype(f32)
    received = lax.ppermute(
        lax.dynamic_index_in_dim(head_done, 1 - dx_index, 0, keepdims=False), "dx", swap
    )
    head_sum = mine(head_done, 0).astype(f32) + received.astype(f32)
    loss_sum = jnp.broadcast_to(jnp.sum(loss_lanes), (8, 128))
    for axis, bits in (("tp", tp_count), ("dx", dx_count), ("dz", dz_count)):
        for bit in range(bits.bit_length() - 1):
            pairs = [(i, i ^ (1 << bit)) for i in range(bits)]
            loss_sum = loss_sum + lax.ppermute(loss_sum, axis, pairs)
    loss_sum = loss_sum[0, 0]
    loss_value = loss_sum / frame_count

    embed_part = E // tp_count
    own_rows_e = lax.dynamic_slice_in_dim(head_full, H + tp_index * embed_part, embed_part, 1)
    post_by_seq = jnp.swapaxes(all_post.reshape(tp_count, FRAMES, seqs, Z), 1, 2)
    embed_grad = jnp.einsum(
        "psfk,ek->psfe",
        post_by_seq,
        jnp.concatenate(list(own_rows_e), axis=1),
        preferred_element_type=f32,
    ).reshape(seq_count, FRAMES, embed_part)
    embed_grad = embed_grad * scale[0]

    grads = [gru_sum[k * shares[0] : (k + 1) * shares[0]] for k in range(3)]
    grads += [head_sum[: shares[3]], head_sum[shares[3] :]]

    def own_rows(matrix, axis_dim):
        share = matrix.shape[axis_dim] // dp_count
        return lax.dynamic_slice_in_dim(matrix, dp_index * share, share, axis_dim)

    gru_moments = own_rows(gru_moment, 1)
    moments = [momentum_keep * gru_moments[k] + grads[k] for k in range(3)]
    moments.append(momentum_keep * own_rows(post_moment, 0) + grads[3])
    moments.append(momentum_keep * own_rows(prior_moment, 0) + grads[4])
    ahead = [(grads[m] + momentum_keep * moments[m]).astype(bf16) for m in range(MATS)]

    owners = [m * dp_count // 8 for m in (0, 3, 4, 7, 5)]
    widest = max(shares)
    base = shares[0]
    holds_post = (dp_index == owners[3]).astype(jnp.int32)
    if dp_count == 8:
        kept = jnp.array([owners.index(d) if d in owners else 0 for d in range(dp_count)])
        blocks = jnp.stack(
            [jnp.pad(block, ((0, widest - block.shape[0]), (0, 0))) for block in ahead]
        )
        where = dp_index.astype(jnp.int32).reshape(1)
        pieces = []
        for step in range(dp_count):
            block = lax.dynamic_index_in_dim(blocks, kept[dp_index ^ step], 0, keepdims=False)
            if step > 0:
                block = lax.ppermute(block, ("dz", "dx"), [(d ^ step, d) for d in owners])
            pieces.append(block)
        turned = run_collect(where, pieces, base)
    else:
        slots = [jnp.zeros((widest, units), bf16)] * dp_count
        for m in range(MATS):
            slots[owners[m]] = jnp.pad(ahead[m], ((0, widest - shares[m]), (0, 0)))
        arrived = exchange(jnp.stack(slots), ("dz", "dx"))
        turned = run_turn(
            jnp.concatenate(
                [arrived[:, :base].reshape(-1, units), arrived[:, base:].reshape(-1, units)], axis=0
            )
        )
    wide = gather(turned).reshape(H, dp_count * widest)
    own = jnp.stack([tp_index, holds_post]).astype(jnp.int32)
    result = run_orthogonal(dp_count * base, units, own, wide, (embed_grad, loss_value.reshape(1, 1)))
    old_rows = (own_rows(gru_weight, 1), own_rows(post_weight, 0), own_rows(prior_weight, 0))
    if dp_count == 8:
        dealt = run_deal(where, result, dp_count, base)
        pieces = [dealt[0]]
        for step in range(1, dp_count):
            pairs = [(d, d ^ step) for d in owners]
            pieces.append(lax.ppermute(dealt[step], ("dz", "dx"), pairs))
        new_gru, new_post, new_prior = run_finish(owners, where, pieces, old_rows)
    else:
        result = result.T
        results = exchange(
            jnp.concatenate(
                [
                    result[: dp_count * base].reshape(dp_count, base, units),
                    result[dp_count * base :].reshape(dp_count, widest - base, units),
                ],
                axis=1,
            ),
            ("dz", "dx"),
        )

        def renew(old, m):
            factor = learn_rate * update_scale * math.sqrt(max(ROWS[m], Z))
            change = results[owners[m], : old.shape[0]].astype(f32)
            return old * (1.0 - learn_rate * weight_decay) - factor * change

        new_gru = jnp.stack([renew(old_rows[0][k], k) for k in range(3)])
        new_post = renew(old_rows[1], 3)
        new_prior = renew(old_rows[2], 4)
    return (
        loss_value,
        embed_grad,
        new_gru,
        new_post,
        new_prior,
        jnp.stack(moments[:3]),
        moments[3],
        moments[4],
    )

def solution(mesh):
    dp_count, tp_count = mesh.devices.shape
    mesh = jax.sharding.Mesh(
        mesh.devices.reshape(dp_count // 2, 2, tp_count), ("dz", "dx", "tp")
    )
    dp = ("dz", "dx")
    in_specs = (
        P(dp, None, None),
        P(dp, None, None),
        P(dp),
        P(None, None, "tp"),
        P(None, "tp"),
        P(None, "tp"),
        P(None, None, "tp"),
        P(None, "tp"),
        P(None, "tp"),
    )
    out_specs = (
        P(),
        P(dp, None, "tp"),
        P(None, dp, "tp"),
        P(dp, "tp"),
        P(dp, "tp"),
        P(None, dp, "tp"),
        P(dp, "tp"),
        P(dp, "tp"),
    )
    return jax.shard_map(
        on_device, mesh=mesh, in_specs=in_specs, out_specs=out_specs, check_vma=False
    )
```

```python
import functools
import math

import jax
import jax.numpy as jnp
from jax import lax
from jax.experimental import pallas as pl
from jax.experimental.pallas import tpu as pltpu
from jax.sharding import PartitionSpec as P

H = 1024
ZC = 32
E = 1536
FRAMES = 56
MATS = 5
Z = 1024
ROWS = (Z + H, Z + H, Z + H, H + E, H)
PACK = 8
CHUNK = 4


coeff_linear = 3.4445
coeff_cubic = -4.775
coeff_quintic = 2.0315
momentum_keep = 0.95
learn_rate = 0.2
weight_decay = 0.01
update_scale = 0.2
tiny_value = 1e-07
mib = 1 << 20
LARGE = 56 * mib
f32 = jnp.float32
bf16 = jnp.bfloat16
NT = (((1,), (1,)), ((), ()))
TN = (((0,), (0,)), ((), ()))


def dot(left, right):
    return jnp.dot(left, right, preferred_element_type=f32)


def dot_tn(left, right):
    return lax.dot_general(left, right, TN, preferred_element_type=f32)


def dot_nt(left, right):
    return lax.dot_general(left, right, NT, preferred_element_type=f32)


def copy(source, target, semaphore):
    return pltpu.make_async_copy(source, target, semaphore)


def scan_forward(
    seqs, chunk, spot_ref, x_ref, *refs
):
    parts, packs = x_ref.shape[:2]
    shards = refs[:parts]
    h_ref, k_hbm, u_hbm, t_hbm, state, w, k_ref, u_ref, t, w_sem, k_sem, u_sem, t_sem = refs[parts:]
    units = w.shape[3]
    per_pack = PACK // seqs
    loads = [copy(shards[n], w.at[spot_ref[0] ^ n], w_sem.at[n]) for n in range(parts)]
    for load in loads:
        load.start()
    state[...] = jnp.zeros_like(state)
    for load in loads:
        load.wait()

    def stores(c):
        at = pl.ds(c * chunk, chunk)
        return (
            copy(k_ref.at[:, at], k_hbm.at[:, at], k_sem.at[c]),
            copy(u_ref.at[at], u_hbm.at[at], u_sem.at[c]),
        )

    def pack(i, carry):
        states = []
        for frame in range(per_pack):
            rows = slice(frame * seqs, (frame + 1) * seqs)
            if frame == 0:
                source, live = jnp.maximum(i - 1, 0), jnp.where(i > 0, 1.0, 0.0)
                spot = slice((per_pack - 1) * seqs, per_pack * seqs)
            else:
                source, live = i, None
                spot = slice((frame - 1) * seqs, frame * seqs)
            before = state[...]
            low = before.astype(bf16)
            news = []
            for p in range(parts):
                cols = slice(p * units, (p + 1) * units)
                given = x_ref[p, source].astype(f32)[spot]
                if live is not None:
                    given = given * live
                pre = [
                    given[:, k * units : (k + 1) * units] + dot(low, w[p, k]) for k in range(3)
                ]
                last = before[:, cols]
                r = jax.nn.sigmoid(pre[0])
                c = jnp.tanh(r * pre[1])
                u = jax.nn.sigmoid(pre[2] - 1.0)
                rest = 1.0 - u
                new = u * c + rest * last
                inner = u * (1.0 - c * c)
                state[:, cols] = new
                news.append(new)
                k_ref[0, i, rows, cols] = inner * pre[1] * r * (1.0 - r)
                k_ref[1, i, rows, cols] = inner * r
                k_ref[2, i, rows, cols] = (c - last) * u * rest
                u_ref[i, rows, cols] = rest
            states.append(jnp.concatenate(news, axis=1))
        h_ref[i] = jnp.concatenate(states, axis=0).astype(bf16)

        @pl.when(i % chunk == chunk - 1)
        def _():
            for store in stores(i // chunk):
                store.start()

        return carry

    def pack_and_turn(i, carry):
        t[pl.ds(pl.multiple_of(i * units, units), units), :] = w[i // 3, i % 3].T
        return pack(i, carry)

    lax.fori_loop(0, 3 * parts, pack_and_turn, 0)
    turned = copy(t, t_hbm, t_sem)
    turned.start()
    lax.fori_loop(3 * parts, packs, pack, 0)
    turned.wait()
    for c in range(packs // chunk):
        for store in stores(c):
            store.wait()


def scan_backward(
    seqs, chunk, d_ref, k_hbm, u_hbm, t_hbm, b_hbm, now, kept, w, k_ref, u_ref, b_ref, t_sem, k_sem, u_sem, b_sem
):
    copies, parts, packs = b_hbm.shape[:3]
    units = b_ref.shape[3] // 3
    per_pack = PACK // seqs
    chunks = packs // chunk

    def loads(c):
        at = pl.ds(c * chunk, chunk)
        return (
            copy(k_hbm.at[:, at], k_ref.at[:, at], k_sem.at[c]),
            copy(u_hbm.at[at], u_ref.at[at], u_sem.at[c]),
        )

    def stores(c):
        at = pl.ds(c * chunk, chunk)
        return [
            copy(b_ref.at[:, at], b_hbm.at[n, :, at], b_sem.at[n * chunks + c]) for n in range(copies)
        ]

    turned = copy(t_hbm, w, t_sem)
    turned.start()
    for c in reversed(range(chunks)):
        for load in loads(c):
            load.start()
    now[...] = jnp.zeros_like(now)
    kept[...] = jnp.zeros_like(kept)
    turned.wait()

    def pack(n, carry):
        i = packs - 1 - n

        @pl.when(i % chunk == chunk - 1)
        def _():
            for load in loads(i // chunk):
                load.wait()

        later = [None] * per_pack
        for frame in reversed(range(per_pack)):
            rows = slice(frame * seqs, (frame + 1) * seqs)
            values = now[...]
            later[frame] = values
            dh = d_ref[i, rows] + kept[...] + dot(values.astype(bf16), w[...])
            kept[...] = dh * u_ref[i, rows]
            for p in range(parts):
                cols = slice(p * units, (p + 1) * units)
                for k in range(3):
                    spot = slice((3 * p + k) * units, (3 * p + k + 1) * units)
                    now[:, spot] = dh[:, cols] * k_ref[k, i, rows, cols]
        stacked = jnp.concatenate(later, axis=0).astype(bf16)
        for p in range(parts):
            b_ref[p, i] = stacked[:, p * 3 * units : (p + 1) * 3 * units]

        @pl.when(i % chunk == 0)
        def _():
            for store in stores(i // chunk):
                store.start()

        return carry

    lax.fori_loop(0, packs, pack, 0)
    for c in range(chunks):
        for store in stores(c):
            store.wait()


def butterfly(values, combine, lane):
    step = 1
    while step < ZC:
        up = pltpu.roll(values, step, 1)
        down = pltpu.roll(values, values.shape[1] - step, 1)
        values = combine(values, jnp.where((lane & step) != 0, up, down))
        step *= 2
    return values


def head_block(h_ref, e_ref, t_ref, m_ref, w_hbm, back_ref, d_ref, loss_ref, w_ref, w_sem):
    parts = w_ref.shape[0]
    loads = [copy(w_hbm.at[p], w_ref.at[p], w_sem.at[p]) for p in range(parts)]
    for load in loads:
        load.start()
    units = w_ref.shape[2]
    rows = h_ref.shape[0]
    low = h_ref[...]
    back_ref[0] = low
    mask = m_ref[...]
    lane = lax.broadcasted_iota(jnp.int32, (rows, 128), 1)
    loss = jnp.zeros((rows, 128), f32)
    for p in range(parts):
        loads[p].wait()
        post = dot(low, w_ref[p, :H]) + dot(e_ref[...], w_ref[p, H : H + E])
        prior = dot(low, w_ref[p, H + E :])
        for head, logits in enumerate((prior, post)):
            for piece in range(units // 128):
                l = logits[:, piece * 128 : (piece + 1) * 128]
                cols = slice(p * units + piece * 128, p * units + (piece + 1) * 128)
                target = t_ref[:, cols].astype(f32)
                top = butterfly(l, jnp.maximum, lane)
                e = jnp.exp(l - top)
                total = butterfly(e, jnp.add, lane)
                loss = loss + mask * ((top + jnp.log(total)) * (1.0 / ZC) - target * l)
                back_ref[head + 2, :, cols] = (mask * (e / total - target)).astype(bf16)
    loss_ref[...] = jnp.sum(loss, axis=0, keepdims=True)
    direct = jnp.zeros((rows, H), f32)
    for p in range(parts):
        cols = slice(p * units, (p + 1) * units)
        direct = direct + dot_nt(back_ref[2, :, cols], w_ref[p, H + E :])
        direct = direct + dot_nt(back_ref[3, :, cols], w_ref[p, :H])
    d_ref[...] = direct


def head_grads(spot_ref, scale_ref, r_hbm, e_hbm, earlier_ref, o_ref, h_ref, r_ref, e_ref, sems):
    parts, rows = e_ref.shape[0], e_ref.shape[1]
    units = o_ref.shape[1]
    frames = parts * rows
    scale = scale_ref[0]
    own = pl.ds(pl.multiple_of(spot_ref[0] * units, units), units)
    loads = [
        copy(r_hbm.at[:, pl.ds(2, 2), :, own], r_ref, sems.at[0]),
        copy(r_hbm.at[:, 0], h_ref, sems.at[1]),
        copy(e_hbm, e_ref, sems.at[2]),
    ]
    for load in loads:
        load.start()
    loads[0].wait()
    loads[1].wait()
    post = r_ref[:, 1].reshape(frames, units)
    both = jnp.concatenate([post, r_ref[:, 0].reshape(frames, units)], axis=1)
    for m in range(H // 256):
        spot = slice(m * 256, (m + 1) * 256)
        grad = (dot_tn(h_ref[:, :, spot].reshape(frames, 256), both) * scale).astype(bf16)
        o_ref[m * 256 : (m + 1) * 256] = grad[:, :units]
        o_ref[H + E + m * 256 : H + E + (m + 1) * 256] = grad[:, units:]
    loads[2].wait()
    for m in range(E // 256):
        spot = slice(m * 256, (m + 1) * 256)
        grad = (dot_tn(e_ref[:, :, spot].reshape(frames, 256), post) * scale).astype(bf16)
        o_ref[H + m * 256 : H + (m + 1) * 256] = grad


def gru_grads(
    spot_ref, scale_ref, one_hbm, r_hbm, b_hbm, earlier_ref, o_ref, one_ref, l_ref, b_ref, sems
):
    parts, rows = b_ref.shape[1], b_ref.shape[2]
    units = o_ref.shape[2]
    frames = parts * rows
    share = o_ref.shape[1] // 3
    half = o_ref.shape[0] // 2
    scale = scale_ref[0]
    me = spot_ref[1]
    loads = [copy(b_hbm, b_ref, sems.at[0]), copy(one_hbm, one_ref, sems.at[1])]
    for z in range(half):
        spot = pl.ds(pl.multiple_of((z * 2 + me) * share, share), share)
        loads.append(copy(r_hbm.at[:, 0, :, spot], l_ref.at[0, z], sems.at[2 + 2 * z]))
        loads.append(copy(r_hbm.at[:, 1, :, spot], l_ref.at[1, z], sems.at[3 + 2 * z]))
    for load in loads:
        load.start()
    loads[0].wait()
    loads[1].wait()
    back = [b_ref[x].reshape(frames, 3 * units) for x in (me, 1 - me)]
    for z in range(2 * half):
        if z < half:
            spot = slice(z * share, (z + 1) * share)
            left = [one_ref[x, :, spot] for x in (me, 1 - me)]
        else:
            loads[2 * (z - half) + 2].wait()
            loads[2 * (z - half) + 3].wait()
            left = [l_ref[n, z - half].reshape(frames, share) for n in (0, 1)]
        grad = (dot_tn(left[0], back[0]) + dot_tn(left[1], back[1])) * scale
        grad = grad.astype(bf16)
        for k in range(3):
            o_ref[z, k * share : (k + 1) * share] = grad[:, k * units : (k + 1) * units]


def orthogonal_block(base, tile, own_ref, g_ref, earlier_ref, last_ref, o_ref, x, a, b):
    side, width = g_ref.shape
    share = o_ref.shape[0]
    own = pl.ds(pl.multiple_of(own_ref[0] * share, share), share)
    wide = own_ref[1] > 0

    def either(run):
        pl.when(wide)(functools.partial(run, width))
        pl.when(jnp.logical_not(wide))(functools.partial(run, base))

    def squares(i, total):
        rows = pl.ds(pl.multiple_of(i * 128, 128), 128)
        v = g_ref[rows, :].astype(f32)
        return total + jnp.sum(v * v)

    total = lax.fori_loop(0, side // 128, squares, jnp.zeros((), f32))
    scale = 1.0 / (jnp.sqrt(jnp.full((1, 128), total, f32)) + tiny_value)
    scale = scale[:, :1]

    def shrink(i, carry):
        rows = pl.ds(pl.multiple_of(i * 128, 128), 128)
        x[rows, :] = (g_ref[rows, :].astype(f32) * scale).astype(bf16)
        return carry

    lax.fori_loop(0, side // 128, shrink, 0)

    def lower(out, product):
        for start in range(0, side, 256):
            stop = start + 256
            block = product(slice(start, side), slice(start, stop)).astype(bf16)
            out[start:, start:stop] = block
            if stop < side:
                out[start:stop, stop:] = block[256:].T

    def square(depth):
        lower(a, lambda rows, cols: dot_nt(x[rows, :depth], x[cols, :depth]))

    def mix():
        lower(
            b,
            lambda rows, cols: coeff_cubic * a[rows, cols].astype(f32)
            + coeff_quintic * dot(a[rows, :], a[:, cols]),
        )

    def renew_all(depth):
        for start in range(0, depth, tile):
            cols = slice(start, start + tile)
            x[:, cols] = (
                coeff_linear * x[:, cols].astype(f32) + dot(b[...], x[:, cols])
            ).astype(bf16)

    def sweep(s, carry):
        either(square)
        mix()
        either(renew_all)
        return carry

    lax.fori_loop(0, 4, sweep, 0)
    either(square)
    part = (coeff_cubic * a[own, :].astype(f32) + coeff_quintic * dot(a[own, :], a[...])).astype(bf16)

    def last(j, carry):
        cols = pl.ds(pl.multiple_of(j * tile, tile), tile)
        o_ref[:, cols] = (
            coeff_linear * x[own, cols].astype(f32) + dot(part, x[:, cols])
        ).astype(bf16)
        return carry

    lax.fori_loop(0, width // tile, last, 0)


def turn_block(tile, g_ref, o_ref):
    def block(i, carry):
        spot = pl.ds(pl.multiple_of(i * tile, tile), tile)
        o_ref[:, spot] = g_ref[spot, :].T
        return carry

    lax.fori_loop(0, g_ref.shape[0] // tile, block, 0)


def collect_block(base, spot_ref, *refs):
    *pieces, o_ref, rows = refs
    steps = len(pieces)
    more = pieces[0].shape[0] - base
    for step, piece in enumerate(pieces):
        d = spot_ref[0] ^ step
        o_ref[:, pl.ds(pl.multiple_of(d * base, base), base)] = piece[:base].T
        rows[pl.ds(pl.multiple_of(d * more, more), more), :] = piece[base:]
    o_ref[:, steps * base :] = rows[...].T


def deal_block(base, spot_ref, g_ref, o_ref, rows):
    steps, widest = o_ref.shape[:2]
    more = widest - base
    rows[...] = g_ref[:, steps * base :].T
    for step in range(steps):
        d = spot_ref[0] ^ step
        o_ref[step, :base] = g_ref[:, pl.ds(pl.multiple_of(d * base, base), base)].T
        o_ref[step, base:] = rows[pl.ds(pl.multiple_of(d * more, more), more), :]


def finish_block(owners, spot_ref, *refs):
    pieces, (gru_ref, post_ref, prior_ref), (gru_out, post_out, prior_out), all_ref = (
        refs[:-7],
        refs[-7:-4],
        refs[-4:-1],
        refs[-1],
    )
    for step, piece in enumerate(pieces):
        all_ref[step] = piece[...]

    def renewed(old, m):
        change = all_ref[spot_ref[0] ^ owners[m], : old.shape[0]].astype(f32)
        factor = learn_rate * update_scale * math.sqrt(max(ROWS[m], Z))
        return old * (1.0 - learn_rate * weight_decay) - factor * change

    for k in range(3):
        gru_out[k] = renewed(gru_ref[k], k)
    post_out[...] = renewed(post_ref[...], 3)
    prior_out[...] = renewed(prior_ref[...], 4)


def in_vmem(count):
    return [pl.BlockSpec(memory_space=pltpu.VMEM)] * count


def cost(flops, touched):
    return pl.CostEstimate(flops=int(flops), bytes_accessed=int(touched), transcendentals=0)


def run_forward(spot, inputs, weights, seqs):
    parts, packs = inputs.shape[:2]
    units = weights[0].shape[2]
    chunks = packs // CHUNK
    return pl.pallas_call(
        functools.partial(scan_forward, seqs, CHUNK),
        out_shape=[
            jax.ShapeDtypeStruct((packs, PACK, H), bf16),
            jax.ShapeDtypeStruct((3, packs, PACK, H), f32),
            jax.ShapeDtypeStruct((packs, PACK, H), f32),
            jax.ShapeDtypeStruct((3 * H, H), bf16),
        ],
        in_specs=in_smem(1) + in_vmem(1) + anywhere(parts),
        out_specs=in_vmem(1) + anywhere(3),
        scratch_shapes=[
            pltpu.VMEM((seqs, H), f32),
            pltpu.VMEM((parts, 3, H, units), bf16),
            pltpu.VMEM((3, packs, PACK, H), f32),
            pltpu.VMEM((packs, PACK, H), f32),
            pltpu.VMEM((3 * H, H), bf16),
            pltpu.SemaphoreType.DMA((parts,)),
            pltpu.SemaphoreType.DMA((chunks,)),
            pltpu.SemaphoreType.DMA((chunks,)),
            pltpu.SemaphoreType.DMA,
        ],
        compiler_params=pltpu.CompilerParams(vmem_limit_bytes=LARGE),
        cost_estimate=cost(6e10, 20 * mib),
        name="scan_forward",
    )(spot, inputs, *weights)


def run_backward(direct, factors, rest, turned, parts, seqs, copies):
    packs = direct.shape[0]
    units = H // parts
    chunks = packs // CHUNK
    return pl.pallas_call(
        functools.partial(scan_backward, seqs, CHUNK),
        out_shape=jax.ShapeDtypeStruct((copies, parts, packs, PACK, 3 * units), bf16),
        in_specs=in_vmem(1) + anywhere(3),
        out_specs=anywhere(1)[0],
        scratch_shapes=[
            pltpu.VMEM((seqs, 3 * H), f32),
            pltpu.VMEM((seqs, H), f32),
            pltpu.VMEM((3 * H, H), bf16),
            pltpu.VMEM((3, packs, PACK, H), f32),
            pltpu.VMEM((packs, PACK, H), f32),
            pltpu.VMEM((parts, packs, PACK, 3 * units), bf16),
            pltpu.SemaphoreType.DMA,
            pltpu.SemaphoreType.DMA((chunks,)),
            pltpu.SemaphoreType.DMA((chunks,)),
            pltpu.SemaphoreType.DMA((copies * chunks,)),
        ],
        compiler_params=pltpu.CompilerParams(vmem_limit_bytes=LARGE),
        cost_estimate=cost(6e10, 20 * mib),
        name="scan_backward",
    )(direct, factors, rest, turned)


def run_heads(hidden, embed, target, mask, weights):
    rows = hidden.shape[0]
    return pl.pallas_call(
        head_block,
        out_shape=[
            jax.ShapeDtypeStruct((4, rows, Z), bf16),
            jax.ShapeDtypeStruct((rows, H), f32),
            jax.ShapeDtypeStruct((1, 128), f32),
        ],
        in_specs=in_vmem(4) + anywhere(1),
        out_specs=in_vmem(3),
        scratch_shapes=[
            pltpu.VMEM(weights.shape, bf16),
            pltpu.SemaphoreType.DMA((weights.shape[0],)),
        ],
        compiler_params=pltpu.CompilerParams(vmem_limit_bytes=LARGE),
        cost_estimate=cost(1e10, 12 * mib),
        name="heads",
    )(hidden, embed, target, mask, weights)


def in_smem(count):
    return [pl.BlockSpec(memory_space=pltpu.SMEM)] * count


def anywhere(count):
    return [pl.BlockSpec(memory_space=pl.ANY)] * count


def run_head_grads(spot, scale, everyone, embed, earlier):
    parts, rows = embed.shape[:2]
    units = H // parts
    return pl.pallas_call(
        head_grads,
        out_shape=jax.ShapeDtypeStruct((H + E + H, units), bf16),
        in_specs=in_smem(2) + anywhere(3),
        out_specs=in_vmem(1)[0],
        scratch_shapes=[
            pltpu.VMEM((parts, rows, H), bf16),
            pltpu.VMEM((parts, 2, rows, units), bf16),
            pltpu.VMEM(embed.shape, bf16),
            pltpu.SemaphoreType.DMA((3,)),
        ],
        compiler_params=pltpu.CompilerParams(vmem_limit_bytes=LARGE),
        cost_estimate=cost(4e9, 12 * mib),
        name="head_grads",
    )(spot, scale, everyone, embed, earlier)


def run_gru_grads(spot, scale, onehot, everyone, back, earlier, dz_count):
    parts, rows = back.shape[1:3]
    units = back.shape[3] // 3
    share = (Z + H) // (2 * dz_count)
    return pl.pallas_call(
        gru_grads,
        out_shape=jax.ShapeDtypeStruct((dz_count, 3 * share, units), bf16),
        in_specs=in_smem(2) + anywhere(4),
        out_specs=in_vmem(1)[0],
        scratch_shapes=[
            pltpu.VMEM(onehot.shape, bf16),
            pltpu.VMEM((2, dz_count // 2, parts, rows, share), bf16),
            pltpu.VMEM(back.shape, bf16),
            pltpu.SemaphoreType.DMA((2 + dz_count,)),
        ],
        compiler_params=pltpu.CompilerParams(vmem_limit_bytes=LARGE),
        cost_estimate=cost(4e9, 12 * mib),
        name="gru_grads",
    )(spot, scale, onehot, everyone, back, earlier)


def plain_gru_grads(dx_index, scale, onehot, everyone, back, dz_count):
    units = back.shape[3] // 3
    share = (Z + H) // (2 * dz_count)
    total = 0.0
    for states, x in ((everyone[:, 0], dx_index), (everyone[:, 1], 1 - dx_index)):
        states = states.reshape(-1, dz_count // 2, 2, share)
        states = lax.dynamic_index_in_dim(states, dx_index, 2, keepdims=False)
        ones = lax.dynamic_index_in_dim(onehot, x, 0, keepdims=False)
        left = jnp.concatenate([ones, states.reshape(ones.shape)], axis=1)
        right = lax.dynamic_index_in_dim(back, x, 0, keepdims=False)
        total = total + dot_tn(left, right.reshape(-1, 3 * units))
    grads = (total * scale).astype(bf16).reshape(dz_count, share, 3, units)
    return jnp.swapaxes(grads, 1, 2).reshape(dz_count, 3 * share, units)


def run_orthogonal(base, share, own, matrix, earlier):
    side, width = matrix.shape
    return pl.pallas_call(
        functools.partial(orthogonal_block, base, 512),
        out_shape=jax.ShapeDtypeStruct((share, width), bf16),
        in_specs=in_smem(1) + in_vmem(1) + anywhere(2),
        out_specs=in_vmem(1)[0],
        scratch_shapes=[
            pltpu.VMEM((side, width), bf16),
            pltpu.VMEM((side, side), bf16),
            pltpu.VMEM((side, side), bf16),
        ],
        compiler_params=pltpu.CompilerParams(vmem_limit_bytes=28 * mib),
        cost_estimate=cost(5e10, 6 * mib),
        name="orthogonal",
    )(own, matrix, *earlier)


def run_turn(matrix):
    return pl.pallas_call(
        functools.partial(turn_block, 256),
        out_shape=jax.ShapeDtypeStruct(matrix.shape[::-1], bf16),
        in_specs=in_vmem(1),
        out_specs=in_vmem(1)[0],
        compiler_params=pltpu.CompilerParams(vmem_limit_bytes=6 * mib),
        cost_estimate=cost(1e6, 3 * mib),
        name="turn",
    )(matrix)


def small_kernel(body, out_shape, scratch, specs, arguments, name):
    return pl.pallas_call(
        body,
        out_shape=out_shape,
        in_specs=specs,
        out_specs=jax.tree.map(lambda _: in_vmem(1)[0], out_shape),
        scratch_shapes=scratch,
        compiler_params=pltpu.CompilerParams(vmem_limit_bytes=8 * mib),
        cost_estimate=cost(1e6, 4 * mib),
        name=name,
    )(*arguments)


def run_collect(spot, pieces, base):
    steps = len(pieces)
    widest, units = pieces[0].shape
    return small_kernel(
        functools.partial(collect_block, base),
        jax.ShapeDtypeStruct((units, steps * widest), bf16),
        [pltpu.VMEM((steps * (widest - base), units), bf16)],
        in_smem(1) + in_vmem(steps),
        (spot, *pieces),
        "collect",
    )


def run_deal(spot, result, steps, base):
    units, width = result.shape
    widest = width // steps
    return small_kernel(
        functools.partial(deal_block, base),
        jax.ShapeDtypeStruct((steps, widest, units), bf16),
        [pltpu.VMEM((steps * (widest - base), units), bf16)],
        in_smem(1) + in_vmem(1),
        (spot, result),
        "deal",
    )


def run_finish(owners, spot, pieces, rows):
    return small_kernel(
        functools.partial(finish_block, owners),
        [jax.ShapeDtypeStruct(block.shape, f32) for block in rows],
        [pltpu.VMEM((len(pieces), *pieces[0].shape), bf16)],
        in_smem(1) + in_vmem(len(pieces) + len(rows)),
        (spot, *pieces, *rows),
        "finish",
    )


def on_device(
    embeddings,
    samples,
    seq_lengths,
    gru_weight,
    post_weight,
    prior_weight,
    gru_moment,
    post_moment,
    prior_moment,
):
    dz_count = lax.axis_size("dz")
    dx_count = lax.axis_size("dx")
    tp_count = lax.axis_size("tp")
    dp_count = dz_count * dx_count
    dx_index = lax.axis_index("dx")
    tp_index = lax.axis_index("tp")
    dp_index = lax.axis_index("dz") * dx_count + dx_index
    seq_count = embeddings.shape[0]
    seqs = seq_count // tp_count
    units = gru_weight.shape[2]
    groups = Z // ZC
    rows = seqs * FRAMES
    packs = rows // PACK

    def gather(block):
        return lax.all_gather(block, "tp", axis=0, tiled=False)

    def exchange(block, axis):
        return lax.all_to_all(block, axis, 0, 0, tiled=True)

    def mine(block, axis):
        return lax.dynamic_index_in_dim(block, dx_index, axis, keepdims=False)

    def across(block, bit):
        return lax.ppermute(block, "tp", [(i, i ^ bit) for i in range(tp_count)])

    own_hidden = gru_weight[:, Z:].astype(bf16)
    far = across(own_hidden, 2)
    weights = [own_hidden, across(own_hidden, 1), far, across(far, 1)]
    gru_input = lax.optimization_barrier(gru_weight)
    head_low = jnp.concatenate([post_weight.astype(bf16), prior_weight.astype(bf16)], axis=0)

    by_part = jnp.swapaxes(samples.reshape(tp_count, seqs, FRAMES, groups), 1, 2)
    by_part = by_part.reshape(tp_count * rows, groups).astype(bf16)

    def one_hot(chosen):
        count = chosen.shape[-1]
        classes = jnp.arange(count * ZC, dtype=jnp.int32)
        expand = (classes[None, :] // ZC == jnp.arange(count)[:, None]).astype(bf16)
        return (dot(chosen, expand) == (classes % ZC).astype(f32)).astype(bf16)

    onehot = one_hot(by_part)
    input_part = jnp.concatenate(
        [dot(onehot, gru_input[k, :Z].astype(bf16)).astype(bf16) for k in range(3)], axis=1
    ).reshape(tp_count, packs, PACK, 3 * units)
    input_part = exchange(input_part, "tp")
    embed_rows = jnp.swapaxes(embeddings.reshape(tp_count, seqs, FRAMES, E), 1, 2)
    embed_rows = embed_rows.reshape(tp_count, rows, E)
    pair_samples = lax.all_gather(by_part, "dx", axis=0, tiled=False)
    half = Z // dx_count
    pair_half = mine(
        pair_samples.reshape(dx_count * tp_count * rows, dz_count // 2, dx_count, -1), 2
    )
    pair_onehot = one_hot(pair_half.reshape(dx_count * tp_count * rows, groups // dx_count))
    pair_onehot = pair_onehot.reshape(dx_count, tp_count * rows, half)
    own_embed = lax.dynamic_index_in_dim(embed_rows, tp_index, 0, keepdims=False)
    onehot = onehot.reshape(tp_count, rows, Z)
    own_target = lax.dynamic_index_in_dim(onehot, tp_index, 0, keepdims=False)
    positions = jnp.arange(FRAMES, dtype=jnp.int32)
    own_lengths = lax.dynamic_slice_in_dim(seq_lengths, tp_index * seqs, seqs, 0)
    frame_mask = (positions[:, None] < own_lengths[None, :]).astype(f32)
    mask_lanes = jnp.broadcast_to(frame_mask.reshape(rows, 1), (rows, 128))

    every_mask = (positions[:, None] < seq_lengths[None, :]).astype(f32)
    frame_count = jnp.broadcast_to(jnp.sum(every_mask), (8, 128))
    for axis, bits in (("dx", dx_count), ("dz", dz_count)):
        for bit in range(bits.bit_length() - 1):
            pairs = [(i, i ^ (1 << bit)) for i in range(bits)]
            frame_count = frame_count + lax.ppermute(frame_count, axis, pairs)
    frame_count = frame_count[0, 0]
    scale = (1.0 / frame_count).reshape(1)

    early = (head_low, own_embed, own_target, mask_lanes, embed_rows, pair_onehot, scale)
    weights, input_part, early = lax.optimization_barrier((weights, input_part, early))
    head_low, own_embed, own_target, mask_lanes, embed_rows, pair_onehot, scale = early
    head_full = gather(head_low)
    hidden, factors, rest, turned = run_forward(tp_index.astype(jnp.int32).reshape(1), input_part, weights, seqs)
    hidden = hidden.reshape(rows, H)
    swap = [(i, i ^ 1) for i in range(dx_count)]
    neighbour = lax.ppermute(hidden, "dx", swap)
    backs, direct, loss_lanes = run_heads(hidden, own_embed, own_target, mask_lanes, head_full)
    everyone = gather(lax.dynamic_update_slice(backs, neighbour[None], (1, 0, 0)))
    back = run_backward(
        direct.reshape(packs, PACK, H), factors, rest, turned, tp_count, seqs, dx_count
    )
    own_back = exchange(back.reshape(dx_count * tp_count, rows, 3 * units), ("dx", "tp"))
    own_back = own_back.reshape(dx_count, tp_count, rows, 3 * units)

    shares = [size // dp_count for size in ROWS]
    all_post = everyone[:, 3]
    spot = jnp.stack([tp_index, dx_index]).astype(jnp.int32)

    head_grad = run_head_grads(spot, scale, everyone, embed_rows, back)

    head_grad = jnp.concatenate(
        [
            block.reshape(dz_count, dx_count, -1, units)
            for block in (head_grad[: H + E], head_grad[H + E :])
        ],
        axis=2,
    )

    def share_rows(block):
        return lax.psum_scatter(block, "dz", scatter_dimension=0, tiled=True)[0]

    head_done = share_rows(head_grad)
    if shares[0] % 128 == 0:
        gru_grad = run_gru_grads(
            spot, scale, pair_onehot, everyone, own_back, head_grad, dz_count
        )
    else:
        gru_grad = plain_gru_grads(dx_index, scale, pair_onehot, everyone, own_back, dz_count)
    gru_grad, head_done = lax.optimization_barrier((gru_grad, head_done))
    gru_sum = share_rows(gru_grad).astype(f32)
    received = lax.ppermute(
        lax.dynamic_index_in_dim(head_done, 1 - dx_index, 0, keepdims=False), "dx", swap
    )
    head_sum = mine(head_done, 0).astype(f32) + received.astype(f32)
    loss_sum = jnp.broadcast_to(jnp.sum(loss_lanes), (8, 128))
    for axis, bits in (("tp", tp_count), ("dx", dx_count), ("dz", dz_count)):
        for bit in range(bits.bit_length() - 1):
            pairs = [(i, i ^ (1 << bit)) for i in range(bits)]
            loss_sum = loss_sum + lax.ppermute(loss_sum, axis, pairs)
    loss_sum = loss_sum[0, 0]
    loss_value = loss_sum / frame_count

    embed_part = E // tp_count
    own_rows_e = lax.dynamic_slice_in_dim(head_full, H + tp_index * embed_part, embed_part, 1)
    post_by_seq = jnp.swapaxes(all_post.reshape(tp_count, FRAMES, seqs, Z), 1, 2)
    embed_grad = jnp.einsum(
        "psfk,ek->psfe",
        post_by_seq,
        jnp.concatenate(list(own_rows_e), axis=1),
        preferred_element_type=f32,
    ).reshape(seq_count, FRAMES, embed_part)
    embed_grad = embed_grad * scale[0]

    grads = [gru_sum[k * shares[0] : (k + 1) * shares[0]] for k in range(3)]
    grads += [head_sum[: shares[3]], head_sum[shares[3] :]]

    def own_rows(matrix, axis_dim):
        share = matrix.shape[axis_dim] // dp_count
        return lax.dynamic_slice_in_dim(matrix, dp_index * share, share, axis_dim)

    gru_moments = own_rows(gru_moment, 1)
    moments = [momentum_keep * gru_moments[k] + grads[k] for k in range(3)]
    moments.append(momentum_keep * own_rows(post_moment, 0) + grads[3])
    moments.append(momentum_keep * own_rows(prior_moment, 0) + grads[4])
    ahead = [(grads[m] + momentum_keep * moments[m]).astype(bf16) for m in range(MATS)]

    owners = [m * dp_count // 8 for m in (0, 3, 4, 7, 5)]
    widest = max(shares)
    base = shares[0]
    holds_post = (dp_index == owners[3]).astype(jnp.int32)
    if dp_count == 8:
        kept = jnp.array([owners.index(d) if d in owners else 0 for d in range(dp_count)])
        blocks = jnp.stack(
            [jnp.pad(block, ((0, widest - block.shape[0]), (0, 0))) for block in ahead]
        )
        where = dp_index.astype(jnp.int32).reshape(1)
        pieces = []
        for step in range(dp_count):
            block = lax.dynamic_index_in_dim(blocks, kept[dp_index ^ step], 0, keepdims=False)
            if step > 0:
                block = lax.ppermute(block, ("dz", "dx"), [(d ^ step, d) for d in owners])
            pieces.append(block)
        turned = run_collect(where, pieces, base)
    else:
        slots = [jnp.zeros((widest, units), bf16)] * dp_count
        for m in range(MATS):
            slots[owners[m]] = jnp.pad(ahead[m], ((0, widest - shares[m]), (0, 0)))
        arrived = exchange(jnp.stack(slots), ("dz", "dx"))
        turned = run_turn(
            jnp.concatenate(
                [arrived[:, :base].reshape(-1, units), arrived[:, base:].reshape(-1, units)], axis=0
            )
        )
    wide = gather(turned).reshape(H, dp_count * widest)
    own = jnp.stack([tp_index, holds_post]).astype(jnp.int32)
    result = run_orthogonal(dp_count * base, units, own, wide, (embed_grad, loss_value.reshape(1, 1)))
    old_rows = (own_rows(gru_weight, 1), own_rows(post_weight, 0), own_rows(prior_weight, 0))
    if dp_count == 8:
        dealt = run_deal(where, result, dp_count, base)
        pieces = [dealt[0]]
        for step in range(1, dp_count):
            pairs = [(d, d ^ step) for d in owners]
            pieces.append(lax.ppermute(dealt[step], ("dz", "dx"), pairs))
        new_gru, new_post, new_prior = run_finish(owners, where, pieces, old_rows)
    else:
        result = result.T
        results = exchange(
            jnp.concatenate(
                [
                    result[: dp_count * base].reshape(dp_count, base, units),
                    result[dp_count * base :].reshape(dp_count, widest - base, units),
                ],
                axis=1,
            ),
            ("dz", "dx"),
        )

        def renew(old, m):
            factor = learn_rate * update_scale * math.sqrt(max(ROWS[m], Z))
            change = results[owners[m], : old.shape[0]].astype(f32)
            return old * (1.0 - learn_rate * weight_decay) - factor * change

        new_gru = jnp.stack([renew(old_rows[0][k], k) for k in range(3)])
        new_post = renew(old_rows[1], 3)
        new_prior = renew(old_rows[2], 4)
    return (
        loss_value,
        embed_grad,
        new_gru,
        new_post,
        new_prior,
        jnp.stack(moments[:3]),
        moments[3],
        moments[4],
    )

def solution(mesh):
    dp_count, tp_count = mesh.devices.shape
    mesh = jax.sharding.Mesh(
        mesh.devices.reshape(dp_count // 2, 2, tp_count), ("dz", "dx", "tp")
    )
    dp = ("dz", "dx")
    in_specs = (
        P(dp, None, None),
        P(dp, None, None),
        P(dp),
        P(None, None, "tp"),
        P(None, "tp"),
        P(None, "tp"),
        P(None, None, "tp"),
        P(None, "tp"),
        P(None, "tp"),
    )
    out_specs = (
        P(),
        P(dp, None, "tp"),
        P(None, dp, "tp"),
        P(dp, "tp"),
        P(dp, "tp"),
        P(None, dp, "tp"),
        P(dp, "tp"),
        P(dp, "tp"),
    )
    return jax.shard_map(
        on_device, mesh=mesh, in_specs=in_specs, out_specs=out_specs, check_vma=False
    )
```

```python
import functools
import math

import jax
import jax.numpy as jnp
from jax import lax
from jax.experimental import pallas as pl
from jax.experimental.pallas import tpu as pltpu
from jax.sharding import PartitionSpec as P

H = 1024
ZC = 32
E = 1536
FRAMES = 56
MATS = 5
Z = 1024
ROWS = (Z + H, Z + H, Z + H, H + E, H)
PACK = 8
CHUNK = 4


coeff_linear = 3.4445
coeff_cubic = -4.775
coeff_quintic = 2.0315
momentum_keep = 0.95
learn_rate = 0.2
weight_decay = 0.01
update_scale = 0.2
tiny_value = 1e-07
mib = 1 << 20
LARGE = 56 * mib
f32 = jnp.float32
bf16 = jnp.bfloat16
NT = (((1,), (1,)), ((), ()))
TN = (((0,), (0,)), ((), ()))


def dot(left, right):
    return jnp.dot(left, right, preferred_element_type=f32)


def dot_tn(left, right):
    return lax.dot_general(left, right, TN, preferred_element_type=f32)


def dot_nt(left, right):
    return lax.dot_general(left, right, NT, preferred_element_type=f32)


def copy(source, target, semaphore):
    return pltpu.make_async_copy(source, target, semaphore)


def scan_forward(
    seqs, chunk, spot_ref, x_ref, *refs
):
    parts, packs = x_ref.shape[:2]
    shards = refs[:parts]
    h_ref, k_hbm, u_hbm, t_hbm, state, w, k_ref, u_ref, t, w_sem, k_sem, u_sem, t_sem = refs[parts:]
    units = w.shape[3]
    per_pack = PACK // seqs
    loads = [copy(shards[n], w.at[spot_ref[0] ^ n], w_sem.at[n]) for n in range(parts)]
    for load in loads:
        load.start()
    state[...] = jnp.zeros_like(state)
    for load in loads:
        load.wait()

    def stores(c):
        at = pl.ds(c * chunk, chunk)
        return (
            copy(k_ref.at[:, at], k_hbm.at[:, at], k_sem.at[c]),
            copy(u_ref.at[at], u_hbm.at[at], u_sem.at[c]),
        )

    def pack(i, carry):
        states = []
        for frame in range(per_pack):
            rows = slice(frame * seqs, (frame + 1) * seqs)
            if frame == 0:
                source, live = jnp.maximum(i - 1, 0), jnp.where(i > 0, 1.0, 0.0)
                spot = slice((per_pack - 1) * seqs, per_pack * seqs)
            else:
                source, live = i, None
                spot = slice((frame - 1) * seqs, frame * seqs)
            before = state[...]
            low = before.astype(bf16)
            news = []
            for p in range(parts):
                cols = slice(p * units, (p + 1) * units)
                given = x_ref[p, source].astype(f32)[spot]
                if live is not None:
                    given = given * live
                pre = [
                    given[:, k * units : (k + 1) * units] + dot(low, w[p, k]) for k in range(3)
                ]
                last = before[:, cols]
                r = jax.nn.sigmoid(pre[0])
                c = jnp.tanh(r * pre[1])
                u = jax.nn.sigmoid(pre[2] - 1.0)
                rest = 1.0 - u
                new = u * c + rest * last
                inner = u * (1.0 - c * c)
                state[:, cols] = new
                news.append(new)
                k_ref[0, i, rows, cols] = inner * pre[1] * r * (1.0 - r)
                k_ref[1, i, rows, cols] = inner * r
                k_ref[2, i, rows, cols] = (c - last) * u * rest
                u_ref[i, rows, cols] = rest
            states.append(jnp.concatenate(news, axis=1))
        h_ref[i] = jnp.concatenate(states, axis=0).astype(bf16)

        @pl.when(i % chunk == chunk - 1)
        def _():
            for store in stores(i // chunk):
                store.start()

        return carry

    def pack_and_turn(i, carry):
        t[pl.ds(pl.multiple_of(i * units, units), units), :] = w[i // 3, i % 3].T
        return pack(i, carry)

    lax.fori_loop(0, 3 * parts, pack_and_turn, 0)
    turned = copy(t, t_hbm, t_sem)
    turned.start()
    lax.fori_loop(3 * parts, packs, pack, 0)
    turned.wait()
    for c in range(packs // chunk):
        for store in stores(c):
            store.wait()


def scan_backward(
    seqs, chunk, d_ref, k_hbm, u_hbm, t_hbm, b_hbm, now, kept, w, k_ref, u_ref, b_ref, t_sem, k_sem, u_sem, b_sem
):
    copies, parts, packs = b_hbm.shape[:3]
    units = b_ref.shape[3] // 3
    per_pack = PACK // seqs
    chunks = packs // chunk

    def loads(c):
        at = pl.ds(c * chunk, chunk)
        return (
            copy(k_hbm.at[:, at], k_ref.at[:, at], k_sem.at[c]),
            copy(u_hbm.at[at], u_ref.at[at], u_sem.at[c]),
        )

    def stores(c):
        at = pl.ds(c * chunk, chunk)
        return [
            copy(b_ref.at[:, at], b_hbm.at[n, :, at], b_sem.at[n * chunks + c]) for n in range(copies)
        ]

    turned = copy(t_hbm, w, t_sem)
    turned.start()
    for c in reversed(range(chunks)):
        for load in loads(c):
            load.start()
    now[...] = jnp.zeros_like(now)
    kept[...] = jnp.zeros_like(kept)
    turned.wait()

    def pack(n, carry):
        i = packs - 1 - n

        @pl.when(i % chunk == chunk - 1)
        def _():
            for load in loads(i // chunk):
                load.wait()

        later = [None] * per_pack
        for frame in reversed(range(per_pack)):
            rows = slice(frame * seqs, (frame + 1) * seqs)
            values = now[...]
            later[frame] = values
            dh = d_ref[i, rows] + kept[...] + dot(values.astype(bf16), w[...])
            kept[...] = dh * u_ref[i, rows]
            for p in range(parts):
                cols = slice(p * units, (p + 1) * units)
                for k in range(3):
                    spot = slice((3 * p + k) * units, (3 * p + k + 1) * units)
                    now[:, spot] = dh[:, cols] * k_ref[k, i, rows, cols]
        stacked = jnp.concatenate(later, axis=0).astype(bf16)
        for p in range(parts):
            b_ref[p, i] = stacked[:, p * 3 * units : (p + 1) * 3 * units]

        @pl.when(i % chunk == 0)
        def _():
            for store in stores(i // chunk):
                store.start()

        return carry

    lax.fori_loop(0, packs, pack, 0)
    for c in range(chunks):
        for store in stores(c):
            store.wait()


def butterfly(values, combine, lane):
    step = 1
    while step < ZC:
        up = pltpu.roll(values, step, 1)
        down = pltpu.roll(values, values.shape[1] - step, 1)
        values = combine(values, jnp.where((lane & step) != 0, up, down))
        step *= 2
    return values


def head_block(h_ref, e_ref, t_ref, m_ref, w_hbm, back_ref, d_ref, loss_ref, w_ref, w_sem):
    parts = w_ref.shape[0]
    loads = [copy(w_hbm.at[p], w_ref.at[p], w_sem.at[p]) for p in range(parts)]
    for load in loads:
        load.start()
    units = w_ref.shape[2]
    rows = h_ref.shape[0]
    low = h_ref[...]
    back_ref[0] = low
    mask = m_ref[...]
    lane = lax.broadcasted_iota(jnp.int32, (rows, 128), 1)
    loss = jnp.zeros((rows, 128), f32)
    for p in range(parts):
        loads[p].wait()
        post = dot(low, w_ref[p, :H]) + dot(e_ref[...], w_ref[p, H : H + E])
        prior = dot(low, w_ref[p, H + E :])
        for head, logits in enumerate((prior, post)):
            for piece in range(units // 128):
                l = logits[:, piece * 128 : (piece + 1) * 128]
                cols = slice(p * units + piece * 128, p * units + (piece + 1) * 128)
                target = t_ref[:, cols].astype(f32)
                top = butterfly(l, jnp.maximum, lane)
                e = jnp.exp(l - top)
                total = butterfly(e, jnp.add, lane)
                loss = loss + mask * ((top + jnp.log(total)) * (1.0 / ZC) - target * l)
                back_ref[head + 2, :, cols] = (mask * (e / total - target)).astype(bf16)
    loss_ref[...] = jnp.sum(loss, axis=0, keepdims=True)
    direct = jnp.zeros((rows, H), f32)
    for p in range(parts):
        cols = slice(p * units, (p + 1) * units)
        direct = direct + dot_nt(back_ref[2, :, cols], w_ref[p, H + E :])
        direct = direct + dot_nt(back_ref[3, :, cols], w_ref[p, :H])
    d_ref[...] = direct


def head_grads(spot_ref, scale_ref, r_hbm, e_hbm, earlier_ref, o_ref, h_ref, r_ref, e_ref, sems):
    parts, rows = e_ref.shape[0], e_ref.shape[1]
    units = o_ref.shape[1]
    frames = parts * rows
    scale = scale_ref[0]
    own = pl.ds(pl.multiple_of(spot_ref[0] * units, units), units)
    loads = [
        copy(r_hbm.at[:, pl.ds(2, 2), :, own], r_ref, sems.at[0]),
        copy(r_hbm.at[:, 0], h_ref, sems.at[1]),
        copy(e_hbm, e_ref, sems.at[2]),
    ]
    for load in loads:
        load.start()
    loads[0].wait()
    loads[1].wait()
    post = r_ref[:, 1].reshape(frames, units)
    both = jnp.concatenate([post, r_ref[:, 0].reshape(frames, units)], axis=1)
    for m in range(H // 256):
        spot = slice(m * 256, (m + 1) * 256)
        grad = (dot_tn(h_ref[:, :, spot].reshape(frames, 256), both) * scale).astype(bf16)
        o_ref[m * 256 : (m + 1) * 256] = grad[:, :units]
        o_ref[H + E + m * 256 : H + E + (m + 1) * 256] = grad[:, units:]
    loads[2].wait()
    for m in range(E // 256):
        spot = slice(m * 256, (m + 1) * 256)
        grad = (dot_tn(e_ref[:, :, spot].reshape(frames, 256), post) * scale).astype(bf16)
        o_ref[H + m * 256 : H + (m + 1) * 256] = grad


def gru_grads(
    spot_ref, scale_ref, one_hbm, r_hbm, b_hbm, earlier_ref, o_ref, one_ref, l_ref, b_ref, sems
):
    parts, rows = b_ref.shape[1], b_ref.shape[2]
    units = o_ref.shape[2]
    frames = parts * rows
    share = o_ref.shape[1] // 3
    half = o_ref.shape[0] // 2
    scale = scale_ref[0]
    me = spot_ref[1]
    loads = [copy(b_hbm, b_ref, sems.at[0]), copy(one_hbm, one_ref, sems.at[1])]
    for z in range(half):
        spot = pl.ds(pl.multiple_of((z * 2 + me) * share, share), share)
        loads.append(copy(r_hbm.at[:, 0, :, spot], l_ref.at[0, z], sems.at[2 + 2 * z]))
        loads.append(copy(r_hbm.at[:, 1, :, spot], l_ref.at[1, z], sems.at[3 + 2 * z]))
    for load in loads:
        load.start()
    loads[0].wait()
    loads[1].wait()
    back = [b_ref[x].reshape(frames, 3 * units) for x in (me, 1 - me)]
    for z in range(2 * half):
        if z < half:
            spot = slice(z * share, (z + 1) * share)
            left = [one_ref[x, :, spot] for x in (me, 1 - me)]
        else:
            loads[2 * (z - half) + 2].wait()
            loads[2 * (z - half) + 3].wait()
            left = [l_ref[n, z - half].reshape(frames, share) for n in (0, 1)]
        grad = (dot_tn(left[0], back[0]) + dot_tn(left[1], back[1])) * scale
        grad = grad.astype(bf16)
        for k in range(3):
            o_ref[z, k * share : (k + 1) * share] = grad[:, k * units : (k + 1) * units]


def orthogonal_block(base, tile, own_ref, g_ref, *refs):
    o_ref, x, a, b = refs[-4:]
    side, width = g_ref.shape
    share = o_ref.shape[0]
    own = pl.ds(pl.multiple_of(own_ref[0] * share, share), share)
    wide = own_ref[1] > 0

    def either(run):
        pl.when(wide)(functools.partial(run, width))
        pl.when(jnp.logical_not(wide))(functools.partial(run, base))

    def squares(i, total):
        rows = pl.ds(pl.multiple_of(i * 128, 128), 128)
        v = g_ref[rows, :].astype(f32)
        return total + jnp.sum(v * v)

    total = lax.fori_loop(0, side // 128, squares, jnp.zeros((), f32))
    scale = 1.0 / (jnp.sqrt(jnp.full((1, 128), total, f32)) + tiny_value)
    scale = scale[:, :1]

    def shrink(i, carry):
        rows = pl.ds(pl.multiple_of(i * 128, 128), 128)
        x[rows, :] = (g_ref[rows, :].astype(f32) * scale).astype(bf16)
        return carry

    lax.fori_loop(0, side // 128, shrink, 0)

    def lower(out, product):
        for start in range(0, side, 256):
            stop = start + 256
            block = product(slice(start, side), slice(start, stop)).astype(bf16)
            out[start:, start:stop] = block
            if stop < side:
                out[start:stop, stop:] = block[256:].T

    def square(depth):
        lower(a, lambda rows, cols: dot_nt(x[rows, :depth], x[cols, :depth]))

    def mix():
        lower(
            b,
            lambda rows, cols: coeff_cubic * a[rows, cols].astype(f32)
            + coeff_quintic * dot(a[rows, :], a[:, cols]),
        )

    def renew_all(depth):
        for start in range(0, depth, tile):
            cols = slice(start, start + tile)
            x[:, cols] = (
                coeff_linear * x[:, cols].astype(f32) + dot(b[...], x[:, cols])
            ).astype(bf16)

    def sweep(s, carry):
        either(square)
        mix()
        either(renew_all)
        return carry

    lax.fori_loop(0, 4, sweep, 0)
    either(square)
    part = (coeff_cubic * a[own, :].astype(f32) + coeff_quintic * dot(a[own, :], a[...])).astype(bf16)

    def last(j, carry):
        cols = pl.ds(pl.multiple_of(j * tile, tile), tile)
        o_ref[:, cols] = (
            coeff_linear * x[own, cols].astype(f32) + dot(part, x[:, cols])
        ).astype(bf16)
        return carry

    lax.fori_loop(0, width // tile, last, 0)


def turn_block(tile, g_ref, o_ref):
    def block(i, carry):
        spot = pl.ds(pl.multiple_of(i * tile, tile), tile)
        o_ref[:, spot] = g_ref[spot, :].T
        return carry

    lax.fori_loop(0, g_ref.shape[0] // tile, block, 0)


def collect_block(base, spot_ref, *refs):
    *pieces, o_ref, rows = refs
    steps = len(pieces)
    more = pieces[0].shape[0] - base
    for step, piece in enumerate(pieces):
        d = spot_ref[0] ^ step
        o_ref[:, pl.ds(pl.multiple_of(d * base, base), base)] = piece[:base].T
        rows[pl.ds(pl.multiple_of(d * more, more), more), :] = piece[base:]
    o_ref[:, steps * base :] = rows[...].T


def deal_block(base, spot_ref, g_ref, o_ref, rows):
    steps, widest = o_ref.shape[:2]
    more = widest - base
    rows[...] = g_ref[:, steps * base :].T
    for step in range(steps):
        d = spot_ref[0] ^ step
        o_ref[step, :base] = g_ref[:, pl.ds(pl.multiple_of(d * base, base), base)].T
        o_ref[step, base:] = rows[pl.ds(pl.multiple_of(d * more, more), more), :]


def finish_block(owners, spot_ref, *refs):
    pieces, (gru_ref, post_ref, prior_ref), (gru_out, post_out, prior_out), all_ref = (
        refs[:-7],
        refs[-7:-4],
        refs[-4:-1],
        refs[-1],
    )
    for step, piece in enumerate(pieces):
        all_ref[step] = piece[...]

    def renewed(old, m):
        change = all_ref[spot_ref[0] ^ owners[m], : old.shape[0]].astype(f32)
        factor = learn_rate * update_scale * math.sqrt(max(ROWS[m], Z))
        return old * (1.0 - learn_rate * weight_decay) - factor * change

    for k in range(3):
        gru_out[k] = renewed(gru_ref[k], k)
    post_out[...] = renewed(post_ref[...], 3)
    prior_out[...] = renewed(prior_ref[...], 4)


def in_vmem(count):
    return [pl.BlockSpec(memory_space=pltpu.VMEM)] * count


def cost(flops, touched):
    return pl.CostEstimate(flops=int(flops), bytes_accessed=int(touched), transcendentals=0)


def run_forward(spot, inputs, weights, seqs):
    parts, packs = inputs.shape[:2]
    units = weights[0].shape[2]
    chunks = packs // CHUNK
    return pl.pallas_call(
        functools.partial(scan_forward, seqs, CHUNK),
        out_shape=[
            jax.ShapeDtypeStruct((packs, PACK, H), bf16),
            jax.ShapeDtypeStruct((3, packs, PACK, H), f32),
            jax.ShapeDtypeStruct((packs, PACK, H), f32),
            jax.ShapeDtypeStruct((3 * H, H), bf16),
        ],
        in_specs=in_smem(1) + in_vmem(1) + anywhere(parts),
        out_specs=in_vmem(1) + anywhere(3),
        scratch_shapes=[
            pltpu.VMEM((seqs, H), f32),
            pltpu.VMEM((parts, 3, H, units), bf16),
            pltpu.VMEM((3, packs, PACK, H), f32),
            pltpu.VMEM((packs, PACK, H), f32),
            pltpu.VMEM((3 * H, H), bf16),
            pltpu.SemaphoreType.DMA((parts,)),
            pltpu.SemaphoreType.DMA((chunks,)),
            pltpu.SemaphoreType.DMA((chunks,)),
            pltpu.SemaphoreType.DMA,
        ],
        compiler_params=pltpu.CompilerParams(vmem_limit_bytes=LARGE),
        cost_estimate=cost(6e10, 20 * mib),
        name="scan_forward",
    )(spot, inputs, *weights)


def run_backward(direct, factors, rest, turned, parts, seqs, copies):
    packs = direct.shape[0]
    units = H // parts
    chunks = packs // CHUNK
    return pl.pallas_call(
        functools.partial(scan_backward, seqs, CHUNK),
        out_shape=jax.ShapeDtypeStruct((copies, parts, packs, PACK, 3 * units), bf16),
        in_specs=in_vmem(1) + anywhere(3),
        out_specs=anywhere(1)[0],
        scratch_shapes=[
            pltpu.VMEM((seqs, 3 * H), f32),
            pltpu.VMEM((seqs, H), f32),
            pltpu.VMEM((3 * H, H), bf16),
            pltpu.VMEM((3, packs, PACK, H), f32),
            pltpu.VMEM((packs, PACK, H), f32),
            pltpu.VMEM((parts, packs, PACK, 3 * units), bf16),
            pltpu.SemaphoreType.DMA,
            pltpu.SemaphoreType.DMA((chunks,)),
            pltpu.SemaphoreType.DMA((chunks,)),
            pltpu.SemaphoreType.DMA((copies * chunks,)),
        ],
        compiler_params=pltpu.CompilerParams(vmem_limit_bytes=LARGE),
        cost_estimate=cost(6e10, 20 * mib),
        name="scan_backward",
    )(direct, factors, rest, turned)


def run_heads(hidden, embed, target, mask, weights):
    rows = hidden.shape[0]
    return pl.pallas_call(
        head_block,
        out_shape=[
            jax.ShapeDtypeStruct((4, rows, Z), bf16),
            jax.ShapeDtypeStruct((rows, H), f32),
            jax.ShapeDtypeStruct((1, 128), f32),
        ],
        in_specs=in_vmem(4) + anywhere(1),
        out_specs=in_vmem(3),
        scratch_shapes=[
            pltpu.VMEM(weights.shape, bf16),
            pltpu.SemaphoreType.DMA((weights.shape[0],)),
        ],
        compiler_params=pltpu.CompilerParams(vmem_limit_bytes=LARGE),
        cost_estimate=cost(1e10, 12 * mib),
        name="heads",
    )(hidden, embed, target, mask, weights)


def in_smem(count):
    return [pl.BlockSpec(memory_space=pltpu.SMEM)] * count


def anywhere(count):
    return [pl.BlockSpec(memory_space=pl.ANY)] * count


def run_head_grads(spot, scale, everyone, embed, earlier):
    parts, rows = embed.shape[:2]
    units = H // parts
    return pl.pallas_call(
        head_grads,
        out_shape=jax.ShapeDtypeStruct((H + E + H, units), bf16),
        in_specs=in_smem(2) + anywhere(3),
        out_specs=in_vmem(1)[0],
        scratch_shapes=[
            pltpu.VMEM((parts, rows, H), bf16),
            pltpu.VMEM((parts, 2, rows, units), bf16),
            pltpu.VMEM(embed.shape, bf16),
            pltpu.SemaphoreType.DMA((3,)),
        ],
        compiler_params=pltpu.CompilerParams(vmem_limit_bytes=LARGE),
        cost_estimate=cost(4e9, 12 * mib),
        name="head_grads",
    )(spot, scale, everyone, embed, earlier)


def run_gru_grads(spot, scale, onehot, everyone, back, earlier, dz_count):
    parts, rows = back.shape[1:3]
    units = back.shape[3] // 3
    share = (Z + H) // (2 * dz_count)
    return pl.pallas_call(
        gru_grads,
        out_shape=jax.ShapeDtypeStruct((dz_count, 3 * share, units), bf16),
        in_specs=in_smem(2) + anywhere(4),
        out_specs=in_vmem(1)[0],
        scratch_shapes=[
            pltpu.VMEM(onehot.shape, bf16),
            pltpu.VMEM((2, dz_count // 2, parts, rows, share), bf16),
            pltpu.VMEM(back.shape, bf16),
            pltpu.SemaphoreType.DMA((2 + dz_count,)),
        ],
        compiler_params=pltpu.CompilerParams(vmem_limit_bytes=LARGE),
        cost_estimate=cost(4e9, 12 * mib),
        name="gru_grads",
    )(spot, scale, onehot, everyone, back, earlier)


def plain_gru_grads(dx_index, scale, onehot, everyone, back, dz_count):
    units = back.shape[3] // 3
    share = (Z + H) // (2 * dz_count)
    total = 0.0
    for states, x in ((everyone[:, 0], dx_index), (everyone[:, 1], 1 - dx_index)):
        states = states.reshape(-1, dz_count // 2, 2, share)
        states = lax.dynamic_index_in_dim(states, dx_index, 2, keepdims=False)
        ones = lax.dynamic_index_in_dim(onehot, x, 0, keepdims=False)
        left = jnp.concatenate([ones, states.reshape(ones.shape)], axis=1)
        right = lax.dynamic_index_in_dim(back, x, 0, keepdims=False)
        total = total + dot_tn(left, right.reshape(-1, 3 * units))
    grads = (total * scale).astype(bf16).reshape(dz_count, share, 3, units)
    return jnp.swapaxes(grads, 1, 2).reshape(dz_count, 3 * share, units)


def run_orthogonal(base, share, own, matrix, earlier):
    side, width = matrix.shape
    return pl.pallas_call(
        functools.partial(orthogonal_block, base, 512),
        out_shape=jax.ShapeDtypeStruct((share, width), bf16),
        in_specs=in_smem(1) + in_vmem(1) + anywhere(len(earlier)),
        out_specs=in_vmem(1)[0],
        scratch_shapes=[
            pltpu.VMEM((side, width), bf16),
            pltpu.VMEM((side, side), bf16),
            pltpu.VMEM((side, side), bf16),
        ],
        compiler_params=pltpu.CompilerParams(vmem_limit_bytes=28 * mib),
        cost_estimate=cost(5e10, 6 * mib),
        name="orthogonal",
    )(own, matrix, *earlier)


def run_turn(matrix):
    return pl.pallas_call(
        functools.partial(turn_block, 256),
        out_shape=jax.ShapeDtypeStruct(matrix.shape[::-1], bf16),
        in_specs=in_vmem(1),
        out_specs=in_vmem(1)[0],
        compiler_params=pltpu.CompilerParams(vmem_limit_bytes=6 * mib),
        cost_estimate=cost(1e6, 3 * mib),
        name="turn",
    )(matrix)


def small_kernel(body, out_shape, scratch, specs, arguments, name):
    return pl.pallas_call(
        body,
        out_shape=out_shape,
        in_specs=specs,
        out_specs=jax.tree.map(lambda _: in_vmem(1)[0], out_shape),
        scratch_shapes=scratch,
        compiler_params=pltpu.CompilerParams(vmem_limit_bytes=8 * mib),
        cost_estimate=cost(1e6, 4 * mib),
        name=name,
    )(*arguments)


def run_collect(spot, pieces, base):
    steps = len(pieces)
    widest, units = pieces[0].shape
    return small_kernel(
        functools.partial(collect_block, base),
        jax.ShapeDtypeStruct((units, steps * widest), bf16),
        [pltpu.VMEM((steps * (widest - base), units), bf16)],
        in_smem(1) + in_vmem(steps),
        (spot, *pieces),
        "collect",
    )


def run_deal(spot, result, steps, base):
    units, width = result.shape
    widest = width // steps
    return small_kernel(
        functools.partial(deal_block, base),
        jax.ShapeDtypeStruct((steps, widest, units), bf16),
        [pltpu.VMEM((steps * (widest - base), units), bf16)],
        in_smem(1) + in_vmem(1),
        (spot, result),
        "deal",
    )


def run_finish(owners, spot, pieces, rows):
    return small_kernel(
        functools.partial(finish_block, owners),
        [jax.ShapeDtypeStruct(block.shape, f32) for block in rows],
        [pltpu.VMEM((len(pieces), *pieces[0].shape), bf16)],
        in_smem(1) + in_vmem(len(pieces) + len(rows)),
        (spot, *pieces, *rows),
        "finish",
    )


def on_device(
    embeddings,
    samples,
    seq_lengths,
    gru_weight,
    post_weight,
    prior_weight,
    gru_moment,
    post_moment,
    prior_moment,
):
    dz_count = lax.axis_size("dz")
    dx_count = lax.axis_size("dx")
    tp_count = lax.axis_size("tp")
    dp_count = dz_count * dx_count
    dx_index = lax.axis_index("dx")
    tp_index = lax.axis_index("tp")
    dp_index = lax.axis_index("dz") * dx_count + dx_index
    seq_count = embeddings.shape[0]
    seqs = seq_count // tp_count
    units = gru_weight.shape[2]
    groups = Z // ZC
    rows = seqs * FRAMES
    packs = rows // PACK

    def gather(block):
        return lax.all_gather(block, "tp", axis=0, tiled=False)

    def exchange(block, axis):
        return lax.all_to_all(block, axis, 0, 0, tiled=True)

    def mine(block, axis):
        return lax.dynamic_index_in_dim(block, dx_index, axis, keepdims=False)

    def across(block, bit):
        return lax.ppermute(block, "tp", [(i, i ^ bit) for i in range(tp_count)])

    own_hidden = gru_weight[:, Z:].astype(bf16)
    far = across(own_hidden, 2)
    near = across(own_hidden, 1)
    gru_input = lax.optimization_barrier(gru_weight)
    head_low = jnp.concatenate([post_weight.astype(bf16), prior_weight.astype(bf16)], axis=0)

    by_part = jnp.swapaxes(samples.reshape(tp_count, seqs, FRAMES, groups), 1, 2)
    by_part = by_part.reshape(tp_count * rows, groups).astype(bf16)

    def one_hot(chosen):
        count = chosen.shape[-1]
        classes = jnp.arange(count * ZC, dtype=jnp.int32)
        expand = (classes[None, :] // ZC == jnp.arange(count)[:, None]).astype(bf16)
        return (dot(chosen, expand) == (classes % ZC).astype(f32)).astype(bf16)

    onehot = one_hot(by_part)
    input_part = jnp.concatenate(
        [dot(onehot, gru_input[k, :Z].astype(bf16)).astype(bf16) for k in range(3)], axis=1
    ).reshape(tp_count, packs, PACK, 3 * units)
    input_part = exchange(input_part, "tp")
    embed_rows = jnp.swapaxes(embeddings.reshape(tp_count, seqs, FRAMES, E), 1, 2)
    embed_rows = embed_rows.reshape(tp_count, rows, E)
    pair_samples = lax.all_gather(by_part, "dx", axis=0, tiled=False)
    half = Z // dx_count
    pair_half = mine(
        pair_samples.reshape(dx_count * tp_count * rows, dz_count // 2, dx_count, -1), 2
    )
    pair_onehot = one_hot(pair_half.reshape(dx_count * tp_count * rows, groups // dx_count))
    pair_onehot = pair_onehot.reshape(dx_count, tp_count * rows, half)
    own_embed = lax.dynamic_index_in_dim(embed_rows, tp_index, 0, keepdims=False)
    onehot = onehot.reshape(tp_count, rows, Z)
    own_target = lax.dynamic_index_in_dim(onehot, tp_index, 0, keepdims=False)
    positions = jnp.arange(FRAMES, dtype=jnp.int32)
    own_lengths = lax.dynamic_slice_in_dim(seq_lengths, tp_index * seqs, seqs, 0)
    frame_mask = (positions[:, None] < own_lengths[None, :]).astype(f32)
    mask_lanes = jnp.broadcast_to(frame_mask.reshape(rows, 1), (rows, 128))

    prepared = (head_low, own_embed, own_target, embed_rows)
    far, prepared = lax.optimization_barrier((far, prepared))
    head_low, own_embed, own_target, embed_rows = prepared
    weights = [own_hidden, near, far, across(far, 1)]
    every_mask = (positions[:, None] < seq_lengths[None, :]).astype(f32)
    frame_count = jnp.broadcast_to(jnp.sum(every_mask), (8, 128))
    for axis, bits in (("dx", dx_count), ("dz", dz_count)):
        for bit in range(bits.bit_length() - 1):
            pairs = [(i, i ^ (1 << bit)) for i in range(bits)]
            frame_count = frame_count + lax.ppermute(frame_count, axis, pairs)
    frame_count = frame_count[0, 0]
    scale = (1.0 / frame_count).reshape(1)

    early = (head_low, own_embed, own_target, mask_lanes, embed_rows, pair_onehot, scale)
    weights, input_part, early = lax.optimization_barrier((weights, input_part, early))
    head_low, own_embed, own_target, mask_lanes, embed_rows, pair_onehot, scale = early
    head_full = gather(head_low)
    hidden, factors, rest, turned = run_forward(tp_index.astype(jnp.int32).reshape(1), input_part, weights, seqs)
    hidden = hidden.reshape(rows, H)
    swap = [(i, i ^ 1) for i in range(dx_count)]
    neighbour = lax.ppermute(hidden, "dx", swap)
    backs, direct, loss_lanes = run_heads(hidden, own_embed, own_target, mask_lanes, head_full)
    everyone = gather(lax.dynamic_update_slice(backs, neighbour[None], (1, 0, 0)))
    back = run_backward(
        direct.reshape(packs, PACK, H), factors, rest, turned, tp_count, seqs, dx_count
    )
    own_back = exchange(back.reshape(dx_count * tp_count, rows, 3 * units), ("dx", "tp"))
    own_back = own_back.reshape(dx_count, tp_count, rows, 3 * units)

    shares = [size // dp_count for size in ROWS]
    all_post = everyone[:, 3]
    spot = jnp.stack([tp_index, dx_index]).astype(jnp.int32)

    head_grad = run_head_grads(spot, scale, everyone, embed_rows, back)

    head_grad = jnp.concatenate(
        [
            block.reshape(dz_count, dx_count, -1, units)
            for block in (head_grad[: H + E], head_grad[H + E :])
        ],
        axis=2,
    )

    def share_rows(block):
        return lax.psum_scatter(block, "dz", scatter_dimension=0, tiled=True)[0]

    head_done = share_rows(head_grad)
    if shares[0] % 128 == 0:
        gru_grad = run_gru_grads(
            spot, scale, pair_onehot, everyone, own_back, head_grad, dz_count
        )
    else:
        gru_grad = plain_gru_grads(dx_index, scale, pair_onehot, everyone, own_back, dz_count)
    gru_grad, head_done = lax.optimization_barrier((gru_grad, head_done))
    gru_sum = share_rows(gru_grad).astype(f32)
    received = lax.ppermute(
        lax.dynamic_index_in_dim(head_done, 1 - dx_index, 0, keepdims=False), "dx", swap
    )
    head_sum = mine(head_done, 0).astype(f32) + received.astype(f32)
    loss_sum = jnp.broadcast_to(jnp.sum(loss_lanes), (8, 128))
    for axis, bits in (("tp", tp_count), ("dx", dx_count), ("dz", dz_count)):
        for bit in range(bits.bit_length() - 1):
            pairs = [(i, i ^ (1 << bit)) for i in range(bits)]
            loss_sum = loss_sum + lax.ppermute(loss_sum, axis, pairs)
    loss_sum = loss_sum[0, 0]
    loss_value = loss_sum / frame_count

    embed_part = E // tp_count
    own_rows_e = lax.dynamic_slice_in_dim(head_full, H + tp_index * embed_part, embed_part, 1)
    post_by_seq = jnp.swapaxes(all_post.reshape(tp_count, FRAMES, seqs, Z), 1, 2)
    embed_grad = jnp.einsum(
        "psfk,ek->psfe",
        post_by_seq,
        jnp.concatenate(list(own_rows_e), axis=1),
        preferred_element_type=f32,
    ).reshape(seq_count, FRAMES, embed_part)
    embed_grad = embed_grad * scale[0]

    grads = [gru_sum[k * shares[0] : (k + 1) * shares[0]] for k in range(3)]
    grads += [head_sum[: shares[3]], head_sum[shares[3] :]]

    def own_rows(matrix, axis_dim):
        share = matrix.shape[axis_dim] // dp_count
        return lax.dynamic_slice_in_dim(matrix, dp_index * share, share, axis_dim)

    gru_moments = own_rows(gru_moment, 1)
    moments = [momentum_keep * gru_moments[k] + grads[k] for k in range(3)]
    moments.append(momentum_keep * own_rows(post_moment, 0) + grads[3])
    moments.append(momentum_keep * own_rows(prior_moment, 0) + grads[4])
    ahead = [(grads[m] + momentum_keep * moments[m]).astype(bf16) for m in range(MATS)]

    owners = [m * dp_count // 8 for m in (0, 3, 4, 7, 5)]
    widest = max(shares)
    base = shares[0]
    holds_post = (dp_index == owners[3]).astype(jnp.int32)
    if dp_count == 8:
        kept = jnp.array([owners.index(d) if d in owners else 0 for d in range(dp_count)])
        blocks = jnp.stack(
            [jnp.pad(block, ((0, widest - block.shape[0]), (0, 0))) for block in ahead]
        )
        where = dp_index.astype(jnp.int32).reshape(1)
        pieces = []
        for step in range(dp_count):
            block = lax.dynamic_index_in_dim(blocks, kept[dp_index ^ step], 0, keepdims=False)
            if step > 0:
                block = lax.ppermute(block, ("dz", "dx"), [(d ^ step, d) for d in owners])
            pieces.append(block)
        turned = run_collect(where, pieces, base)
    else:
        slots = [jnp.zeros((widest, units), bf16)] * dp_count
        for m in range(MATS):
            slots[owners[m]] = jnp.pad(ahead[m], ((0, widest - shares[m]), (0, 0)))
        arrived = exchange(jnp.stack(slots), ("dz", "dx"))
        turned = run_turn(
            jnp.concatenate(
                [arrived[:, :base].reshape(-1, units), arrived[:, base:].reshape(-1, units)], axis=0
            )
        )
    wide = gather(turned).reshape(H, dp_count * widest)
    own = jnp.stack([tp_index, holds_post]).astype(jnp.int32)
    old_rows = (own_rows(gru_weight, 1), own_rows(post_weight, 0), own_rows(prior_weight, 0))
    old_rows = lax.optimization_barrier(old_rows)
    result = run_orthogonal(
        dp_count * base, units, own, wide, (embed_grad, loss_value.reshape(1, 1), *old_rows)
    )
    if dp_count == 8:
        dealt = run_deal(where, result, dp_count, base)
        pieces = [dealt[0]]
        for step in range(1, dp_count):
            pairs = [(d, d ^ step) for d in owners]
            pieces.append(lax.ppermute(dealt[step], ("dz", "dx"), pairs))
        new_gru, new_post, new_prior = run_finish(owners, where, pieces, old_rows)
    else:
        result = result.T
        results = exchange(
            jnp.concatenate(
                [
                    result[: dp_count * base].reshape(dp_count, base, units),
                    result[dp_count * base :].reshape(dp_count, widest - base, units),
                ],
                axis=1,
            ),
            ("dz", "dx"),
        )

        def renew(old, m):
            factor = learn_rate * update_scale * math.sqrt(max(ROWS[m], Z))
            change = results[owners[m], : old.shape[0]].astype(f32)
            return old * (1.0 - learn_rate * weight_decay) - factor * change

        new_gru = jnp.stack([renew(old_rows[0][k], k) for k in range(3)])
        new_post = renew(old_rows[1], 3)
        new_prior = renew(old_rows[2], 4)
    return (
        loss_value,
        embed_grad,
        new_gru,
        new_post,
        new_prior,
        jnp.stack(moments[:3]),
        moments[3],
        moments[4],
    )

def solution(mesh):
    dp_count, tp_count = mesh.devices.shape
    mesh = jax.sharding.Mesh(
        mesh.devices.reshape(dp_count // 2, 2, tp_count), ("dz", "dx", "tp")
    )
    dp = ("dz", "dx")
    in_specs = (
        P(dp, None, None),
        P(dp, None, None),
        P(dp),
        P(None, None, "tp"),
        P(None, "tp"),
        P(None, "tp"),
        P(None, None, "tp"),
        P(None, "tp"),
        P(None, "tp"),
    )
    out_specs = (
        P(),
        P(dp, None, "tp"),
        P(None, dp, "tp"),
        P(dp, "tp"),
        P(dp, "tp"),
        P(None, dp, "tp"),
        P(dp, "tp"),
        P(dp, "tp"),
    )
    return jax.shard_map(
        on_device, mesh=mesh, in_specs=in_specs, out_specs=out_specs, check_vma=False
    )
```

```python
import functools
import math

import jax
import jax.numpy as jnp
from jax import lax
from jax.experimental import pallas as pl
from jax.experimental.pallas import tpu as pltpu
from jax.sharding import PartitionSpec as P

H = 1024
ZC = 32
E = 1536
FRAMES = 56
MATS = 5
Z = 1024
ROWS = (Z + H, Z + H, Z + H, H + E, H)
PACK = 8
CHUNK = 4


coeff_linear = 3.4445
coeff_cubic = -4.775
coeff_quintic = 2.0315
momentum_keep = 0.95
learn_rate = 0.2
weight_decay = 0.01
update_scale = 0.2
tiny_value = 1e-07
mib = 1 << 20
LARGE = 56 * mib
f32 = jnp.float32
bf16 = jnp.bfloat16
NT = (((1,), (1,)), ((), ()))
TN = (((0,), (0,)), ((), ()))


def dot(left, right):
    return jnp.dot(left, right, preferred_element_type=f32)


def dot_tn(left, right):
    return lax.dot_general(left, right, TN, preferred_element_type=f32)


def dot_nt(left, right):
    return lax.dot_general(left, right, NT, preferred_element_type=f32)


def copy(source, target, semaphore):
    return pltpu.make_async_copy(source, target, semaphore)


def scan_forward(
    seqs, chunk, spot_ref, x_ref, *refs
):
    parts, packs = x_ref.shape[:2]
    shards = refs[:parts]
    h_ref, k_hbm, u_hbm, t_hbm, state, w, k_ref, u_ref, t, w_sem, k_sem, u_sem, t_sem = refs[parts:]
    units = w.shape[3]
    per_pack = PACK // seqs
    loads = [copy(shards[n], w.at[spot_ref[0] ^ n], w_sem.at[n]) for n in range(parts)]
    for load in loads:
        load.start()
    state[...] = jnp.zeros_like(state)
    for load in loads:
        load.wait()

    def stores(c):
        at = pl.ds(c * chunk, chunk)
        return (
            copy(k_ref.at[:, at], k_hbm.at[:, at], k_sem.at[c]),
            copy(u_ref.at[at], u_hbm.at[at], u_sem.at[c]),
        )

    def pack(i, carry):
        states = []
        for frame in range(per_pack):
            rows = slice(frame * seqs, (frame + 1) * seqs)
            if frame == 0:
                source, live = jnp.maximum(i - 1, 0), jnp.where(i > 0, 1.0, 0.0)
                spot = slice((per_pack - 1) * seqs, per_pack * seqs)
            else:
                source, live = i, None
                spot = slice((frame - 1) * seqs, frame * seqs)
            before = state[...]
            low = before.astype(bf16)
            news = []
            for p in range(parts):
                cols = slice(p * units, (p + 1) * units)
                given = x_ref[p, source].astype(f32)[spot]
                if live is not None:
                    given = given * live
                pre = [
                    given[:, k * units : (k + 1) * units] + dot(low, w[p, k]) for k in range(3)
                ]
                last = before[:, cols]
                r = jax.nn.sigmoid(pre[0])
                c = jnp.tanh(r * pre[1])
                u = jax.nn.sigmoid(pre[2] - 1.0)
                rest = 1.0 - u
                new = u * c + rest * last
                inner = u * (1.0 - c * c)
                state[:, cols] = new
                news.append(new)
                k_ref[0, i, rows, cols] = inner * pre[1] * r * (1.0 - r)
                k_ref[1, i, rows, cols] = inner * r
                k_ref[2, i, rows, cols] = (c - last) * u * rest
                u_ref[i, rows, cols] = rest
            states.append(jnp.concatenate(news, axis=1))
        h_ref[i] = jnp.concatenate(states, axis=0).astype(bf16)

        @pl.when(i % chunk == chunk - 1)
        def _():
            for store in stores(i // chunk):
                store.start()

        return carry

    def pack_and_turn(i, carry):
        t[pl.ds(pl.multiple_of(i * units, units), units), :] = w[i // 3, i % 3].T
        return pack(i, carry)

    lax.fori_loop(0, 3 * parts, pack_and_turn, 0)
    turned = copy(t, t_hbm, t_sem)
    turned.start()
    lax.fori_loop(3 * parts, packs, pack, 0)
    turned.wait()
    for c in range(packs // chunk):
        for store in stores(c):
            store.wait()


def scan_backward(
    seqs, chunk, d_ref, k_hbm, u_hbm, t_hbm, b_hbm, now, kept, w, k_ref, u_ref, b_ref, t_sem, k_sem, u_sem, b_sem
):
    copies, parts, packs = b_hbm.shape[:3]
    units = b_ref.shape[3] // 3
    per_pack = PACK // seqs
    chunks = packs // chunk

    def loads(c):
        at = pl.ds(c * chunk, chunk)
        return (
            copy(k_hbm.at[:, at], k_ref.at[:, at], k_sem.at[c]),
            copy(u_hbm.at[at], u_ref.at[at], u_sem.at[c]),
        )

    def stores(c):
        at = pl.ds(c * chunk, chunk)
        return [
            copy(b_ref.at[:, at], b_hbm.at[n, :, at], b_sem.at[n * chunks + c]) for n in range(copies)
        ]

    turned = copy(t_hbm, w, t_sem)
    turned.start()
    for c in reversed(range(chunks)):
        for load in loads(c):
            load.start()
    now[...] = jnp.zeros_like(now)
    kept[...] = jnp.zeros_like(kept)
    turned.wait()

    def pack(n, carry):
        i = packs - 1 - n

        @pl.when(i % chunk == chunk - 1)
        def _():
            for load in loads(i // chunk):
                load.wait()

        later = [None] * per_pack
        for frame in reversed(range(per_pack)):
            rows = slice(frame * seqs, (frame + 1) * seqs)
            values = now[...]
            later[frame] = values
            dh = d_ref[i, rows] + kept[...] + dot(values.astype(bf16), w[...])
            kept[...] = dh * u_ref[i, rows]
            for p in range(parts):
                cols = slice(p * units, (p + 1) * units)
                for k in range(3):
                    spot = slice((3 * p + k) * units, (3 * p + k + 1) * units)
                    now[:, spot] = dh[:, cols] * k_ref[k, i, rows, cols]
        stacked = jnp.concatenate(later, axis=0).astype(bf16)
        for p in range(parts):
            b_ref[p, i] = stacked[:, p * 3 * units : (p + 1) * 3 * units]

        @pl.when(i % chunk == 0)
        def _():
            for store in stores(i // chunk):
                store.start()

        return carry

    lax.fori_loop(0, packs, pack, 0)
    for c in range(chunks):
        for store in stores(c):
            store.wait()


def head_block(h_ref, e_ref, t_ref, m_ref, r_ref, w_hbm, back_ref, d_ref, loss_ref, w_ref, w_sem):
    parts = w_ref.shape[0]
    loads = [copy(w_hbm.at[p], w_ref.at[p], w_sem.at[p]) for p in range(parts)]
    for load in loads:
        load.start()
    units = w_ref.shape[2]
    rows = h_ref.shape[0]
    low = h_ref[...]
    back_ref[0] = low
    mask = m_ref[...]
    given = jnp.zeros((rows, 128), f32)
    normal = jnp.zeros((1, rows), f32)
    for p in range(parts):
        loads[p].wait()
        post = dot(low, w_ref[p, :H]) + dot(e_ref[...], w_ref[p, H : H + E])
        prior = dot(low, w_ref[p, H + E :])
        for head, logits in enumerate((prior, post)):
            for piece in range(units // 128):
                l = logits[:, piece * 128 : (piece + 1) * 128]
                cols = slice(p * units + piece * 128, p * units + (piece + 1) * 128)
                target = t_ref[:, cols].astype(f32)
                turned = l.T.reshape(128 // ZC, ZC, rows)
                top = jnp.max(turned, axis=1, keepdims=True)
                e = jnp.exp(turned - top)
                total = jnp.sum(e, axis=1, keepdims=True)
                normal = normal + jnp.sum(top + jnp.log(total), axis=0)
                probs = (e * (1.0 / total)).reshape(128, rows).T
                given = given + target * l
                back_ref[head + 2, :, cols] = (mask * (probs - target)).astype(bf16)
    loss_ref[...] = jnp.sum(r_ref[...] * normal, axis=1, keepdims=True) - jnp.sum(
        jnp.sum(mask * given, axis=0, keepdims=True), axis=1, keepdims=True
    )
    direct = jnp.zeros((rows, H), f32)
    for p in range(parts):
        cols = slice(p * units, (p + 1) * units)
        direct = direct + dot_nt(back_ref[2, :, cols], w_ref[p, H + E :])
        direct = direct + dot_nt(back_ref[3, :, cols], w_ref[p, :H])
    d_ref[...] = direct


def head_grads(spot_ref, scale_ref, r_hbm, e_hbm, earlier_ref, o_ref, h_ref, r_ref, e_ref, sems):
    parts, rows = e_ref.shape[0], e_ref.shape[1]
    units = o_ref.shape[1]
    frames = parts * rows
    scale = scale_ref[0]
    own = pl.ds(pl.multiple_of(spot_ref[0] * units, units), units)
    loads = [
        copy(r_hbm.at[:, pl.ds(2, 2), :, own], r_ref, sems.at[0]),
        copy(r_hbm.at[:, 0], h_ref, sems.at[1]),
        copy(e_hbm, e_ref, sems.at[2]),
    ]
    for load in loads:
        load.start()
    loads[0].wait()
    loads[1].wait()
    post = r_ref[:, 1].reshape(frames, units)
    both = jnp.concatenate([post, r_ref[:, 0].reshape(frames, units)], axis=1)
    for m in range(H // 256):
        spot = slice(m * 256, (m + 1) * 256)
        grad = (dot_tn(h_ref[:, :, spot].reshape(frames, 256), both) * scale).astype(bf16)
        o_ref[m * 256 : (m + 1) * 256] = grad[:, :units]
        o_ref[H + E + m * 256 : H + E + (m + 1) * 256] = grad[:, units:]
    loads[2].wait()
    for m in range(E // 256):
        spot = slice(m * 256, (m + 1) * 256)
        grad = (dot_tn(e_ref[:, :, spot].reshape(frames, 256), post) * scale).astype(bf16)
        o_ref[H + m * 256 : H + (m + 1) * 256] = grad


def gru_grads(
    spot_ref, scale_ref, one_hbm, r_hbm, b_hbm, earlier_ref, o_ref, one_ref, l_ref, b_ref, sems
):
    parts, rows = b_ref.shape[1], b_ref.shape[2]
    units = o_ref.shape[2]
    frames = parts * rows
    share = o_ref.shape[1] // 3
    half = o_ref.shape[0] // 2
    scale = scale_ref[0]
    me = spot_ref[1]
    loads = [copy(b_hbm, b_ref, sems.at[0]), copy(one_hbm, one_ref, sems.at[1])]
    for z in range(half):
        spot = pl.ds(pl.multiple_of((z * 2 + me) * share, share), share)
        loads.append(copy(r_hbm.at[:, 0, :, spot], l_ref.at[0, z], sems.at[2 + 2 * z]))
        loads.append(copy(r_hbm.at[:, 1, :, spot], l_ref.at[1, z], sems.at[3 + 2 * z]))
    for load in loads:
        load.start()
    loads[0].wait()
    loads[1].wait()
    back = [b_ref[x].reshape(frames, 3 * units) for x in (me, 1 - me)]
    for z in range(2 * half):
        if z < half:
            spot = slice(z * share, (z + 1) * share)
            left = [one_ref[x, :, spot] for x in (me, 1 - me)]
        else:
            loads[2 * (z - half) + 2].wait()
            loads[2 * (z - half) + 3].wait()
            left = [l_ref[n, z - half].reshape(frames, share) for n in (0, 1)]
        grad = (dot_tn(left[0], back[0]) + dot_tn(left[1], back[1])) * scale
        grad = grad.astype(bf16)
        for k in range(3):
            o_ref[z, k * share : (k + 1) * share] = grad[:, k * units : (k + 1) * units]


def orthogonal_block(base, tile, own_ref, g_ref, *refs):
    o_ref, x, a, b = refs[-4:]
    side, width = g_ref.shape
    share = o_ref.shape[0]
    own = pl.ds(pl.multiple_of(own_ref[0] * share, share), share)
    wide = own_ref[1] > 0

    def either(run):
        pl.when(wide)(functools.partial(run, width))
        pl.when(jnp.logical_not(wide))(functools.partial(run, base))

    def squares(i, total):
        rows = pl.ds(pl.multiple_of(i * 128, 128), 128)
        v = g_ref[rows, :].astype(f32)
        return total + jnp.sum(v * v)

    total = lax.fori_loop(0, side // 128, squares, jnp.zeros((), f32))
    scale = 1.0 / (jnp.sqrt(jnp.full((1, 128), total, f32)) + tiny_value)
    scale = scale[:, :1]

    def shrink(i, carry):
        rows = pl.ds(pl.multiple_of(i * 128, 128), 128)
        x[rows, :] = (g_ref[rows, :].astype(f32) * scale).astype(bf16)
        return carry

    lax.fori_loop(0, side // 128, shrink, 0)

    def lower(out, product):
        for start in range(0, side, 256):
            stop = start + 256
            block = product(slice(start, side), slice(start, stop)).astype(bf16)
            out[start:, start:stop] = block
            if stop < side:
                out[start:stop, stop:] = block[256:].T

    def square(depth):
        lower(a, lambda rows, cols: dot_nt(x[rows, :depth], x[cols, :depth]))

    def mix():
        lower(
            b,
            lambda rows, cols: coeff_cubic * a[rows, cols].astype(f32)
            + coeff_quintic * dot(a[rows, :], a[:, cols]),
        )

    def renew_all(depth):
        for start in range(0, depth, tile):
            cols = slice(start, start + tile)
            x[:, cols] = (
                coeff_linear * x[:, cols].astype(f32) + dot(b[...], x[:, cols])
            ).astype(bf16)

    def sweep(s, carry):
        either(square)
        mix()
        either(renew_all)
        return carry

    lax.fori_loop(0, 4, sweep, 0)
    either(square)
    part = (coeff_cubic * a[own, :].astype(f32) + coeff_quintic * dot(a[own, :], a[...])).astype(bf16)

    def last(j, carry):
        cols = pl.ds(pl.multiple_of(j * tile, tile), tile)
        o_ref[:, cols] = (
            coeff_linear * x[own, cols].astype(f32) + dot(part, x[:, cols])
        ).astype(bf16)
        return carry

    lax.fori_loop(0, width // tile, last, 0)


def turn_block(tile, g_ref, o_ref):
    def block(i, carry):
        spot = pl.ds(pl.multiple_of(i * tile, tile), tile)
        o_ref[:, spot] = g_ref[spot, :].T
        return carry

    lax.fori_loop(0, g_ref.shape[0] // tile, block, 0)


def collect_block(base, spot_ref, *refs):
    *pieces, o_ref, rows = refs
    steps = len(pieces)
    more = pieces[0].shape[0] - base
    for step, piece in enumerate(pieces):
        d = spot_ref[0] ^ step
        o_ref[:, pl.ds(pl.multiple_of(d * base, base), base)] = piece[:base].T
        rows[pl.ds(pl.multiple_of(d * more, more), more), :] = piece[base:]
    o_ref[:, steps * base :] = rows[...].T


def deal_block(base, spot_ref, g_ref, o_ref, rows):
    steps, widest = o_ref.shape[:2]
    more = widest - base
    rows[...] = g_ref[:, steps * base :].T
    for step in range(steps):
        d = spot_ref[0] ^ step
        o_ref[step, :base] = g_ref[:, pl.ds(pl.multiple_of(d * base, base), base)].T
        o_ref[step, base:] = rows[pl.ds(pl.multiple_of(d * more, more), more), :]


def finish_block(owners, spot_ref, *refs):
    pieces, (gru_ref, post_ref, prior_ref), (gru_out, post_out, prior_out), all_ref = (
        refs[:-7],
        refs[-7:-4],
        refs[-4:-1],
        refs[-1],
    )
    for step, piece in enumerate(pieces):
        all_ref[step] = piece[...]

    def renewed(old, m):
        change = all_ref[spot_ref[0] ^ owners[m], : old.shape[0]].astype(f32)
        factor = learn_rate * update_scale * math.sqrt(max(ROWS[m], Z))
        return old * (1.0 - learn_rate * weight_decay) - factor * change

    for k in range(3):
        gru_out[k] = renewed(gru_ref[k], k)
    post_out[...] = renewed(post_ref[...], 3)
    prior_out[...] = renewed(prior_ref[...], 4)


def in_vmem(count):
    return [pl.BlockSpec(memory_space=pltpu.VMEM)] * count


def cost(flops, touched):
    return pl.CostEstimate(flops=int(flops), bytes_accessed=int(touched), transcendentals=0)


def run_forward(spot, inputs, weights, seqs):
    parts, packs = inputs.shape[:2]
    units = weights[0].shape[2]
    chunks = packs // CHUNK
    return pl.pallas_call(
        functools.partial(scan_forward, seqs, CHUNK),
        out_shape=[
            jax.ShapeDtypeStruct((packs, PACK, H), bf16),
            jax.ShapeDtypeStruct((3, packs, PACK, H), f32),
            jax.ShapeDtypeStruct((packs, PACK, H), f32),
            jax.ShapeDtypeStruct((3 * H, H), bf16),
        ],
        in_specs=in_smem(1) + in_vmem(1) + anywhere(parts),
        out_specs=in_vmem(1) + anywhere(3),
        scratch_shapes=[
            pltpu.VMEM((seqs, H), f32),
            pltpu.VMEM((parts, 3, H, units), bf16),
            pltpu.VMEM((3, packs, PACK, H), f32),
            pltpu.VMEM((packs, PACK, H), f32),
            pltpu.VMEM((3 * H, H), bf16),
            pltpu.SemaphoreType.DMA((parts,)),
            pltpu.SemaphoreType.DMA((chunks,)),
            pltpu.SemaphoreType.DMA((chunks,)),
            pltpu.SemaphoreType.DMA,
        ],
        compiler_params=pltpu.CompilerParams(vmem_limit_bytes=LARGE),
        cost_estimate=cost(6e10, 20 * mib),
        name="scan_forward",
    )(spot, inputs, *weights)


def run_backward(direct, factors, rest, turned, parts, seqs, copies):
    packs = direct.shape[0]
    units = H // parts
    chunks = packs // CHUNK
    return pl.pallas_call(
        functools.partial(scan_backward, seqs, CHUNK),
        out_shape=jax.ShapeDtypeStruct((copies, parts, packs, PACK, 3 * units), bf16),
        in_specs=in_vmem(1) + anywhere(3),
        out_specs=anywhere(1)[0],
        scratch_shapes=[
            pltpu.VMEM((seqs, 3 * H), f32),
            pltpu.VMEM((seqs, H), f32),
            pltpu.VMEM((3 * H, H), bf16),
            pltpu.VMEM((3, packs, PACK, H), f32),
            pltpu.VMEM((packs, PACK, H), f32),
            pltpu.VMEM((parts, packs, PACK, 3 * units), bf16),
            pltpu.SemaphoreType.DMA,
            pltpu.SemaphoreType.DMA((chunks,)),
            pltpu.SemaphoreType.DMA((chunks,)),
            pltpu.SemaphoreType.DMA((copies * chunks,)),
        ],
        compiler_params=pltpu.CompilerParams(vmem_limit_bytes=LARGE),
        cost_estimate=cost(6e10, 20 * mib),
        name="scan_backward",
    )(direct, factors, rest, turned)


def run_heads(hidden, embed, target, mask, mask_row, weights):
    rows = hidden.shape[0]
    return pl.pallas_call(
        head_block,
        out_shape=[
            jax.ShapeDtypeStruct((4, rows, Z), bf16),
            jax.ShapeDtypeStruct((rows, H), f32),
            jax.ShapeDtypeStruct((1, 1), f32),
        ],
        in_specs=in_vmem(5) + anywhere(1),
        out_specs=in_vmem(3),
        scratch_shapes=[
            pltpu.VMEM(weights.shape, bf16),
            pltpu.SemaphoreType.DMA((weights.shape[0],)),
        ],
        compiler_params=pltpu.CompilerParams(vmem_limit_bytes=LARGE),
        cost_estimate=cost(1e10, 12 * mib),
        name="heads",
    )(hidden, embed, target, mask, mask_row, weights)


def in_smem(count):
    return [pl.BlockSpec(memory_space=pltpu.SMEM)] * count


def anywhere(count):
    return [pl.BlockSpec(memory_space=pl.ANY)] * count


def run_head_grads(spot, scale, everyone, embed, earlier):
    parts, rows = embed.shape[:2]
    units = H // parts
    return pl.pallas_call(
        head_grads,
        out_shape=jax.ShapeDtypeStruct((H + E + H, units), bf16),
        in_specs=in_smem(2) + anywhere(3),
        out_specs=in_vmem(1)[0],
        scratch_shapes=[
            pltpu.VMEM((parts, rows, H), bf16),
            pltpu.VMEM((parts, 2, rows, units), bf16),
            pltpu.VMEM(embed.shape, bf16),
            pltpu.SemaphoreType.DMA((3,)),
        ],
        compiler_params=pltpu.CompilerParams(vmem_limit_bytes=LARGE),
        cost_estimate=cost(4e9, 12 * mib),
        name="head_grads",
    )(spot, scale, everyone, embed, earlier)


def run_gru_grads(spot, scale, onehot, everyone, back, earlier, dz_count):
    parts, rows = back.shape[1:3]
    units = back.shape[3] // 3
    share = (Z + H) // (2 * dz_count)
    return pl.pallas_call(
        gru_grads,
        out_shape=jax.ShapeDtypeStruct((dz_count, 3 * share, units), bf16),
        in_specs=in_smem(2) + anywhere(4),
        out_specs=in_vmem(1)[0],
        scratch_shapes=[
            pltpu.VMEM(onehot.shape, bf16),
            pltpu.VMEM((2, dz_count // 2, parts, rows, share), bf16),
            pltpu.VMEM(back.shape, bf16),
            pltpu.SemaphoreType.DMA((2 + dz_count,)),
        ],
        compiler_params=pltpu.CompilerParams(vmem_limit_bytes=LARGE),
        cost_estimate=cost(4e9, 12 * mib),
        name="gru_grads",
    )(spot, scale, onehot, everyone, back, earlier)


def plain_gru_grads(dx_index, scale, onehot, everyone, back, dz_count):
    units = back.shape[3] // 3
    share = (Z + H) // (2 * dz_count)
    total = 0.0
    for states, x in ((everyone[:, 0], dx_index), (everyone[:, 1], 1 - dx_index)):
        states = states.reshape(-1, dz_count // 2, 2, share)
        states = lax.dynamic_index_in_dim(states, dx_index, 2, keepdims=False)
        ones = lax.dynamic_index_in_dim(onehot, x, 0, keepdims=False)
        left = jnp.concatenate([ones, states.reshape(ones.shape)], axis=1)
        right = lax.dynamic_index_in_dim(back, x, 0, keepdims=False)
        total = total + dot_tn(left, right.reshape(-1, 3 * units))
    grads = (total * scale).astype(bf16).reshape(dz_count, share, 3, units)
    return jnp.swapaxes(grads, 1, 2).reshape(dz_count, 3 * share, units)


def run_orthogonal(base, share, own, matrix, earlier):
    side, width = matrix.shape
    return pl.pallas_call(
        functools.partial(orthogonal_block, base, 512),
        out_shape=jax.ShapeDtypeStruct((share, width), bf16),
        in_specs=in_smem(1) + in_vmem(1) + anywhere(len(earlier)),
        out_specs=in_vmem(1)[0],
        scratch_shapes=[
            pltpu.VMEM((side, width), bf16),
            pltpu.VMEM((side, side), bf16),
            pltpu.VMEM((side, side), bf16),
        ],
        compiler_params=pltpu.CompilerParams(vmem_limit_bytes=28 * mib),
        cost_estimate=cost(5e10, 6 * mib),
        name="orthogonal",
    )(own, matrix, *earlier)


def run_turn(matrix):
    return pl.pallas_call(
        functools.partial(turn_block, 256),
        out_shape=jax.ShapeDtypeStruct(matrix.shape[::-1], bf16),
        in_specs=in_vmem(1),
        out_specs=in_vmem(1)[0],
        compiler_params=pltpu.CompilerParams(vmem_limit_bytes=6 * mib),
        cost_estimate=cost(1e6, 3 * mib),
        name="turn",
    )(matrix)


def small_kernel(body, out_shape, scratch, specs, arguments, name):
    return pl.pallas_call(
        body,
        out_shape=out_shape,
        in_specs=specs,
        out_specs=jax.tree.map(lambda _: in_vmem(1)[0], out_shape),
        scratch_shapes=scratch,
        compiler_params=pltpu.CompilerParams(vmem_limit_bytes=8 * mib),
        cost_estimate=cost(1e6, 4 * mib),
        name=name,
    )(*arguments)


def run_collect(spot, pieces, base):
    steps = len(pieces)
    widest, units = pieces[0].shape
    return small_kernel(
        functools.partial(collect_block, base),
        jax.ShapeDtypeStruct((units, steps * widest), bf16),
        [pltpu.VMEM((steps * (widest - base), units), bf16)],
        in_smem(1) + in_vmem(steps),
        (spot, *pieces),
        "collect",
    )


def run_deal(spot, result, steps, base):
    units, width = result.shape
    widest = width // steps
    return small_kernel(
        functools.partial(deal_block, base),
        jax.ShapeDtypeStruct((steps, widest, units), bf16),
        [pltpu.VMEM((steps * (widest - base), units), bf16)],
        in_smem(1) + in_vmem(1),
        (spot, result),
        "deal",
    )


def run_finish(owners, spot, pieces, rows):
    return small_kernel(
        functools.partial(finish_block, owners),
        [jax.ShapeDtypeStruct(block.shape, f32) for block in rows],
        [pltpu.VMEM((len(pieces), *pieces[0].shape), bf16)],
        in_smem(1) + in_vmem(len(pieces) + len(rows)),
        (spot, *pieces, *rows),
        "finish",
    )


def on_device(
    embeddings,
    samples,
    seq_lengths,
    gru_weight,
    post_weight,
    prior_weight,
    gru_moment,
    post_moment,
    prior_moment,
):
    dz_count = lax.axis_size("dz")
    dx_count = lax.axis_size("dx")
    tp_count = lax.axis_size("tp")
    dp_count = dz_count * dx_count
    dx_index = lax.axis_index("dx")
    tp_index = lax.axis_index("tp")
    dp_index = lax.axis_index("dz") * dx_count + dx_index
    seq_count = embeddings.shape[0]
    seqs = seq_count // tp_count
    units = gru_weight.shape[2]
    groups = Z // ZC
    rows = seqs * FRAMES
    packs = rows // PACK

    def gather(block):
        return lax.all_gather(block, "tp", axis=0, tiled=False)

    def exchange(block, axis):
        return lax.all_to_all(block, axis, 0, 0, tiled=True)

    def mine(block, axis):
        return lax.dynamic_index_in_dim(block, dx_index, axis, keepdims=False)

    def across(block, bit):
        return lax.ppermute(block, "tp", [(i, i ^ bit) for i in range(tp_count)])

    own_hidden = gru_weight[:, Z:].astype(bf16)
    far = across(own_hidden, 2)
    near = across(own_hidden, 1)
    gru_input = lax.optimization_barrier(gru_weight)
    head_low = jnp.concatenate([post_weight.astype(bf16), prior_weight.astype(bf16)], axis=0)

    by_part = jnp.swapaxes(samples.reshape(tp_count, seqs, FRAMES, groups), 1, 2)
    by_part = by_part.reshape(tp_count * rows, groups).astype(bf16)

    def one_hot(chosen):
        count = chosen.shape[-1]
        classes = jnp.arange(count * ZC, dtype=jnp.int32)
        expand = (classes[None, :] // ZC == jnp.arange(count)[:, None]).astype(bf16)
        return (dot(chosen, expand) == (classes % ZC).astype(f32)).astype(bf16)

    onehot = one_hot(by_part)
    input_part = jnp.concatenate(
        [dot(onehot, gru_input[k, :Z].astype(bf16)).astype(bf16) for k in range(3)], axis=1
    ).reshape(tp_count, packs, PACK, 3 * units)
    input_part = exchange(input_part, "tp")
    embed_rows = jnp.swapaxes(embeddings.reshape(tp_count, seqs, FRAMES, E), 1, 2)
    embed_rows = embed_rows.reshape(tp_count, rows, E)
    pair_samples = lax.all_gather(by_part, "dx", axis=0, tiled=False)
    half = Z // dx_count
    pair_half = mine(
        pair_samples.reshape(dx_count * tp_count * rows, dz_count // 2, dx_count, -1), 2
    )
    pair_onehot = one_hot(pair_half.reshape(dx_count * tp_count * rows, groups // dx_count))
    pair_onehot = pair_onehot.reshape(dx_count, tp_count * rows, half)
    own_embed = lax.dynamic_index_in_dim(embed_rows, tp_index, 0, keepdims=False)
    onehot = onehot.reshape(tp_count, rows, Z)
    own_target = lax.dynamic_index_in_dim(onehot, tp_index, 0, keepdims=False)
    positions = jnp.arange(FRAMES, dtype=jnp.int32)
    own_lengths = lax.dynamic_slice_in_dim(seq_lengths, tp_index * seqs, seqs, 0)
    frame_mask = (positions[:, None] < own_lengths[None, :]).astype(f32)
    mask_lanes = jnp.broadcast_to(frame_mask.reshape(rows, 1), (rows, 128))

    far, head_low, own_target = lax.optimization_barrier((far, head_low, own_target))
    weights = [own_hidden, near, far, across(far, 1)]
    every_mask = (positions[:, None] < seq_lengths[None, :]).astype(f32)
    frame_count = jnp.broadcast_to(jnp.sum(every_mask), (8, 128))
    for axis, bits in (("dx", dx_count), ("dz", dz_count)):
        for bit in range(bits.bit_length() - 1):
            pairs = [(i, i ^ (1 << bit)) for i in range(bits)]
            frame_count = frame_count + lax.ppermute(frame_count, axis, pairs)
    frame_count = frame_count[0, 0]
    scale = (1.0 / frame_count).reshape(1)

    early = (head_low, own_embed, own_target, mask_lanes, embed_rows, pair_onehot, scale)
    weights, input_part, early = lax.optimization_barrier((weights, input_part, early))
    head_low, own_embed, own_target, mask_lanes, embed_rows, pair_onehot, scale = early
    head_full = gather(head_low)
    hidden, factors, rest, turned = run_forward(tp_index.astype(jnp.int32).reshape(1), input_part, weights, seqs)
    hidden = hidden.reshape(rows, H)
    swap = [(i, i ^ 1) for i in range(dx_count)]
    neighbour = lax.ppermute(hidden, "dx", swap)
    backs, direct, loss_lanes = run_heads(
        hidden, own_embed, own_target, mask_lanes, frame_mask.reshape(1, rows), head_full
    )
    everyone = gather(lax.dynamic_update_slice(backs, neighbour[None], (1, 0, 0)))
    back = run_backward(
        direct.reshape(packs, PACK, H), factors, rest, turned, tp_count, seqs, dx_count
    )
    own_back = exchange(back.reshape(dx_count * tp_count, rows, 3 * units), ("dx", "tp"))
    own_back = own_back.reshape(dx_count, tp_count, rows, 3 * units)

    shares = [size // dp_count for size in ROWS]
    all_post = everyone[:, 3]
    spot = jnp.stack([tp_index, dx_index]).astype(jnp.int32)

    head_grad = run_head_grads(spot, scale, everyone, embed_rows, back)

    head_grad = jnp.concatenate(
        [
            block.reshape(dz_count, dx_count, -1, units)
            for block in (head_grad[: H + E], head_grad[H + E :])
        ],
        axis=2,
    )

    def share_rows(block):
        return lax.psum_scatter(block, "dz", scatter_dimension=0, tiled=True)[0]

    head_done = share_rows(head_grad)
    if shares[0] % 128 == 0:
        gru_grad = run_gru_grads(
            spot, scale, pair_onehot, everyone, own_back, head_grad, dz_count
        )
    else:
        gru_grad = plain_gru_grads(dx_index, scale, pair_onehot, everyone, own_back, dz_count)
    gru_grad, head_done = lax.optimization_barrier((gru_grad, head_done))
    gru_sum = share_rows(gru_grad).astype(f32)
    received = lax.ppermute(
        lax.dynamic_index_in_dim(head_done, 1 - dx_index, 0, keepdims=False), "dx", swap
    )
    head_sum = mine(head_done, 0).astype(f32) + received.astype(f32)
    loss_sum = jnp.broadcast_to(jnp.sum(loss_lanes), (8, 128))
    for axis, bits in (("tp", tp_count), ("dx", dx_count), ("dz", dz_count)):
        for bit in range(bits.bit_length() - 1):
            pairs = [(i, i ^ (1 << bit)) for i in range(bits)]
            loss_sum = loss_sum + lax.ppermute(loss_sum, axis, pairs)
    loss_sum = loss_sum[0, 0]
    loss_value = loss_sum / frame_count

    embed_part = E // tp_count
    own_rows_e = lax.dynamic_slice_in_dim(head_full, H + tp_index * embed_part, embed_part, 1)
    post_by_seq = jnp.swapaxes(all_post.reshape(tp_count, FRAMES, seqs, Z), 1, 2)
    embed_grad = jnp.einsum(
        "psfk,ek->psfe",
        post_by_seq,
        jnp.concatenate(list(own_rows_e), axis=1),
        preferred_element_type=f32,
    ).reshape(seq_count, FRAMES, embed_part)
    embed_grad = embed_grad * scale[0]

    grads = [gru_sum[k * shares[0] : (k + 1) * shares[0]] for k in range(3)]
    grads += [head_sum[: shares[3]], head_sum[shares[3] :]]

    def own_rows(matrix, axis_dim):
        share = matrix.shape[axis_dim] // dp_count
        return lax.dynamic_slice_in_dim(matrix, dp_index * share, share, axis_dim)

    gru_moments = own_rows(gru_moment, 1)
    moments = [momentum_keep * gru_moments[k] + grads[k] for k in range(3)]
    moments.append(momentum_keep * own_rows(post_moment, 0) + grads[3])
    moments.append(momentum_keep * own_rows(prior_moment, 0) + grads[4])
    ahead = [(grads[m] + momentum_keep * moments[m]).astype(bf16) for m in range(MATS)]

    owners = [m * dp_count // 8 for m in (0, 3, 4, 7, 5)]
    widest = max(shares)
    base = shares[0]
    holds_post = (dp_index == owners[3]).astype(jnp.int32)
    if dp_count == 8:
        kept = jnp.array([owners.index(d) if d in owners else 0 for d in range(dp_count)])
        blocks = jnp.stack(
            [jnp.pad(block, ((0, widest - block.shape[0]), (0, 0))) for block in ahead]
        )
        where = dp_index.astype(jnp.int32).reshape(1)
        pieces = []
        for step in range(dp_count):
            block = lax.dynamic_index_in_dim(blocks, kept[dp_index ^ step], 0, keepdims=False)
            if step > 0:
                block = lax.ppermute(block, ("dz", "dx"), [(d ^ step, d) for d in owners])
            pieces.append(block)
        turned = run_collect(where, pieces, base)
    else:
        slots = [jnp.zeros((widest, units), bf16)] * dp_count
        for m in range(MATS):
            slots[owners[m]] = jnp.pad(ahead[m], ((0, widest - shares[m]), (0, 0)))
        arrived = exchange(jnp.stack(slots), ("dz", "dx"))
        turned = run_turn(
            jnp.concatenate(
                [arrived[:, :base].reshape(-1, units), arrived[:, base:].reshape(-1, units)], axis=0
            )
        )
    wide = gather(turned).reshape(H, dp_count * widest)
    own = jnp.stack([tp_index, holds_post]).astype(jnp.int32)
    old_rows = (own_rows(gru_weight, 1), own_rows(post_weight, 0), own_rows(prior_weight, 0))
    old_rows = lax.optimization_barrier(old_rows)
    result = run_orthogonal(
        dp_count * base, units, own, wide, (embed_grad, loss_value.reshape(1, 1), *old_rows)
    )
    if dp_count == 8:
        dealt = run_deal(where, result, dp_count, base)
        pieces = [dealt[0]]
        for step in range(1, dp_count):
            pairs = [(d, d ^ step) for d in owners]
            pieces.append(lax.ppermute(dealt[step], ("dz", "dx"), pairs))
        new_gru, new_post, new_prior = run_finish(owners, where, pieces, old_rows)
    else:
        result = result.T
        results = exchange(
            jnp.concatenate(
                [
                    result[: dp_count * base].reshape(dp_count, base, units),
                    result[dp_count * base :].reshape(dp_count, widest - base, units),
                ],
                axis=1,
            ),
            ("dz", "dx"),
        )

        def renew(old, m):
            factor = learn_rate * update_scale * math.sqrt(max(ROWS[m], Z))
            change = results[owners[m], : old.shape[0]].astype(f32)
            return old * (1.0 - learn_rate * weight_decay) - factor * change

        new_gru = jnp.stack([renew(old_rows[0][k], k) for k in range(3)])
        new_post = renew(old_rows[1], 3)
        new_prior = renew(old_rows[2], 4)
    return (
        loss_value,
        embed_grad,
        new_gru,
        new_post,
        new_prior,
        jnp.stack(moments[:3]),
        moments[3],
        moments[4],
    )

def solution(mesh):
    dp_count, tp_count = mesh.devices.shape
    mesh = jax.sharding.Mesh(
        mesh.devices.reshape(dp_count // 2, 2, tp_count), ("dz", "dx", "tp")
    )
    dp = ("dz", "dx")
    in_specs = (
        P(dp, None, None),
        P(dp, None, None),
        P(dp),
        P(None, None, "tp"),
        P(None, "tp"),
        P(None, "tp"),
        P(None, None, "tp"),
        P(None, "tp"),
        P(None, "tp"),
    )
    out_specs = (
        P(),
        P(dp, None, "tp"),
        P(None, dp, "tp"),
        P(dp, "tp"),
        P(dp, "tp"),
        P(None, dp, "tp"),
        P(dp, "tp"),
        P(dp, "tp"),
    )
    return jax.shard_map(
        on_device, mesh=mesh, in_specs=in_specs, out_specs=out_specs, check_vma=False
    )
```

```python
import functools
import math

import jax
import jax.numpy as jnp
from jax import lax
from jax.experimental import pallas as pl
from jax.experimental.pallas import tpu as pltpu
from jax.sharding import PartitionSpec as P

H = 1024
ZC = 32
E = 1536
FRAMES = 56
MATS = 5
Z = 1024
ROWS = (Z + H, Z + H, Z + H, H + E, H)
PACK = 8
CHUNK = 4


coeff_linear = 3.4445
coeff_cubic = -4.775
coeff_quintic = 2.0315
momentum_keep = 0.95
learn_rate = 0.2
weight_decay = 0.01
update_scale = 0.2
tiny_value = 1e-07
mib = 1 << 20
LARGE = 56 * mib
f32 = jnp.float32
bf16 = jnp.bfloat16
NT = (((1,), (1,)), ((), ()))
TN = (((0,), (0,)), ((), ()))


def dot(left, right):
    return jnp.dot(left, right, preferred_element_type=f32)


def dot_tn(left, right):
    return lax.dot_general(left, right, TN, preferred_element_type=f32)


def dot_nt(left, right):
    return lax.dot_general(left, right, NT, preferred_element_type=f32)


def copy(source, target, semaphore):
    return pltpu.make_async_copy(source, target, semaphore)


def scan_forward(
    seqs, chunk, spot_ref, x_ref, *refs
):
    parts, packs = x_ref.shape[:2]
    shards = refs[:parts]
    h_ref, k_hbm, u_hbm, t_hbm, state, w, k_ref, u_ref, t, w_sem, k_sem, u_sem, t_sem = refs[parts:]
    units = w.shape[3]
    per_pack = PACK // seqs
    loads = [copy(shards[n], w.at[spot_ref[0] ^ n], w_sem.at[n]) for n in range(parts)]
    for load in loads:
        load.start()
    state[...] = jnp.zeros_like(state)
    for load in loads:
        load.wait()

    def stores(c):
        at = pl.ds(c * chunk, chunk)
        return (
            copy(k_ref.at[:, at], k_hbm.at[:, at], k_sem.at[c]),
            copy(u_ref.at[at], u_hbm.at[at], u_sem.at[c]),
        )

    def pack(i, carry):
        states = []
        for frame in range(per_pack):
            rows = slice(frame * seqs, (frame + 1) * seqs)
            if frame == 0:
                source, live = jnp.maximum(i - 1, 0), jnp.where(i > 0, 1.0, 0.0)
                spot = slice((per_pack - 1) * seqs, per_pack * seqs)
            else:
                source, live = i, None
                spot = slice((frame - 1) * seqs, frame * seqs)
            before = state[...]
            low = before.astype(bf16)
            news = []
            for p in range(parts):
                cols = slice(p * units, (p + 1) * units)
                given = x_ref[p, source].astype(f32)[spot]
                if live is not None:
                    given = given * live
                pre = [
                    given[:, k * units : (k + 1) * units] + dot(low, w[p, k]) for k in range(3)
                ]
                last = before[:, cols]
                r = jax.nn.sigmoid(pre[0])
                c = jnp.tanh(r * pre[1])
                u = jax.nn.sigmoid(pre[2] - 1.0)
                rest = 1.0 - u
                new = u * c + rest * last
                inner = u * (1.0 - c * c)
                state[:, cols] = new
                news.append(new)
                k_ref[0, i, rows, cols] = inner * pre[1] * r * (1.0 - r)
                k_ref[1, i, rows, cols] = inner * r
                k_ref[2, i, rows, cols] = (c - last) * u * rest
                u_ref[i, rows, cols] = rest
            states.append(jnp.concatenate(news, axis=1))
        h_ref[i] = jnp.concatenate(states, axis=0).astype(bf16)

        @pl.when(i % chunk == chunk - 1)
        def _():
            for store in stores(i // chunk):
                store.start()

        return carry

    def pack_and_turn(i, carry):
        t[pl.ds(pl.multiple_of(i * units, units), units), :] = w[i // 3, i % 3].T
        return pack(i, carry)

    lax.fori_loop(0, 3 * parts, pack_and_turn, 0)
    turned = copy(t, t_hbm, t_sem)
    turned.start()
    lax.fori_loop(3 * parts, packs, pack, 0)
    turned.wait()
    for c in range(packs // chunk):
        for store in stores(c):
            store.wait()


def scan_backward(
    seqs, chunk, d_ref, k_hbm, u_hbm, t_hbm, b_hbm, now, kept, w, k_ref, u_ref, b_ref, t_sem, k_sem, u_sem, b_sem
):
    copies, parts, packs = b_hbm.shape[:3]
    units = b_ref.shape[3] // 3
    per_pack = PACK // seqs
    chunks = packs // chunk

    def loads(c):
        at = pl.ds(c * chunk, chunk)
        return (
            copy(k_hbm.at[:, at], k_ref.at[:, at], k_sem.at[c]),
            copy(u_hbm.at[at], u_ref.at[at], u_sem.at[c]),
        )

    def stores(c):
        at = pl.ds(c * chunk, chunk)
        return [
            copy(b_ref.at[:, at], b_hbm.at[n, :, at], b_sem.at[n * chunks + c]) for n in range(copies)
        ]

    turned = copy(t_hbm, w, t_sem)
    turned.start()
    for c in reversed(range(chunks)):
        for load in loads(c):
            load.start()
    now[...] = jnp.zeros_like(now)
    kept[...] = jnp.zeros_like(kept)
    turned.wait()

    def pack(n, carry):
        i = packs - 1 - n

        @pl.when(i % chunk == chunk - 1)
        def _():
            for load in loads(i // chunk):
                load.wait()

        later = [None] * per_pack
        for frame in reversed(range(per_pack)):
            rows = slice(frame * seqs, (frame + 1) * seqs)
            values = now[...]
            later[frame] = values
            dh = d_ref[i, rows] + kept[...] + dot(values.astype(bf16), w[...])
            kept[...] = dh * u_ref[i, rows]
            for p in range(parts):
                cols = slice(p * units, (p + 1) * units)
                for k in range(3):
                    spot = slice((3 * p + k) * units, (3 * p + k + 1) * units)
                    now[:, spot] = dh[:, cols] * k_ref[k, i, rows, cols]
        stacked = jnp.concatenate(later, axis=0).astype(bf16)
        for p in range(parts):
            b_ref[p, i] = stacked[:, p * 3 * units : (p + 1) * 3 * units]

        @pl.when(i % chunk == 0)
        def _():
            for store in stores(i // chunk):
                store.start()

        return carry

    lax.fori_loop(0, packs, pack, 0)
    for c in range(chunks):
        for store in stores(c):
            store.wait()


def head_block(h_ref, e_ref, t_ref, m_ref, r_ref, w_hbm, back_ref, d_ref, loss_ref, w_ref, w_sem):
    parts = w_ref.shape[0]
    loads = [copy(w_hbm.at[p], w_ref.at[p], w_sem.at[p]) for p in range(parts)]
    for load in loads:
        load.start()
    units = w_ref.shape[2]
    rows = h_ref.shape[0]
    low = h_ref[...]
    back_ref[0] = low
    mask = m_ref[...]
    given = jnp.zeros((rows, 128), f32)
    normal = jnp.zeros((1, rows), f32)
    for p in range(parts):
        loads[p].wait()
        post = dot(low, w_ref[p, :H]) + dot(e_ref[...], w_ref[p, H : H + E])
        prior = dot(low, w_ref[p, H + E :])
        for head, logits in enumerate((prior, post)):
            for piece in range(units // 128):
                l = logits[:, piece * 128 : (piece + 1) * 128]
                cols = slice(p * units + piece * 128, p * units + (piece + 1) * 128)
                target = t_ref[:, cols].astype(f32)
                turned = l.T.reshape(128 // ZC, ZC, rows)
                top = jnp.max(turned, axis=1, keepdims=True)
                e = jnp.exp(turned - top)
                total = jnp.sum(e, axis=1, keepdims=True)
                normal = normal + jnp.sum(top + jnp.log(total), axis=0)
                probs = (e * (1.0 / total)).reshape(128, rows).T
                given = given + target * l
                back_ref[head + 2, :, cols] = (mask * (probs - target)).astype(bf16)
    loss_ref[...] = jnp.sum(r_ref[...] * normal, axis=1, keepdims=True) - jnp.sum(
        jnp.sum(mask * given, axis=0, keepdims=True), axis=1, keepdims=True
    )
    direct = jnp.zeros((rows, H), f32)
    for p in range(parts):
        cols = slice(p * units, (p + 1) * units)
        direct = direct + dot_nt(back_ref[2, :, cols], w_ref[p, H + E :])
        direct = direct + dot_nt(back_ref[3, :, cols], w_ref[p, :H])
    d_ref[...] = direct


def head_grads(spot_ref, scale_ref, r_hbm, e_hbm, earlier_ref, o_ref, h_ref, r_ref, e_ref, sems):
    parts, rows = e_ref.shape[0], e_ref.shape[1]
    units = o_ref.shape[1]
    frames = parts * rows
    scale = scale_ref[0]
    own = pl.ds(pl.multiple_of(spot_ref[0] * units, units), units)
    loads = [
        copy(r_hbm.at[:, pl.ds(2, 2), :, own], r_ref, sems.at[0]),
        copy(r_hbm.at[:, 0], h_ref, sems.at[1]),
        copy(e_hbm, e_ref, sems.at[2]),
    ]
    for load in loads:
        load.start()
    loads[0].wait()
    loads[1].wait()
    post = r_ref[:, 1].reshape(frames, units)
    both = jnp.concatenate([post, r_ref[:, 0].reshape(frames, units)], axis=1)
    for m in range(H // 256):
        spot = slice(m * 256, (m + 1) * 256)
        grad = (dot_tn(h_ref[:, :, spot].reshape(frames, 256), both) * scale).astype(bf16)
        o_ref[m * 256 : (m + 1) * 256] = grad[:, :units]
        o_ref[H + E + m * 256 : H + E + (m + 1) * 256] = grad[:, units:]
    loads[2].wait()
    for m in range(E // 256):
        spot = slice(m * 256, (m + 1) * 256)
        grad = (dot_tn(e_ref[:, :, spot].reshape(frames, 256), post) * scale).astype(bf16)
        o_ref[H + m * 256 : H + (m + 1) * 256] = grad


def gru_grads(
    spot_ref, scale_ref, one_hbm, r_hbm, b_hbm, earlier_ref, o_ref, one_ref, l_ref, b_ref, sems
):
    parts, rows = b_ref.shape[1], b_ref.shape[2]
    units = o_ref.shape[2]
    frames = parts * rows
    share = o_ref.shape[1] // 3
    half = o_ref.shape[0] // 2
    scale = scale_ref[0]
    me = spot_ref[1]
    loads = [copy(b_hbm, b_ref, sems.at[0]), copy(one_hbm, one_ref, sems.at[1])]
    for z in range(half):
        spot = pl.ds(pl.multiple_of((z * 2 + me) * share, share), share)
        loads.append(copy(r_hbm.at[:, 0, :, spot], l_ref.at[0, z], sems.at[2 + 2 * z]))
        loads.append(copy(r_hbm.at[:, 1, :, spot], l_ref.at[1, z], sems.at[3 + 2 * z]))
    for load in loads:
        load.start()
    loads[0].wait()
    loads[1].wait()
    back = [b_ref[x].reshape(frames, 3 * units) for x in (me, 1 - me)]
    for z in range(2 * half):
        if z < half:
            spot = slice(z * share, (z + 1) * share)
            left = [one_ref[x, :, spot] for x in (me, 1 - me)]
        else:
            loads[2 * (z - half) + 2].wait()
            loads[2 * (z - half) + 3].wait()
            left = [l_ref[n, z - half].reshape(frames, share) for n in (0, 1)]
        grad = (dot_tn(left[0], back[0]) + dot_tn(left[1], back[1])) * scale
        grad = grad.astype(bf16)
        for k in range(3):
            o_ref[z, k * share : (k + 1) * share] = grad[:, k * units : (k + 1) * units]


def orthogonal_block(base, tile, own_ref, g_ref, *refs):
    o_ref, x, a, b = refs[-4:]
    side, width = g_ref.shape
    share = o_ref.shape[0]
    own = pl.ds(pl.multiple_of(own_ref[0] * share, share), share)
    wide = own_ref[1] > 0

    def either(run):
        pl.when(wide)(functools.partial(run, width))
        pl.when(jnp.logical_not(wide))(functools.partial(run, base))

    def squares(i, total):
        rows = pl.ds(pl.multiple_of(i * 128, 128), 128)
        v = g_ref[rows, :].astype(f32)
        return total + jnp.sum(v * v)

    total = lax.fori_loop(0, side // 128, squares, jnp.zeros((), f32))
    scale = 1.0 / (jnp.sqrt(jnp.full((1, 128), total, f32)) + tiny_value)
    scale = scale[:, :1]

    def shrink(i, carry):
        rows = pl.ds(pl.multiple_of(i * 128, 128), 128)
        x[rows, :] = (g_ref[rows, :].astype(f32) * scale).astype(bf16)
        return carry

    lax.fori_loop(0, side // 128, shrink, 0)

    def lower(out, product):
        for start in range(0, side, 256):
            stop = start + 256
            block = product(slice(start, side), slice(start, stop)).astype(bf16)
            out[start:, start:stop] = block
            if stop < side:
                out[start:stop, stop:] = block[256:].T

    def square(depth):
        lower(a, lambda rows, cols: dot_nt(x[rows, :depth], x[cols, :depth]))

    def mix():
        lower(
            b,
            lambda rows, cols: coeff_cubic * a[rows, cols].astype(f32)
            + coeff_quintic * dot(a[rows, :], a[:, cols]),
        )

    def renew_all(depth):
        for start in range(0, depth, tile):
            cols = slice(start, start + tile)
            x[:, cols] = (
                coeff_linear * x[:, cols].astype(f32) + dot(b[...], x[:, cols])
            ).astype(bf16)

    def sweep(s, carry):
        either(square)
        mix()
        either(renew_all)
        return carry

    lax.fori_loop(0, 4, sweep, 0)
    either(square)
    part = (coeff_cubic * a[own, :].astype(f32) + coeff_quintic * dot(a[own, :], a[...])).astype(bf16)

    def last(j, carry):
        cols = pl.ds(pl.multiple_of(j * tile, tile), tile)
        o_ref[:, cols] = (
            coeff_linear * x[own, cols].astype(f32) + dot(part, x[:, cols])
        ).astype(bf16)
        return carry

    lax.fori_loop(0, width // tile, last, 0)


def turn_block(tile, g_ref, o_ref):
    def block(i, carry):
        spot = pl.ds(pl.multiple_of(i * tile, tile), tile)
        o_ref[:, spot] = g_ref[spot, :].T
        return carry

    lax.fori_loop(0, g_ref.shape[0] // tile, block, 0)


def collect_block(base, spot_ref, *refs):
    *pieces, o_ref, rows = refs
    steps = len(pieces)
    more = pieces[0].shape[0] - base
    for step, piece in enumerate(pieces):
        d = spot_ref[0] ^ step
        o_ref[:, pl.ds(pl.multiple_of(d * base, base), base)] = piece[:base].T
        rows[pl.ds(pl.multiple_of(d * more, more), more), :] = piece[base:]
    o_ref[:, steps * base :] = rows[...].T


def deal_block(base, spot_ref, g_ref, o_ref, rows):
    steps, widest = o_ref.shape[:2]
    more = widest - base
    rows[...] = g_ref[:, steps * base :].T
    for step in range(steps):
        d = spot_ref[0] ^ step
        o_ref[step, :base] = g_ref[:, pl.ds(pl.multiple_of(d * base, base), base)].T
        o_ref[step, base:] = rows[pl.ds(pl.multiple_of(d * more, more), more), :]


def finish_block(owners, spot_ref, *refs):
    pieces, (gru_ref, post_ref, prior_ref), (gru_out, post_out, prior_out), all_ref = (
        refs[:-7],
        refs[-7:-4],
        refs[-4:-1],
        refs[-1],
    )
    for step, piece in enumerate(pieces):
        all_ref[step] = piece[...]

    def renewed(old, m):
        change = all_ref[spot_ref[0] ^ owners[m], : old.shape[0]].astype(f32)
        factor = learn_rate * update_scale * math.sqrt(max(ROWS[m], Z))
        return old * (1.0 - learn_rate * weight_decay) - factor * change

    for k in range(3):
        gru_out[k] = renewed(gru_ref[k], k)
    post_out[...] = renewed(post_ref[...], 3)
    prior_out[...] = renewed(prior_ref[...], 4)


def in_vmem(count):
    return [pl.BlockSpec(memory_space=pltpu.VMEM)] * count


def cost(flops, touched):
    return pl.CostEstimate(flops=int(flops), bytes_accessed=int(touched), transcendentals=0)


def run_forward(spot, inputs, weights, seqs):
    parts, packs = inputs.shape[:2]
    units = weights[0].shape[2]
    chunks = packs // CHUNK
    return pl.pallas_call(
        functools.partial(scan_forward, seqs, CHUNK),
        out_shape=[
            jax.ShapeDtypeStruct((packs, PACK, H), bf16),
            jax.ShapeDtypeStruct((3, packs, PACK, H), f32),
            jax.ShapeDtypeStruct((packs, PACK, H), f32),
            jax.ShapeDtypeStruct((3 * H, H), bf16),
        ],
        in_specs=in_smem(1) + in_vmem(1) + anywhere(parts),
        out_specs=in_vmem(1) + anywhere(3),
        scratch_shapes=[
            pltpu.VMEM((seqs, H), f32),
            pltpu.VMEM((parts, 3, H, units), bf16),
            pltpu.VMEM((3, packs, PACK, H), f32),
            pltpu.VMEM((packs, PACK, H), f32),
            pltpu.VMEM((3 * H, H), bf16),
            pltpu.SemaphoreType.DMA((parts,)),
            pltpu.SemaphoreType.DMA((chunks,)),
            pltpu.SemaphoreType.DMA((chunks,)),
            pltpu.SemaphoreType.DMA,
        ],
        compiler_params=pltpu.CompilerParams(vmem_limit_bytes=LARGE),
        cost_estimate=cost(6e10, 20 * mib),
        name="scan_forward",
    )(spot, inputs, *weights)


def run_backward(direct, factors, rest, turned, parts, seqs, copies):
    packs = direct.shape[0]
    units = H // parts
    chunks = packs // CHUNK
    return pl.pallas_call(
        functools.partial(scan_backward, seqs, CHUNK),
        out_shape=jax.ShapeDtypeStruct((copies, parts, packs, PACK, 3 * units), bf16),
        in_specs=in_vmem(1) + anywhere(3),
        out_specs=anywhere(1)[0],
        scratch_shapes=[
            pltpu.VMEM((seqs, 3 * H), f32),
            pltpu.VMEM((seqs, H), f32),
            pltpu.VMEM((3 * H, H), bf16),
            pltpu.VMEM((3, packs, PACK, H), f32),
            pltpu.VMEM((packs, PACK, H), f32),
            pltpu.VMEM((parts, packs, PACK, 3 * units), bf16),
            pltpu.SemaphoreType.DMA,
            pltpu.SemaphoreType.DMA((chunks,)),
            pltpu.SemaphoreType.DMA((chunks,)),
            pltpu.SemaphoreType.DMA((copies * chunks,)),
        ],
        compiler_params=pltpu.CompilerParams(vmem_limit_bytes=LARGE),
        cost_estimate=cost(6e10, 20 * mib),
        name="scan_backward",
    )(direct, factors, rest, turned)


def run_heads(hidden, embed, target, mask, mask_row, weights):
    rows = hidden.shape[0]
    return pl.pallas_call(
        head_block,
        out_shape=[
            jax.ShapeDtypeStruct((4, rows, Z), bf16),
            jax.ShapeDtypeStruct((rows, H), f32),
            jax.ShapeDtypeStruct((1, 1), f32),
        ],
        in_specs=in_vmem(5) + anywhere(1),
        out_specs=in_vmem(3),
        scratch_shapes=[
            pltpu.VMEM(weights.shape, bf16),
            pltpu.SemaphoreType.DMA((weights.shape[0],)),
        ],
        compiler_params=pltpu.CompilerParams(vmem_limit_bytes=LARGE),
        cost_estimate=cost(1e10, 12 * mib),
        name="heads",
    )(hidden, embed, target, mask, mask_row, weights)


def in_smem(count):
    return [pl.BlockSpec(memory_space=pltpu.SMEM)] * count


def anywhere(count):
    return [pl.BlockSpec(memory_space=pl.ANY)] * count


def run_head_grads(spot, scale, everyone, embed, earlier):
    parts, rows = embed.shape[:2]
    units = H // parts
    return pl.pallas_call(
        head_grads,
        out_shape=jax.ShapeDtypeStruct((H + E + H, units), bf16),
        in_specs=in_smem(2) + anywhere(3),
        out_specs=in_vmem(1)[0],
        scratch_shapes=[
            pltpu.VMEM((parts, rows, H), bf16),
            pltpu.VMEM((parts, 2, rows, units), bf16),
            pltpu.VMEM(embed.shape, bf16),
            pltpu.SemaphoreType.DMA((3,)),
        ],
        compiler_params=pltpu.CompilerParams(vmem_limit_bytes=LARGE),
        cost_estimate=cost(4e9, 12 * mib),
        name="head_grads",
    )(spot, scale, everyone, embed, earlier)


def run_gru_grads(spot, scale, onehot, everyone, back, earlier, dz_count):
    parts, rows = back.shape[1:3]
    units = back.shape[3] // 3
    share = (Z + H) // (2 * dz_count)
    return pl.pallas_call(
        gru_grads,
        out_shape=jax.ShapeDtypeStruct((dz_count, 3 * share, units), bf16),
        in_specs=in_smem(2) + anywhere(4),
        out_specs=in_vmem(1)[0],
        scratch_shapes=[
            pltpu.VMEM(onehot.shape, bf16),
            pltpu.VMEM((2, dz_count // 2, parts, rows, share), bf16),
            pltpu.VMEM(back.shape, bf16),
            pltpu.SemaphoreType.DMA((2 + dz_count,)),
        ],
        compiler_params=pltpu.CompilerParams(vmem_limit_bytes=LARGE),
        cost_estimate=cost(4e9, 12 * mib),
        name="gru_grads",
    )(spot, scale, onehot, everyone, back, earlier)


def plain_gru_grads(dx_index, scale, onehot, everyone, back, dz_count):
    units = back.shape[3] // 3
    share = (Z + H) // (2 * dz_count)
    total = 0.0
    for states, x in ((everyone[:, 0], dx_index), (everyone[:, 1], 1 - dx_index)):
        states = states.reshape(-1, dz_count // 2, 2, share)
        states = lax.dynamic_index_in_dim(states, dx_index, 2, keepdims=False)
        ones = lax.dynamic_index_in_dim(onehot, x, 0, keepdims=False)
        left = jnp.concatenate([ones, states.reshape(ones.shape)], axis=1)
        right = lax.dynamic_index_in_dim(back, x, 0, keepdims=False)
        total = total + dot_tn(left, right.reshape(-1, 3 * units))
    grads = (total * scale).astype(bf16).reshape(dz_count, share, 3, units)
    return jnp.swapaxes(grads, 1, 2).reshape(dz_count, 3 * share, units)


def run_orthogonal(base, share, own, matrix, earlier):
    side, width = matrix.shape
    return pl.pallas_call(
        functools.partial(orthogonal_block, base, 512),
        out_shape=jax.ShapeDtypeStruct((share, width), bf16),
        in_specs=in_smem(1) + in_vmem(1) + anywhere(len(earlier)),
        out_specs=in_vmem(1)[0],
        scratch_shapes=[
            pltpu.VMEM((side, width), bf16),
            pltpu.VMEM((side, side), bf16),
            pltpu.VMEM((side, side), bf16),
        ],
        compiler_params=pltpu.CompilerParams(vmem_limit_bytes=28 * mib),
        cost_estimate=cost(5e10, 6 * mib),
        name="orthogonal",
    )(own, matrix, *earlier)


def run_turn(matrix):
    return pl.pallas_call(
        functools.partial(turn_block, 256),
        out_shape=jax.ShapeDtypeStruct(matrix.shape[::-1], bf16),
        in_specs=in_vmem(1),
        out_specs=in_vmem(1)[0],
        compiler_params=pltpu.CompilerParams(vmem_limit_bytes=6 * mib),
        cost_estimate=cost(1e6, 3 * mib),
        name="turn",
    )(matrix)


def small_kernel(body, out_shape, scratch, specs, arguments, name):
    return pl.pallas_call(
        body,
        out_shape=out_shape,
        in_specs=specs,
        out_specs=jax.tree.map(lambda _: in_vmem(1)[0], out_shape),
        scratch_shapes=scratch,
        compiler_params=pltpu.CompilerParams(vmem_limit_bytes=8 * mib),
        cost_estimate=cost(1e6, 4 * mib),
        name=name,
    )(*arguments)


def run_collect(spot, pieces, base):
    steps = len(pieces)
    widest, units = pieces[0].shape
    return small_kernel(
        functools.partial(collect_block, base),
        jax.ShapeDtypeStruct((units, steps * widest), bf16),
        [pltpu.VMEM((steps * (widest - base), units), bf16)],
        in_smem(1) + in_vmem(steps),
        (spot, *pieces),
        "collect",
    )


def run_deal(spot, result, steps, base):
    units, width = result.shape
    widest = width // steps
    return small_kernel(
        functools.partial(deal_block, base),
        jax.ShapeDtypeStruct((steps, widest, units), bf16),
        [pltpu.VMEM((steps * (widest - base), units), bf16)],
        in_smem(1) + in_vmem(1),
        (spot, result),
        "deal",
    )


def run_finish(owners, spot, pieces, rows):
    return small_kernel(
        functools.partial(finish_block, owners),
        [jax.ShapeDtypeStruct(block.shape, f32) for block in rows],
        [pltpu.VMEM((len(pieces), *pieces[0].shape), bf16)],
        in_smem(1) + in_vmem(len(pieces) + len(rows)),
        (spot, *pieces, *rows),
        "finish",
    )


def on_device(
    embeddings,
    samples,
    seq_lengths,
    gru_weight,
    post_weight,
    prior_weight,
    gru_moment,
    post_moment,
    prior_moment,
):
    dz_count = lax.axis_size("dz")
    dx_count = lax.axis_size("dx")
    tp_count = lax.axis_size("tp")
    dp_count = dz_count * dx_count
    dx_index = lax.axis_index("dx")
    tp_index = lax.axis_index("tp")
    dp_index = lax.axis_index("dz") * dx_count + dx_index
    seq_count = embeddings.shape[0]
    seqs = seq_count // tp_count
    units = gru_weight.shape[2]
    groups = Z // ZC
    rows = seqs * FRAMES
    packs = rows // PACK

    def gather(block):
        return lax.all_gather(block, "tp", axis=0, tiled=False)

    def exchange(block, axis):
        return lax.all_to_all(block, axis, 0, 0, tiled=True)

    def mine(block, axis):
        return lax.dynamic_index_in_dim(block, dx_index, axis, keepdims=False)

    def across(block, bit):
        return lax.ppermute(block, "tp", [(i, i ^ bit) for i in range(tp_count)])

    own_hidden = gru_weight[:, Z:].astype(bf16)
    far = across(own_hidden, 2)
    near = across(own_hidden, 1)
    gru_input = lax.optimization_barrier(gru_weight)
    head_low = jnp.concatenate([post_weight.astype(bf16), prior_weight.astype(bf16)], axis=0)

    by_part = jnp.swapaxes(samples.reshape(tp_count, seqs, FRAMES, groups), 1, 2)
    by_part = by_part.reshape(tp_count * rows, groups).astype(bf16)

    def one_hot(chosen):
        count = chosen.shape[-1]
        classes = jnp.arange(count * ZC, dtype=jnp.int32)
        expand = (classes[None, :] // ZC == jnp.arange(count)[:, None]).astype(bf16)
        return (dot(chosen, expand) == (classes % ZC).astype(f32)).astype(bf16)

    onehot = one_hot(by_part)
    input_part = jnp.concatenate(
        [dot(onehot, gru_input[k, :Z].astype(bf16)).astype(bf16) for k in range(3)], axis=1
    ).reshape(tp_count, packs, PACK, 3 * units)
    input_part = exchange(input_part, "tp")
    embed_rows = jnp.swapaxes(embeddings.reshape(tp_count, seqs, FRAMES, E), 1, 2)
    embed_rows = embed_rows.reshape(tp_count, rows, E)
    pair_samples = lax.all_gather(by_part, "dx", axis=0, tiled=False)
    half = Z // dx_count
    pair_half = mine(
        pair_samples.reshape(dx_count * tp_count * rows, dz_count // 2, dx_count, -1), 2
    )
    pair_onehot = one_hot(pair_half.reshape(dx_count * tp_count * rows, groups // dx_count))
    pair_onehot = pair_onehot.reshape(dx_count, tp_count * rows, half)
    own_embed = lax.dynamic_index_in_dim(embed_rows, tp_index, 0, keepdims=False)
    onehot = onehot.reshape(tp_count, rows, Z)
    own_target = lax.dynamic_index_in_dim(onehot, tp_index, 0, keepdims=False)
    positions = jnp.arange(FRAMES, dtype=jnp.int32)
    own_lengths = lax.dynamic_slice_in_dim(seq_lengths, tp_index * seqs, seqs, 0)
    frame_mask = (positions[:, None] < own_lengths[None, :]).astype(f32)
    mask_lanes = jnp.broadcast_to(frame_mask.reshape(rows, 1), (rows, 128))

    weights = [own_hidden, near, far, across(far, 1)]
    every_mask = (positions[:, None] < seq_lengths[None, :]).astype(f32)
    frame_count = jnp.broadcast_to(jnp.sum(every_mask), (8, 128))
    for axis, bits in (("dx", dx_count), ("dz", dz_count)):
        for bit in range(bits.bit_length() - 1):
            pairs = [(i, i ^ (1 << bit)) for i in range(bits)]
            frame_count = frame_count + lax.ppermute(frame_count, axis, pairs)
    frame_count = frame_count[0, 0]
    scale = (1.0 / frame_count).reshape(1)

    early = (head_low, own_embed, own_target, mask_lanes, embed_rows, pair_onehot, scale)
    weights, input_part, early = lax.optimization_barrier((weights, input_part, early))
    head_low, own_embed, own_target, mask_lanes, embed_rows, pair_onehot, scale = early
    head_full = gather(head_low)
    hidden, factors, rest, turned = run_forward(tp_index.astype(jnp.int32).reshape(1), input_part, weights, seqs)
    hidden = hidden.reshape(rows, H)
    swap = [(i, i ^ 1) for i in range(dx_count)]
    neighbour = lax.ppermute(hidden, "dx", swap)
    backs, direct, loss_lanes = run_heads(
        hidden, own_embed, own_target, mask_lanes, frame_mask.reshape(1, rows), head_full
    )
    everyone = gather(lax.dynamic_update_slice(backs, neighbour[None], (1, 0, 0)))
    back = run_backward(
        direct.reshape(packs, PACK, H), factors, rest, turned, tp_count, seqs, dx_count
    )
    own_back = exchange(back.reshape(dx_count * tp_count, rows, 3 * units), ("dx", "tp"))
    own_back = own_back.reshape(dx_count, tp_count, rows, 3 * units)

    shares = [size // dp_count for size in ROWS]
    all_post = everyone[:, 3]
    spot = jnp.stack([tp_index, dx_index]).astype(jnp.int32)

    head_grad = run_head_grads(spot, scale, everyone, embed_rows, back)
    own_back, _ = lax.optimization_barrier((own_back, head_grad))

    head_grad = jnp.concatenate(
        [
            block.reshape(dz_count, dx_count, -1, units)
            for block in (head_grad[: H + E], head_grad[H + E :])
        ],
        axis=2,
    )

    def share_rows(block):
        return lax.psum_scatter(block, "dz", scatter_dimension=0, tiled=True)[0]

    head_done = share_rows(head_grad)
    if shares[0] % 128 == 0:
        gru_grad = run_gru_grads(
            spot, scale, pair_onehot, everyone, own_back, head_grad, dz_count
        )
    else:
        gru_grad = plain_gru_grads(dx_index, scale, pair_onehot, everyone, own_back, dz_count)
    gru_grad, head_done = lax.optimization_barrier((gru_grad, head_done))
    gru_sum = share_rows(gru_grad).astype(f32)
    received = lax.ppermute(
        lax.dynamic_index_in_dim(head_done, 1 - dx_index, 0, keepdims=False), "dx", swap
    )
    head_sum = mine(head_done, 0).astype(f32) + received.astype(f32)
    loss_sum = jnp.broadcast_to(jnp.sum(loss_lanes), (8, 128))
    for axis, bits in (("tp", tp_count), ("dx", dx_count), ("dz", dz_count)):
        for bit in range(bits.bit_length() - 1):
            pairs = [(i, i ^ (1 << bit)) for i in range(bits)]
            loss_sum = loss_sum + lax.ppermute(loss_sum, axis, pairs)
    loss_sum = loss_sum[0, 0]
    loss_value = loss_sum / frame_count

    embed_part = E // tp_count
    own_rows_e = lax.dynamic_slice_in_dim(head_full, H + tp_index * embed_part, embed_part, 1)
    post_by_seq = jnp.swapaxes(all_post.reshape(tp_count, FRAMES, seqs, Z), 1, 2)
    embed_grad = jnp.einsum(
        "psfk,ek->psfe",
        post_by_seq,
        jnp.concatenate(list(own_rows_e), axis=1),
        preferred_element_type=f32,
    ).reshape(seq_count, FRAMES, embed_part)
    embed_grad = embed_grad * scale[0]

    grads = [gru_sum[k * shares[0] : (k + 1) * shares[0]] for k in range(3)]
    grads += [head_sum[: shares[3]], head_sum[shares[3] :]]

    def own_rows(matrix, axis_dim):
        share = matrix.shape[axis_dim] // dp_count
        return lax.dynamic_slice_in_dim(matrix, dp_index * share, share, axis_dim)

    gru_moments = own_rows(gru_moment, 1)
    moments = [momentum_keep * gru_moments[k] + grads[k] for k in range(3)]
    moments.append(momentum_keep * own_rows(post_moment, 0) + grads[3])
    moments.append(momentum_keep * own_rows(prior_moment, 0) + grads[4])
    ahead = [(grads[m] + momentum_keep * moments[m]).astype(bf16) for m in range(MATS)]

    owners = [m * dp_count // 8 for m in (0, 3, 4, 7, 5)]
    widest = max(shares)
    base = shares[0]
    holds_post = (dp_index == owners[3]).astype(jnp.int32)
    if dp_count == 8:
        kept = jnp.array([owners.index(d) if d in owners else 0 for d in range(dp_count)])
        blocks = jnp.stack(
            [jnp.pad(block, ((0, widest - block.shape[0]), (0, 0))) for block in ahead]
        )
        where = dp_index.astype(jnp.int32).reshape(1)
        pieces = []
        for step in range(dp_count):
            block = lax.dynamic_index_in_dim(blocks, kept[dp_index ^ step], 0, keepdims=False)
            if step > 0:
                block = lax.ppermute(block, ("dz", "dx"), [(d ^ step, d) for d in owners])
            pieces.append(block)
        turned = run_collect(where, pieces, base)
    else:
        slots = [jnp.zeros((widest, units), bf16)] * dp_count
        for m in range(MATS):
            slots[owners[m]] = jnp.pad(ahead[m], ((0, widest - shares[m]), (0, 0)))
        arrived = exchange(jnp.stack(slots), ("dz", "dx"))
        turned = run_turn(
            jnp.concatenate(
                [arrived[:, :base].reshape(-1, units), arrived[:, base:].reshape(-1, units)], axis=0
            )
        )
    wide = gather(turned).reshape(H, dp_count * widest)
    own = jnp.stack([tp_index, holds_post]).astype(jnp.int32)
    old_rows = (own_rows(gru_weight, 1), own_rows(post_weight, 0), own_rows(prior_weight, 0))
    old_rows = lax.optimization_barrier(old_rows)
    result = run_orthogonal(
        dp_count * base, units, own, wide, (embed_grad, loss_value.reshape(1, 1), *old_rows)
    )
    if dp_count == 8:
        dealt = run_deal(where, result, dp_count, base)
        pieces = [dealt[0]]
        for step in range(1, dp_count):
            pairs = [(d, d ^ step) for d in owners]
            pieces.append(lax.ppermute(dealt[step], ("dz", "dx"), pairs))
        new_gru, new_post, new_prior = run_finish(owners, where, pieces, old_rows)
    else:
        result = result.T
        results = exchange(
            jnp.concatenate(
                [
                    result[: dp_count * base].reshape(dp_count, base, units),
                    result[dp_count * base :].reshape(dp_count, widest - base, units),
                ],
                axis=1,
            ),
            ("dz", "dx"),
        )

        def renew(old, m):
            factor = learn_rate * update_scale * math.sqrt(max(ROWS[m], Z))
            change = results[owners[m], : old.shape[0]].astype(f32)
            return old * (1.0 - learn_rate * weight_decay) - factor * change

        new_gru = jnp.stack([renew(old_rows[0][k], k) for k in range(3)])
        new_post = renew(old_rows[1], 3)
        new_prior = renew(old_rows[2], 4)
    return (
        loss_value,
        embed_grad,
        new_gru,
        new_post,
        new_prior,
        jnp.stack(moments[:3]),
        moments[3],
        moments[4],
    )

def solution(mesh):
    dp_count, tp_count = mesh.devices.shape
    mesh = jax.sharding.Mesh(
        mesh.devices.reshape(dp_count // 2, 2, tp_count), ("dz", "dx", "tp")
    )
    dp = ("dz", "dx")
    in_specs = (
        P(dp, None, None),
        P(dp, None, None),
        P(dp),
        P(None, None, "tp"),
        P(None, "tp"),
        P(None, "tp"),
        P(None, None, "tp"),
        P(None, "tp"),
        P(None, "tp"),
    )
    out_specs = (
        P(),
        P(dp, None, "tp"),
        P(None, dp, "tp"),
        P(dp, "tp"),
        P(dp, "tp"),
        P(None, dp, "tp"),
        P(dp, "tp"),
        P(dp, "tp"),
    )
    return jax.shard_map(
        on_device, mesh=mesh, in_specs=in_specs, out_specs=out_specs, check_vma=False
    )
```

```python
import functools
import math

import jax
import jax.numpy as jnp
import numpy as np
from jax import lax
from jax.experimental import pallas as pl
from jax.experimental.pallas import tpu as pltpu
from jax.sharding import PartitionSpec as P

H = 1024
ZC = 32
E = 1536
FRAMES = 56
MATS = 5
Z = 1024
ROWS = (Z + H, Z + H, Z + H, H + E, H)
PACK = 8
CHUNK = 4


coeff_linear = 3.4445
coeff_cubic = -4.775
coeff_quintic = 2.0315
momentum_keep = 0.95
learn_rate = 0.2
weight_decay = 0.01
update_scale = 0.2
tiny_value = 1e-07
mib = 1 << 20
LARGE = 56 * mib
f32 = jnp.float32
bf16 = jnp.bfloat16
NT = (((1,), (1,)), ((), ()))
TN = (((0,), (0,)), ((), ()))


def dot(left, right):
    return jnp.dot(left, right, preferred_element_type=f32)


def dot_tn(left, right):
    return lax.dot_general(left, right, TN, preferred_element_type=f32)


def dot_nt(left, right):
    return lax.dot_general(left, right, NT, preferred_element_type=f32)


def copy(source, target, semaphore):
    return pltpu.make_async_copy(source, target, semaphore)


def scan_forward(
    seqs, chunk, spot_ref, x_ref, *refs
):
    parts, packs = x_ref.shape[:2]
    shards = refs[:parts]
    h_ref, k_hbm, u_hbm, t_hbm, state, w, k_ref, u_ref, t, w_sem, k_sem, u_sem, t_sem = refs[parts:]
    units = w.shape[3]
    per_pack = PACK // seqs
    loads = [copy(shards[n], w.at[spot_ref[0] ^ n], w_sem.at[n]) for n in range(parts)]
    for load in loads:
        load.start()
    state[...] = jnp.zeros_like(state)
    for load in loads:
        load.wait()

    def stores(c):
        at = pl.ds(c * chunk, chunk)
        return (
            copy(k_ref.at[:, at], k_hbm.at[:, at], k_sem.at[c]),
            copy(u_ref.at[at], u_hbm.at[at], u_sem.at[c]),
        )

    def pack(i, carry):
        states = []
        for frame in range(per_pack):
            rows = slice(frame * seqs, (frame + 1) * seqs)
            if frame == 0:
                source, live = jnp.maximum(i - 1, 0), jnp.where(i > 0, 1.0, 0.0)
                spot = slice((per_pack - 1) * seqs, per_pack * seqs)
            else:
                source, live = i, None
                spot = slice((frame - 1) * seqs, frame * seqs)
            before = state[...]
            low = before.astype(bf16)
            news = []
            for p in range(parts):
                cols = slice(p * units, (p + 1) * units)
                given = x_ref[p, source].astype(f32)[spot]
                if live is not None:
                    given = given * live
                pre = [
                    given[:, k * units : (k + 1) * units] + dot(low, w[p, k]) for k in range(3)
                ]
                last = before[:, cols]
                r = jax.nn.sigmoid(pre[0])
                c = jnp.tanh(r * pre[1])
                u = jax.nn.sigmoid(pre[2] - 1.0)
                rest = 1.0 - u
                new = u * c + rest * last
                inner = u * (1.0 - c * c)
                state[:, cols] = new
                news.append(new)
                k_ref[0, i, rows, cols] = inner * pre[1] * r * (1.0 - r)
                k_ref[1, i, rows, cols] = inner * r
                k_ref[2, i, rows, cols] = (c - last) * u * rest
                u_ref[i, rows, cols] = rest
            states.append(jnp.concatenate(news, axis=1))
        h_ref[i] = jnp.concatenate(states, axis=0).astype(bf16)

        @pl.when(i % chunk == chunk - 1)
        def _():
            for store in stores(i // chunk):
                store.start()

        return carry

    def pack_and_turn(i, carry):
        t[pl.ds(pl.multiple_of(i * units, units), units), :] = w[i // 3, i % 3].T
        return pack(i, carry)

    lax.fori_loop(0, 3 * parts, pack_and_turn, 0)
    turned = copy(t, t_hbm, t_sem)
    turned.start()
    lax.fori_loop(3 * parts, packs, pack, 0)
    turned.wait()
    for c in range(packs // chunk):
        for store in stores(c):
            store.wait()


def scan_backward(
    seqs, chunk, d_ref, k_hbm, u_hbm, t_hbm, b_hbm, now, kept, w, k_ref, u_ref, b_ref, t_sem, k_sem, u_sem, b_sem
):
    copies, parts, packs = b_hbm.shape[:3]
    units = b_ref.shape[3] // 3
    per_pack = PACK // seqs
    chunks = packs // chunk

    def loads(c):
        at = pl.ds(c * chunk, chunk)
        return (
            copy(k_hbm.at[:, at], k_ref.at[:, at], k_sem.at[c]),
            copy(u_hbm.at[at], u_ref.at[at], u_sem.at[c]),
        )

    def stores(c):
        at = pl.ds(c * chunk, chunk)
        return [
            copy(b_ref.at[:, at], b_hbm.at[n, :, at], b_sem.at[n * chunks + c]) for n in range(copies)
        ]

    turned = copy(t_hbm, w, t_sem)
    turned.start()
    for c in reversed(range(chunks)):
        for load in loads(c):
            load.start()
    now[...] = jnp.zeros_like(now)
    kept[...] = jnp.zeros_like(kept)
    turned.wait()

    def pack(n, carry):
        i = packs - 1 - n

        @pl.when(i % chunk == chunk - 1)
        def _():
            for load in loads(i // chunk):
                load.wait()

        later = [None] * per_pack
        for frame in reversed(range(per_pack)):
            rows = slice(frame * seqs, (frame + 1) * seqs)
            values = now[...]
            later[frame] = values
            dh = d_ref[i, rows] + kept[...] + dot(values.astype(bf16), w[...])
            kept[...] = dh * u_ref[i, rows]
            for p in range(parts):
                cols = slice(p * units, (p + 1) * units)
                for k in range(3):
                    spot = slice((3 * p + k) * units, (3 * p + k + 1) * units)
                    now[:, spot] = dh[:, cols] * k_ref[k, i, rows, cols]
        stacked = jnp.concatenate(later, axis=0).astype(bf16)
        for p in range(parts):
            b_ref[p, i] = stacked[:, p * 3 * units : (p + 1) * 3 * units]

        @pl.when(i % chunk == 0)
        def _():
            for store in stores(i // chunk):
                store.start()

        return carry

    lax.fori_loop(0, packs, pack, 0)
    for c in range(chunks):
        for store in stores(c):
            store.wait()


def head_block(
    spot_ref, h_ref, p_ref, t_ref, m_ref, r_ref, e_hbm, w_hbm, back_ref, d_ref, loss_ref, w_ref, n_ref, e_ref, w_sem, e_sem
):
    parts = w_ref.shape[0]
    embed = copy(e_hbm.at[spot_ref[0]], n_ref, e_sem)
    embed.start()
    loads = [copy(w_hbm.at[p], w_ref.at[p], w_sem.at[p]) for p in range(parts)]
    for load in loads:
        load.start()
    embed.wait()
    e_ref[...] = dot(p_ref[...], n_ref[...]).astype(bf16)
    units = w_ref.shape[2]
    rows = h_ref.shape[0]
    low = h_ref[...]
    back_ref[0] = low
    mask = m_ref[...]
    given = jnp.zeros((rows, 128), f32)
    normal = jnp.zeros((1, rows), f32)
    for p in range(parts):
        loads[p].wait()
        post = dot(low, w_ref[p, :H]) + dot(e_ref[...], w_ref[p, H : H + E])
        prior = dot(low, w_ref[p, H + E :])
        for head, logits in enumerate((prior, post)):
            for piece in range(units // 128):
                l = logits[:, piece * 128 : (piece + 1) * 128]
                cols = slice(p * units + piece * 128, p * units + (piece + 1) * 128)
                target = t_ref[:, cols].astype(f32)
                turned = l.T.reshape(128 // ZC, ZC, rows)
                top = jnp.max(turned, axis=1, keepdims=True)
                e = jnp.exp(turned - top)
                total = jnp.sum(e, axis=1, keepdims=True)
                normal = normal + jnp.sum(top + jnp.log(total), axis=0)
                probs = (e * (1.0 / total)).reshape(128, rows).T
                given = given + target * l
                back_ref[head + 2, :, cols] = (mask * (probs - target)).astype(bf16)
    loss_ref[...] = jnp.sum(r_ref[...] * normal, axis=1, keepdims=True) - jnp.sum(
        jnp.sum(mask * given, axis=0, keepdims=True), axis=1, keepdims=True
    )
    direct = jnp.zeros((rows, H), f32)
    for p in range(parts):
        cols = slice(p * units, (p + 1) * units)
        direct = direct + dot_nt(back_ref[2, :, cols], w_ref[p, H + E :])
        direct = direct + dot_nt(back_ref[3, :, cols], w_ref[p, :H])
    d_ref[...] = direct


def head_grads(spot_ref, scale_ref, p_ref, r_hbm, e_hbm, earlier_ref, o_ref, h_ref, r_ref, e_ref, sems):
    parts, rows = e_ref.shape[0], e_ref.shape[1]
    units = o_ref.shape[1]
    frames = parts * rows
    scale = scale_ref[0]
    own = pl.ds(pl.multiple_of(spot_ref[0] * units, units), units)
    loads = [
        copy(r_hbm.at[:, pl.ds(2, 2), :, own], r_ref, sems.at[0]),
        copy(r_hbm.at[:, 0], h_ref, sems.at[1]),
        copy(e_hbm, e_ref, sems.at[2]),
    ]
    for load in loads:
        load.start()
    loads[0].wait()
    loads[1].wait()
    post = r_ref[:, 1].reshape(frames, units)
    both = jnp.concatenate([post, r_ref[:, 0].reshape(frames, units)], axis=1)
    for m in range(H // 256):
        spot = slice(m * 256, (m + 1) * 256)
        grad = (dot_tn(h_ref[:, :, spot].reshape(frames, 256), both) * scale).astype(bf16)
        o_ref[m * 256 : (m + 1) * 256] = grad[:, :units]
        o_ref[H + E + m * 256 : H + E + (m + 1) * 256] = grad[:, units:]
    post = jnp.concatenate(
        [dot_tn(p_ref[...], r_ref[p, 1]).astype(bf16) for p in range(parts)], axis=0
    )
    loads[2].wait()
    for m in range(E // 256):
        spot = slice(m * 256, (m + 1) * 256)
        grad = (dot_tn(e_ref[:, :, spot].reshape(frames, 256), post) * scale).astype(bf16)
        o_ref[H + m * 256 : H + (m + 1) * 256] = grad


def gru_grads(
    spot_ref, scale_ref, one_hbm, r_hbm, b_hbm, earlier_ref, o_ref, one_ref, l_ref, b_ref, sems
):
    parts, rows = b_ref.shape[1], b_ref.shape[2]
    units = o_ref.shape[2]
    frames = parts * rows
    share = o_ref.shape[1] // 3
    half = o_ref.shape[0] // 2
    scale = scale_ref[0]
    me = spot_ref[1]
    loads = [copy(b_hbm, b_ref, sems.at[0]), copy(one_hbm, one_ref, sems.at[1])]
    for z in range(half):
        spot = pl.ds(pl.multiple_of((z * 2 + me) * share, share), share)
        loads.append(copy(r_hbm.at[:, 0, :, spot], l_ref.at[0, z], sems.at[2 + 2 * z]))
        loads.append(copy(r_hbm.at[:, 1, :, spot], l_ref.at[1, z], sems.at[3 + 2 * z]))
    for load in loads:
        load.start()
    loads[0].wait()
    loads[1].wait()
    back = [b_ref[x].reshape(frames, 3 * units) for x in (me, 1 - me)]
    for z in range(2 * half):
        if z < half:
            spot = slice(z * share, (z + 1) * share)
            left = [one_ref[x, :, spot] for x in (me, 1 - me)]
        else:
            loads[2 * (z - half) + 2].wait()
            loads[2 * (z - half) + 3].wait()
            left = [l_ref[n, z - half].reshape(frames, share) for n in (0, 1)]
        grad = (dot_tn(left[0], back[0]) + dot_tn(left[1], back[1])) * scale
        grad = grad.astype(bf16)
        for k in range(3):
            o_ref[z, k * share : (k + 1) * share] = grad[:, k * units : (k + 1) * units]


def orthogonal_block(base, tile, own_ref, g_ref, *refs):
    o_ref, x, a, b = refs[-4:]
    side, width = g_ref.shape
    share = o_ref.shape[0]
    own = pl.ds(pl.multiple_of(own_ref[0] * share, share), share)
    wide = own_ref[1] > 0

    def either(run):
        pl.when(wide)(functools.partial(run, width))
        pl.when(jnp.logical_not(wide))(functools.partial(run, base))

    def squares(i, total):
        rows = pl.ds(pl.multiple_of(i * 128, 128), 128)
        v = g_ref[rows, :].astype(f32)
        return total + jnp.sum(v * v)

    total = lax.fori_loop(0, side // 128, squares, jnp.zeros((), f32))
    scale = 1.0 / (jnp.sqrt(jnp.full((1, 128), total, f32)) + tiny_value)
    scale = scale[:, :1]

    def shrink(i, carry):
        rows = pl.ds(pl.multiple_of(i * 128, 128), 128)
        x[rows, :] = (g_ref[rows, :].astype(f32) * scale).astype(bf16)
        return carry

    lax.fori_loop(0, side // 128, shrink, 0)

    def lower(out, product):
        for start in range(0, side, 256):
            stop = start + 256
            block = product(slice(start, side), slice(start, stop)).astype(bf16)
            out[start:, start:stop] = block
            if stop < side:
                out[start:stop, stop:] = block[256:].T

    def square(depth):
        lower(a, lambda rows, cols: dot_nt(x[rows, :depth], x[cols, :depth]))

    def mix():
        lower(
            b,
            lambda rows, cols: coeff_cubic * a[rows, cols].astype(f32)
            + coeff_quintic * dot(a[rows, :], a[:, cols]),
        )

    def renew_all(depth):
        for start in range(0, depth, tile):
            cols = slice(start, start + tile)
            x[:, cols] = (
                coeff_linear * x[:, cols].astype(f32) + dot(b[...], x[:, cols])
            ).astype(bf16)

    def sweep(s, carry):
        either(square)
        mix()
        either(renew_all)
        return carry

    lax.fori_loop(0, 4, sweep, 0)
    either(square)
    part = (coeff_cubic * a[own, :].astype(f32) + coeff_quintic * dot(a[own, :], a[...])).astype(bf16)

    def last(j, carry):
        cols = pl.ds(pl.multiple_of(j * tile, tile), tile)
        o_ref[:, cols] = (
            coeff_linear * x[own, cols].astype(f32) + dot(part, x[:, cols])
        ).astype(bf16)
        return carry

    lax.fori_loop(0, width // tile, last, 0)


def turn_block(tile, g_ref, o_ref):
    def block(i, carry):
        spot = pl.ds(pl.multiple_of(i * tile, tile), tile)
        o_ref[:, spot] = g_ref[spot, :].T
        return carry

    lax.fori_loop(0, g_ref.shape[0] // tile, block, 0)


def collect_block(base, spot_ref, *refs):
    *pieces, o_ref, rows = refs
    steps = len(pieces)
    more = pieces[0].shape[0] - base
    for step, piece in enumerate(pieces):
        d = spot_ref[0] ^ step
        o_ref[:, pl.ds(pl.multiple_of(d * base, base), base)] = piece[:base].T
        rows[pl.ds(pl.multiple_of(d * more, more), more), :] = piece[base:]
    o_ref[:, steps * base :] = rows[...].T


def deal_block(base, spot_ref, g_ref, o_ref, rows):
    steps, widest = o_ref.shape[:2]
    more = widest - base
    rows[...] = g_ref[:, steps * base :].T
    for step in range(steps):
        d = spot_ref[0] ^ step
        o_ref[step, :base] = g_ref[:, pl.ds(pl.multiple_of(d * base, base), base)].T
        o_ref[step, base:] = rows[pl.ds(pl.multiple_of(d * more, more), more), :]


def finish_block(owners, spot_ref, *refs):
    pieces, (gru_ref, post_ref, prior_ref), (gru_out, post_out, prior_out), all_ref = (
        refs[:-7],
        refs[-7:-4],
        refs[-4:-1],
        refs[-1],
    )
    for step, piece in enumerate(pieces):
        all_ref[step] = piece[...]

    def renewed(old, m):
        change = all_ref[spot_ref[0] ^ owners[m], : old.shape[0]].astype(f32)
        factor = learn_rate * update_scale * math.sqrt(max(ROWS[m], Z))
        return old * (1.0 - learn_rate * weight_decay) - factor * change

    for k in range(3):
        gru_out[k] = renewed(gru_ref[k], k)
    post_out[...] = renewed(post_ref[...], 3)
    prior_out[...] = renewed(prior_ref[...], 4)


def in_vmem(count):
    return [pl.BlockSpec(memory_space=pltpu.VMEM)] * count


def cost(flops, touched):
    return pl.CostEstimate(flops=int(flops), bytes_accessed=int(touched), transcendentals=0)


def run_forward(spot, inputs, weights, seqs):
    parts, packs = inputs.shape[:2]
    units = weights[0].shape[2]
    chunks = packs // CHUNK
    return pl.pallas_call(
        functools.partial(scan_forward, seqs, CHUNK),
        out_shape=[
            jax.ShapeDtypeStruct((packs, PACK, H), bf16),
            jax.ShapeDtypeStruct((3, packs, PACK, H), f32),
            jax.ShapeDtypeStruct((packs, PACK, H), f32),
            jax.ShapeDtypeStruct((3 * H, H), bf16),
        ],
        in_specs=in_smem(1) + in_vmem(1) + anywhere(parts),
        out_specs=in_vmem(1) + anywhere(3),
        scratch_shapes=[
            pltpu.VMEM((seqs, H), f32),
            pltpu.VMEM((parts, 3, H, units), bf16),
            pltpu.VMEM((3, packs, PACK, H), f32),
            pltpu.VMEM((packs, PACK, H), f32),
            pltpu.VMEM((3 * H, H), bf16),
            pltpu.SemaphoreType.DMA((parts,)),
            pltpu.SemaphoreType.DMA((chunks,)),
            pltpu.SemaphoreType.DMA((chunks,)),
            pltpu.SemaphoreType.DMA,
        ],
        compiler_params=pltpu.CompilerParams(vmem_limit_bytes=LARGE),
        cost_estimate=cost(6e10, 20 * mib),
        name="scan_forward",
    )(spot, inputs, *weights)


def run_backward(direct, factors, rest, turned, parts, seqs, copies):
    packs = direct.shape[0]
    units = H // parts
    chunks = packs // CHUNK
    return pl.pallas_call(
        functools.partial(scan_backward, seqs, CHUNK),
        out_shape=jax.ShapeDtypeStruct((copies, parts, packs, PACK, 3 * units), bf16),
        in_specs=in_vmem(1) + anywhere(3),
        out_specs=anywhere(1)[0],
        scratch_shapes=[
            pltpu.VMEM((seqs, 3 * H), f32),
            pltpu.VMEM((seqs, H), f32),
            pltpu.VMEM((3 * H, H), bf16),
            pltpu.VMEM((3, packs, PACK, H), f32),
            pltpu.VMEM((packs, PACK, H), f32),
            pltpu.VMEM((parts, packs, PACK, 3 * units), bf16),
            pltpu.SemaphoreType.DMA,
            pltpu.SemaphoreType.DMA((chunks,)),
            pltpu.SemaphoreType.DMA((chunks,)),
            pltpu.SemaphoreType.DMA((copies * chunks,)),
        ],
        compiler_params=pltpu.CompilerParams(vmem_limit_bytes=LARGE),
        cost_estimate=cost(6e10, 20 * mib),
        name="scan_backward",
    )(direct, factors, rest, turned)


def run_heads(spot, hidden, order, target, mask, mask_row, embed, weights):
    rows = hidden.shape[0]
    return pl.pallas_call(
        head_block,
        out_shape=[
            jax.ShapeDtypeStruct((4, rows, Z), bf16),
            jax.ShapeDtypeStruct((rows, H), f32),
            jax.ShapeDtypeStruct((1, 1), f32),
        ],
        in_specs=in_smem(1) + in_vmem(5) + anywhere(2),
        out_specs=in_vmem(3),
        scratch_shapes=[
            pltpu.VMEM(weights.shape, bf16),
            pltpu.VMEM((rows, E), bf16),
            pltpu.VMEM((rows, E), bf16),
            pltpu.SemaphoreType.DMA((weights.shape[0],)),
            pltpu.SemaphoreType.DMA,
        ],
        compiler_params=pltpu.CompilerParams(vmem_limit_bytes=LARGE),
        cost_estimate=cost(1e10, 12 * mib),
        name="heads",
    )(spot, hidden, order, target, mask, mask_row, embed, weights)


def in_smem(count):
    return [pl.BlockSpec(memory_space=pltpu.SMEM)] * count


def anywhere(count):
    return [pl.BlockSpec(memory_space=pl.ANY)] * count


def run_head_grads(spot, scale, order, everyone, embed, earlier):
    parts, rows = embed.shape[:2]
    units = H // parts
    return pl.pallas_call(
        head_grads,
        out_shape=jax.ShapeDtypeStruct((H + E + H, units), bf16),
        in_specs=in_smem(2) + in_vmem(1) + anywhere(3),
        out_specs=in_vmem(1)[0],
        scratch_shapes=[
            pltpu.VMEM((parts, rows, H), bf16),
            pltpu.VMEM((parts, 2, rows, units), bf16),
            pltpu.VMEM(embed.shape, bf16),
            pltpu.SemaphoreType.DMA((3,)),
        ],
        compiler_params=pltpu.CompilerParams(vmem_limit_bytes=LARGE),
        cost_estimate=cost(4e9, 12 * mib),
        name="head_grads",
    )(spot, scale, order, everyone, embed, earlier)


def run_gru_grads(spot, scale, onehot, everyone, back, earlier, dz_count):
    parts, rows = back.shape[1:3]
    units = back.shape[3] // 3
    share = (Z + H) // (2 * dz_count)
    return pl.pallas_call(
        gru_grads,
        out_shape=jax.ShapeDtypeStruct((dz_count, 3 * share, units), bf16),
        in_specs=in_smem(2) + anywhere(4),
        out_specs=in_vmem(1)[0],
        scratch_shapes=[
            pltpu.VMEM(onehot.shape, bf16),
            pltpu.VMEM((2, dz_count // 2, parts, rows, share), bf16),
            pltpu.VMEM(back.shape, bf16),
            pltpu.SemaphoreType.DMA((2 + dz_count,)),
        ],
        compiler_params=pltpu.CompilerParams(vmem_limit_bytes=LARGE),
        cost_estimate=cost(4e9, 12 * mib),
        name="gru_grads",
    )(spot, scale, onehot, everyone, back, earlier)


def plain_gru_grads(dx_index, scale, onehot, everyone, back, dz_count):
    units = back.shape[3] // 3
    share = (Z + H) // (2 * dz_count)
    total = 0.0
    for states, x in ((everyone[:, 0], dx_index), (everyone[:, 1], 1 - dx_index)):
        states = states.reshape(-1, dz_count // 2, 2, share)
        states = lax.dynamic_index_in_dim(states, dx_index, 2, keepdims=False)
        ones = lax.dynamic_index_in_dim(onehot, x, 0, keepdims=False)
        left = jnp.concatenate([ones, states.reshape(ones.shape)], axis=1)
        right = lax.dynamic_index_in_dim(back, x, 0, keepdims=False)
        total = total + dot_tn(left, right.reshape(-1, 3 * units))
    grads = (total * scale).astype(bf16).reshape(dz_count, share, 3, units)
    return jnp.swapaxes(grads, 1, 2).reshape(dz_count, 3 * share, units)


def run_orthogonal(base, share, own, matrix, earlier):
    side, width = matrix.shape
    return pl.pallas_call(
        functools.partial(orthogonal_block, base, 512),
        out_shape=jax.ShapeDtypeStruct((share, width), bf16),
        in_specs=in_smem(1) + in_vmem(1) + anywhere(len(earlier)),
        out_specs=in_vmem(1)[0],
        scratch_shapes=[
            pltpu.VMEM((side, width), bf16),
            pltpu.VMEM((side, side), bf16),
            pltpu.VMEM((side, side), bf16),
        ],
        compiler_params=pltpu.CompilerParams(vmem_limit_bytes=28 * mib),
        cost_estimate=cost(5e10, 6 * mib),
        name="orthogonal",
    )(own, matrix, *earlier)


def run_turn(matrix):
    return pl.pallas_call(
        functools.partial(turn_block, 256),
        out_shape=jax.ShapeDtypeStruct(matrix.shape[::-1], bf16),
        in_specs=in_vmem(1),
        out_specs=in_vmem(1)[0],
        compiler_params=pltpu.CompilerParams(vmem_limit_bytes=6 * mib),
        cost_estimate=cost(1e6, 3 * mib),
        name="turn",
    )(matrix)


def small_kernel(body, out_shape, scratch, specs, arguments, name):
    return pl.pallas_call(
        body,
        out_shape=out_shape,
        in_specs=specs,
        out_specs=jax.tree.map(lambda _: in_vmem(1)[0], out_shape),
        scratch_shapes=scratch,
        compiler_params=pltpu.CompilerParams(vmem_limit_bytes=8 * mib),
        cost_estimate=cost(1e6, 4 * mib),
        name=name,
    )(*arguments)


def run_collect(spot, pieces, base):
    steps = len(pieces)
    widest, units = pieces[0].shape
    return small_kernel(
        functools.partial(collect_block, base),
        jax.ShapeDtypeStruct((units, steps * widest), bf16),
        [pltpu.VMEM((steps * (widest - base), units), bf16)],
        in_smem(1) + in_vmem(steps),
        (spot, *pieces),
        "collect",
    )


def run_deal(spot, result, steps, base):
    units, width = result.shape
    widest = width // steps
    return small_kernel(
        functools.partial(deal_block, base),
        jax.ShapeDtypeStruct((steps, widest, units), bf16),
        [pltpu.VMEM((steps * (widest - base), units), bf16)],
        in_smem(1) + in_vmem(1),
        (spot, result),
        "deal",
    )


def run_finish(owners, spot, pieces, rows):
    return small_kernel(
        functools.partial(finish_block, owners),
        [jax.ShapeDtypeStruct(block.shape, f32) for block in rows],
        [pltpu.VMEM((len(pieces), *pieces[0].shape), bf16)],
        in_smem(1) + in_vmem(len(pieces) + len(rows)),
        (spot, *pieces, *rows),
        "finish",
    )


def on_device(
    embeddings,
    samples,
    seq_lengths,
    gru_weight,
    post_weight,
    prior_weight,
    gru_moment,
    post_moment,
    prior_moment,
):
    dz_count = lax.axis_size("dz")
    dx_count = lax.axis_size("dx")
    tp_count = lax.axis_size("tp")
    dp_count = dz_count * dx_count
    dx_index = lax.axis_index("dx")
    tp_index = lax.axis_index("tp")
    dp_index = lax.axis_index("dz") * dx_count + dx_index
    seq_count = embeddings.shape[0]
    seqs = seq_count // tp_count
    units = gru_weight.shape[2]
    groups = Z // ZC
    rows = seqs * FRAMES
    packs = rows // PACK

    def gather(block):
        return lax.all_gather(block, "tp", axis=0, tiled=False)

    def exchange(block, axis):
        return lax.all_to_all(block, axis, 0, 0, tiled=True)

    def mine(block, axis):
        return lax.dynamic_index_in_dim(block, dx_index, axis, keepdims=False)

    def across(block, bit):
        return lax.ppermute(block, "tp", [(i, i ^ bit) for i in range(tp_count)])

    own_hidden = gru_weight[:, Z:].astype(bf16)
    far = across(own_hidden, 2)
    near = across(own_hidden, 1)
    gru_input = lax.optimization_barrier(gru_weight)
    head_low = jnp.concatenate([post_weight.astype(bf16), prior_weight.astype(bf16)], axis=0)

    by_part = jnp.swapaxes(samples.reshape(tp_count, seqs, FRAMES, groups), 1, 2)
    by_part = by_part.reshape(tp_count * rows, groups).astype(bf16)

    def one_hot(chosen):
        count = chosen.shape[-1]
        classes = jnp.arange(count * ZC, dtype=jnp.int32)
        expand = (classes[None, :] // ZC == jnp.arange(count)[:, None]).astype(bf16)
        return (dot(chosen, expand) == (classes % ZC).astype(f32)).astype(bf16)

    onehot = one_hot(by_part)
    input_part = jnp.concatenate(
        [dot(onehot, gru_input[k, :Z].astype(bf16)).astype(bf16) for k in range(3)], axis=1
    ).reshape(tp_count, packs, PACK, 3 * units)
    input_part = exchange(input_part, "tp")
    embed_rows = embeddings.reshape(tp_count, rows, E)
    order = np.zeros((rows, rows), np.float32)
    order[np.arange(rows), np.arange(rows) % seqs * FRAMES + np.arange(rows) // seqs] = 1.0
    order = jnp.asarray(order, bf16)
    swap = [(i, i ^ 1) for i in range(dx_count)]
    other = lax.ppermute(by_part, "dx", swap)
    pair_samples = jnp.where(
        dx_index == 0, jnp.stack([by_part, other]), jnp.stack([other, by_part])
    )
    half = Z // dx_count
    pair_half = mine(
        pair_samples.reshape(dx_count * tp_count * rows, dz_count // 2, dx_count, -1), 2
    )
    pair_onehot = one_hot(pair_half.reshape(dx_count * tp_count * rows, groups // dx_count))
    pair_onehot = pair_onehot.reshape(dx_count, tp_count * rows, half)
    onehot = onehot.reshape(tp_count, rows, Z)
    own_target = lax.dynamic_index_in_dim(onehot, tp_index, 0, keepdims=False)
    positions = jnp.arange(FRAMES, dtype=jnp.int32)
    own_lengths = lax.dynamic_slice_in_dim(seq_lengths, tp_index * seqs, seqs, 0)
    frame_mask = (positions[:, None] < own_lengths[None, :]).astype(f32)
    mask_lanes = jnp.broadcast_to(frame_mask.reshape(rows, 1), (rows, 128))

    weights = [own_hidden, near, far, across(far, 1)]
    every_mask = (positions[:, None] < seq_lengths[None, :]).astype(f32)
    frame_count = jnp.broadcast_to(jnp.sum(every_mask), (8, 128))
    for axis, bits in (("dx", dx_count), ("dz", dz_count)):
        for bit in range(bits.bit_length() - 1):
            pairs = [(i, i ^ (1 << bit)) for i in range(bits)]
            frame_count = frame_count + lax.ppermute(frame_count, axis, pairs)
    frame_count = frame_count[0, 0]
    scale = (1.0 / frame_count).reshape(1)

    early = (head_low, own_target, mask_lanes, pair_onehot, scale)
    weights, input_part, early = lax.optimization_barrier((weights, input_part, early))
    head_low, own_target, mask_lanes, pair_onehot, scale = early
    head_full = gather(head_low)
    hidden, factors, rest, turned = run_forward(tp_index.astype(jnp.int32).reshape(1), input_part, weights, seqs)
    hidden = hidden.reshape(rows, H)
    neighbour = lax.ppermute(hidden, "dx", swap)
    backs, direct, loss_lanes = run_heads(
        tp_index.astype(jnp.int32).reshape(1),
        hidden,
        order,
        own_target,
        mask_lanes,
        frame_mask.reshape(1, rows),
        embed_rows,
        head_full,
    )
    everyone = gather(lax.dynamic_update_slice(backs, neighbour[None], (1, 0, 0)))
    back = run_backward(
        direct.reshape(packs, PACK, H), factors, rest, turned, tp_count, seqs, dx_count
    )
    own_back = exchange(back.reshape(dx_count * tp_count, rows, 3 * units), ("dx", "tp"))
    own_back = own_back.reshape(dx_count, tp_count, rows, 3 * units)

    shares = [size // dp_count for size in ROWS]
    all_post = everyone[:, 3]
    spot = jnp.stack([tp_index, dx_index]).astype(jnp.int32)

    head_grad = run_head_grads(spot, scale, order, everyone, embed_rows, back)

    head_grad = jnp.concatenate(
        [
            block.reshape(dz_count, dx_count, -1, units)
            for block in (head_grad[: H + E], head_grad[H + E :])
        ],
        axis=2,
    )

    def share_rows(block):
        return lax.psum_scatter(block, "dz", scatter_dimension=0, tiled=True)[0]

    head_done = share_rows(head_grad)
    if shares[0] % 128 == 0:
        gru_grad = run_gru_grads(
            spot, scale, pair_onehot, everyone, own_back, head_grad, dz_count
        )
    else:
        gru_grad = plain_gru_grads(dx_index, scale, pair_onehot, everyone, own_back, dz_count)
    gru_grad, head_done = lax.optimization_barrier((gru_grad, head_done))
    gru_sum = share_rows(gru_grad).astype(f32)
    received = lax.ppermute(
        lax.dynamic_index_in_dim(head_done, 1 - dx_index, 0, keepdims=False), "dx", swap
    )
    head_sum = mine(head_done, 0).astype(f32) + received.astype(f32)
    loss_sum = jnp.broadcast_to(jnp.sum(loss_lanes), (8, 128))
    for axis, bits in (("tp", tp_count), ("dx", dx_count), ("dz", dz_count)):
        for bit in range(bits.bit_length() - 1):
            pairs = [(i, i ^ (1 << bit)) for i in range(bits)]
            loss_sum = loss_sum + lax.ppermute(loss_sum, axis, pairs)
    loss_sum = loss_sum[0, 0]
    loss_value = loss_sum / frame_count

    embed_part = E // tp_count
    own_rows_e = lax.dynamic_slice_in_dim(head_full, H + tp_index * embed_part, embed_part, 1)
    post_by_seq = jnp.swapaxes(all_post.reshape(tp_count, FRAMES, seqs, Z), 1, 2)
    embed_grad = jnp.einsum(
        "psfk,ek->psfe",
        post_by_seq,
        jnp.concatenate(list(own_rows_e), axis=1),
        preferred_element_type=f32,
    ).reshape(seq_count, FRAMES, embed_part)
    embed_grad = embed_grad * scale[0]

    grads = [gru_sum[k * shares[0] : (k + 1) * shares[0]] for k in range(3)]
    grads += [head_sum[: shares[3]], head_sum[shares[3] :]]

    def own_rows(matrix, axis_dim):
        share = matrix.shape[axis_dim] // dp_count
        return lax.dynamic_slice_in_dim(matrix, dp_index * share, share, axis_dim)

    gru_moments = own_rows(gru_moment, 1)
    moments = [momentum_keep * gru_moments[k] + grads[k] for k in range(3)]
    moments.append(momentum_keep * own_rows(post_moment, 0) + grads[3])
    moments.append(momentum_keep * own_rows(prior_moment, 0) + grads[4])
    ahead = [(grads[m] + momentum_keep * moments[m]).astype(bf16) for m in range(MATS)]

    owners = [m * dp_count // 8 for m in (0, 3, 4, 7, 5)]
    widest = max(shares)
    base = shares[0]
    holds_post = (dp_index == owners[3]).astype(jnp.int32)
    if dp_count == 8:
        kept = jnp.array([owners.index(d) if d in owners else 0 for d in range(dp_count)])
        blocks = jnp.stack(
            [jnp.pad(block, ((0, widest - block.shape[0]), (0, 0))) for block in ahead]
        )
        where = dp_index.astype(jnp.int32).reshape(1)
        pieces = []
        for step in range(dp_count):
            block = lax.dynamic_index_in_dim(blocks, kept[dp_index ^ step], 0, keepdims=False)
            if step > 0:
                block = lax.ppermute(block, ("dz", "dx"), [(d ^ step, d) for d in owners])
            pieces.append(block)
        turned = run_collect(where, pieces, base)
    else:
        slots = [jnp.zeros((widest, units), bf16)] * dp_count
        for m in range(MATS):
            slots[owners[m]] = jnp.pad(ahead[m], ((0, widest - shares[m]), (0, 0)))
        arrived = exchange(jnp.stack(slots), ("dz", "dx"))
        turned = run_turn(
            jnp.concatenate(
                [arrived[:, :base].reshape(-1, units), arrived[:, base:].reshape(-1, units)], axis=0
            )
        )
    wide = gather(turned).reshape(H, dp_count * widest)
    own = jnp.stack([tp_index, holds_post]).astype(jnp.int32)
    old_rows = (own_rows(gru_weight, 1), own_rows(post_weight, 0), own_rows(prior_weight, 0))
    old_rows = lax.optimization_barrier(old_rows)
    result = run_orthogonal(
        dp_count * base, units, own, wide, (embed_grad, loss_value.reshape(1, 1), *old_rows)
    )
    if dp_count == 8:
        dealt = run_deal(where, result, dp_count, base)
        pieces = [dealt[0]]
        for step in range(1, dp_count):
            pairs = [(d, d ^ step) for d in owners]
            pieces.append(lax.ppermute(dealt[step], ("dz", "dx"), pairs))
        new_gru, new_post, new_prior = run_finish(owners, where, pieces, old_rows)
    else:
        result = result.T
        results = exchange(
            jnp.concatenate(
                [
                    result[: dp_count * base].reshape(dp_count, base, units),
                    result[dp_count * base :].reshape(dp_count, widest - base, units),
                ],
                axis=1,
            ),
            ("dz", "dx"),
        )

        def renew(old, m):
            factor = learn_rate * update_scale * math.sqrt(max(ROWS[m], Z))
            change = results[owners[m], : old.shape[0]].astype(f32)
            return old * (1.0 - learn_rate * weight_decay) - factor * change

        new_gru = jnp.stack([renew(old_rows[0][k], k) for k in range(3)])
        new_post = renew(old_rows[1], 3)
        new_prior = renew(old_rows[2], 4)
    return (
        loss_value,
        embed_grad,
        new_gru,
        new_post,
        new_prior,
        jnp.stack(moments[:3]),
        moments[3],
        moments[4],
    )

def solution(mesh):
    dp_count, tp_count = mesh.devices.shape
    mesh = jax.sharding.Mesh(
        mesh.devices.reshape(dp_count // 2, 2, tp_count), ("dz", "dx", "tp")
    )
    dp = ("dz", "dx")
    in_specs = (
        P(dp, None, None),
        P(dp, None, None),
        P(dp),
        P(None, None, "tp"),
        P(None, "tp"),
        P(None, "tp"),
        P(None, None, "tp"),
        P(None, "tp"),
        P(None, "tp"),
    )
    out_specs = (
        P(),
        P(dp, None, "tp"),
        P(None, dp, "tp"),
        P(dp, "tp"),
        P(dp, "tp"),
        P(None, dp, "tp"),
        P(dp, "tp"),
        P(dp, "tp"),
    )
    return jax.shard_map(
        on_device, mesh=mesh, in_specs=in_specs, out_specs=out_specs, check_vma=False
    )
```

```python
import functools
import math

import jax
import jax.numpy as jnp
import numpy as np
from jax import lax
from jax.experimental import pallas as pl
from jax.experimental.pallas import tpu as pltpu
from jax.sharding import PartitionSpec as P

H = 1024
ZC = 32
E = 1536
FRAMES = 56
MATS = 5
Z = 1024
ROWS = (Z + H, Z + H, Z + H, H + E, H)
PACK = 8
CHUNK = 4


coeff_linear = 3.4445
coeff_cubic = -4.775
coeff_quintic = 2.0315
momentum_keep = 0.95
learn_rate = 0.2
weight_decay = 0.01
update_scale = 0.2
tiny_value = 1e-07
mib = 1 << 20
LARGE = 56 * mib
f32 = jnp.float32
bf16 = jnp.bfloat16
NT = (((1,), (1,)), ((), ()))
TN = (((0,), (0,)), ((), ()))


def dot(left, right):
    return jnp.dot(left, right, preferred_element_type=f32)


def dot_tn(left, right):
    return lax.dot_general(left, right, TN, preferred_element_type=f32)


def dot_nt(left, right):
    return lax.dot_general(left, right, NT, preferred_element_type=f32)


def copy(source, target, semaphore):
    return pltpu.make_async_copy(source, target, semaphore)


def scan_forward(
    seqs, chunk, spot_ref, x_ref, *refs
):
    parts, packs = x_ref.shape[:2]
    shards = refs[:parts]
    h_ref, k_hbm, u_hbm, t_hbm, state, w, k_ref, u_ref, t, w_sem, k_sem, u_sem, t_sem = refs[parts:]
    units = w.shape[3]
    per_pack = PACK // seqs
    loads = [copy(shards[n], w.at[spot_ref[0] ^ n], w_sem.at[n]) for n in range(parts)]
    for load in loads:
        load.start()
    state[...] = jnp.zeros_like(state)
    for load in loads:
        load.wait()

    def stores(c):
        at = pl.ds(c * chunk, chunk)
        return (
            copy(k_ref.at[:, at], k_hbm.at[:, at], k_sem.at[c]),
            copy(u_ref.at[at], u_hbm.at[at], u_sem.at[c]),
        )

    def pack(i, carry):
        states = []
        for frame in range(per_pack):
            rows = slice(frame * seqs, (frame + 1) * seqs)
            if frame == 0:
                source, live = jnp.maximum(i - 1, 0), jnp.where(i > 0, 1.0, 0.0)
                spot = slice((per_pack - 1) * seqs, per_pack * seqs)
            else:
                source, live = i, None
                spot = slice((frame - 1) * seqs, frame * seqs)
            before = state[...]
            low = before.astype(bf16)
            news = []
            for p in range(parts):
                cols = slice(p * units, (p + 1) * units)
                given = x_ref[p, source].astype(f32)[spot]
                if live is not None:
                    given = given * live
                pre = [
                    given[:, k * units : (k + 1) * units] + dot(low, w[p, k]) for k in range(3)
                ]
                last = before[:, cols]
                r = jax.nn.sigmoid(pre[0])
                c = jnp.tanh(r * pre[1])
                u = jax.nn.sigmoid(pre[2] - 1.0)
                rest = 1.0 - u
                new = u * c + rest * last
                inner = u * (1.0 - c * c)
                state[:, cols] = new
                news.append(new)
                k_ref[0, i, rows, cols] = inner * pre[1] * r * (1.0 - r)
                k_ref[1, i, rows, cols] = inner * r
                k_ref[2, i, rows, cols] = (c - last) * u * rest
                u_ref[i, rows, cols] = rest
            states.append(jnp.concatenate(news, axis=1))
        h_ref[i] = jnp.concatenate(states, axis=0).astype(bf16)

        @pl.when(i % chunk == chunk - 1)
        def _():
            for store in stores(i // chunk):
                store.start()

        return carry

    def pack_and_turn(i, carry):
        t[pl.ds(pl.multiple_of(i * units, units), units), :] = w[i // 3, i % 3].T
        return pack(i, carry)

    lax.fori_loop(0, 3 * parts, pack_and_turn, 0)
    turned = copy(t, t_hbm, t_sem)
    turned.start()
    lax.fori_loop(3 * parts, packs, pack, 0)
    turned.wait()
    for c in range(packs // chunk):
        for store in stores(c):
            store.wait()


def scan_backward(
    seqs, chunk, d_ref, k_hbm, u_hbm, t_hbm, b_hbm, now, kept, w, k_ref, u_ref, b_ref, t_sem, k_sem, u_sem, b_sem
):
    copies, parts, packs = b_hbm.shape[:3]
    units = b_ref.shape[3] // 3
    per_pack = PACK // seqs
    chunks = packs // chunk

    def loads(c):
        at = pl.ds(c * chunk, chunk)
        return (
            copy(k_hbm.at[:, at], k_ref.at[:, at], k_sem.at[c]),
            copy(u_hbm.at[at], u_ref.at[at], u_sem.at[c]),
        )

    def stores(c):
        at = pl.ds(c * chunk, chunk)
        return [
            copy(b_ref.at[:, at], b_hbm.at[n, :, at], b_sem.at[n * chunks + c]) for n in range(copies)
        ]

    turned = copy(t_hbm, w, t_sem)
    turned.start()
    for c in reversed(range(chunks)):
        for load in loads(c):
            load.start()
    now[...] = jnp.zeros_like(now)
    kept[...] = jnp.zeros_like(kept)
    turned.wait()

    def pack(n, carry):
        i = packs - 1 - n

        @pl.when(i % chunk == chunk - 1)
        def _():
            for load in loads(i // chunk):
                load.wait()

        later = [None] * per_pack
        for frame in reversed(range(per_pack)):
            rows = slice(frame * seqs, (frame + 1) * seqs)
            values = now[...]
            later[frame] = values
            dh = d_ref[i, rows] + kept[...] + dot(values.astype(bf16), w[...])
            kept[...] = dh * u_ref[i, rows]
            for p in range(parts):
                cols = slice(p * units, (p + 1) * units)
                for k in range(3):
                    spot = slice((3 * p + k) * units, (3 * p + k + 1) * units)
                    now[:, spot] = dh[:, cols] * k_ref[k, i, rows, cols]
        stacked = jnp.concatenate(later, axis=0).astype(bf16)
        for p in range(parts):
            b_ref[p, i] = stacked[:, p * 3 * units : (p + 1) * 3 * units]

        @pl.when(i % chunk == 0)
        def _():
            for store in stores(i // chunk):
                store.start()

        return carry

    lax.fori_loop(0, packs, pack, 0)
    for c in range(chunks):
        for store in stores(c):
            store.wait()


def head_block(
    spot_ref, h_ref, p_ref, t_ref, m_ref, r_ref, e_hbm, w_hbm, back_ref, d_ref, loss_ref, w_ref, n_ref, e_ref, w_sem, e_sem
):
    parts = w_ref.shape[0]
    embed = copy(e_hbm.at[spot_ref[0]], n_ref, e_sem)
    embed.start()
    loads = [copy(w_hbm.at[p], w_ref.at[p], w_sem.at[p]) for p in range(parts)]
    for load in loads:
        load.start()
    embed.wait()
    e_ref[...] = dot(p_ref[...], n_ref[...]).astype(bf16)
    units = w_ref.shape[2]
    rows = h_ref.shape[0]
    low = h_ref[...]
    back_ref[0] = low
    mask = m_ref[...]
    given = jnp.zeros((rows, 128), f32)
    normal = jnp.zeros((1, rows), f32)
    for p in range(parts):
        loads[p].wait()
        post = dot(low, w_ref[p, :H]) + dot(e_ref[...], w_ref[p, H : H + E])
        prior = dot(low, w_ref[p, H + E :])
        for head, logits in enumerate((prior, post)):
            for piece in range(units // 128):
                l = logits[:, piece * 128 : (piece + 1) * 128]
                cols = slice(p * units + piece * 128, p * units + (piece + 1) * 128)
                target = t_ref[:, cols].astype(f32)
                turned = l.T.reshape(128 // ZC, ZC, rows)
                top = jnp.max(turned, axis=1, keepdims=True)
                e = jnp.exp(turned - top)
                total = jnp.sum(e, axis=1, keepdims=True)
                normal = normal + jnp.sum(top + jnp.log(total), axis=0)
                probs = (e * (1.0 / total)).reshape(128, rows).T
                given = given + target * l
                back_ref[head + 2, :, cols] = (mask * (probs - target)).astype(bf16)
    loss_ref[...] = jnp.sum(r_ref[...] * normal, axis=1, keepdims=True) - jnp.sum(
        jnp.sum(mask * given, axis=0, keepdims=True), axis=1, keepdims=True
    )
    direct = jnp.zeros((rows, H), f32)
    for p in range(parts):
        cols = slice(p * units, (p + 1) * units)
        direct = direct + dot_nt(back_ref[2, :, cols], w_ref[p, H + E :])
        direct = direct + dot_nt(back_ref[3, :, cols], w_ref[p, :H])
    d_ref[...] = direct


def head_grads(spot_ref, p_ref, r_hbm, e_hbm, earlier_ref, o_ref, h_ref, r_ref, e_ref, sems):
    parts, rows = e_ref.shape[0], e_ref.shape[1]
    units = o_ref.shape[1]
    frames = parts * rows
    own = pl.ds(pl.multiple_of(spot_ref[0] * units, units), units)
    loads = [
        copy(r_hbm.at[:, pl.ds(2, 2), :, own], r_ref, sems.at[0]),
        copy(r_hbm.at[:, 0], h_ref, sems.at[1]),
        copy(e_hbm, e_ref, sems.at[2]),
    ]
    for load in loads:
        load.start()
    loads[0].wait()
    loads[1].wait()
    post = r_ref[:, 1].reshape(frames, units)
    both = jnp.concatenate([post, r_ref[:, 0].reshape(frames, units)], axis=1)
    for m in range(H // 256):
        spot = slice(m * 256, (m + 1) * 256)
        grad = (dot_tn(h_ref[:, :, spot].reshape(frames, 256), both)).astype(bf16)
        o_ref[m * 256 : (m + 1) * 256] = grad[:, :units]
        o_ref[H + E + m * 256 : H + E + (m + 1) * 256] = grad[:, units:]
    post = jnp.concatenate(
        [dot_tn(p_ref[...], r_ref[p, 1]).astype(bf16) for p in range(parts)], axis=0
    )
    loads[2].wait()
    for m in range(E // 256):
        spot = slice(m * 256, (m + 1) * 256)
        grad = (dot_tn(e_ref[:, :, spot].reshape(frames, 256), post)).astype(bf16)
        o_ref[H + m * 256 : H + (m + 1) * 256] = grad


def gru_grads(
    spot_ref, one_hbm, r_hbm, b_hbm, earlier_ref, o_ref, one_ref, l_ref, b_ref, sems
):
    parts, rows = b_ref.shape[1], b_ref.shape[2]
    units = o_ref.shape[2]
    frames = parts * rows
    share = o_ref.shape[1] // 3
    half = o_ref.shape[0] // 2
    me = spot_ref[1]
    loads = [copy(b_hbm, b_ref, sems.at[0]), copy(one_hbm, one_ref, sems.at[1])]
    for z in range(half):
        spot = pl.ds(pl.multiple_of((z * 2 + me) * share, share), share)
        loads.append(copy(r_hbm.at[:, 0, :, spot], l_ref.at[0, z], sems.at[2 + 2 * z]))
        loads.append(copy(r_hbm.at[:, 1, :, spot], l_ref.at[1, z], sems.at[3 + 2 * z]))
    for load in loads:
        load.start()
    loads[0].wait()
    loads[1].wait()
    back = [b_ref[x].reshape(frames, 3 * units) for x in (me, 1 - me)]
    for z in range(2 * half):
        if z < half:
            spot = slice(z * share, (z + 1) * share)
            left = [one_ref[x, :, spot] for x in (me, 1 - me)]
        else:
            loads[2 * (z - half) + 2].wait()
            loads[2 * (z - half) + 3].wait()
            left = [l_ref[n, z - half].reshape(frames, share) for n in (0, 1)]
        grad = dot_tn(left[0], back[0]) + dot_tn(left[1], back[1])
        grad = grad.astype(bf16)
        for k in range(3):
            o_ref[z, k * share : (k + 1) * share] = grad[:, k * units : (k + 1) * units]


def orthogonal_block(base, tile, own_ref, g_ref, *refs):
    o_ref, x, a, b = refs[-4:]
    side, width = g_ref.shape
    share = o_ref.shape[0]
    own = pl.ds(pl.multiple_of(own_ref[0] * share, share), share)
    wide = own_ref[1] > 0

    def either(run):
        pl.when(wide)(functools.partial(run, width))
        pl.when(jnp.logical_not(wide))(functools.partial(run, base))

    def squares(i, total):
        rows = pl.ds(pl.multiple_of(i * 128, 128), 128)
        v = g_ref[rows, :].astype(f32)
        return total + jnp.sum(v * v)

    total = lax.fori_loop(0, side // 128, squares, jnp.zeros((), f32))
    scale = 1.0 / (jnp.sqrt(jnp.full((1, 128), total, f32)) + tiny_value)
    scale = scale[:, :1]

    def shrink(i, carry):
        rows = pl.ds(pl.multiple_of(i * 128, 128), 128)
        x[rows, :] = (g_ref[rows, :].astype(f32) * scale).astype(bf16)
        return carry

    lax.fori_loop(0, side // 128, shrink, 0)

    def lower(out, product):
        for start in range(0, side, 256):
            stop = start + 256
            block = product(slice(start, side), slice(start, stop)).astype(bf16)
            out[start:, start:stop] = block
            if stop < side:
                out[start:stop, stop:] = block[256:].T

    def square(depth):
        lower(a, lambda rows, cols: dot_nt(x[rows, :depth], x[cols, :depth]))

    def mix():
        lower(
            b,
            lambda rows, cols: coeff_cubic * a[rows, cols].astype(f32)
            + coeff_quintic * dot(a[rows, :], a[:, cols]),
        )

    def renew_all(depth):
        for start in range(0, depth, tile):
            cols = slice(start, start + tile)
            x[:, cols] = (
                coeff_linear * x[:, cols].astype(f32) + dot(b[...], x[:, cols])
            ).astype(bf16)

    def sweep(s, carry):
        either(square)
        mix()
        either(renew_all)
        return carry

    lax.fori_loop(0, 4, sweep, 0)
    either(square)
    part = (coeff_cubic * a[own, :].astype(f32) + coeff_quintic * dot(a[own, :], a[...])).astype(bf16)

    def last(j, carry):
        cols = pl.ds(pl.multiple_of(j * tile, tile), tile)
        o_ref[:, cols] = (
            coeff_linear * x[own, cols].astype(f32) + dot(part, x[:, cols])
        ).astype(bf16)
        return carry

    lax.fori_loop(0, width // tile, last, 0)


def turn_block(tile, g_ref, o_ref):
    def block(i, carry):
        spot = pl.ds(pl.multiple_of(i * tile, tile), tile)
        o_ref[:, spot] = g_ref[spot, :].T
        return carry

    lax.fori_loop(0, g_ref.shape[0] // tile, block, 0)


def collect_block(base, spot_ref, *refs):
    *pieces, o_ref, rows = refs
    steps = len(pieces)
    more = pieces[0].shape[0] - base
    for step, piece in enumerate(pieces):
        d = spot_ref[0] ^ step
        o_ref[:, pl.ds(pl.multiple_of(d * base, base), base)] = piece[:base].T
        rows[pl.ds(pl.multiple_of(d * more, more), more), :] = piece[base:]
    o_ref[:, steps * base :] = rows[...].T


def deal_block(base, spot_ref, g_ref, o_ref, rows):
    steps, widest = o_ref.shape[:2]
    more = widest - base
    rows[...] = g_ref[:, steps * base :].T
    for step in range(steps):
        d = spot_ref[0] ^ step
        o_ref[step, :base] = g_ref[:, pl.ds(pl.multiple_of(d * base, base), base)].T
        o_ref[step, base:] = rows[pl.ds(pl.multiple_of(d * more, more), more), :]


def finish_block(owners, spot_ref, *refs):
    pieces, (gru_ref, post_ref, prior_ref), (gru_out, post_out, prior_out), all_ref = (
        refs[:-7],
        refs[-7:-4],
        refs[-4:-1],
        refs[-1],
    )
    for step, piece in enumerate(pieces):
        all_ref[step] = piece[...]

    def renewed(old, m):
        change = all_ref[spot_ref[0] ^ owners[m], : old.shape[0]].astype(f32)
        factor = learn_rate * update_scale * math.sqrt(max(ROWS[m], Z))
        return old * (1.0 - learn_rate * weight_decay) - factor * change

    for k in range(3):
        gru_out[k] = renewed(gru_ref[k], k)
    post_out[...] = renewed(post_ref[...], 3)
    prior_out[...] = renewed(prior_ref[...], 4)


def in_vmem(count):
    return [pl.BlockSpec(memory_space=pltpu.VMEM)] * count


def cost(flops, touched):
    return pl.CostEstimate(flops=int(flops), bytes_accessed=int(touched), transcendentals=0)


def run_forward(spot, inputs, weights, seqs):
    parts, packs = inputs.shape[:2]
    units = weights[0].shape[2]
    chunks = packs // CHUNK
    return pl.pallas_call(
        functools.partial(scan_forward, seqs, CHUNK),
        out_shape=[
            jax.ShapeDtypeStruct((packs, PACK, H), bf16),
            jax.ShapeDtypeStruct((3, packs, PACK, H), f32),
            jax.ShapeDtypeStruct((packs, PACK, H), f32),
            jax.ShapeDtypeStruct((3 * H, H), bf16),
        ],
        in_specs=in_smem(1) + in_vmem(1) + anywhere(parts),
        out_specs=in_vmem(1) + anywhere(3),
        scratch_shapes=[
            pltpu.VMEM((seqs, H), f32),
            pltpu.VMEM((parts, 3, H, units), bf16),
            pltpu.VMEM((3, packs, PACK, H), f32),
            pltpu.VMEM((packs, PACK, H), f32),
            pltpu.VMEM((3 * H, H), bf16),
            pltpu.SemaphoreType.DMA((parts,)),
            pltpu.SemaphoreType.DMA((chunks,)),
            pltpu.SemaphoreType.DMA((chunks,)),
            pltpu.SemaphoreType.DMA,
        ],
        compiler_params=pltpu.CompilerParams(vmem_limit_bytes=LARGE),
        cost_estimate=cost(6e10, 20 * mib),
        name="scan_forward",
    )(spot, inputs, *weights)


def run_backward(direct, factors, rest, turned, parts, seqs, copies):
    packs = direct.shape[0]
    units = H // parts
    chunks = packs // CHUNK
    return pl.pallas_call(
        functools.partial(scan_backward, seqs, CHUNK),
        out_shape=jax.ShapeDtypeStruct((copies, parts, packs, PACK, 3 * units), bf16),
        in_specs=in_vmem(1) + anywhere(3),
        out_specs=anywhere(1)[0],
        scratch_shapes=[
            pltpu.VMEM((seqs, 3 * H), f32),
            pltpu.VMEM((seqs, H), f32),
            pltpu.VMEM((3 * H, H), bf16),
            pltpu.VMEM((3, packs, PACK, H), f32),
            pltpu.VMEM((packs, PACK, H), f32),
            pltpu.VMEM((parts, packs, PACK, 3 * units), bf16),
            pltpu.SemaphoreType.DMA,
            pltpu.SemaphoreType.DMA((chunks,)),
            pltpu.SemaphoreType.DMA((chunks,)),
            pltpu.SemaphoreType.DMA((copies * chunks,)),
        ],
        compiler_params=pltpu.CompilerParams(vmem_limit_bytes=LARGE),
        cost_estimate=cost(6e10, 20 * mib),
        name="scan_backward",
    )(direct, factors, rest, turned)


def run_heads(spot, hidden, order, target, mask, mask_row, embed, weights):
    rows = hidden.shape[0]
    return pl.pallas_call(
        head_block,
        out_shape=[
            jax.ShapeDtypeStruct((4, rows, Z), bf16),
            jax.ShapeDtypeStruct((rows, H), f32),
            jax.ShapeDtypeStruct((1, 1), f32),
        ],
        in_specs=in_smem(1) + in_vmem(5) + anywhere(2),
        out_specs=in_vmem(3),
        scratch_shapes=[
            pltpu.VMEM(weights.shape, bf16),
            pltpu.VMEM((rows, E), bf16),
            pltpu.VMEM((rows, E), bf16),
            pltpu.SemaphoreType.DMA((weights.shape[0],)),
            pltpu.SemaphoreType.DMA,
        ],
        compiler_params=pltpu.CompilerParams(vmem_limit_bytes=LARGE),
        cost_estimate=cost(1e10, 12 * mib),
        name="heads",
    )(spot, hidden, order, target, mask, mask_row, embed, weights)


def in_smem(count):
    return [pl.BlockSpec(memory_space=pltpu.SMEM)] * count


def anywhere(count):
    return [pl.BlockSpec(memory_space=pl.ANY)] * count


def run_head_grads(spot, order, everyone, embed, earlier):
    parts, rows = embed.shape[:2]
    units = H // parts
    return pl.pallas_call(
        head_grads,
        out_shape=jax.ShapeDtypeStruct((H + E + H, units), bf16),
        in_specs=in_smem(1) + in_vmem(1) + anywhere(3),
        out_specs=in_vmem(1)[0],
        scratch_shapes=[
            pltpu.VMEM((parts, rows, H), bf16),
            pltpu.VMEM((parts, 2, rows, units), bf16),
            pltpu.VMEM(embed.shape, bf16),
            pltpu.SemaphoreType.DMA((3,)),
        ],
        compiler_params=pltpu.CompilerParams(vmem_limit_bytes=LARGE),
        cost_estimate=cost(4e9, 12 * mib),
        name="head_grads",
    )(spot, order, everyone, embed, earlier)


def run_gru_grads(spot, onehot, everyone, back, earlier, dz_count):
    parts, rows = back.shape[1:3]
    units = back.shape[3] // 3
    share = (Z + H) // (2 * dz_count)
    return pl.pallas_call(
        gru_grads,
        out_shape=jax.ShapeDtypeStruct((dz_count, 3 * share, units), bf16),
        in_specs=in_smem(1) + anywhere(4),
        out_specs=in_vmem(1)[0],
        scratch_shapes=[
            pltpu.VMEM(onehot.shape, bf16),
            pltpu.VMEM((2, dz_count // 2, parts, rows, share), bf16),
            pltpu.VMEM(back.shape, bf16),
            pltpu.SemaphoreType.DMA((2 + dz_count,)),
        ],
        compiler_params=pltpu.CompilerParams(vmem_limit_bytes=LARGE),
        cost_estimate=cost(4e9, 12 * mib),
        name="gru_grads",
    )(spot, onehot, everyone, back, earlier)


def plain_gru_grads(dx_index, onehot, everyone, back, dz_count):
    units = back.shape[3] // 3
    share = (Z + H) // (2 * dz_count)
    total = 0.0
    for states, x in ((everyone[:, 0], dx_index), (everyone[:, 1], 1 - dx_index)):
        states = states.reshape(-1, dz_count // 2, 2, share)
        states = lax.dynamic_index_in_dim(states, dx_index, 2, keepdims=False)
        ones = lax.dynamic_index_in_dim(onehot, x, 0, keepdims=False)
        left = jnp.concatenate([ones, states.reshape(ones.shape)], axis=1)
        right = lax.dynamic_index_in_dim(back, x, 0, keepdims=False)
        total = total + dot_tn(left, right.reshape(-1, 3 * units))
    grads = total.astype(bf16).reshape(dz_count, share, 3, units)
    return jnp.swapaxes(grads, 1, 2).reshape(dz_count, 3 * share, units)


def run_orthogonal(base, share, own, matrix, earlier):
    side, width = matrix.shape
    return pl.pallas_call(
        functools.partial(orthogonal_block, base, 512),
        out_shape=jax.ShapeDtypeStruct((share, width), bf16),
        in_specs=in_smem(1) + in_vmem(1) + anywhere(len(earlier)),
        out_specs=in_vmem(1)[0],
        scratch_shapes=[
            pltpu.VMEM((side, width), bf16),
            pltpu.VMEM((side, side), bf16),
            pltpu.VMEM((side, side), bf16),
        ],
        compiler_params=pltpu.CompilerParams(vmem_limit_bytes=28 * mib),
        cost_estimate=cost(5e10, 6 * mib),
        name="orthogonal",
    )(own, matrix, *earlier)


def run_turn(matrix):
    return pl.pallas_call(
        functools.partial(turn_block, 256),
        out_shape=jax.ShapeDtypeStruct(matrix.shape[::-1], bf16),
        in_specs=in_vmem(1),
        out_specs=in_vmem(1)[0],
        compiler_params=pltpu.CompilerParams(vmem_limit_bytes=6 * mib),
        cost_estimate=cost(1e6, 3 * mib),
        name="turn",
    )(matrix)


def small_kernel(body, out_shape, scratch, specs, arguments, name):
    return pl.pallas_call(
        body,
        out_shape=out_shape,
        in_specs=specs,
        out_specs=jax.tree.map(lambda _: in_vmem(1)[0], out_shape),
        scratch_shapes=scratch,
        compiler_params=pltpu.CompilerParams(vmem_limit_bytes=8 * mib),
        cost_estimate=cost(1e6, 4 * mib),
        name=name,
    )(*arguments)


def run_collect(spot, pieces, base):
    steps = len(pieces)
    widest, units = pieces[0].shape
    return small_kernel(
        functools.partial(collect_block, base),
        jax.ShapeDtypeStruct((units, steps * widest), bf16),
        [pltpu.VMEM((steps * (widest - base), units), bf16)],
        in_smem(1) + in_vmem(steps),
        (spot, *pieces),
        "collect",
    )


def run_deal(spot, result, steps, base):
    units, width = result.shape
    widest = width // steps
    return small_kernel(
        functools.partial(deal_block, base),
        jax.ShapeDtypeStruct((steps, widest, units), bf16),
        [pltpu.VMEM((steps * (widest - base), units), bf16)],
        in_smem(1) + in_vmem(1),
        (spot, result),
        "deal",
    )


def run_finish(owners, spot, pieces, rows):
    return small_kernel(
        functools.partial(finish_block, owners),
        [jax.ShapeDtypeStruct(block.shape, f32) for block in rows],
        [pltpu.VMEM((len(pieces), *pieces[0].shape), bf16)],
        in_smem(1) + in_vmem(len(pieces) + len(rows)),
        (spot, *pieces, *rows),
        "finish",
    )


def on_device(
    embeddings,
    samples,
    seq_lengths,
    gru_weight,
    post_weight,
    prior_weight,
    gru_moment,
    post_moment,
    prior_moment,
):
    dz_count = lax.axis_size("dz")
    dx_count = lax.axis_size("dx")
    tp_count = lax.axis_size("tp")
    dp_count = dz_count * dx_count
    dx_index = lax.axis_index("dx")
    tp_index = lax.axis_index("tp")
    dp_index = lax.axis_index("dz") * dx_count + dx_index
    seq_count = embeddings.shape[0]
    seqs = seq_count // tp_count
    units = gru_weight.shape[2]
    groups = Z // ZC
    rows = seqs * FRAMES
    packs = rows // PACK

    def gather(block):
        return lax.all_gather(block, "tp", axis=0, tiled=False)

    def exchange(block, axis):
        return lax.all_to_all(block, axis, 0, 0, tiled=True)

    def mine(block, axis):
        return lax.dynamic_index_in_dim(block, dx_index, axis, keepdims=False)

    def across(block, bit):
        return lax.ppermute(block, "tp", [(i, i ^ bit) for i in range(tp_count)])

    own_hidden = gru_weight[:, Z:].astype(bf16)
    far = across(own_hidden, 2)
    near = across(own_hidden, 1)
    gru_input = lax.optimization_barrier(gru_weight)
    head_low = jnp.concatenate([post_weight.astype(bf16), prior_weight.astype(bf16)], axis=0)

    by_part = jnp.swapaxes(samples.reshape(tp_count, seqs, FRAMES, groups), 1, 2)
    by_part = by_part.reshape(tp_count * rows, groups).astype(bf16)

    def one_hot(chosen):
        count = chosen.shape[-1]
        classes = jnp.arange(count * ZC, dtype=jnp.int32)
        expand = (classes[None, :] // ZC == jnp.arange(count)[:, None]).astype(bf16)
        return (dot(chosen, expand) == (classes % ZC).astype(f32)).astype(bf16)

    onehot = one_hot(by_part)
    input_part = jnp.concatenate(
        [dot(onehot, gru_input[k, :Z].astype(bf16)).astype(bf16) for k in range(3)], axis=1
    ).reshape(tp_count, packs, PACK, 3 * units)
    input_part = exchange(input_part, "tp")
    embed_rows = embeddings.reshape(tp_count, rows, E)
    order = np.zeros((rows, rows), np.float32)
    order[np.arange(rows), np.arange(rows) % seqs * FRAMES + np.arange(rows) // seqs] = 1.0
    order = jnp.asarray(order, bf16)
    swap = [(i, i ^ 1) for i in range(dx_count)]
    other = lax.ppermute(by_part, "dx", swap)
    pair_samples = jnp.where(
        dx_index == 0, jnp.stack([by_part, other]), jnp.stack([other, by_part])
    )
    half = Z // dx_count
    pair_half = mine(
        pair_samples.reshape(dx_count * tp_count * rows, dz_count // 2, dx_count, -1), 2
    )
    pair_onehot = one_hot(pair_half.reshape(dx_count * tp_count * rows, groups // dx_count))
    pair_onehot = pair_onehot.reshape(dx_count, tp_count * rows, half)
    onehot = onehot.reshape(tp_count, rows, Z)
    own_target = lax.dynamic_index_in_dim(onehot, tp_index, 0, keepdims=False)
    positions = jnp.arange(FRAMES, dtype=jnp.int32)
    own_lengths = lax.dynamic_slice_in_dim(seq_lengths, tp_index * seqs, seqs, 0)
    frame_mask = (positions[:, None] < own_lengths[None, :]).astype(f32)
    mask_lanes = jnp.broadcast_to(frame_mask.reshape(rows, 1), (rows, 128))

    weights = [own_hidden, near, far, across(far, 1)]
    early = (head_low, own_target, mask_lanes, pair_onehot)
    weights, input_part, early = lax.optimization_barrier((weights, input_part, early))
    head_low, own_target, mask_lanes, pair_onehot = early
    head_full = gather(head_low)
    hidden, factors, rest, turned = run_forward(tp_index.astype(jnp.int32).reshape(1), input_part, weights, seqs)
    hidden = hidden.reshape(rows, H)
    neighbour = lax.ppermute(hidden, "dx", swap)
    backs, direct, loss_lanes = run_heads(
        tp_index.astype(jnp.int32).reshape(1),
        hidden,
        order,
        own_target,
        mask_lanes,
        frame_mask.reshape(1, rows),
        embed_rows,
        head_full,
    )
    everyone = gather(lax.dynamic_update_slice(backs, neighbour[None], (1, 0, 0)))
    back = run_backward(
        direct.reshape(packs, PACK, H), factors, rest, turned, tp_count, seqs, dx_count
    )
    own_back = exchange(back.reshape(dx_count * tp_count, rows, 3 * units), ("dx", "tp"))
    own_back = own_back.reshape(dx_count, tp_count, rows, 3 * units)

    shares = [size // dp_count for size in ROWS]
    all_post = everyone[:, 3]
    spot = jnp.stack([tp_index, dx_index]).astype(jnp.int32)

    head_grad = run_head_grads(spot, order, everyone, embed_rows, back)

    head_grad = jnp.concatenate(
        [
            block.reshape(dz_count, dx_count, -1, units)
            for block in (head_grad[: H + E], head_grad[H + E :])
        ],
        axis=2,
    )

    def share_rows(block):
        return lax.psum_scatter(block, "dz", scatter_dimension=0, tiled=True)[0]

    head_done = share_rows(head_grad)
    if shares[0] % 128 == 0:
        gru_grad = run_gru_grads(
            spot, pair_onehot, everyone, own_back, head_grad, dz_count
        )
    else:
        gru_grad = plain_gru_grads(dx_index, pair_onehot, everyone, own_back, dz_count)
    gru_grad, head_done = lax.optimization_barrier((gru_grad, head_done))
    every_mask = (positions[:, None] < seq_lengths[None, :]).astype(f32)
    frame_count = jnp.broadcast_to(jnp.sum(every_mask), (8, 128))
    frame_count, _ = lax.optimization_barrier((frame_count, gru_grad))
    for axis, bits in (("dx", dx_count), ("dz", dz_count)):
        for bit in range(bits.bit_length() - 1):
            pairs = [(i, i ^ (1 << bit)) for i in range(bits)]
            frame_count = frame_count + lax.ppermute(frame_count, axis, pairs)
    frame_count = frame_count[0, 0]
    scale = (1.0 / frame_count).reshape(1)
    gru_sum = share_rows(gru_grad).astype(f32) * scale[0]
    received = lax.ppermute(
        lax.dynamic_index_in_dim(head_done, 1 - dx_index, 0, keepdims=False), "dx", swap
    )
    head_sum = (mine(head_done, 0).astype(f32) + received.astype(f32)) * scale[0]
    loss_sum = jnp.broadcast_to(jnp.sum(loss_lanes), (8, 128))
    for axis, bits in (("tp", tp_count), ("dx", dx_count), ("dz", dz_count)):
        for bit in range(bits.bit_length() - 1):
            pairs = [(i, i ^ (1 << bit)) for i in range(bits)]
            loss_sum = loss_sum + lax.ppermute(loss_sum, axis, pairs)
    loss_sum = loss_sum[0, 0]
    loss_value = loss_sum / frame_count

    embed_part = E // tp_count
    own_rows_e = lax.dynamic_slice_in_dim(head_full, H + tp_index * embed_part, embed_part, 1)
    post_by_seq = jnp.swapaxes(all_post.reshape(tp_count, FRAMES, seqs, Z), 1, 2)
    embed_grad = jnp.einsum(
        "psfk,ek->psfe",
        post_by_seq,
        jnp.concatenate(list(own_rows_e), axis=1),
        preferred_element_type=f32,
    ).reshape(seq_count, FRAMES, embed_part)
    embed_grad = embed_grad * scale[0]

    grads = [gru_sum[k * shares[0] : (k + 1) * shares[0]] for k in range(3)]
    grads += [head_sum[: shares[3]], head_sum[shares[3] :]]

    def own_rows(matrix, axis_dim):
        share = matrix.shape[axis_dim] // dp_count
        return lax.dynamic_slice_in_dim(matrix, dp_index * share, share, axis_dim)

    gru_moments = own_rows(gru_moment, 1)
    moments = [momentum_keep * gru_moments[k] + grads[k] for k in range(3)]
    moments.append(momentum_keep * own_rows(post_moment, 0) + grads[3])
    moments.append(momentum_keep * own_rows(prior_moment, 0) + grads[4])
    ahead = [(grads[m] + momentum_keep * moments[m]).astype(bf16) for m in range(MATS)]

    owners = [m * dp_count // 8 for m in (0, 3, 4, 7, 5)]
    widest = max(shares)
    base = shares[0]
    holds_post = (dp_index == owners[3]).astype(jnp.int32)
    if dp_count == 8:
        kept = jnp.array([owners.index(d) if d in owners else 0 for d in range(dp_count)])
        blocks = jnp.stack(
            [jnp.pad(block, ((0, widest - block.shape[0]), (0, 0))) for block in ahead]
        )
        where = dp_index.astype(jnp.int32).reshape(1)
        pieces = []
        for step in range(dp_count):
            block = lax.dynamic_index_in_dim(blocks, kept[dp_index ^ step], 0, keepdims=False)
            if step > 0:
                block = lax.ppermute(block, ("dz", "dx"), [(d ^ step, d) for d in owners])
            pieces.append(block)
        turned = run_collect(where, pieces, base)
    else:
        slots = [jnp.zeros((widest, units), bf16)] * dp_count
        for m in range(MATS):
            slots[owners[m]] = jnp.pad(ahead[m], ((0, widest - shares[m]), (0, 0)))
        arrived = exchange(jnp.stack(slots), ("dz", "dx"))
        turned = run_turn(
            jnp.concatenate(
                [arrived[:, :base].reshape(-1, units), arrived[:, base:].reshape(-1, units)], axis=0
            )
        )
    wide = gather(turned).reshape(H, dp_count * widest)
    own = jnp.stack([tp_index, holds_post]).astype(jnp.int32)
    old_rows = (own_rows(gru_weight, 1), own_rows(post_weight, 0), own_rows(prior_weight, 0))
    old_rows = lax.optimization_barrier(old_rows)
    result = run_orthogonal(
        dp_count * base, units, own, wide, (embed_grad, loss_value.reshape(1, 1), *old_rows)
    )
    if dp_count == 8:
        dealt = run_deal(where, result, dp_count, base)
        pieces = [dealt[0]]
        for step in range(1, dp_count):
            pairs = [(d, d ^ step) for d in owners]
            pieces.append(lax.ppermute(dealt[step], ("dz", "dx"), pairs))
        new_gru, new_post, new_prior = run_finish(owners, where, pieces, old_rows)
    else:
        result = result.T
        results = exchange(
            jnp.concatenate(
                [
                    result[: dp_count * base].reshape(dp_count, base, units),
                    result[dp_count * base :].reshape(dp_count, widest - base, units),
                ],
                axis=1,
            ),
            ("dz", "dx"),
        )

        def renew(old, m):
            factor = learn_rate * update_scale * math.sqrt(max(ROWS[m], Z))
            change = results[owners[m], : old.shape[0]].astype(f32)
            return old * (1.0 - learn_rate * weight_decay) - factor * change

        new_gru = jnp.stack([renew(old_rows[0][k], k) for k in range(3)])
        new_post = renew(old_rows[1], 3)
        new_prior = renew(old_rows[2], 4)
    return (
        loss_value,
        embed_grad,
        new_gru,
        new_post,
        new_prior,
        jnp.stack(moments[:3]),
        moments[3],
        moments[4],
    )

def solution(mesh):
    dp_count, tp_count = mesh.devices.shape
    mesh = jax.sharding.Mesh(
        mesh.devices.reshape(dp_count // 2, 2, tp_count), ("dz", "dx", "tp")
    )
    dp = ("dz", "dx")
    in_specs = (
        P(dp, None, None),
        P(dp, None, None),
        P(dp),
        P(None, None, "tp"),
        P(None, "tp"),
        P(None, "tp"),
        P(None, None, "tp"),
        P(None, "tp"),
        P(None, "tp"),
    )
    out_specs = (
        P(),
        P(dp, None, "tp"),
        P(None, dp, "tp"),
        P(dp, "tp"),
        P(dp, "tp"),
        P(None, dp, "tp"),
        P(dp, "tp"),
        P(dp, "tp"),
    )
    return jax.shard_map(
        on_device, mesh=mesh, in_specs=in_specs, out_specs=out_specs, check_vma=False
    )
```

```python
import functools
import math

import jax
import jax.numpy as jnp
import numpy as np
from jax import lax
from jax.experimental import pallas as pl
from jax.experimental.pallas import tpu as pltpu
from jax.sharding import PartitionSpec as P

H = 1024
ZC = 32
E = 1536
FRAMES = 56
MATS = 5
Z = 1024
ROWS = (Z + H, Z + H, Z + H, H + E, H)
PACK = 8
CHUNK = 4
FAR_FIRST = (4, 5, 6, 7, 2, 3, 1, 0)


coeff_linear = 3.4445
coeff_cubic = -4.775
coeff_quintic = 2.0315
momentum_keep = 0.95
learn_rate = 0.2
weight_decay = 0.01
update_scale = 0.2
tiny_value = 1e-07
mib = 1 << 20
LARGE = 56 * mib
f32 = jnp.float32
bf16 = jnp.bfloat16
NT = (((1,), (1,)), ((), ()))
TN = (((0,), (0,)), ((), ()))


def dot(left, right):
    return jnp.dot(left, right, preferred_element_type=f32)


def dot_tn(left, right):
    return lax.dot_general(left, right, TN, preferred_element_type=f32)


def dot_nt(left, right):
    return lax.dot_general(left, right, NT, preferred_element_type=f32)


def copy(source, target, semaphore):
    return pltpu.make_async_copy(source, target, semaphore)


def scan_forward(
    seqs, chunk, spot_ref, x_ref, *refs
):
    parts, packs = x_ref.shape[:2]
    shards = refs[:parts]
    h_ref, k_hbm, u_hbm, t_hbm, state, w, k_ref, u_ref, t, w_sem, k_sem, u_sem, t_sem = refs[parts:]
    units = w.shape[3]
    per_pack = PACK // seqs
    loads = [copy(shards[n], w.at[spot_ref[0] ^ n], w_sem.at[n]) for n in range(parts)]
    for load in loads:
        load.start()
    state[...] = jnp.zeros_like(state)
    for load in loads:
        load.wait()

    def stores(c):
        at = pl.ds(c * chunk, chunk)
        return (
            copy(k_ref.at[:, at], k_hbm.at[:, at], k_sem.at[c]),
            copy(u_ref.at[at], u_hbm.at[at], u_sem.at[c]),
        )

    def pack(i, carry):
        states = []
        for frame in range(per_pack):
            rows = slice(frame * seqs, (frame + 1) * seqs)
            if frame == 0:
                source, live = jnp.maximum(i - 1, 0), jnp.where(i > 0, 1.0, 0.0)
                spot = slice((per_pack - 1) * seqs, per_pack * seqs)
            else:
                source, live = i, None
                spot = slice((frame - 1) * seqs, frame * seqs)
            before = state[...]
            low = before.astype(bf16)
            news = []
            for p in range(parts):
                cols = slice(p * units, (p + 1) * units)
                given = x_ref[p, source].astype(f32)[spot]
                if live is not None:
                    given = given * live
                pre = [
                    given[:, k * units : (k + 1) * units] + dot(low, w[p, k]) for k in range(3)
                ]
                last = before[:, cols]
                r = jax.nn.sigmoid(pre[0])
                c = jnp.tanh(r * pre[1])
                u = jax.nn.sigmoid(pre[2] - 1.0)
                rest = 1.0 - u
                new = u * c + rest * last
                inner = u * (1.0 - c * c)
                state[:, cols] = new
                news.append(new)
                k_ref[0, i, rows, cols] = inner * pre[1] * r * (1.0 - r)
                k_ref[1, i, rows, cols] = inner * r
                k_ref[2, i, rows, cols] = (c - last) * u * rest
                u_ref[i, rows, cols] = rest
            states.append(jnp.concatenate(news, axis=1))
        h_ref[i] = jnp.concatenate(states, axis=0).astype(bf16)

        @pl.when(i % chunk == chunk - 1)
        def _():
            for store in stores(i // chunk):
                store.start()

        return carry

    def pack_and_turn(i, carry):
        t[pl.ds(pl.multiple_of(i * units, units), units), :] = w[i // 3, i % 3].T
        return pack(i, carry)

    lax.fori_loop(0, 3 * parts, pack_and_turn, 0)
    turned = copy(t, t_hbm, t_sem)
    turned.start()
    lax.fori_loop(3 * parts, packs, pack, 0)
    turned.wait()
    for c in range(packs // chunk):
        for store in stores(c):
            store.wait()


def scan_backward(
    seqs, chunk, d_ref, k_hbm, u_hbm, t_hbm, b_hbm, now, kept, w, k_ref, u_ref, b_ref, t_sem, k_sem, u_sem, b_sem
):
    copies, parts, packs = b_hbm.shape[:3]
    units = b_ref.shape[3] // 3
    per_pack = PACK // seqs
    chunks = packs // chunk

    def loads(c):
        at = pl.ds(c * chunk, chunk)
        return (
            copy(k_hbm.at[:, at], k_ref.at[:, at], k_sem.at[c]),
            copy(u_hbm.at[at], u_ref.at[at], u_sem.at[c]),
        )

    def stores(c):
        at = pl.ds(c * chunk, chunk)
        return [
            copy(b_ref.at[:, at], b_hbm.at[n, :, at], b_sem.at[n * chunks + c]) for n in range(copies)
        ]

    turned = copy(t_hbm, w, t_sem)
    turned.start()
    for c in reversed(range(chunks)):
        for load in loads(c):
            load.start()
    now[...] = jnp.zeros_like(now)
    kept[...] = jnp.zeros_like(kept)
    turned.wait()

    def pack(n, carry):
        i = packs - 1 - n

        @pl.when(i % chunk == chunk - 1)
        def _():
            for load in loads(i // chunk):
                load.wait()

        later = [None] * per_pack
        for frame in reversed(range(per_pack)):
            rows = slice(frame * seqs, (frame + 1) * seqs)
            values = now[...]
            later[frame] = values
            dh = d_ref[i, rows] + kept[...] + dot(values.astype(bf16), w[...])
            kept[...] = dh * u_ref[i, rows]
            for p in range(parts):
                cols = slice(p * units, (p + 1) * units)
                for k in range(3):
                    spot = slice((3 * p + k) * units, (3 * p + k + 1) * units)
                    now[:, spot] = dh[:, cols] * k_ref[k, i, rows, cols]
        stacked = jnp.concatenate(later, axis=0).astype(bf16)
        for p in range(parts):
            b_ref[p, i] = stacked[:, p * 3 * units : (p + 1) * 3 * units]

        @pl.when(i % chunk == 0)
        def _():
            for store in stores(i // chunk):
                store.start()

        return carry

    lax.fori_loop(0, packs, pack, 0)
    for c in range(chunks):
        for store in stores(c):
            store.wait()


def head_block(
    spot_ref, h_ref, p_ref, t_ref, m_ref, r_ref, e_hbm, w_hbm, back_ref, d_ref, loss_ref, w_ref, n_ref, e_ref, w_sem, e_sem
):
    parts = w_ref.shape[0]
    embed = copy(e_hbm.at[spot_ref[0]], n_ref, e_sem)
    embed.start()
    loads = [copy(w_hbm.at[p], w_ref.at[p], w_sem.at[p]) for p in range(parts)]
    for load in loads:
        load.start()
    embed.wait()
    e_ref[...] = dot(p_ref[...], n_ref[...]).astype(bf16)
    units = w_ref.shape[2]
    rows = h_ref.shape[0]
    low = h_ref[...]
    back_ref[0] = low
    mask = m_ref[...]
    given = jnp.zeros((rows, 128), f32)
    normal = jnp.zeros((1, rows), f32)
    for p in range(parts):
        loads[p].wait()
        post = dot(low, w_ref[p, :H]) + dot(e_ref[...], w_ref[p, H : H + E])
        prior = dot(low, w_ref[p, H + E :])
        for head, logits in enumerate((prior, post)):
            for piece in range(units // 128):
                l = logits[:, piece * 128 : (piece + 1) * 128]
                cols = slice(p * units + piece * 128, p * units + (piece + 1) * 128)
                target = t_ref[:, cols].astype(f32)
                turned = l.T.reshape(128 // ZC, ZC, rows)
                top = jnp.max(turned, axis=1, keepdims=True)
                e = jnp.exp(turned - top)
                total = jnp.sum(e, axis=1, keepdims=True)
                normal = normal + jnp.sum(top + jnp.log(total), axis=0)
                probs = (e * (1.0 / total)).reshape(128, rows).T
                given = given + target * l
                back_ref[head + 2, :, cols] = (mask * (probs - target)).astype(bf16)
    loss_ref[...] = jnp.sum(r_ref[...] * normal, axis=1, keepdims=True) - jnp.sum(
        jnp.sum(mask * given, axis=0, keepdims=True), axis=1, keepdims=True
    )
    direct = jnp.zeros((rows, H), f32)
    for p in range(parts):
        cols = slice(p * units, (p + 1) * units)
        direct = direct + dot_nt(back_ref[2, :, cols], w_ref[p, H + E :])
        direct = direct + dot_nt(back_ref[3, :, cols], w_ref[p, :H])
    d_ref[...] = direct


def head_grads(spot_ref, scale_ref, p_ref, r_hbm, e_hbm, earlier_ref, o_ref, h_ref, r_ref, e_ref, sems):
    parts, rows = e_ref.shape[0], e_ref.shape[1]
    units = o_ref.shape[1]
    frames = parts * rows
    scale = scale_ref[0]
    own = pl.ds(pl.multiple_of(spot_ref[0] * units, units), units)
    loads = [
        copy(r_hbm.at[:, pl.ds(2, 2), :, own], r_ref, sems.at[0]),
        copy(r_hbm.at[:, 0], h_ref, sems.at[1]),
        copy(e_hbm, e_ref, sems.at[2]),
    ]
    for load in loads:
        load.start()
    loads[0].wait()
    loads[1].wait()
    post = r_ref[:, 1].reshape(frames, units)
    both = jnp.concatenate([post, r_ref[:, 0].reshape(frames, units)], axis=1)
    for m in range(H // 256):
        spot = slice(m * 256, (m + 1) * 256)
        grad = (dot_tn(h_ref[:, :, spot].reshape(frames, 256), both) * scale).astype(bf16)
        o_ref[m * 256 : (m + 1) * 256] = grad[:, :units]
        o_ref[H + E + m * 256 : H + E + (m + 1) * 256] = grad[:, units:]
    post = jnp.concatenate(
        [dot_tn(p_ref[...], r_ref[p, 1]).astype(bf16) for p in range(parts)], axis=0
    )
    loads[2].wait()
    for m in range(E // 256):
        spot = slice(m * 256, (m + 1) * 256)
        grad = (dot_tn(e_ref[:, :, spot].reshape(frames, 256), post) * scale).astype(bf16)
        o_ref[H + m * 256 : H + (m + 1) * 256] = grad


def gru_grads(
    spot_ref, scale_ref, one_hbm, r_hbm, b_hbm, earlier_ref, o_ref, one_ref, l_ref, b_ref, sems
):
    parts, rows = b_ref.shape[1], b_ref.shape[2]
    units = o_ref.shape[2]
    frames = parts * rows
    share = o_ref.shape[1] // 3
    half = o_ref.shape[0] // 2
    scale = scale_ref[0]
    me = spot_ref[1]
    loads = [copy(b_hbm, b_ref, sems.at[0]), copy(one_hbm, one_ref, sems.at[1])]
    for z in range(half):
        spot = pl.ds(pl.multiple_of((z * 2 + me) * share, share), share)
        loads.append(copy(r_hbm.at[:, 0, :, spot], l_ref.at[0, z], sems.at[2 + 2 * z]))
        loads.append(copy(r_hbm.at[:, 1, :, spot], l_ref.at[1, z], sems.at[3 + 2 * z]))
    for load in loads:
        load.start()
    loads[0].wait()
    loads[1].wait()
    back = [b_ref[x].reshape(frames, 3 * units) for x in (me, 1 - me)]
    for z in range(2 * half):
        if z < half:
            spot = slice(z * share, (z + 1) * share)
            left = [one_ref[x, :, spot] for x in (me, 1 - me)]
        else:
            loads[2 * (z - half) + 2].wait()
            loads[2 * (z - half) + 3].wait()
            left = [l_ref[n, z - half].reshape(frames, share) for n in (0, 1)]
        grad = (dot_tn(left[0], back[0]) + dot_tn(left[1], back[1])) * scale
        grad = grad.astype(bf16)
        for k in range(3):
            o_ref[z, k * share : (k + 1) * share] = grad[:, k * units : (k + 1) * units]


def orthogonal_block(base, tile, own_ref, g_ref, *refs):
    o_ref, x, a, b = refs[-4:]
    side, width = g_ref.shape
    share = o_ref.shape[0]
    own = pl.ds(pl.multiple_of(own_ref[0] * share, share), share)
    wide = own_ref[1] > 0

    def either(run):
        pl.when(wide)(functools.partial(run, width))
        pl.when(jnp.logical_not(wide))(functools.partial(run, base))

    def squares(i, total):
        rows = pl.ds(pl.multiple_of(i * 128, 128), 128)
        v = g_ref[rows, :].astype(f32)
        return total + jnp.sum(v * v)

    total = lax.fori_loop(0, side // 128, squares, jnp.zeros((), f32))
    scale = 1.0 / (jnp.sqrt(jnp.full((1, 128), total, f32)) + tiny_value)
    scale = scale[:, :1]

    def shrink(i, carry):
        rows = pl.ds(pl.multiple_of(i * 128, 128), 128)
        x[rows, :] = (g_ref[rows, :].astype(f32) * scale).astype(bf16)
        return carry

    lax.fori_loop(0, side // 128, shrink, 0)

    def lower(out, product):
        for start in range(0, side, 256):
            stop = start + 256
            block = product(slice(start, side), slice(start, stop)).astype(bf16)
            out[start:, start:stop] = block
            if stop < side:
                out[start:stop, stop:] = block[256:].T

    def square(depth):
        lower(a, lambda rows, cols: dot_nt(x[rows, :depth], x[cols, :depth]))

    def mix():
        lower(
            b,
            lambda rows, cols: coeff_cubic * a[rows, cols].astype(f32)
            + coeff_quintic * dot(a[rows, :], a[:, cols]),
        )

    def renew_all(depth):
        for start in range(0, depth, tile):
            cols = slice(start, start + tile)
            x[:, cols] = (
                coeff_linear * x[:, cols].astype(f32) + dot(b[...], x[:, cols])
            ).astype(bf16)

    def sweep(s, carry):
        either(square)
        mix()
        either(renew_all)
        return carry

    lax.fori_loop(0, 4, sweep, 0)
    either(square)
    part = (coeff_cubic * a[own, :].astype(f32) + coeff_quintic * dot(a[own, :], a[...])).astype(bf16)

    def last(j, carry):
        cols = pl.ds(pl.multiple_of(j * tile, tile), tile)
        o_ref[:, cols] = (
            coeff_linear * x[own, cols].astype(f32) + dot(part, x[:, cols])
        ).astype(bf16)
        return carry

    lax.fori_loop(0, width // tile, last, 0)


def turn_block(tile, g_ref, o_ref):
    def block(i, carry):
        spot = pl.ds(pl.multiple_of(i * tile, tile), tile)
        o_ref[:, spot] = g_ref[spot, :].T
        return carry

    lax.fori_loop(0, g_ref.shape[0] // tile, block, 0)


def collect_block(base, spot_ref, *refs):
    *pieces, o_ref, rows = refs
    steps = len(pieces)
    more = pieces[0].shape[0] - base
    for step, piece in enumerate(pieces):
        d = spot_ref[0] ^ step
        o_ref[:, pl.ds(pl.multiple_of(d * base, base), base)] = piece[:base].T
        rows[pl.ds(pl.multiple_of(d * more, more), more), :] = piece[base:]
    o_ref[:, steps * base :] = rows[...].T


def deal_block(base, spot_ref, g_ref, o_ref, rows):
    steps, widest = o_ref.shape[:2]
    more = widest - base
    rows[...] = g_ref[:, steps * base :].T
    for step in range(steps):
        d = spot_ref[0] ^ step
        o_ref[step, :base] = g_ref[:, pl.ds(pl.multiple_of(d * base, base), base)].T
        o_ref[step, base:] = rows[pl.ds(pl.multiple_of(d * more, more), more), :]


def finish_block(owners, spot_ref, *refs):
    pieces, (gru_ref, post_ref, prior_ref), (gru_out, post_out, prior_out), all_ref = (
        refs[:-7],
        refs[-7:-4],
        refs[-4:-1],
        refs[-1],
    )
    for step, piece in enumerate(pieces):
        all_ref[step] = piece[...]

    def renewed(old, m):
        change = all_ref[spot_ref[0] ^ owners[m], : old.shape[0]].astype(f32)
        factor = learn_rate * update_scale * math.sqrt(max(ROWS[m], Z))
        return old * (1.0 - learn_rate * weight_decay) - factor * change

    for k in range(3):
        gru_out[k] = renewed(gru_ref[k], k)
    post_out[...] = renewed(post_ref[...], 3)
    prior_out[...] = renewed(prior_ref[...], 4)


def in_vmem(count):
    return [pl.BlockSpec(memory_space=pltpu.VMEM)] * count


def cost(flops, touched):
    return pl.CostEstimate(flops=int(flops), bytes_accessed=int(touched), transcendentals=0)


def run_forward(spot, inputs, weights, seqs):
    parts, packs = inputs.shape[:2]
    units = weights[0].shape[2]
    chunks = packs // CHUNK
    return pl.pallas_call(
        functools.partial(scan_forward, seqs, CHUNK),
        out_shape=[
            jax.ShapeDtypeStruct((packs, PACK, H), bf16),
            jax.ShapeDtypeStruct((3, packs, PACK, H), f32),
            jax.ShapeDtypeStruct((packs, PACK, H), f32),
            jax.ShapeDtypeStruct((3 * H, H), bf16),
        ],
        in_specs=in_smem(1) + in_vmem(1) + anywhere(parts),
        out_specs=in_vmem(1) + anywhere(3),
        scratch_shapes=[
            pltpu.VMEM((seqs, H), f32),
            pltpu.VMEM((parts, 3, H, units), bf16),
            pltpu.VMEM((3, packs, PACK, H), f32),
            pltpu.VMEM((packs, PACK, H), f32),
            pltpu.VMEM((3 * H, H), bf16),
            pltpu.SemaphoreType.DMA((parts,)),
            pltpu.SemaphoreType.DMA((chunks,)),
            pltpu.SemaphoreType.DMA((chunks,)),
            pltpu.SemaphoreType.DMA,
        ],
        compiler_params=pltpu.CompilerParams(vmem_limit_bytes=LARGE),
        cost_estimate=cost(6e10, 20 * mib),
        name="scan_forward",
    )(spot, inputs, *weights)


def run_backward(direct, factors, rest, turned, parts, seqs, copies):
    packs = direct.shape[0]
    units = H // parts
    chunks = packs // CHUNK
    return pl.pallas_call(
        functools.partial(scan_backward, seqs, CHUNK),
        out_shape=jax.ShapeDtypeStruct((copies, parts, packs, PACK, 3 * units), bf16),
        in_specs=in_vmem(1) + anywhere(3),
        out_specs=anywhere(1)[0],
        scratch_shapes=[
            pltpu.VMEM((seqs, 3 * H), f32),
            pltpu.VMEM((seqs, H), f32),
            pltpu.VMEM((3 * H, H), bf16),
            pltpu.VMEM((3, packs, PACK, H), f32),
            pltpu.VMEM((packs, PACK, H), f32),
            pltpu.VMEM((parts, packs, PACK, 3 * units), bf16),
            pltpu.SemaphoreType.DMA,
            pltpu.SemaphoreType.DMA((chunks,)),
            pltpu.SemaphoreType.DMA((chunks,)),
            pltpu.SemaphoreType.DMA((copies * chunks,)),
        ],
        compiler_params=pltpu.CompilerParams(vmem_limit_bytes=LARGE),
        cost_estimate=cost(6e10, 20 * mib),
        name="scan_backward",
    )(direct, factors, rest, turned)


def run_heads(spot, hidden, order, target, mask, mask_row, embed, weights):
    rows = hidden.shape[0]
    return pl.pallas_call(
        head_block,
        out_shape=[
            jax.ShapeDtypeStruct((4, rows, Z), bf16),
            jax.ShapeDtypeStruct((rows, H), f32),
            jax.ShapeDtypeStruct((1, 1), f32),
        ],
        in_specs=in_smem(1) + in_vmem(5) + anywhere(2),
        out_specs=in_vmem(3),
        scratch_shapes=[
            pltpu.VMEM(weights.shape, bf16),
            pltpu.VMEM((rows, E), bf16),
            pltpu.VMEM((rows, E), bf16),
            pltpu.SemaphoreType.DMA((weights.shape[0],)),
            pltpu.SemaphoreType.DMA,
        ],
        compiler_params=pltpu.CompilerParams(vmem_limit_bytes=LARGE),
        cost_estimate=cost(1e10, 12 * mib),
        name="heads",
    )(spot, hidden, order, target, mask, mask_row, embed, weights)


def in_smem(count):
    return [pl.BlockSpec(memory_space=pltpu.SMEM)] * count


def anywhere(count):
    return [pl.BlockSpec(memory_space=pl.ANY)] * count


def run_head_grads(spot, scale, order, everyone, embed, earlier):
    parts, rows = embed.shape[:2]
    units = H // parts
    return pl.pallas_call(
        head_grads,
        out_shape=jax.ShapeDtypeStruct((H + E + H, units), bf16),
        in_specs=in_smem(2) + in_vmem(1) + anywhere(3),
        out_specs=in_vmem(1)[0],
        scratch_shapes=[
            pltpu.VMEM((parts, rows, H), bf16),
            pltpu.VMEM((parts, 2, rows, units), bf16),
            pltpu.VMEM(embed.shape, bf16),
            pltpu.SemaphoreType.DMA((3,)),
        ],
        compiler_params=pltpu.CompilerParams(vmem_limit_bytes=LARGE),
        cost_estimate=cost(4e9, 12 * mib),
        name="head_grads",
    )(spot, scale, order, everyone, embed, earlier)


def run_gru_grads(spot, scale, onehot, everyone, back, earlier, dz_count):
    parts, rows = back.shape[1:3]
    units = back.shape[3] // 3
    share = (Z + H) // (2 * dz_count)
    return pl.pallas_call(
        gru_grads,
        out_shape=jax.ShapeDtypeStruct((dz_count, 3 * share, units), bf16),
        in_specs=in_smem(2) + anywhere(4),
        out_specs=in_vmem(1)[0],
        scratch_shapes=[
            pltpu.VMEM(onehot.shape, bf16),
            pltpu.VMEM((2, dz_count // 2, parts, rows, share), bf16),
            pltpu.VMEM(back.shape, bf16),
            pltpu.SemaphoreType.DMA((2 + dz_count,)),
        ],
        compiler_params=pltpu.CompilerParams(vmem_limit_bytes=LARGE),
        cost_estimate=cost(4e9, 12 * mib),
        name="gru_grads",
    )(spot, scale, onehot, everyone, back, earlier)


def plain_gru_grads(dx_index, scale, onehot, everyone, back, dz_count):
    units = back.shape[3] // 3
    share = (Z + H) // (2 * dz_count)
    total = 0.0
    for states, x in ((everyone[:, 0], dx_index), (everyone[:, 1], 1 - dx_index)):
        states = states.reshape(-1, dz_count // 2, 2, share)
        states = lax.dynamic_index_in_dim(states, dx_index, 2, keepdims=False)
        ones = lax.dynamic_index_in_dim(onehot, x, 0, keepdims=False)
        left = jnp.concatenate([ones, states.reshape(ones.shape)], axis=1)
        right = lax.dynamic_index_in_dim(back, x, 0, keepdims=False)
        total = total + dot_tn(left, right.reshape(-1, 3 * units))
    grads = (total * scale).astype(bf16).reshape(dz_count, share, 3, units)
    return jnp.swapaxes(grads, 1, 2).reshape(dz_count, 3 * share, units)


def run_orthogonal(base, share, own, matrix, earlier):
    side, width = matrix.shape
    return pl.pallas_call(
        functools.partial(orthogonal_block, base, 512),
        out_shape=jax.ShapeDtypeStruct((share, width), bf16),
        in_specs=in_smem(1) + in_vmem(1) + anywhere(len(earlier)),
        out_specs=in_vmem(1)[0],
        scratch_shapes=[
            pltpu.VMEM((side, width), bf16),
            pltpu.VMEM((side, side), bf16),
            pltpu.VMEM((side, side), bf16),
        ],
        compiler_params=pltpu.CompilerParams(vmem_limit_bytes=28 * mib),
        cost_estimate=cost(5e10, 6 * mib),
        name="orthogonal",
    )(own, matrix, *earlier)


def run_turn(matrix):
    return pl.pallas_call(
        functools.partial(turn_block, 256),
        out_shape=jax.ShapeDtypeStruct(matrix.shape[::-1], bf16),
        in_specs=in_vmem(1),
        out_specs=in_vmem(1)[0],
        compiler_params=pltpu.CompilerParams(vmem_limit_bytes=6 * mib),
        cost_estimate=cost(1e6, 3 * mib),
        name="turn",
    )(matrix)


def small_kernel(body, out_shape, scratch, specs, arguments, name):
    return pl.pallas_call(
        body,
        out_shape=out_shape,
        in_specs=specs,
        out_specs=jax.tree.map(lambda _: in_vmem(1)[0], out_shape),
        scratch_shapes=scratch,
        compiler_params=pltpu.CompilerParams(vmem_limit_bytes=8 * mib),
        cost_estimate=cost(1e6, 4 * mib),
        name=name,
    )(*arguments)


def run_collect(spot, pieces, base):
    steps = len(pieces)
    widest, units = pieces[0].shape
    return small_kernel(
        functools.partial(collect_block, base),
        jax.ShapeDtypeStruct((units, steps * widest), bf16),
        [pltpu.VMEM((steps * (widest - base), units), bf16)],
        in_smem(1) + in_vmem(steps),
        (spot, *pieces),
        "collect",
    )


def run_deal(spot, result, steps, base):
    units, width = result.shape
    widest = width // steps
    return small_kernel(
        functools.partial(deal_block, base),
        jax.ShapeDtypeStruct((steps, widest, units), bf16),
        [pltpu.VMEM((steps * (widest - base), units), bf16)],
        in_smem(1) + in_vmem(1),
        (spot, result),
        "deal",
    )


def run_finish(owners, spot, pieces, rows):
    return small_kernel(
        functools.partial(finish_block, owners),
        [jax.ShapeDtypeStruct(block.shape, f32) for block in rows],
        [pltpu.VMEM((len(pieces), *pieces[0].shape), bf16)],
        in_smem(1) + in_vmem(len(pieces) + len(rows)),
        (spot, *pieces, *rows),
        "finish",
    )


def on_device(
    embeddings,
    samples,
    seq_lengths,
    gru_weight,
    post_weight,
    prior_weight,
    gru_moment,
    post_moment,
    prior_moment,
):
    dz_count = lax.axis_size("dz")
    dx_count = lax.axis_size("dx")
    tp_count = lax.axis_size("tp")
    dp_count = dz_count * dx_count
    dx_index = lax.axis_index("dx")
    tp_index = lax.axis_index("tp")
    dp_index = lax.axis_index("dz") * dx_count + dx_index
    seq_count = embeddings.shape[0]
    seqs = seq_count // tp_count
    units = gru_weight.shape[2]
    groups = Z // ZC
    rows = seqs * FRAMES
    packs = rows // PACK

    def gather(block):
        return lax.all_gather(block, "tp", axis=0, tiled=False)

    def exchange(block, axis):
        return lax.all_to_all(block, axis, 0, 0, tiled=True)

    def mine(block, axis):
        return lax.dynamic_index_in_dim(block, dx_index, axis, keepdims=False)

    def across(block, bit):
        return lax.ppermute(block, "tp", [(i, i ^ bit) for i in range(tp_count)])

    own_hidden = gru_weight[:, Z:].astype(bf16)
    far = across(own_hidden, 2)
    near = across(own_hidden, 1)
    gru_input = lax.optimization_barrier(gru_weight)
    head_low = jnp.concatenate([post_weight.astype(bf16), prior_weight.astype(bf16)], axis=0)

    by_part = jnp.swapaxes(samples.reshape(tp_count, seqs, FRAMES, groups), 1, 2)
    by_part = by_part.reshape(tp_count * rows, groups).astype(bf16)

    def one_hot(chosen):
        count = chosen.shape[-1]
        classes = jnp.arange(count * ZC, dtype=jnp.int32)
        expand = (classes[None, :] // ZC == jnp.arange(count)[:, None]).astype(bf16)
        return (dot(chosen, expand) == (classes % ZC).astype(f32)).astype(bf16)

    onehot = one_hot(by_part)
    input_part = jnp.concatenate(
        [dot(onehot, gru_input[k, :Z].astype(bf16)).astype(bf16) for k in range(3)], axis=1
    ).reshape(tp_count, packs, PACK, 3 * units)
    input_part = exchange(input_part, "tp")
    embed_rows = embeddings.reshape(tp_count, rows, E)
    order = np.zeros((rows, rows), np.float32)
    order[np.arange(rows), np.arange(rows) % seqs * FRAMES + np.arange(rows) // seqs] = 1.0
    order = jnp.asarray(order, bf16)
    swap = [(i, i ^ 1) for i in range(dx_count)]
    other = lax.ppermute(by_part, "dx", swap)
    pair_samples = jnp.where(
        dx_index == 0, jnp.stack([by_part, other]), jnp.stack([other, by_part])
    )
    half = Z // dx_count
    pair_half = mine(
        pair_samples.reshape(dx_count * tp_count * rows, dz_count // 2, dx_count, -1), 2
    )
    pair_onehot = one_hot(pair_half.reshape(dx_count * tp_count * rows, groups // dx_count))
    pair_onehot = pair_onehot.reshape(dx_count, tp_count * rows, half)
    onehot = onehot.reshape(tp_count, rows, Z)
    own_target = lax.dynamic_index_in_dim(onehot, tp_index, 0, keepdims=False)
    positions = jnp.arange(FRAMES, dtype=jnp.int32)
    own_lengths = lax.dynamic_slice_in_dim(seq_lengths, tp_index * seqs, seqs, 0)
    frame_mask = (positions[:, None] < own_lengths[None, :]).astype(f32)
    mask_lanes = jnp.broadcast_to(frame_mask.reshape(rows, 1), (rows, 128))

    weights = [own_hidden, near, far, across(far, 1)]
    every_mask = (positions[:, None] < seq_lengths[None, :]).astype(f32)
    frame_count = jnp.broadcast_to(jnp.sum(every_mask), (8, 128))
    for axis, bits in (("dx", dx_count), ("dz", dz_count)):
        for bit in range(bits.bit_length() - 1):
            pairs = [(i, i ^ (1 << bit)) for i in range(bits)]
            frame_count = frame_count + lax.ppermute(frame_count, axis, pairs)
    frame_count = frame_count[0, 0]
    scale = (1.0 / frame_count).reshape(1)

    early = (head_low, own_target, mask_lanes, pair_onehot, scale)
    weights, input_part, early = lax.optimization_barrier((weights, input_part, early))
    head_low, own_target, mask_lanes, pair_onehot, scale = early
    head_full = gather(head_low)
    hidden, factors, rest, turned = run_forward(tp_index.astype(jnp.int32).reshape(1), input_part, weights, seqs)
    hidden = hidden.reshape(rows, H)
    neighbour = lax.ppermute(hidden, "dx", swap)
    backs, direct, loss_lanes = run_heads(
        tp_index.astype(jnp.int32).reshape(1),
        hidden,
        order,
        own_target,
        mask_lanes,
        frame_mask.reshape(1, rows),
        embed_rows,
        head_full,
    )
    everyone = gather(lax.dynamic_update_slice(backs, neighbour[None], (1, 0, 0)))
    back = run_backward(
        direct.reshape(packs, PACK, H), factors, rest, turned, tp_count, seqs, dx_count
    )
    own_back = exchange(back.reshape(dx_count * tp_count, rows, 3 * units), ("dx", "tp"))
    own_back = own_back.reshape(dx_count, tp_count, rows, 3 * units)

    shares = [size // dp_count for size in ROWS]
    all_post = everyone[:, 3]
    spot = jnp.stack([tp_index, dx_index]).astype(jnp.int32)

    head_grad = run_head_grads(spot, scale, order, everyone, embed_rows, back)

    head_grad = jnp.concatenate(
        [
            block.reshape(dz_count, dx_count, -1, units)
            for block in (head_grad[: H + E], head_grad[H + E :])
        ],
        axis=2,
    )

    def share_rows(block):
        return lax.psum_scatter(block, "dz", scatter_dimension=0, tiled=True)[0]

    head_done = share_rows(head_grad)
    if shares[0] % 128 == 0:
        gru_grad = run_gru_grads(
            spot, scale, pair_onehot, everyone, own_back, head_grad, dz_count
        )
    else:
        gru_grad = plain_gru_grads(dx_index, scale, pair_onehot, everyone, own_back, dz_count)
    gru_grad, head_done = lax.optimization_barrier((gru_grad, head_done))
    gru_sum = share_rows(gru_grad).astype(f32)
    received = lax.ppermute(
        lax.dynamic_index_in_dim(head_done, 1 - dx_index, 0, keepdims=False), "dx", swap
    )
    head_sum = mine(head_done, 0).astype(f32) + received.astype(f32)
    loss_sum = jnp.broadcast_to(jnp.sum(loss_lanes), (8, 128))
    for axis, bits in (("tp", tp_count), ("dx", dx_count), ("dz", dz_count)):
        for bit in range(bits.bit_length() - 1):
            pairs = [(i, i ^ (1 << bit)) for i in range(bits)]
            loss_sum = loss_sum + lax.ppermute(loss_sum, axis, pairs)
    loss_sum = loss_sum[0, 0]
    loss_value = loss_sum / frame_count

    embed_part = E // tp_count
    own_rows_e = lax.dynamic_slice_in_dim(head_full, H + tp_index * embed_part, embed_part, 1)
    post_by_seq = jnp.swapaxes(all_post.reshape(tp_count, FRAMES, seqs, Z), 1, 2)
    embed_grad = jnp.einsum(
        "psfk,ek->psfe",
        post_by_seq,
        jnp.concatenate(list(own_rows_e), axis=1),
        preferred_element_type=f32,
    ).reshape(seq_count, FRAMES, embed_part)
    embed_grad = embed_grad * scale[0]

    grads = [gru_sum[k * shares[0] : (k + 1) * shares[0]] for k in range(3)]
    grads += [head_sum[: shares[3]], head_sum[shares[3] :]]

    def own_rows(matrix, axis_dim):
        share = matrix.shape[axis_dim] // dp_count
        return lax.dynamic_slice_in_dim(matrix, dp_index * share, share, axis_dim)

    gru_moments = own_rows(gru_moment, 1)
    moments = [momentum_keep * gru_moments[k] + grads[k] for k in range(3)]
    moments.append(momentum_keep * own_rows(post_moment, 0) + grads[3])
    moments.append(momentum_keep * own_rows(prior_moment, 0) + grads[4])
    ahead = [(grads[m] + momentum_keep * moments[m]).astype(bf16) for m in range(MATS)]

    owners = [m * dp_count // 8 for m in (0, 3, 4, 7, 5)]
    widest = max(shares)
    base = shares[0]
    holds_post = (dp_index == owners[3]).astype(jnp.int32)
    if dp_count == 8:
        kept = jnp.array([owners.index(d) if d in owners else 0 for d in range(dp_count)])
        blocks = jnp.stack(
            [jnp.pad(block, ((0, widest - block.shape[0]), (0, 0))) for block in ahead]
        )
        where = dp_index.astype(jnp.int32).reshape(1)
        pieces = [None] * dp_count
        for step in FAR_FIRST:
            block = lax.dynamic_index_in_dim(blocks, kept[dp_index ^ step], 0, keepdims=False)
            if step > 0:
                block = lax.ppermute(block, ("dz", "dx"), [(d ^ step, d) for d in owners])
            pieces[step] = block
        turned = run_collect(where, pieces, base)
    else:
        slots = [jnp.zeros((widest, units), bf16)] * dp_count
        for m in range(MATS):
            slots[owners[m]] = jnp.pad(ahead[m], ((0, widest - shares[m]), (0, 0)))
        arrived = exchange(jnp.stack(slots), ("dz", "dx"))
        turned = run_turn(
            jnp.concatenate(
                [arrived[:, :base].reshape(-1, units), arrived[:, base:].reshape(-1, units)], axis=0
            )
        )
    wide = gather(turned).reshape(H, dp_count * widest)
    own = jnp.stack([tp_index, holds_post]).astype(jnp.int32)
    old_rows = (own_rows(gru_weight, 1), own_rows(post_weight, 0), own_rows(prior_weight, 0))
    old_rows = lax.optimization_barrier(old_rows)
    result = run_orthogonal(
        dp_count * base, units, own, wide, (embed_grad, loss_value.reshape(1, 1), *old_rows)
    )
    if dp_count == 8:
        dealt = run_deal(where, result, dp_count, base)
        pieces = [dealt[0]] * dp_count
        for step in FAR_FIRST[:-1]:
            pairs = [(d, d ^ step) for d in owners]
            pieces[step] = lax.ppermute(dealt[step], ("dz", "dx"), pairs)
        new_gru, new_post, new_prior = run_finish(owners, where, pieces, old_rows)
    else:
        result = result.T
        results = exchange(
            jnp.concatenate(
                [
                    result[: dp_count * base].reshape(dp_count, base, units),
                    result[dp_count * base :].reshape(dp_count, widest - base, units),
                ],
                axis=1,
            ),
            ("dz", "dx"),
        )

        def renew(old, m):
            factor = learn_rate * update_scale * math.sqrt(max(ROWS[m], Z))
            change = results[owners[m], : old.shape[0]].astype(f32)
            return old * (1.0 - learn_rate * weight_decay) - factor * change

        new_gru = jnp.stack([renew(old_rows[0][k], k) for k in range(3)])
        new_post = renew(old_rows[1], 3)
        new_prior = renew(old_rows[2], 4)
    return (
        loss_value,
        embed_grad,
        new_gru,
        new_post,
        new_prior,
        jnp.stack(moments[:3]),
        moments[3],
        moments[4],
    )

def solution(mesh):
    dp_count, tp_count = mesh.devices.shape
    mesh = jax.sharding.Mesh(
        mesh.devices.reshape(dp_count // 2, 2, tp_count), ("dz", "dx", "tp")
    )
    dp = ("dz", "dx")
    in_specs = (
        P(dp, None, None),
        P(dp, None, None),
        P(dp),
        P(None, None, "tp"),
        P(None, "tp"),
        P(None, "tp"),
        P(None, None, "tp"),
        P(None, "tp"),
        P(None, "tp"),
    )
    out_specs = (
        P(),
        P(dp, None, "tp"),
        P(None, dp, "tp"),
        P(dp, "tp"),
        P(dp, "tp"),
        P(None, dp, "tp"),
        P(dp, "tp"),
        P(dp, "tp"),
    )
    return jax.shard_map(
        on_device, mesh=mesh, in_specs=in_specs, out_specs=out_specs, check_vma=False
    )
```
